32 devices in a mesh: group: 2 (over y), dp: 8 (over z, x), tensor: 2 (over core).
Axes of the slice: x: 2, y: 2, z: 4, core: 2. Of those that a mesh axis runs over, the one named last changes fastest.
Arguments:
- activations: bfloat16 [2048, 8192], P(('group', 'dp'), 'tensor'), parts along dimension 0, may hold values from -6 to 6
- cotangent: bfloat16 [2048, 8192], P(('group', 'dp'), 'tensor'), parts along dimension 0, may hold values from -6 to 6
- adapter_weight_pair: bfloat16 [96, 2, 4096, 128], P(None, 'tensor', 'dp'), may hold values from -0.119628906 to 0.119628906
- adapter_of_block: int32 [16, 1], P('group'), parts along dimension 0, may hold values from 0 to 95
- block_live_length: int32 [16, 1], P('group'), parts along dimension 0, may hold values from 32 to 128
Outputs:
- grad_input: bfloat16 [2048, 8192], P(('group', 'dp'), 'tensor'), parts along dimension 0
- adapter_pair_gradient: bfloat16 [192, 2, 4096, 128], P('group', 'tensor', 'dp'), parts along dimension 0
The draws below stay inside these ranges and needn't reach their ends.
There are 2 independent parts, one for each index of `group`. The reference program is written for one: setup_inputs(seed, part) draws one part's arguments, and reference() takes and returns one part's arrays. A program takes and returns all parts, laid end to end along the dimension named above; an argument that names none is the same for every part. Nothing has to cross between parts.
All inputs are finite; a program needn't handle non-finite values.
Results may differ from the reference program's by a relative error of at most 0.005.
Values may be sent and summed in bfloat16 or wider, within the bound.
No kernel may reach another device: no remote copies, remote signals or barrier semaphores. Data moves between devices by JAX's collectives and lax.ppermute only.
A program may use at most 128 MiB of HBM per device.

```python
import jax
import jax.numpy as jnp
from jax import lax

MODEL_WIDTH = 8192
ADAPTER_RANK = 64
ADAPTER_COUNT = 96
BLOCK = 128
TOKEN_TOTAL = 1024
N_DP = 8


def with_ends(drawn, stream_key, smallest, largest):
    longest = drawn.shape.index(max(drawn.shape))
    spots = []
    for shift in (0, 1):
        where = [jax.random.randint(jax.random.fold_in(stream_key, axis), (), 0, length) for axis, length in enumerate(drawn.shape)]
        where[longest] = (where[longest] + shift) % drawn.shape[longest]
        spots.append(tuple(where))
    return drawn.at[spots[0]].set(smallest).at[spots[1]].set(largest)


def levels(own_key, dims, shards, low, top_value):
    factor_of, own = 1.0, jax.random.fold_in(own_key, 6)
    for dim, parts in shards:
        steps = jnp.exp(jax.random.uniform(jax.random.fold_in(own, dim), (parts,), jnp.float32, low / len(shards), top_value / len(shards)))
        factor_of = factor_of * jnp.repeat(steps, dims[dim] // parts).reshape([-1 if axis == dim else 1 for axis in range(len(dims))])
    return factor_of


def gaussian(key, dims, scale, limit, split=(), kind=jnp.bfloat16):
    drawn = jax.random.normal(key, dims, jnp.float32) * scale
    if len(split) > 0:
        drawn = levels(key, dims, split, -0.22, 0.18) * drawn
    return jnp.clip(drawn, min=-limit, max=limit).astype(kind)


def setup_inputs(seed: int = 0, part: int = 0) -> dict:
    arg_keys = jax.random.split(jax.random.key(seed), 6)
    part_keys = jax.random.split(jax.random.fold_in(arg_keys[5], part), 6)
    activations = gaussian(part_keys[0], (TOKEN_TOTAL, MODEL_WIDTH), 1.0, 6.0, ((0, 8), (1, 2)))
    cotangent = gaussian(part_keys[1], (TOKEN_TOTAL, MODEL_WIDTH), 1.0, 6.0, ((0, 8), (1, 2)))
    adapter_weight_pair = gaussian(arg_keys[2], (ADAPTER_COUNT, 2, MODEL_WIDTH // 2, 2 * ADAPTER_RANK), 0.02, 0.119628906, ((1, 2), (2, 8)))
    adapter_of_block = with_ends(jax.random.randint(part_keys[3], (N_DP, 1), 0, ADAPTER_COUNT), jax.random.fold_in(part_keys[3], 1), 0, ADAPTER_COUNT - 1).astype(jnp.int32)
    block_live_length = with_ends(jax.random.randint(part_keys[4], (N_DP, 1), BLOCK // 4, BLOCK + 1), jax.random.fold_in(part_keys[4], 1), BLOCK // 4, BLOCK).astype(jnp.int32)
    return dict(activations=activations, cotangent=cotangent, adapter_weight_pair=adapter_weight_pair, adapter_of_block=adapter_of_block, block_live_length=block_live_length)


adapter_alpha = 128.0


def reference(activations, cotangent, adapter_weight_pair, adapter_of_block, block_live_length):
    branch_scale = adapter_alpha / ADAPTER_RANK
    adapters = adapter_of_block[:, 0].astype(jnp.int32)
    lengths = block_live_length[:, 0].astype(jnp.int32)
    lookup_table = adapter_weight_pair.reshape(ADAPTER_COUNT, MODEL_WIDTH, 2 * ADAPTER_RANK)
    blocks_x = activations.reshape(N_DP, BLOCK, MODEL_WIDTH)
    blocks_y = cotangent.reshape(N_DP, BLOCK, MODEL_WIDTH)
    positions = jnp.arange(BLOCK, dtype=jnp.int32)

    def step(grand_total, item):
        x_blk, y_blk, which, token_count = item
        keep = (positions < token_count)[:, None]
        x_blk = jnp.where(keep, x_blk, jnp.zeros_like(x_blk))
        y_blk = jnp.where(keep, y_blk, jnp.zeros_like(y_blk))
        pair = lax.dynamic_index_in_dim(lookup_table, which, 0, keepdims=False)
        down = pair[:, :ADAPTER_RANK]
        upward = pair[:, ADAPTER_RANK:]
        hidden = jnp.dot(x_blk, down, preferred_element_type=jnp.float32)
        dhidden = branch_scale * jnp.dot(y_blk, upward, preferred_element_type=jnp.float32)
        hidden16 = hidden.astype(jnp.bfloat16)
        dhidden16 = dhidden.astype(jnp.bfloat16)
        incoming_gradient = jnp.dot(dhidden16, down.T, preferred_element_type=jnp.float32).astype(jnp.bfloat16)
        d_down = jnp.dot(x_blk.T, dhidden16, preferred_element_type=jnp.float32)
        d_up = branch_scale * jnp.dot(y_blk.T, hidden16, preferred_element_type=jnp.float32)
        piece = jnp.concatenate([d_down, d_up], axis=1)
        current = lax.dynamic_index_in_dim(grand_total, which, 0, keepdims=False)
        grand_total = lax.dynamic_update_index_in_dim(grand_total, current + piece, which, 0)
        return grand_total, incoming_gradient

    start = jnp.zeros((ADAPTER_COUNT, MODEL_WIDTH, 2 * ADAPTER_RANK), jnp.float32)
    grand_total, incoming_gradient = lax.scan(step, start, (blocks_x, blocks_y, adapters, lengths))
    onehot = (adapters[None, :] == jnp.arange(ADAPTER_COUNT, dtype=jnp.int32)[:, None]).astype(jnp.float32)
    token_count = jnp.sum(onehot * lengths[None, :].astype(jnp.float32), axis=1)
    adapter_pair_gradient = (grand_total / jnp.maximum(token_count, 1.0)[:, None, None]).astype(jnp.bfloat16)
    return incoming_gradient.reshape(TOKEN_TOTAL, MODEL_WIDTH), adapter_pair_gradient.reshape(ADAPTER_COUNT, 2, MODEL_WIDTH // 2, 2 * ADAPTER_RANK)
```

```python
import functools

import jax
import jax.numpy as jnp
from jax import lax
from jax.experimental import pallas as pl
from jax.experimental.pallas import tpu as pltpu
from jax.sharding import PartitionSpec as P

adapter_alpha = 128.0
VMEM_LIMIT = 40 * 1024 * 1024

in_vmem = pl.BlockSpec(memory_space=pltpu.VMEM)
in_smem = pl.BlockSpec(memory_space=pltpu.SMEM)
in_hbm = pl.BlockSpec(memory_space=pltpu.HBM)


def low_lanes(rows, width):
    return lax.broadcasted_iota(jnp.int32, (rows, width), 1) < width // 2


def swap_halves(value):
    return pltpu.roll(value, value.shape[-1] // 2, 1)


def call(kernel, out_shape, in_specs, out_specs, scratch=(), flops=0, moved=0, aliases=None):
    return pl.pallas_call(
        kernel,
        out_shape=out_shape,
        in_specs=in_specs,
        out_specs=out_specs,
        scratch_shapes=list(scratch),
        input_output_aliases=aliases or {},
        compiler_params=pltpu.CompilerParams(vmem_limit_bytes=VMEM_LIMIT),
        cost_estimate=pl.CostEstimate(flops=flops, bytes_accessed=moved, transcendentals=0),
    )


def pack_kernel(owners, ids, here, table, *refs):
    up, down = refs[:owners], refs[owners : 2 * owners]
    held, sems = refs[2 * owners :]
    half = held.shape[1] // 2
    me = here[0]
    copies = []
    for k in range(owners):
        adapter = ids[me ^ k, 0]
        copies.append(pltpu.make_async_copy(table.at[adapter], held.at[k], sems.at[k]))
        copies[-1].start()
    low = low_lanes(half, held.shape[2])
    for k in range(owners):
        copies[k].wait()
        first = held[k, :half].astype(jnp.float32)
        second = held[k, half:].astype(jnp.float32)
        up[k][...] = jnp.where(low, swap_halves(first), second).astype(jnp.bfloat16)
        down[k][...] = jnp.where(low, first, swap_halves(second)).astype(jnp.bfloat16)


def prep_kernel(half, after, x, y, x_turned, y_turned, blank, zeros, sem):
    zeros[...] = jnp.zeros_like(zeros)
    step = zeros.shape[0]
    copies = [
        pltpu.make_async_copy(zeros, blank.at[pl.ds(s, step)], sem.at[s // step])
        for s in range(0, blank.shape[0], step)
    ]
    for copy in copies:
        copy.start()
    owners = x.shape[1] // (2 * half)
    tokens = x.shape[0]

    @pl.loop(0, owners)
    def _(owner):
        for part in range(2):
            columns = pl.ds(pl.multiple_of(owner * 2 * half + part * half, half), half)
            lanes = pl.ds(part * tokens, tokens)
            x_turned[owner, :, lanes] = x[:, columns].T
            y_turned[owner, :, lanes] = y[:, columns].T

    for copy in copies:
        copy.wait()


def rank_kernel(owners, here, tokens, *refs):
    packed, out = refs[:owners], refs[owners]
    half, width = packed[0].shape
    me = here[0]
    first = jnp.zeros((tokens.shape[0], width), jnp.float32)
    second = jnp.zeros((tokens.shape[0], width), jnp.float32)
    for k in range(owners):
        start = (me ^ k) * (2 * half)
        lo = tokens[:, pl.ds(pl.multiple_of(start, half), half)]
        hi = tokens[:, pl.ds(pl.multiple_of(start + half, half), half)]
        first += jnp.dot(lo, packed[k][...], preferred_element_type=jnp.float32)
        second += jnp.dot(hi, packed[k][...], preferred_element_type=jnp.float32)
    out[...] = jnp.where(low_lanes(*out.shape), first, second)


def rounded_twice(mine, other, length, scale):
    total = mine[...] + other[...]
    total = scale * (total + swap_halves(total))
    rows, width = total.shape
    live = lax.broadcasted_iota(jnp.int32, (rows, width), 0) < length
    total = jnp.where(live, total, 0.0)
    low = low_lanes(rows, width)
    top = jnp.where(low, total, 0.0).astype(jnp.bfloat16)
    bottom = jnp.where(low, 0.0, total).astype(jnp.bfloat16)
    return jnp.concatenate([top, bottom], axis=0)


def piece_kernel(owners, scale, out_scale, here, lengths, mine, other, turned, *refs):
    me = here[0]
    pair = rounded_twice(mine, other, lengths[me, 0], scale)
    for k in range(owners):
        piece = jnp.dot(turned[me ^ k], pair, preferred_element_type=jnp.float32)
        refs[k][...] = (out_scale * piece).astype(jnp.bfloat16)


def input_kernel(owners, scale, here, lengths, mine, other, *refs):
    packed, out = refs[:owners], refs[owners]
    me = here[0]
    pair = rounded_twice(mine, other, lengths[me, 0], scale)
    rows = out.shape[0]
    half = packed[0].shape[0]
    for k in range(owners):
        both = lax.dot_general(
            pair, packed[k][...], (((1,), (1,)), ((), ())), preferred_element_type=jnp.float32
        ).astype(jnp.bfloat16)
        start = (me ^ k) * (2 * half)
        out[:, pl.ds(pl.multiple_of(start, half), half)] = both[:rows]
        out[:, pl.ds(pl.multiple_of(start + half, half), half)] = both[rows:]


def merge_kernel(owners, ids, here, lengths, *refs):
    down, up = refs[:owners], refs[owners : 2 * owners]
    out, total, held, sems = refs[2 * owners + 1 :]
    me = here[0]
    half = held.shape[1] // 2
    low = low_lanes(half, held.shape[2])
    copies = []
    for k in range(owners):
        adapter = ids[me ^ k, 0]
        copies.append(pltpu.make_async_copy(held.at[k], out.at[adapter], sems.at[k]))
        same = [ids[me ^ other, 0] == adapter for other in range(owners)]
        earlier = functools.reduce(jnp.logical_or, same[:k], jnp.bool_(False))

        @pl.when(jnp.logical_not(earlier))
        def _():
            total[0] = down[k][...].astype(jnp.float32)
            total[1] = up[k][...].astype(jnp.float32)
            count = lengths[me ^ k, 0]
            for other in range(k + 1, owners):
                count += jnp.where(same[other], lengths[me ^ other, 0], 0)

                @pl.when(same[other])
                def _():
                    total[0] += down[other][...].astype(jnp.float32)
                    total[1] += up[other][...].astype(jnp.float32)

            denom = jnp.maximum(count.astype(jnp.float32), 1.0)
            g_down = total[0] / denom
            g_up = total[1] / denom
            held[k, :half] = jnp.where(low, g_down, swap_halves(g_up)).astype(jnp.bfloat16)
            held[k, half:] = jnp.where(low, swap_halves(g_down), g_up).astype(jnp.bfloat16)
            copies[k].start()

    for k in range(owners):
        adapter = ids[me ^ k, 0]
        same = [ids[me ^ other, 0] == adapter for other in range(k)]
        earlier = functools.reduce(jnp.logical_or, same, jnp.bool_(False))
        pl.when(jnp.logical_not(earlier))(copies[k].wait)


def send_all(pieces, owners):
    order = sorted(range(1, owners), reverse=True)
    out = {0: pieces[0]}
    for k in order:
        out[k] = lax.ppermute(pieces[k], "dp", [(i, i ^ k) for i in range(owners)])
    return [out[k] for k in range(owners)]


def across_cores(value):
    cores = lax.axis_size("tensor")
    return lax.ppermute(value, "tensor", [(i, i ^ 1) for i in range(cores)])


def with_kernels(activations, cotangent, adapter_weight_pair, adapter_of_block, block_live_length):
    owners = lax.axis_size("dp")
    here = lax.axis_index("dp").astype(jnp.int32).reshape(1)
    count, _, rows, width = adapter_weight_pair.shape
    table = adapter_weight_pair.reshape(count, rows, width)
    tokens, features = activations.shape
    half = rows // 2
    scale = adapter_alpha / (width // 2)
    bf16, f32 = jnp.bfloat16, jnp.float32
    packed_shape = jax.ShapeDtypeStruct((half, width), bf16)
    packed_bytes = half * width * 2

    sent = call(
        functools.partial(pack_kernel, owners),
        [packed_shape] * (2 * owners),
        [in_smem, in_smem, in_hbm],
        [in_vmem] * (2 * owners),
        [pltpu.VMEM((owners, rows, width), bf16), pltpu.SemaphoreType.DMA((owners,))],
        moved=4 * owners * packed_bytes,
    )(adapter_of_block, here, table)
    up = send_all(sent[:owners], owners)
    down = send_all(sent[owners:], owners)

    step = 8
    turned_shape = jax.ShapeDtypeStruct((owners, half, 2 * tokens), bf16)
    x_turned, y_turned, blank = call(
        functools.partial(prep_kernel, half),
        [turned_shape, turned_shape, jax.ShapeDtypeStruct(table.shape, bf16)],
        [in_hbm, in_vmem, in_vmem],
        [in_vmem, in_vmem, in_hbm],
        [pltpu.VMEM((step, rows, width), bf16), pltpu.SemaphoreType.DMA((count // step,))],
        moved=8 * tokens * features + 2 * count * rows * width,
    )(sent[0], activations, cotangent)

    partial_shape = jax.ShapeDtypeStruct((tokens, width), f32)

    def rank_product(values, packed):
        return call(
            functools.partial(rank_kernel, owners),
            partial_shape,
            [in_smem, in_vmem] + [in_vmem] * owners,
            in_vmem,
            flops=2 * tokens * features * width,
            moved=2 * tokens * features + owners * packed_bytes,
        )(here, values, *packed)

    def pieces(mine, other, turned, in_scale, out_scale):
        return call(
            functools.partial(piece_kernel, owners, in_scale, out_scale),
            [packed_shape] * owners,
            [in_smem, in_smem, in_vmem, in_vmem, in_vmem],
            [in_vmem] * owners,
            flops=2 * tokens * features * width,
            moved=2 * tokens * features + owners * packed_bytes,
        )(here, block_live_length, mine, other, turned)

    dhidden = rank_product(cotangent, up)
    dhidden_other = across_cores(dhidden)
    d_down = send_all(pieces(dhidden, dhidden_other, x_turned, scale, 1.0), owners)
    hidden = rank_product(activations, down)
    hidden_other = across_cores(hidden)
    d_up = send_all(pieces(hidden, hidden_other, y_turned, 1.0, scale), owners)

    grad_input = call(
        functools.partial(input_kernel, owners, scale),
        jax.ShapeDtypeStruct((tokens, features), bf16),
        [in_smem, in_smem, in_vmem, in_vmem] + [in_vmem] * owners,
        in_vmem,
        flops=2 * tokens * features * width,
        moved=2 * tokens * features + owners * packed_bytes,
    )(here, block_live_length, dhidden, dhidden_other, *down)

    gradient = call(
        functools.partial(merge_kernel, owners),
        jax.ShapeDtypeStruct(table.shape, bf16),
        [in_smem] * 3 + [in_vmem] * (2 * owners) + [in_hbm],
        in_hbm,
        [
            pltpu.VMEM((2, half, width), f32),
            pltpu.VMEM((owners, rows, width), bf16),
            pltpu.SemaphoreType.DMA((owners,)),
        ],
        moved=4 * owners * packed_bytes,
        aliases={3 + 2 * owners: 0},
    )(adapter_of_block, here, block_live_length, *d_down, *d_up, blank)
    return grad_input, gradient[:, None]


def without_kernels(activations, cotangent, adapter_weight_pair, adapter_of_block, block_live_length):
    owners = lax.axis_size("dp")
    here = lax.axis_index("dp")
    count, _, rows, width = adapter_weight_pair.shape
    rank = width // 2
    scale = adapter_alpha / rank
    adapters = adapter_of_block[:, 0]
    lengths = block_live_length[:, 0]
    keep = (jnp.arange(activations.shape[0], dtype=jnp.int32) < lengths[here])[:, None]
    inputs = jnp.where(keep, activations, jnp.zeros_like(activations))
    grads_out = jnp.where(keep, cotangent, jnp.zeros_like(cotangent))
    fetched = lax.all_to_all(
        adapter_weight_pair[:, 0][adapters], "dp", split_axis=0, concat_axis=0, tiled=True
    )
    pair = fetched.reshape(-1, width)
    down, upward = pair[:, :rank], pair[:, rank:]
    f32 = jnp.float32
    hidden_part = jnp.dot(inputs, down, preferred_element_type=f32)
    dhidden_part = scale * jnp.dot(grads_out, upward, preferred_element_type=f32)
    hidden, dhidden = lax.psum((hidden_part, dhidden_part), "tensor")
    hidden16, dhidden16 = hidden.astype(jnp.bfloat16), dhidden.astype(jnp.bfloat16)
    d_down = jnp.dot(inputs.T, dhidden16, preferred_element_type=f32)
    d_up = scale * jnp.dot(grads_out.T, hidden16, preferred_element_type=f32)
    sent = jnp.concatenate([d_down, d_up], axis=1).astype(jnp.bfloat16).reshape(owners, rows, width)
    received = lax.all_to_all(sent, "dp", split_axis=0, concat_axis=0, tiled=True).astype(f32)
    same = adapters[:, None] == adapters[None, :]
    total = jnp.sum(jnp.where(same, lengths[None, :], 0), axis=1).astype(f32)
    summed = jax.ops.segment_sum(received, adapters, num_segments=count)
    denom = jnp.ones((count,), f32).at[adapters].set(jnp.maximum(total, 1.0))
    gradient = (summed / denom[:, None, None]).astype(jnp.bfloat16)
    grad_input = jnp.dot(dhidden16, down.T, preferred_element_type=f32).astype(jnp.bfloat16)
    return grad_input, gradient[:, None]


def solution(mesh):
    owners, cores = mesh.shape["dp"], mesh.shape["tensor"]

    def on_device(activations, cotangent, adapter_weight_pair, *rest):
        rows = adapter_weight_pair.shape[2]
        fits = owners & (owners - 1) == 0 and cores == 2 and rows % 256 == 0
        body = with_kernels if fits else without_kernels
        return body(activations, cotangent, adapter_weight_pair, *rest)

    in_specs = (
        P(("group", "dp"), "tensor"),
        P(("group", "dp"), "tensor"),
        P(None, "tensor", "dp", None),
        P("group", None),
        P("group", None),
    )
    out_specs = (P(("group", "dp"), "tensor"), P("group", "tensor", "dp", None))
    return jax.shard_map(
        on_device, mesh=mesh, in_specs=in_specs, out_specs=out_specs, check_vma=False
    )
```

```python
import functools

import jax
import jax.numpy as jnp
from jax import lax
from jax.experimental import pallas as pl
from jax.experimental.pallas import tpu as pltpu
from jax.sharding import PartitionSpec as P

adapter_alpha = 128.0

in_vmem = pl.BlockSpec(memory_space=pltpu.VMEM)
in_smem = pl.BlockSpec(memory_space=pltpu.SMEM)
in_hbm = pl.BlockSpec(memory_space=pltpu.HBM)


def low_lanes(rows, width):
    return lax.broadcasted_iota(jnp.int32, (rows, width), 1) < width // 2


def swap_halves(value):
    return pltpu.roll(value, value.shape[-1] // 2, 1)


def call(kernel, out_shape, in_specs, out_specs, scratch=(), flops=0, moved=0, aliases=None, vmem=40):
    return pl.pallas_call(
        kernel,
        out_shape=out_shape,
        in_specs=in_specs,
        out_specs=out_specs,
        scratch_shapes=list(scratch),
        input_output_aliases=aliases or {},
        compiler_params=pltpu.CompilerParams(vmem_limit_bytes=vmem * 1024 * 1024),
        cost_estimate=pl.CostEstimate(flops=flops, bytes_accessed=moved, transcendentals=0),
    )


def pack_kernel(ids, table, up, down, held, sems):
    owners, rows, width = held.shape
    half = rows // 2
    copies = []
    for k in range(owners):
        copies.append(pltpu.make_async_copy(table.at[ids[k]], held.at[k], sems.at[k]))
        copies[-1].start()
    low = low_lanes(half, width)
    for k in range(owners):
        copies[k].wait()
        first = held[k, :half].astype(jnp.float32)
        second = held[k, half:].astype(jnp.float32)
        up[k] = jnp.where(low, swap_halves(first), second).astype(jnp.bfloat16)
        down[k] = jnp.where(low, first, swap_halves(second)).astype(jnp.bfloat16)


def prep_kernel(half, after, x, y, x_turned, y_turned, blank, zeros, sem):
    zeros[...] = jnp.zeros_like(zeros)
    step = zeros.shape[0]
    copies = [
        pltpu.make_async_copy(zeros, blank.at[pl.ds(s, step)], sem.at[s // step])
        for s in range(0, blank.shape[0], step)
    ]
    for copy in copies:
        copy.start()
    owners = x.shape[1] // (2 * half)
    tokens = x.shape[0]

    @pl.loop(0, owners)
    def _(owner):
        for part in range(2):
            columns = pl.ds(pl.multiple_of(owner * 2 * half + part * half, half), half)
            lanes = pl.ds(part * tokens, tokens)
            x_turned[owner, :, lanes] = x[:, columns].T
            y_turned[owner, :, lanes] = y[:, columns].T

    for copy in copies:
        copy.wait()


def rank_kernel(tokens, packed, out):
    owners, half, width = packed.shape
    first = jnp.zeros((tokens.shape[0], width), jnp.float32)
    second = jnp.zeros((tokens.shape[0], width), jnp.float32)
    for k in range(owners):
        start = k * 2 * half
        lo = tokens[:, start : start + half]
        hi = tokens[:, start + half : start + 2 * half]
        first += jnp.dot(lo, packed[k], preferred_element_type=jnp.float32)
        second += jnp.dot(hi, packed[k], preferred_element_type=jnp.float32)
    out[...] = jnp.where(low_lanes(*out.shape), first, second)


def rounded_twice(mine, other, length, scale):
    total = mine[...] + other[...]
    total = scale * (total + swap_halves(total))
    rows, width = total.shape
    live = lax.broadcasted_iota(jnp.int32, (rows, width), 0) < length
    total = jnp.where(live, total, 0.0)
    low = low_lanes(rows, width)
    top = jnp.where(low, total, 0.0).astype(jnp.bfloat16)
    bottom = jnp.where(low, 0.0, total).astype(jnp.bfloat16)
    return jnp.concatenate([top, bottom], axis=0)


def piece_kernel(scale, out_scale, here, lengths, mine, other, turned, out):
    pair = rounded_twice(mine, other, lengths[here[0]], scale)
    for k in range(out.shape[0]):
        piece = jnp.dot(turned[k], pair, preferred_element_type=jnp.float32)
        out[k] = (out_scale * piece).astype(jnp.bfloat16)


def input_kernel(scale, here, lengths, mine, other, packed, out):
    pair = rounded_twice(mine, other, lengths[here[0]], scale)
    rows = out.shape[0]
    owners, half, _ = packed.shape
    for k in range(owners):
        both = lax.dot_general(
            pair, packed[k], (((1,), (1,)), ((), ())), preferred_element_type=jnp.float32
        ).astype(jnp.bfloat16)
        start = k * 2 * half
        out[:, start : start + half] = both[:rows]
        out[:, start + half : start + 2 * half] = both[rows:]


def merge_kernel(ids, lengths, down, up, blank, out, total, held, sems):
    owners, half, width = down.shape
    low = low_lanes(half, width)
    copies, firsts = [], []
    for k in range(owners):
        adapter = ids[k]
        copies.append(pltpu.make_async_copy(held.at[k], out.at[adapter], sems.at[k]))
        same = [ids[other] == adapter for other in range(owners)]
        earlier = functools.reduce(jnp.logical_or, same[:k], jnp.bool_(False))
        firsts.append(jnp.logical_not(earlier))

        @pl.when(firsts[k])
        def _():
            total[0] = down[k].astype(jnp.float32)
            total[1] = up[k].astype(jnp.float32)
            count = lengths[k]
            for other in range(k + 1, owners):
                count += jnp.where(same[other], lengths[other], 0)

                @pl.when(same[other])
                def _():
                    total[0] += down[other].astype(jnp.float32)
                    total[1] += up[other].astype(jnp.float32)

            denom = jnp.maximum(count.astype(jnp.float32), 1.0)
            part = 1.0 / jnp.full((1, width), denom)
            g_down = total[0] * part
            g_up = total[1] * part
            held[k, :half] = jnp.where(low, g_down, swap_halves(g_up)).astype(jnp.bfloat16)
            held[k, half:] = jnp.where(low, swap_halves(g_down), g_up).astype(jnp.bfloat16)
            copies[k].start()

    for k in range(owners):
        pl.when(firsts[k])(copies[k].wait)


def exchange(pieces):
    return lax.all_to_all(pieces, "dp", split_axis=0, concat_axis=0, tiled=True)


def across_cores(value):
    cores = lax.axis_size("tensor")
    return lax.ppermute(value, "tensor", [(i, i ^ 1) for i in range(cores)])


def with_kernels(activations, cotangent, adapter_weight_pair, adapter_of_block, block_live_length):
    owners = lax.axis_size("dp")
    here = lax.axis_index("dp").astype(jnp.int32).reshape(1)
    ids, lengths = adapter_of_block[:, 0], block_live_length[:, 0]
    count, _, rows, width = adapter_weight_pair.shape
    table = adapter_weight_pair.reshape(count, rows, width)
    tokens, features = activations.shape
    half = rows // 2
    scale = adapter_alpha / (width // 2)
    bf16, f32 = jnp.bfloat16, jnp.float32
    packed_shape = jax.ShapeDtypeStruct((owners, half, width), bf16)
    packed_bytes = owners * half * width * 2

    up_sent, down_sent = call(
        pack_kernel,
        [packed_shape] * 2,
        [in_smem, in_hbm],
        [in_vmem] * 2,
        [pltpu.VMEM((owners, rows, width), bf16), pltpu.SemaphoreType.DMA((owners,))],
        moved=4 * packed_bytes,
        vmem=60,
    )(ids, table)
    up = exchange(up_sent)
    down = exchange(down_sent)

    step = 8
    turned_shape = jax.ShapeDtypeStruct((owners, half, 2 * tokens), bf16)
    x_turned, y_turned, blank = call(
        functools.partial(prep_kernel, half),
        [turned_shape, turned_shape, jax.ShapeDtypeStruct(table.shape, bf16)],
        [in_hbm, in_vmem, in_vmem],
        [in_vmem, in_vmem, in_hbm],
        [pltpu.VMEM((step, rows, width), bf16), pltpu.SemaphoreType.DMA((count // step,))],
        moved=8 * tokens * features + 2 * count * rows * width,
        vmem=60,
    )(up_sent, activations, cotangent)

    partial_shape = jax.ShapeDtypeStruct((tokens, width), f32)

    def rank_product(values, packed):
        return call(
            rank_kernel,
            partial_shape,
            [in_vmem, in_vmem],
            in_vmem,
            flops=2 * tokens * features * width,
            moved=2 * tokens * features + packed_bytes,
        )(values, packed)

    def pieces(mine, other, turned, in_scale, out_scale):
        return call(
            functools.partial(piece_kernel, in_scale, out_scale),
            packed_shape,
            [in_smem, in_smem, in_vmem, in_vmem, in_vmem],
            in_vmem,
            flops=2 * tokens * features * width,
            moved=2 * tokens * features + packed_bytes,
        )(here, lengths, mine, other, turned)

    dhidden = rank_product(cotangent, up)
    dhidden_other = across_cores(dhidden)
    d_down = exchange(pieces(dhidden, dhidden_other, x_turned, scale, 1.0))
    hidden = rank_product(activations, down)
    hidden_other = across_cores(hidden)
    d_up = exchange(pieces(hidden, hidden_other, y_turned, 1.0, scale))

    grad_input = call(
        functools.partial(input_kernel, scale),
        jax.ShapeDtypeStruct((tokens, features), bf16),
        [in_smem, in_smem, in_vmem, in_vmem, in_vmem],
        in_vmem,
        flops=2 * tokens * features * width,
        moved=2 * tokens * features + packed_bytes,
    )(here, lengths, dhidden, dhidden_other, down)

    gradient = call(
        merge_kernel,
        jax.ShapeDtypeStruct(table.shape, bf16),
        [in_smem, in_smem, in_vmem, in_vmem, in_hbm],
        in_hbm,
        [
            pltpu.VMEM((2, half, width), f32),
            pltpu.VMEM((owners, rows, width), bf16),
            pltpu.SemaphoreType.DMA((owners,)),
        ],
        moved=4 * packed_bytes,
        aliases={4: 0},
    )(ids, lengths, d_down, d_up, blank)
    return grad_input, gradient[:, None]


def without_kernels(activations, cotangent, adapter_weight_pair, adapter_of_block, block_live_length):
    owners = lax.axis_size("dp")
    here = lax.axis_index("dp")
    count, _, rows, width = adapter_weight_pair.shape
    rank = width // 2
    scale = adapter_alpha / rank
    adapters = adapter_of_block[:, 0]
    lengths = block_live_length[:, 0]
    keep = (jnp.arange(activations.shape[0], dtype=jnp.int32) < lengths[here])[:, None]
    inputs = jnp.where(keep, activations, jnp.zeros_like(activations))
    grads_out = jnp.where(keep, cotangent, jnp.zeros_like(cotangent))
    fetched = lax.all_to_all(
        adapter_weight_pair[:, 0][adapters], "dp", split_axis=0, concat_axis=0, tiled=True
    )
    pair = fetched.reshape(-1, width)
    down, upward = pair[:, :rank], pair[:, rank:]
    f32 = jnp.float32
    hidden_part = jnp.dot(inputs, down, preferred_element_type=f32)
    dhidden_part = scale * jnp.dot(grads_out, upward, preferred_element_type=f32)
    hidden, dhidden = lax.psum((hidden_part, dhidden_part), "tensor")
    hidden16, dhidden16 = hidden.astype(jnp.bfloat16), dhidden.astype(jnp.bfloat16)
    d_down = jnp.dot(inputs.T, dhidden16, preferred_element_type=f32)
    d_up = scale * jnp.dot(grads_out.T, hidden16, preferred_element_type=f32)
    sent = jnp.concatenate([d_down, d_up], axis=1).astype(jnp.bfloat16).reshape(owners, rows, width)
    received = lax.all_to_all(sent, "dp", split_axis=0, concat_axis=0, tiled=True).astype(f32)
    same = adapters[:, None] == adapters[None, :]
    total = jnp.sum(jnp.where(same, lengths[None, :], 0), axis=1).astype(f32)
    summed = jax.ops.segment_sum(received, adapters, num_segments=count)
    denom = jnp.ones((count,), f32).at[adapters].set(jnp.maximum(total, 1.0))
    gradient = (summed / denom[:, None, None]).astype(jnp.bfloat16)
    grad_input = jnp.dot(dhidden16, down.T, preferred_element_type=f32).astype(jnp.bfloat16)
    return grad_input, gradient[:, None]


def solution(mesh):
    owners, cores = mesh.shape["dp"], mesh.shape["tensor"]

    def on_device(activations, cotangent, adapter_weight_pair, *rest):
        rows = adapter_weight_pair.shape[2]
        fits = owners & (owners - 1) == 0 and cores == 2 and rows % 256 == 0
        body = with_kernels if fits else without_kernels
        return body(activations, cotangent, adapter_weight_pair, *rest)

    in_specs = (
        P(("group", "dp"), "tensor"),
        P(("group", "dp"), "tensor"),
        P(None, "tensor", "dp", None),
        P("group", None),
        P("group", None),
    )
    out_specs = (P(("group", "dp"), "tensor"), P("group", "tensor", "dp", None))
    return jax.shard_map(
        on_device, mesh=mesh, in_specs=in_specs, out_specs=out_specs, check_vma=False
    )
```

```python
import functools

import jax
import jax.numpy as jnp
from jax import lax
from jax.experimental import pallas as pl
from jax.experimental.pallas import tpu as pltpu
from jax.sharding import PartitionSpec as P

adapter_alpha = 128.0

in_vmem = pl.BlockSpec(memory_space=pltpu.VMEM)
in_smem = pl.BlockSpec(memory_space=pltpu.SMEM)
in_hbm = pl.BlockSpec(memory_space=pltpu.HBM)


def low_lanes(rows, width):
    return lax.broadcasted_iota(jnp.int32, (rows, width), 1) < width // 2


def call(kernel, out_shape, in_specs, out_specs, scratch=(), flops=0, moved=0, aliases=None, vmem=40):
    return pl.pallas_call(
        kernel,
        out_shape=out_shape,
        in_specs=in_specs,
        out_specs=out_specs,
        scratch_shapes=list(scratch),
        input_output_aliases=aliases or {},
        compiler_params=pltpu.CompilerParams(vmem_limit_bytes=vmem * 1024 * 1024),
        cost_estimate=pl.CostEstimate(flops=flops, bytes_accessed=moved, transcendentals=0),
    )


def gather_kernel(owners, ids, here, table, *refs):
    out, sems = refs[:owners], refs[owners]
    copies = [
        pltpu.make_async_copy(table.at[ids[here[0] ^ k]], out[k], sems.at[k])
        for k in range(owners)
    ]
    for copy in copies:
        copy.start()
    for copy in copies:
        copy.wait()


def prep_kernel(rows, after, x, y, turned, blank, zeros, sem):
    zeros[...] = jnp.zeros_like(zeros)
    step = zeros.shape[0]
    copies = [
        pltpu.make_async_copy(zeros, blank.at[pl.ds(s, step)], sem.at[s // step])
        for s in range(0, blank.shape[0], step)
    ]
    for copy in copies:
        copy.start()
    tokens = x.shape[0]

    @pl.loop(0, x.shape[1] // rows)
    def _(owner):
        columns = pl.ds(pl.multiple_of(owner * rows, rows), rows)
        turned[owner, :, pl.ds(0, tokens)] = x[:, columns].T
        turned[owner, :, pl.ds(tokens, tokens)] = y[:, columns].T

    for copy in copies:
        copy.wait()


def rank_kernel(owners, here, x, y, *refs):
    pairs, out = refs[:owners], refs[owners]
    rows, width = pairs[0].shape
    tokens = x.shape[0]
    x_rank = jnp.zeros((tokens, width), jnp.float32)
    y_rank = jnp.zeros((tokens, width), jnp.float32)
    for k in range(owners):
        columns = pl.ds(pl.multiple_of((here[0] ^ k) * rows, rows), rows)
        x_rank += jnp.dot(x[:, columns], pairs[k][...], preferred_element_type=jnp.float32)
        y_rank += jnp.dot(y[:, columns], pairs[k][...], preferred_element_type=jnp.float32)
    out[...] = jnp.where(low_lanes(tokens, width), x_rank, y_rank)


def rounded(mine, other, length, scale):
    total = mine[...] + other[...]
    rows, width = total.shape
    total = jnp.where(low_lanes(rows, width), total, scale * total)
    live = lax.broadcasted_iota(jnp.int32, (rows, width), 0) < length
    return jnp.where(live, total, 0.0)


def swap_halves(value):
    return pltpu.roll(value, value.shape[-1] // 2, 1)


def piece_kernel(owners, scale, here, lengths, mine, other, turned, *refs):
    me = here[0]
    both = swap_halves(rounded(mine, other, lengths[me], scale))
    low = low_lanes(*both.shape)
    top = jnp.where(low, both, 0.0).astype(jnp.bfloat16)
    bottom = jnp.where(low, 0.0, both).astype(jnp.bfloat16)
    ranks = jnp.concatenate([top, bottom], axis=0)
    for k in range(owners):
        piece = jnp.dot(turned[me ^ k], ranks, preferred_element_type=jnp.float32)
        refs[k][...] = jnp.where(low_lanes(*piece.shape), piece, scale * piece).astype(jnp.bfloat16)


def input_kernel(owners, scale, here, lengths, mine, other, *refs):
    pairs, out = refs[:owners], refs[owners]
    me = here[0]
    both = swap_halves(rounded(mine, other, lengths[me], scale))
    ranks = jnp.where(low_lanes(*both.shape), both, 0.0).astype(jnp.bfloat16)
    rows = pairs[0].shape[0]
    for k in range(owners):
        columns = pl.ds(pl.multiple_of((me ^ k) * rows, rows), rows)
        out[:, columns] = lax.dot_general(
            ranks, pairs[k][...], (((1,), (1,)), ((), ())), preferred_element_type=jnp.float32
        ).astype(jnp.bfloat16)


def merge_kernel(owners, ids, here, lengths, *refs):
    pieces = refs[:owners]
    out, total, held, sems = refs[owners + 1 :]
    blocks = [here[0] ^ k for k in range(owners)]
    copies, firsts = [], []
    for k in range(owners):
        adapter = ids[blocks[k]]
        copies.append(pltpu.make_async_copy(held.at[k], out.at[adapter], sems.at[k]))
        same = [ids[blocks[other]] == adapter for other in range(owners)]
        earlier = functools.reduce(jnp.logical_or, same[:k], jnp.bool_(False))
        later = functools.reduce(jnp.logical_or, same[k + 1 :], jnp.bool_(False))
        firsts.append(jnp.logical_not(earlier))

        def store(value, count):
            denom = jnp.maximum(count.astype(jnp.float32), 1.0)
            part = 1.0 / jnp.full((1, value.shape[1]), denom)
            held[k] = (value * part).astype(jnp.bfloat16)
            copies[k].start()

        @pl.when(firsts[k] & jnp.logical_not(later))
        def _():
            store(pieces[k][...].astype(jnp.float32), lengths[blocks[k]])

        @pl.when(firsts[k] & later)
        def _():
            total[...] = pieces[k][...].astype(jnp.float32)
            count = lengths[blocks[k]]
            for other in range(k + 1, owners):
                count += jnp.where(same[other], lengths[blocks[other]], 0)

                @pl.when(same[other])
                def _():
                    total[...] += pieces[other][...].astype(jnp.float32)

            store(total[...], count)

    for k in range(owners):
        pl.when(firsts[k])(copies[k].wait)


def exchange(pieces):
    owners = len(pieces)
    far = list(range(owners // 2, owners))
    near = list(range(1, owners // 2))
    order = [near[0], far[0], near[1], far[1], far[2], far[3], near[2]] if owners == 8 else near + far
    after = {far[3]: near[0], near[2]: near[1]} if owners == 8 else {}
    out = {0: pieces[0]}
    for k in order:
        piece = pieces[k]
        if k in after:
            piece, out[after[k]] = lax.optimization_barrier((piece, out[after[k]]))
        out[k] = lax.ppermute(piece, "dp", [(i, i ^ k) for i in range(owners)])
    return [out[k] for k in range(owners)]


def across_cores(value):
    cores = lax.axis_size("tensor")
    return lax.ppermute(value, "tensor", [(i, i ^ 1) for i in range(cores)])


def with_kernels(activations, cotangent, adapter_weight_pair, adapter_of_block, block_live_length):
    owners = lax.axis_size("dp")
    here = lax.axis_index("dp").astype(jnp.int32).reshape(1)
    ids, lengths = adapter_of_block[:, 0], block_live_length[:, 0]
    count, _, rows, width = adapter_weight_pair.shape
    table = adapter_weight_pair.reshape(count, rows, width)
    tokens, features = activations.shape
    scale = adapter_alpha / (width // 2)
    bf16, f32 = jnp.bfloat16, jnp.float32
    pair_shapes = [jax.ShapeDtypeStruct((rows, width), bf16)] * owners
    pair_bytes = owners * rows * width * 2
    token_bytes = tokens * features * 2

    sent = call(
        functools.partial(gather_kernel, owners),
        pair_shapes,
        [in_smem, in_smem, in_hbm],
        [in_vmem] * owners,
        [pltpu.SemaphoreType.DMA((owners,))],
        moved=2 * pair_bytes,
        vmem=53,
    )(ids, here, table)
    pairs = exchange(sent)

    step = 8
    turned, blank = call(
        functools.partial(prep_kernel, rows),
        [
            jax.ShapeDtypeStruct((owners, rows, 2 * tokens), bf16),
            jax.ShapeDtypeStruct(table.shape, bf16),
        ],
        [in_hbm, in_vmem, in_vmem],
        [in_vmem, in_hbm],
        [pltpu.VMEM((step, rows, width), bf16), pltpu.SemaphoreType.DMA((count // step,))],
        moved=4 * token_bytes + 2 * count * rows * width,
    )(pairs[2], activations, cotangent)
    *pairs, turned, blank = lax.optimization_barrier((*pairs, turned, blank))

    mine = call(
        functools.partial(rank_kernel, owners),
        jax.ShapeDtypeStruct((tokens, width), f32),
        [in_smem] + [in_vmem] * (2 + owners),
        in_vmem,
        flops=4 * tokens * features * width,
        moved=2 * token_bytes + pair_bytes,
    )(here, activations, cotangent, *pairs)
    other = across_cores(mine)

    pieces = call(
        functools.partial(piece_kernel, owners, scale),
        pair_shapes,
        [in_smem] * 2 + [in_vmem] * 3,
        [in_vmem] * owners,
        flops=4 * tokens * features * width,
        moved=2 * token_bytes + pair_bytes,
    )(here, lengths, mine, other, turned)
    arrived = exchange(pieces)

    grad_input = call(
        functools.partial(input_kernel, owners, scale),
        jax.ShapeDtypeStruct((tokens, features), bf16),
        [in_smem] * 2 + [in_vmem] * (2 + owners),
        in_vmem,
        flops=2 * tokens * features * width,
        moved=token_bytes + pair_bytes,
    )(here, lengths, mine, other, *pairs)

    gradient = call(
        functools.partial(merge_kernel, owners),
        jax.ShapeDtypeStruct(table.shape, bf16),
        [in_smem] * 3 + [in_vmem] * owners + [in_hbm],
        in_hbm,
        [
            pltpu.VMEM((rows, width), f32),
            pltpu.VMEM((owners, rows, width), bf16),
            pltpu.SemaphoreType.DMA((owners,)),
        ],
        moved=2 * pair_bytes,
        aliases={3 + owners: 0},
    )(ids, here, lengths, *arrived, blank)
    return grad_input, gradient[:, None]


def without_kernels(activations, cotangent, adapter_weight_pair, adapter_of_block, block_live_length):
    owners = lax.axis_size("dp")
    here = lax.axis_index("dp")
    count, _, rows, width = adapter_weight_pair.shape
    rank = width // 2
    scale = adapter_alpha / rank
    adapters = adapter_of_block[:, 0]
    lengths = block_live_length[:, 0]
    keep = (jnp.arange(activations.shape[0], dtype=jnp.int32) < lengths[here])[:, None]
    inputs = jnp.where(keep, activations, jnp.zeros_like(activations))
    grads_out = jnp.where(keep, cotangent, jnp.zeros_like(cotangent))
    fetched = lax.all_to_all(
        adapter_weight_pair[:, 0][adapters], "dp", split_axis=0, concat_axis=0, tiled=True
    )
    pair = fetched.reshape(-1, width)
    down, upward = pair[:, :rank], pair[:, rank:]
    f32 = jnp.float32
    hidden_part = jnp.dot(inputs, down, preferred_element_type=f32)
    dhidden_part = scale * jnp.dot(grads_out, upward, preferred_element_type=f32)
    hidden, dhidden = lax.psum((hidden_part, dhidden_part), "tensor")
    hidden16, dhidden16 = hidden.astype(jnp.bfloat16), dhidden.astype(jnp.bfloat16)
    d_down = jnp.dot(inputs.T, dhidden16, preferred_element_type=f32)
    d_up = scale * jnp.dot(grads_out.T, hidden16, preferred_element_type=f32)
    sent = jnp.concatenate([d_down, d_up], axis=1).astype(jnp.bfloat16).reshape(owners, rows, width)
    received = lax.all_to_all(sent, "dp", split_axis=0, concat_axis=0, tiled=True).astype(f32)
    same = adapters[:, None] == adapters[None, :]
    total = jnp.sum(jnp.where(same, lengths[None, :], 0), axis=1).astype(f32)
    summed = jax.ops.segment_sum(received, adapters, num_segments=count)
    denom = jnp.ones((count,), f32).at[adapters].set(jnp.maximum(total, 1.0))
    gradient = (summed / denom[:, None, None]).astype(jnp.bfloat16)
    grad_input = jnp.dot(dhidden16, down.T, preferred_element_type=f32).astype(jnp.bfloat16)
    return grad_input, gradient[:, None]


def solution(mesh):
    owners, cores = mesh.shape["dp"], mesh.shape["tensor"]

    def on_device(activations, cotangent, adapter_weight_pair, *rest):
        rows = adapter_weight_pair.shape[2]
        fits = owners & (owners - 1) == 0 and cores == 2 and rows % 256 == 0
        body = with_kernels if fits else without_kernels
        return body(activations, cotangent, adapter_weight_pair, *rest)

    in_specs = (
        P(("group", "dp"), "tensor"),
        P(("group", "dp"), "tensor"),
        P(None, "tensor", "dp", None),
        P("group", None),
        P("group", None),
    )
    out_specs = (P(("group", "dp"), "tensor"), P("group", "tensor", "dp", None))
    return jax.shard_map(
        on_device, mesh=mesh, in_specs=in_specs, out_specs=out_specs, check_vma=False
    )
```

```python
import functools

import jax
import jax.numpy as jnp
from jax import lax
from jax.experimental import pallas as pl
from jax.experimental.pallas import tpu as pltpu
from jax.sharding import PartitionSpec as P

adapter_alpha = 128.0

in_vmem = pl.BlockSpec(memory_space=pltpu.VMEM)
in_smem = pl.BlockSpec(memory_space=pltpu.SMEM)
in_hbm = pl.BlockSpec(memory_space=pltpu.HBM)


def low_lanes(rows, width):
    return lax.broadcasted_iota(jnp.int32, (rows, width), 1) < width // 2


def call(kernel, out_shape, in_specs, out_specs, scratch=(), flops=0, moved=0, aliases=None, vmem=40):
    return pl.pallas_call(
        kernel,
        out_shape=out_shape,
        in_specs=in_specs,
        out_specs=out_specs,
        scratch_shapes=list(scratch),
        input_output_aliases=aliases or {},
        compiler_params=pltpu.CompilerParams(vmem_limit_bytes=vmem * 1024 * 1024),
        cost_estimate=pl.CostEstimate(flops=flops, bytes_accessed=moved, transcendentals=0),
    )


def gather_kernel(owners, ids, here, table, *refs):
    out, sems = refs[:owners], refs[owners]
    copies = [
        pltpu.make_async_copy(table.at[ids[here[0] ^ k]], out[k], sems.at[k])
        for k in range(owners)
    ]
    for copy in copies:
        copy.start()
    for copy in copies:
        copy.wait()


def prep_kernel(rows, after, x, y, turned, blank, zeros, sem):
    zeros[...] = jnp.zeros_like(zeros)
    step = zeros.shape[0]
    copies = [
        pltpu.make_async_copy(zeros, blank.at[pl.ds(s, step)], sem.at[s // step])
        for s in range(0, blank.shape[0], step)
    ]
    for copy in copies:
        copy.start()
    tokens = x.shape[0]

    @pl.loop(0, x.shape[1] // rows)
    def _(owner):
        columns = pl.ds(pl.multiple_of(owner * rows, rows), rows)
        turned[owner, :, pl.ds(0, tokens)] = x[:, columns].T
        turned[owner, :, pl.ds(tokens, tokens)] = y[:, columns].T

    for copy in copies:
        copy.wait()


def rank_kernel(owners, here, x, y, *refs):
    pairs, out = refs[:owners], refs[owners]
    rows, width = pairs[0].shape
    tokens = x.shape[0]
    x_rank = jnp.zeros((tokens, width), jnp.float32)
    y_rank = jnp.zeros((tokens, width), jnp.float32)
    for k in range(owners):
        columns = pl.ds(pl.multiple_of((here[0] ^ k) * rows, rows), rows)
        x_rank += jnp.dot(x[:, columns], pairs[k][...], preferred_element_type=jnp.float32)
        y_rank += jnp.dot(y[:, columns], pairs[k][...], preferred_element_type=jnp.float32)
    out[...] = jnp.where(low_lanes(tokens, width), x_rank, y_rank)


def rounded(mine, other, length, scale):
    total = mine[...] + other[...]
    rows, width = total.shape
    total = jnp.where(low_lanes(rows, width), total, scale * total)
    live = lax.broadcasted_iota(jnp.int32, (rows, width), 0) < length
    return jnp.where(live, total, 0.0)


def swap_halves(value):
    return pltpu.roll(value, value.shape[-1] // 2, 1)


def piece_kernel(owners, scale, here, lengths, mine, other, turned, *refs):
    me = here[0]
    both = swap_halves(rounded(mine, other, lengths[me], scale))
    low = low_lanes(*both.shape)
    top = jnp.where(low, both, 0.0).astype(jnp.bfloat16)
    bottom = jnp.where(low, 0.0, both).astype(jnp.bfloat16)
    ranks = jnp.concatenate([top, bottom], axis=0)
    for k in range(owners):
        piece = jnp.dot(turned[me ^ k], ranks, preferred_element_type=jnp.float32)
        refs[k][...] = jnp.where(low_lanes(*piece.shape), piece, scale * piece).astype(jnp.bfloat16)


def input_kernel(owners, scale, here, lengths, mine, other, *refs):
    pairs, out = refs[:owners], refs[owners]
    me = here[0]
    both = swap_halves(rounded(mine, other, lengths[me], scale))
    ranks = jnp.where(low_lanes(*both.shape), both, 0.0).astype(jnp.bfloat16)
    rows = pairs[0].shape[0]
    for k in range(owners):
        columns = pl.ds(pl.multiple_of((me ^ k) * rows, rows), rows)
        out[:, columns] = lax.dot_general(
            ranks, pairs[k][...], (((1,), (1,)), ((), ())), preferred_element_type=jnp.float32
        ).astype(jnp.bfloat16)


def merge_kernel(owners, ids, here, lengths, *refs):
    pieces = refs[:owners]
    out, total, held, sems = refs[owners + 1 :]
    blocks = [here[0] ^ k for k in range(owners)]
    copies, firsts = [], []
    for k in range(owners):
        adapter = ids[blocks[k]]
        copies.append(pltpu.make_async_copy(held.at[k], out.at[adapter], sems.at[k]))
        same = [ids[blocks[other]] == adapter for other in range(owners)]
        earlier = functools.reduce(jnp.logical_or, same[:k], jnp.bool_(False))
        later = functools.reduce(jnp.logical_or, same[k + 1 :], jnp.bool_(False))
        firsts.append(jnp.logical_not(earlier))

        def store(value, count):
            denom = jnp.maximum(count.astype(jnp.float32), 1.0)
            part = 1.0 / jnp.full((1, value.shape[1]), denom)
            held[k] = (value * part).astype(jnp.bfloat16)
            copies[k].start()

        @pl.when(firsts[k] & jnp.logical_not(later))
        def _():
            store(pieces[k][...].astype(jnp.float32), lengths[blocks[k]])

        @pl.when(firsts[k] & later)
        def _():
            total[...] = pieces[k][...].astype(jnp.float32)
            count = lengths[blocks[k]]
            for other in range(k + 1, owners):
                count += jnp.where(same[other], lengths[blocks[other]], 0)

                @pl.when(same[other])
                def _():
                    total[...] += pieces[other][...].astype(jnp.float32)

            store(total[...], count)

    for k in range(owners):
        pl.when(firsts[k])(copies[k].wait)


def exchange(pieces):
    owners = len(pieces)
    order = list(range(owners // 2, owners)) + list(range(1, owners // 2))
    out = {0: pieces[0]}
    for k in order:
        piece = pieces[k]
        if 1 < k < owners // 2:
            piece, out[k - 1] = lax.optimization_barrier((piece, out[k - 1]))
        out[k] = lax.ppermute(piece, "dp", [(i, i ^ k) for i in range(owners)])
    return [out[k] for k in range(owners)]


def across_cores(value):
    cores = lax.axis_size("tensor")
    return lax.ppermute(value, "tensor", [(i, i ^ 1) for i in range(cores)])


def with_kernels(activations, cotangent, adapter_weight_pair, adapter_of_block, block_live_length):
    owners = lax.axis_size("dp")
    here = lax.axis_index("dp").astype(jnp.int32).reshape(1)
    ids, lengths = adapter_of_block[:, 0], block_live_length[:, 0]
    count, _, rows, width = adapter_weight_pair.shape
    table = adapter_weight_pair.reshape(count, rows, width)
    tokens, features = activations.shape
    scale = adapter_alpha / (width // 2)
    bf16, f32 = jnp.bfloat16, jnp.float32
    pair_shapes = [jax.ShapeDtypeStruct((rows, width), bf16)] * owners
    pair_bytes = owners * rows * width * 2
    token_bytes = tokens * features * 2

    sent = call(
        functools.partial(gather_kernel, owners),
        pair_shapes,
        [in_smem, in_smem, in_hbm],
        [in_vmem] * owners,
        [pltpu.SemaphoreType.DMA((owners,))],
        moved=2 * pair_bytes,
        vmem=53,
    )(ids, here, table)
    pairs = exchange(sent)

    step = 8
    turned, blank = call(
        functools.partial(prep_kernel, rows),
        [
            jax.ShapeDtypeStruct((owners, rows, 2 * tokens), bf16),
            jax.ShapeDtypeStruct(table.shape, bf16),
        ],
        [in_hbm, in_vmem, in_vmem],
        [in_vmem, in_hbm],
        [pltpu.VMEM((step, rows, width), bf16), pltpu.SemaphoreType.DMA((count // step,))],
        moved=4 * token_bytes + 2 * count * rows * width,
    )(pairs[2], activations, cotangent)
    *pairs, turned, blank = lax.optimization_barrier((*pairs, turned, blank))

    mine = call(
        functools.partial(rank_kernel, owners),
        jax.ShapeDtypeStruct((tokens, width), f32),
        [in_smem] + [in_vmem] * (2 + owners),
        in_vmem,
        flops=4 * tokens * features * width,
        moved=2 * token_bytes + pair_bytes,
    )(here, activations, cotangent, *pairs)
    other = across_cores(mine)

    pieces = call(
        functools.partial(piece_kernel, owners, scale),
        pair_shapes,
        [in_smem] * 2 + [in_vmem] * 3,
        [in_vmem] * owners,
        flops=4 * tokens * features * width,
        moved=2 * token_bytes + pair_bytes,
    )(here, lengths, mine, other, turned)
    arrived = exchange(pieces)

    grad_input = call(
        functools.partial(input_kernel, owners, scale),
        jax.ShapeDtypeStruct((tokens, features), bf16),
        [in_smem] * 2 + [in_vmem] * (2 + owners),
        in_vmem,
        flops=2 * tokens * features * width,
        moved=token_bytes + pair_bytes,
    )(here, lengths, mine, other, *pairs)

    gradient = call(
        functools.partial(merge_kernel, owners),
        jax.ShapeDtypeStruct(table.shape, bf16),
        [in_smem] * 3 + [in_vmem] * owners + [in_hbm],
        in_hbm,
        [
            pltpu.VMEM((rows, width), f32),
            pltpu.VMEM((owners, rows, width), bf16),
            pltpu.SemaphoreType.DMA((owners,)),
        ],
        moved=2 * pair_bytes,
        aliases={3 + owners: 0},
    )(ids, here, lengths, *arrived, blank)
    return grad_input, gradient[:, None]


def without_kernels(activations, cotangent, adapter_weight_pair, adapter_of_block, block_live_length):
    owners = lax.axis_size("dp")
    here = lax.axis_index("dp")
    count, _, rows, width = adapter_weight_pair.shape
    rank = width // 2
    scale = adapter_alpha / rank
    adapters = adapter_of_block[:, 0]
    lengths = block_live_length[:, 0]
    keep = (jnp.arange(activations.shape[0], dtype=jnp.int32) < lengths[here])[:, None]
    inputs = jnp.where(keep, activations, jnp.zeros_like(activations))
    grads_out = jnp.where(keep, cotangent, jnp.zeros_like(cotangent))
    fetched = lax.all_to_all(
        adapter_weight_pair[:, 0][adapters], "dp", split_axis=0, concat_axis=0, tiled=True
    )
    pair = fetched.reshape(-1, width)
    down, upward = pair[:, :rank], pair[:, rank:]
    f32 = jnp.float32
    hidden_part = jnp.dot(inputs, down, preferred_element_type=f32)
    dhidden_part = scale * jnp.dot(grads_out, upward, preferred_element_type=f32)
    hidden, dhidden = lax.psum((hidden_part, dhidden_part), "tensor")
    hidden16, dhidden16 = hidden.astype(jnp.bfloat16), dhidden.astype(jnp.bfloat16)
    d_down = jnp.dot(inputs.T, dhidden16, preferred_element_type=f32)
    d_up = scale * jnp.dot(grads_out.T, hidden16, preferred_element_type=f32)
    sent = jnp.concatenate([d_down, d_up], axis=1).astype(jnp.bfloat16).reshape(owners, rows, width)
    received = lax.all_to_all(sent, "dp", split_axis=0, concat_axis=0, tiled=True).astype(f32)
    same = adapters[:, None] == adapters[None, :]
    total = jnp.sum(jnp.where(same, lengths[None, :], 0), axis=1).astype(f32)
    summed = jax.ops.segment_sum(received, adapters, num_segments=count)
    denom = jnp.ones((count,), f32).at[adapters].set(jnp.maximum(total, 1.0))
    gradient = (summed / denom[:, None, None]).astype(jnp.bfloat16)
    grad_input = jnp.dot(dhidden16, down.T, preferred_element_type=f32).astype(jnp.bfloat16)
    return grad_input, gradient[:, None]


def solution(mesh):
    owners, cores = mesh.shape["dp"], mesh.shape["tensor"]

    def on_device(activations, cotangent, adapter_weight_pair, *rest):
        rows = adapter_weight_pair.shape[2]
        fits = owners & (owners - 1) == 0 and cores == 2 and rows % 256 == 0
        body = with_kernels if fits else without_kernels
        return body(activations, cotangent, adapter_weight_pair, *rest)

    in_specs = (
        P(("group", "dp"), "tensor"),
        P(("group", "dp"), "tensor"),
        P(None, "tensor", "dp", None),
        P("group", None),
        P("group", None),
    )
    out_specs = (P(("group", "dp"), "tensor"), P("group", "tensor", "dp", None))
    return jax.shard_map(
        on_device, mesh=mesh, in_specs=in_specs, out_specs=out_specs, check_vma=False
    )
```

```python
import functools

import jax
import jax.numpy as jnp
from jax import lax
from jax.experimental import pallas as pl
from jax.experimental.pallas import tpu as pltpu
from jax.sharding import PartitionSpec as P

adapter_alpha = 128.0

in_vmem = pl.BlockSpec(memory_space=pltpu.VMEM)
in_smem = pl.BlockSpec(memory_space=pltpu.SMEM)
in_hbm = pl.BlockSpec(memory_space=pltpu.HBM)


def low_lanes(rows, width):
    return lax.broadcasted_iota(jnp.int32, (rows, width), 1) < width // 2


def call(kernel, out_shape, in_specs, out_specs, scratch=(), flops=0, moved=0, aliases=None, vmem=40):
    return pl.pallas_call(
        kernel,
        out_shape=out_shape,
        in_specs=in_specs,
        out_specs=out_specs,
        scratch_shapes=list(scratch),
        input_output_aliases=aliases or {},
        compiler_params=pltpu.CompilerParams(vmem_limit_bytes=vmem * 1024 * 1024),
        cost_estimate=pl.CostEstimate(flops=flops, bytes_accessed=moved, transcendentals=0),
    )


def gather_kernel(peers, ids, here, table, *refs):
    out, sems = refs[: len(peers)], refs[len(peers)]
    copies = [
        pltpu.make_async_copy(table.at[ids[here[0] ^ k]], out[n], sems.at[n])
        for n, k in enumerate(peers)
    ]
    for copy in copies:
        copy.start()
    for copy in copies:
        copy.wait()


def prep_kernel(rows, after, x, y, turned, blank, zeros, sem):
    zeros[...] = jnp.zeros_like(zeros)
    step = zeros.shape[0]
    copies = [
        pltpu.make_async_copy(zeros, blank.at[pl.ds(s, step)], sem.at[s // step])
        for s in range(0, blank.shape[0], step)
    ]
    for copy in copies:
        copy.start()
    tokens = x.shape[0]

    @pl.loop(0, x.shape[1] // rows)
    def _(owner):
        columns = pl.ds(pl.multiple_of(owner * rows, rows), rows)
        turned[owner, :, pl.ds(0, tokens)] = x[:, columns].T
        turned[owner, :, pl.ds(tokens, tokens)] = y[:, columns].T

    for copy in copies:
        copy.wait()


def rank_kernel(peers, here, x, y, *refs):
    pairs, out = refs[: len(peers)], refs[len(peers)]
    rows, width = pairs[0].shape
    tokens = x.shape[0]
    x_rank = jnp.zeros((tokens, width), jnp.float32)
    y_rank = jnp.zeros((tokens, width), jnp.float32)
    for n, k in enumerate(peers):
        columns = pl.ds(pl.multiple_of((here[0] ^ k) * rows, rows), rows)
        x_rank += jnp.dot(x[:, columns], pairs[n][...], preferred_element_type=jnp.float32)
        y_rank += jnp.dot(y[:, columns], pairs[n][...], preferred_element_type=jnp.float32)
    out[...] = jnp.where(low_lanes(tokens, width), x_rank, y_rank)


def rounded(mine, other, length, scale):
    total = mine[...] + other[...]
    rows, width = total.shape
    total = jnp.where(low_lanes(rows, width), total, scale * total)
    live = lax.broadcasted_iota(jnp.int32, (rows, width), 0) < length
    return jnp.where(live, total, 0.0)


def swap_halves(value):
    return pltpu.roll(value, value.shape[-1] // 2, 1)


def piece_kernel(peers, scale, here, lengths, mine, other, turned, *refs):
    me = here[0]
    both = swap_halves(rounded(mine, other, lengths[me], scale))
    low = low_lanes(*both.shape)
    top = jnp.where(low, both, 0.0).astype(jnp.bfloat16)
    bottom = jnp.where(low, 0.0, both).astype(jnp.bfloat16)
    ranks = jnp.concatenate([top, bottom], axis=0)
    for n, k in enumerate(peers):
        piece = jnp.dot(turned[me ^ k], ranks, preferred_element_type=jnp.float32)
        refs[n][...] = jnp.where(low_lanes(*piece.shape), piece, scale * piece).astype(jnp.bfloat16)


def input_kernel(peers, scale, here, lengths, mine, other, *refs):
    pairs, out = refs[: len(peers)], refs[len(peers)]
    me = here[0]
    both = swap_halves(rounded(mine, other, lengths[me], scale))
    ranks = jnp.where(low_lanes(*both.shape), both, 0.0).astype(jnp.bfloat16)
    rows = pairs[0].shape[0]
    for n, k in enumerate(peers):
        columns = pl.ds(pl.multiple_of((me ^ k) * rows, rows), rows)
        out[:, columns] = lax.dot_general(
            ranks, pairs[n][...], (((1,), (1,)), ((), ())), preferred_element_type=jnp.float32
        ).astype(jnp.bfloat16)


def merge_kernel(peers, ids, here, lengths, *refs):
    owners = len(peers)
    pieces = refs[:owners]
    out, total, held, sems = refs[owners + 1 :]
    blocks = [here[0] ^ k for k in peers]
    copies, firsts = [], []
    for k in range(owners):
        adapter = ids[blocks[k]]
        copies.append(pltpu.make_async_copy(held.at[k], out.at[adapter], sems.at[k]))
        same = [ids[blocks[other]] == adapter for other in range(owners)]
        earlier = functools.reduce(jnp.logical_or, same[:k], jnp.bool_(False))
        later = functools.reduce(jnp.logical_or, same[k + 1 :], jnp.bool_(False))
        firsts.append(jnp.logical_not(earlier))

        def store(value, count):
            denom = jnp.maximum(count.astype(jnp.float32), 1.0)
            part = 1.0 / jnp.full((1, value.shape[1]), denom)
            held[k] = (value * part).astype(jnp.bfloat16)
            copies[k].start()

        @pl.when(firsts[k] & jnp.logical_not(later))
        def _():
            store(pieces[k][...].astype(jnp.float32), lengths[blocks[k]])

        @pl.when(firsts[k] & later)
        def _():
            total[...] = pieces[k][...].astype(jnp.float32)
            count = lengths[blocks[k]]
            for other in range(k + 1, owners):
                count += jnp.where(same[other], lengths[blocks[other]], 0)

                @pl.when(same[other])
                def _():
                    total[...] += pieces[other][...].astype(jnp.float32)

            store(total[...], count)

    for k in range(owners):
        pl.when(firsts[k])(copies[k].wait)


def peer_order(owners):
    near = list(range(1, owners // 2))
    return (0, *range(owners // 2, owners), *near[:1], *near[:0:-1])


def exchange(pieces, peers):
    out = [pieces[0]]
    for k, piece in zip(peers[1:], pieces[1:]):
        out.append(lax.ppermute(piece, "dp", [(i, i ^ k) for i in range(len(peers))]))
    return out


def across_cores(value):
    cores = lax.axis_size("tensor")
    return lax.ppermute(value, "tensor", [(i, i ^ 1) for i in range(cores)])


def with_kernels(activations, cotangent, adapter_weight_pair, adapter_of_block, block_live_length):
    owners = lax.axis_size("dp")
    peers = peer_order(owners)
    here = lax.axis_index("dp").astype(jnp.int32).reshape(1)
    ids, lengths = adapter_of_block[:, 0], block_live_length[:, 0]
    count, _, rows, width = adapter_weight_pair.shape
    table = adapter_weight_pair.reshape(count, rows, width)
    tokens, features = activations.shape
    scale = adapter_alpha / (width // 2)
    bf16, f32 = jnp.bfloat16, jnp.float32
    pair_shapes = [jax.ShapeDtypeStruct((rows, width), bf16)] * owners
    pair_bytes = owners * rows * width * 2
    token_bytes = tokens * features * 2

    sent = call(
        functools.partial(gather_kernel, peers),
        pair_shapes,
        [in_smem, in_smem, in_hbm],
        [in_vmem] * owners,
        [pltpu.SemaphoreType.DMA((owners,))],
        moved=2 * pair_bytes,
        vmem=53,
    )(ids, here, table)
    pairs = exchange(sent, peers)

    step = 8
    turned, blank = call(
        functools.partial(prep_kernel, rows),
        [
            jax.ShapeDtypeStruct((owners, rows, 2 * tokens), bf16),
            jax.ShapeDtypeStruct(table.shape, bf16),
        ],
        [in_hbm, in_vmem, in_vmem],
        [in_vmem, in_hbm],
        [pltpu.VMEM((step, rows, width), bf16), pltpu.SemaphoreType.DMA((count // step,))],
        moved=4 * token_bytes + 2 * count * rows * width,
    )(pairs[5], activations, cotangent)
    *pairs, turned, blank = lax.optimization_barrier((*pairs, turned, blank))

    mine = call(
        functools.partial(rank_kernel, peers),
        jax.ShapeDtypeStruct((tokens, width), f32),
        [in_smem] + [in_vmem] * (2 + owners),
        in_vmem,
        flops=4 * tokens * features * width,
        moved=2 * token_bytes + pair_bytes,
    )(here, activations, cotangent, *pairs)
    other = across_cores(mine)

    pieces = call(
        functools.partial(piece_kernel, peers, scale),
        pair_shapes,
        [in_smem] * 2 + [in_vmem] * 3,
        [in_vmem] * owners,
        flops=4 * tokens * features * width,
        moved=2 * token_bytes + pair_bytes,
    )(here, lengths, mine, other, turned)
    arrived = exchange(pieces, peers)

    grad_input = call(
        functools.partial(input_kernel, peers, scale),
        jax.ShapeDtypeStruct((tokens, features), bf16),
        [in_smem] * 2 + [in_vmem] * (2 + owners),
        in_vmem,
        flops=2 * tokens * features * width,
        moved=token_bytes + pair_bytes,
    )(here, lengths, mine, other, *pairs)

    gradient = call(
        functools.partial(merge_kernel, peers),
        jax.ShapeDtypeStruct(table.shape, bf16),
        [in_smem] * 3 + [in_vmem] * owners + [in_hbm],
        in_hbm,
        [
            pltpu.VMEM((rows, width), f32),
            pltpu.VMEM((owners, rows, width), bf16),
            pltpu.SemaphoreType.DMA((owners,)),
        ],
        moved=2 * pair_bytes,
        aliases={3 + owners: 0},
    )(ids, here, lengths, *arrived, blank)
    return grad_input, gradient[:, None]


def without_kernels(activations, cotangent, adapter_weight_pair, adapter_of_block, block_live_length):
    owners = lax.axis_size("dp")
    here = lax.axis_index("dp")
    count, _, rows, width = adapter_weight_pair.shape
    rank = width // 2
    scale = adapter_alpha / rank
    adapters = adapter_of_block[:, 0]
    lengths = block_live_length[:, 0]
    keep = (jnp.arange(activations.shape[0], dtype=jnp.int32) < lengths[here])[:, None]
    inputs = jnp.where(keep, activations, jnp.zeros_like(activations))
    grads_out = jnp.where(keep, cotangent, jnp.zeros_like(cotangent))
    fetched = lax.all_to_all(
        adapter_weight_pair[:, 0][adapters], "dp", split_axis=0, concat_axis=0, tiled=True
    )
    pair = fetched.reshape(-1, width)
    down, upward = pair[:, :rank], pair[:, rank:]
    f32 = jnp.float32
    hidden_part = jnp.dot(inputs, down, preferred_element_type=f32)
    dhidden_part = scale * jnp.dot(grads_out, upward, preferred_element_type=f32)
    hidden, dhidden = lax.psum((hidden_part, dhidden_part), "tensor")
    hidden16, dhidden16 = hidden.astype(jnp.bfloat16), dhidden.astype(jnp.bfloat16)
    d_down = jnp.dot(inputs.T, dhidden16, preferred_element_type=f32)
    d_up = scale * jnp.dot(grads_out.T, hidden16, preferred_element_type=f32)
    sent = jnp.concatenate([d_down, d_up], axis=1).astype(jnp.bfloat16).reshape(owners, rows, width)
    received = lax.all_to_all(sent, "dp", split_axis=0, concat_axis=0, tiled=True).astype(f32)
    same = adapters[:, None] == adapters[None, :]
    total = jnp.sum(jnp.where(same, lengths[None, :], 0), axis=1).astype(f32)
    summed = jax.ops.segment_sum(received, adapters, num_segments=count)
    denom = jnp.ones((count,), f32).at[adapters].set(jnp.maximum(total, 1.0))
    gradient = (summed / denom[:, None, None]).astype(jnp.bfloat16)
    grad_input = jnp.dot(dhidden16, down.T, preferred_element_type=f32).astype(jnp.bfloat16)
    return grad_input, gradient[:, None]


def solution(mesh):
    owners, cores = mesh.shape["dp"], mesh.shape["tensor"]

    def on_device(activations, cotangent, adapter_weight_pair, *rest):
        rows = adapter_weight_pair.shape[2]
        fits = owners & (owners - 1) == 0 and cores == 2 and rows % 256 == 0
        body = with_kernels if fits else without_kernels
        return body(activations, cotangent, adapter_weight_pair, *rest)

    in_specs = (
        P(("group", "dp"), "tensor"),
        P(("group", "dp"), "tensor"),
        P(None, "tensor", "dp", None),
        P("group", None),
        P("group", None),
    )
    out_specs = (P(("group", "dp"), "tensor"), P("group", "tensor", "dp", None))
    return jax.shard_map(
        on_device, mesh=mesh, in_specs=in_specs, out_specs=out_specs, check_vma=False
    )
```

```python
import functools

import jax
import jax.numpy as jnp
from jax import lax
from jax.experimental import pallas as pl
from jax.experimental.pallas import tpu as pltpu
from jax.sharding import PartitionSpec as P

adapter_alpha = 128.0

in_vmem = pl.BlockSpec(memory_space=pltpu.VMEM)
in_smem = pl.BlockSpec(memory_space=pltpu.SMEM)
in_hbm = pl.BlockSpec(memory_space=pltpu.HBM)


def low_lanes(rows, width):
    return lax.broadcasted_iota(jnp.int32, (rows, width), 1) < width // 2


def call(kernel, out_shape, in_specs, out_specs, scratch=(), flops=0, moved=0, aliases=None, vmem=40):
    return pl.pallas_call(
        kernel,
        out_shape=out_shape,
        in_specs=in_specs,
        out_specs=out_specs,
        scratch_shapes=list(scratch),
        input_output_aliases=aliases or {},
        compiler_params=pltpu.CompilerParams(vmem_limit_bytes=vmem * 1024 * 1024),
        cost_estimate=pl.CostEstimate(flops=flops, bytes_accessed=moved, transcendentals=0),
    )


def swap_halves(value):
    return pltpu.roll(value, value.shape[-1] // 2, 1)


def gather_kernel(plan, ids, here, table, *refs):
    split, whole, near = plan
    parts = len(split)
    up, rest = refs[:parts], refs[parts:]
    straight, rest = rest[: len(whole)], rest[len(whole) :]
    close, rest = rest[0], rest[1:]
    down, (held, sems) = rest[:parts], rest[parts:]
    me = here[0]
    targets = [(me ^ k, held.at[n]) for n, k in enumerate(split)]
    targets += [(me ^ k, straight[n]) for n, k in enumerate(whole)]
    targets += [((me & -near) | n, close.at[n]) for n in range(near)]
    copies = [
        pltpu.make_async_copy(table.at[ids[block]], target, sems.at[n])
        for n, (block, target) in enumerate(targets)
    ]
    for copy in copies:
        copy.start()
    half = held.shape[1] // 2
    low = low_lanes(half, held.shape[2])
    for n in range(parts):
        copies[n].wait()
        first = held[n, :half].astype(jnp.float32)
        second = held[n, half:].astype(jnp.float32)
        up[n][...] = jnp.where(low, swap_halves(first), second).astype(jnp.bfloat16)
        down[n][...] = jnp.where(low, first, swap_halves(second)).astype(jnp.bfloat16)
    for copy in copies[parts:]:
        copy.wait()


def prep_kernel(rows, after, x, y, turned, blank, zeros, sem):
    zeros[...] = jnp.zeros_like(zeros)
    step = zeros.shape[0]
    copies = [
        pltpu.make_async_copy(zeros, blank.at[pl.ds(s, step)], sem.at[s // step])
        for s in range(0, blank.shape[0], step)
    ]
    for copy in copies:
        copy.start()
    tokens = x.shape[0]

    @pl.loop(0, x.shape[1] // rows)
    def _(owner):
        columns = pl.ds(pl.multiple_of(owner * rows, rows), rows)
        turned[owner, :, pl.ds(0, tokens)] = x[:, columns].T
        turned[owner, :, pl.ds(tokens, tokens)] = y[:, columns].T

    for copy in copies:
        copy.wait()


def halves_product(values, packed, owner):
    half = packed.shape[0]
    first = pl.ds(pl.multiple_of(owner * 2 * half, half), half)
    second = pl.ds(pl.multiple_of(owner * 2 * half + half, half), half)
    one = jnp.dot(values[:, first], packed[...], preferred_element_type=jnp.float32)
    two = jnp.dot(values[:, second], packed[...], preferred_element_type=jnp.float32)
    return one, two


def rank_kernel(plan, here, x, y, *refs):
    split, whole, near = plan
    up, straight = refs[: len(split)], refs[len(split) : -3]
    close, dhidden, hidden = refs[-3:]
    _, rows, width = close.shape
    tokens = x.shape[0]
    me = here[0]
    x_rank = jnp.zeros((tokens, width), jnp.float32)
    y_rank = jnp.zeros((tokens, width), jnp.float32)
    y_first = jnp.zeros((tokens, width), jnp.float32)
    pairs = [((me & -near) | n, close.at[n]) for n in range(near)]
    pairs += [(me ^ k, straight[n]) for n, k in enumerate(whole)]
    for owner, pair in pairs:
        columns = pl.ds(pl.multiple_of(owner * rows, rows), rows)
        x_rank += jnp.dot(x[:, columns], pair[...], preferred_element_type=jnp.float32)
        y_rank += jnp.dot(y[:, columns], pair[...], preferred_element_type=jnp.float32)
    for n, k in enumerate(split):
        first, second = halves_product(y, up[n], me ^ k)
        y_first += first
        y_rank += second
    y_rank += swap_halves(y_first)
    half = tokens // 2
    low = low_lanes(half, width)
    dhidden[...] = jnp.where(low, swap_halves(y_rank[:half]), y_rank[half:])
    hidden[...] = jnp.where(low, x_rank[:half], swap_halves(x_rank[half:]))


def rank_rest_kernel(plan, here, x, partial, *refs):
    split, _, _ = plan
    down, out = refs[:-1], refs[-1]
    tokens, width = x.shape[0], partial.shape[1]
    x_first = jnp.zeros((tokens, width), jnp.float32)
    x_second = jnp.zeros((tokens, width), jnp.float32)
    for n, k in enumerate(split):
        first, second = halves_product(x, down[n], here[0] ^ k)
        x_first += first
        x_second += second
    x_rank = x_first + swap_halves(x_second)
    half = tokens // 2
    low = low_lanes(half, width)
    out[...] = partial[...] + jnp.where(low, x_rank[:half], swap_halves(x_rank[half:]))


def rounded(mine, other, length, scale):
    total = scale * (mine[...] + other[...])
    swapped = swap_halves(total)
    low = low_lanes(*total.shape)
    live = lax.broadcasted_iota(jnp.int32, (2 * total.shape[0], total.shape[1]), 0) < length
    left = [jnp.where(low, total, 0.0), jnp.where(low, swapped, 0.0)]
    right = [jnp.where(low, 0.0, swapped), jnp.where(low, 0.0, total)]
    return [jnp.where(live, jnp.concatenate(v, axis=0), 0.0).astype(jnp.bfloat16) for v in (left, right)]


def packed_piece(turned, owner, lanes, left, right):
    half = turned.shape[1] // 2
    first = jnp.dot(turned[owner, :half, lanes], left, preferred_element_type=jnp.float32)
    second = jnp.dot(turned[owner, half:, lanes], right, preferred_element_type=jnp.float32)
    return first + second


def down_piece_kernel(plan, scale, here, lengths, mine, other, turned, *out):
    split, _, _ = plan
    me = here[0]
    left, right = rounded(mine, other, lengths[me], scale)
    tokens = left.shape[0]
    for n, k in enumerate(split):
        out[n][...] = packed_piece(turned, me ^ k, slice(0, tokens), left, right).astype(jnp.bfloat16)


def piece_kernel(plan, scale, here, lengths, d_mine, d_other, mine, other, turned, *refs):
    split, whole, near = plan
    up, straight, close = refs[: len(split)], refs[len(split) : -1], refs[-1]
    me = here[0]
    dhidden, _ = rounded(d_mine, d_other, lengths[me], scale)
    left, right = rounded(mine, other, lengths[me], 1.0)
    tokens = left.shape[0]
    ranks = jnp.concatenate([dhidden, right], axis=0)

    def rows_for(owner):
        piece = jnp.dot(turned[owner], ranks, preferred_element_type=jnp.float32)
        return jnp.where(low_lanes(*piece.shape), piece, scale * piece).astype(jnp.bfloat16)

    for n, k in enumerate(split):
        piece = packed_piece(turned, me ^ k, slice(tokens, 2 * tokens), left, right)
        up[n][...] = (scale * piece).astype(jnp.bfloat16)
    for n, k in enumerate(whole):
        straight[n][...] = rows_for(me ^ k)
    for n in range(near):
        close[n] = rows_for((me & -near) | n)


def input_kernel(plan, scale, here, lengths, mine, other, *refs):
    split, whole, near = plan
    down, straight = refs[: len(split)], refs[len(split) : -2]
    close, out = refs[-2:]
    rows = close.shape[1]
    half = rows // 2
    me = here[0]
    left, right = rounded(mine, other, lengths[me], scale)

    def product(ranks, columns):
        value = lax.dot_general(
            ranks, columns, (((1,), (1,)), ((), ())), preferred_element_type=jnp.float32
        )
        return value.astype(jnp.bfloat16)

    pairs = [((me & -near) | n, close.at[n]) for n in range(near)]
    pairs += [(me ^ k, straight[n]) for n, k in enumerate(whole)]
    for owner, pair in pairs:
        out[:, pl.ds(pl.multiple_of(owner * rows, rows), rows)] = product(left, pair[...])
    for n, k in enumerate(split):
        start = (me ^ k) * rows
        out[:, pl.ds(pl.multiple_of(start, half), half)] = product(left, down[n][...])
        out[:, pl.ds(pl.multiple_of(start + half, half), half)] = product(right, down[n][...])


def merge_kernel(plan, ids, here, lengths, *refs):
    split, whole, near = plan
    parts = len(split)
    down, up, straight = refs[:parts], refs[parts : 2 * parts], refs[2 * parts : 2 * parts + len(whole)]
    close, _, out, total, held, sems = refs[2 * parts + len(whole) :]
    me = here[0]
    rows, width = total.shape
    half = rows // 2
    low = low_lanes(half, width)

    def unpacked(n):
        d_down, d_up = down[n][...].astype(jnp.float32), up[n][...].astype(jnp.float32)
        first = jnp.where(low, d_down, swap_halves(d_up))
        second = jnp.where(low, swap_halves(d_down), d_up)
        return jnp.concatenate([first, second], axis=0)

    def read(ref):
        return lambda: ref[...].astype(jnp.float32)

    pieces = [((me & -near) | n, read(close.at[n])) for n in range(near)]
    pieces += [(me ^ k, read(straight[n])) for n, k in enumerate(whole)]
    pieces += [(me ^ k, functools.partial(unpacked, n)) for n, k in enumerate(split)]
    owners = len(pieces)
    adapters = [ids[block] for block, _ in pieces]
    counts = [lengths[block] for block, _ in pieces]
    copies, firsts = [], []
    for k, (_, value) in enumerate(pieces):
        copies.append(pltpu.make_async_copy(held.at[k], out.at[adapters[k]], sems.at[k]))
        same = [adapters[other] == adapters[k] for other in range(owners)]
        earlier = functools.reduce(jnp.logical_or, same[:k], jnp.bool_(False))
        later = functools.reduce(jnp.logical_or, same[k + 1 :], jnp.bool_(False))
        firsts.append(jnp.logical_not(earlier))

        def store(sum_of, count):
            denom = jnp.maximum(count.astype(jnp.float32), 1.0)
            part = 1.0 / jnp.full((1, width), denom)
            held[k] = (sum_of * part).astype(jnp.bfloat16)
            copies[k].start()

        @pl.when(firsts[k] & jnp.logical_not(later))
        def _():
            store(value(), counts[k])

        @pl.when(firsts[k] & later)
        def _():
            total[...] = value()
            count = counts[k]
            for other in range(k + 1, owners):
                count += jnp.where(same[other], counts[other], 0)

                @pl.when(same[other])
                def _():
                    total[...] += pieces[other][1]()

            store(total[...], count)

    for k in range(owners):
        pl.when(firsts[k])(copies[k].wait)


def to_partner(pieces, partners, owners):
    return [
        lax.ppermute(piece, "dp", [(i, i ^ k) for i in range(owners)])
        for k, piece in zip(partners, pieces)
    ]


def among_near(pieces, owners):
    near = pieces.shape[0]
    groups = [list(range(start, start + near)) for start in range(0, owners, near)]
    return lax.all_to_all(
        pieces, "dp", split_axis=0, concat_axis=0, tiled=True, axis_index_groups=groups
    )


def after(value, *others):
    return lax.optimization_barrier((value, *others))[0]


def across_cores(value):
    cores = lax.axis_size("tensor")
    return lax.ppermute(value, "tensor", [(i, i ^ 1) for i in range(cores)])


def with_kernels(activations, cotangent, adapter_weight_pair, adapter_of_block, block_live_length):
    owners = lax.axis_size("dp")
    near = owners // 2
    far = list(range(near, owners))
    plan = split, whole, _ = tuple(far[-2:]), tuple(far[:-2]), near
    here = lax.axis_index("dp").astype(jnp.int32).reshape(1)
    ids, lengths = adapter_of_block[:, 0], block_live_length[:, 0]
    count, _, rows, width = adapter_weight_pair.shape
    table = adapter_weight_pair.reshape(count, rows, width)
    tokens, features = activations.shape
    scale = adapter_alpha / (width // 2)
    bf16, f32 = jnp.bfloat16, jnp.float32
    packed = jax.ShapeDtypeStruct((rows // 2, width), bf16)
    straight = jax.ShapeDtypeStruct((rows, width), bf16)
    stacked = jax.ShapeDtypeStruct((near, rows, width), bf16)
    rank_space = jax.ShapeDtypeStruct((tokens // 2, width), f32)
    parts, wholes = len(split), len(whole)
    pair_bytes = owners * rows * width * 2
    token_bytes = tokens * features * 2

    sent = call(
        functools.partial(gather_kernel, plan),
        [packed] * parts + [straight] * wholes + [stacked] + [packed] * parts,
        [in_smem, in_smem, in_hbm],
        [in_vmem] * (2 * parts + wholes + 1),
        [pltpu.VMEM((parts, rows, width), bf16), pltpu.SemaphoreType.DMA((owners,))],
        moved=2 * pair_bytes,
        vmem=53,
    )(ids, here, table)
    ups = to_partner(sent[:parts], split, owners)
    pairs = to_partner(sent[parts : parts + wholes], whole, owners)
    close = among_near(sent[parts + wholes], owners)
    downs = to_partner(sent[parts + wholes + 1 :], split, owners)

    step = 8
    turned, blank = call(
        functools.partial(prep_kernel, rows),
        [
            jax.ShapeDtypeStruct((owners, rows, 2 * tokens), bf16),
            jax.ShapeDtypeStruct(table.shape, bf16),
        ],
        [in_hbm, in_vmem, in_vmem],
        [in_vmem, in_hbm],
        [pltpu.VMEM((step, rows, width), bf16), pltpu.SemaphoreType.DMA((count // step,))],
        moved=4 * token_bytes + 2 * count * rows * width,
    )(sent[0], activations, cotangent)
    *ups, turned, blank = lax.optimization_barrier((*ups, turned, blank))

    dhidden, partial = call(
        functools.partial(rank_kernel, plan),
        [rank_space, rank_space],
        [in_smem] + [in_vmem] * (3 + parts + wholes),
        [in_vmem, in_vmem],
        flops=4 * tokens * features * width,
        moved=2 * token_bytes + pair_bytes,
    )(here, activations, cotangent, *ups, *pairs, close)
    dhidden_other = across_cores(dhidden)
    down_pieces = call(
        functools.partial(down_piece_kernel, plan, scale),
        [packed] * parts,
        [in_smem] * 2 + [in_vmem] * 3,
        [in_vmem] * parts,
        flops=parts * 2 * tokens * rows * width,
        moved=pair_bytes,
    )(here, lengths, dhidden, dhidden_other, turned)
    d_downs = to_partner(down_pieces, split, owners)

    hidden = call(
        functools.partial(rank_rest_kernel, plan),
        rank_space,
        [in_smem] + [in_vmem] * (2 + parts),
        in_vmem,
        flops=parts * 2 * tokens * rows * width,
        moved=pair_bytes,
    )(here, activations, after(partial, *down_pieces), *downs)
    hidden_other = across_cores(hidden)
    pieces = call(
        functools.partial(piece_kernel, plan, scale),
        [packed] * parts + [straight] * wholes + [stacked],
        [in_smem] * 2 + [in_vmem] * 5,
        [in_vmem] * (parts + wholes + 1),
        flops=4 * tokens * features * width,
        moved=2 * token_bytes + pair_bytes,
    )(here, lengths, dhidden, dhidden_other, hidden, hidden_other, turned)
    d_ups = to_partner(pieces[:parts], split, owners)
    d_pairs = to_partner(pieces[parts : parts + wholes], whole, owners)
    d_close = among_near(pieces[-1], owners)

    grad_input = call(
        functools.partial(input_kernel, plan, scale),
        jax.ShapeDtypeStruct((tokens, features), bf16),
        [in_smem] * 2 + [in_vmem] * (3 + parts + wholes),
        in_vmem,
        flops=2 * tokens * features * width,
        moved=token_bytes + pair_bytes,
    )(here, lengths, after(dhidden, *pieces), dhidden_other, *downs, *pairs, close)

    gradient = call(
        functools.partial(merge_kernel, plan),
        jax.ShapeDtypeStruct(table.shape, bf16),
        [in_smem] * 3 + [in_vmem] * (2 * parts + wholes + 1) + [in_hbm],
        in_hbm,
        [
            pltpu.VMEM((rows, width), f32),
            pltpu.VMEM((owners, rows, width), bf16),
            pltpu.SemaphoreType.DMA((owners,)),
        ],
        moved=2 * pair_bytes,
        aliases={4 + 2 * parts + wholes: 0},
    )(ids, here, lengths, *d_downs, *d_ups, *d_pairs, d_close, blank)
    return grad_input, gradient[:, None]


def without_kernels(activations, cotangent, adapter_weight_pair, adapter_of_block, block_live_length):
    owners = lax.axis_size("dp")
    here = lax.axis_index("dp")
    count, _, rows, width = adapter_weight_pair.shape
    rank = width // 2
    scale = adapter_alpha / rank
    adapters = adapter_of_block[:, 0]
    lengths = block_live_length[:, 0]
    keep = (jnp.arange(activations.shape[0], dtype=jnp.int32) < lengths[here])[:, None]
    inputs = jnp.where(keep, activations, jnp.zeros_like(activations))
    grads_out = jnp.where(keep, cotangent, jnp.zeros_like(cotangent))
    fetched = lax.all_to_all(
        adapter_weight_pair[:, 0][adapters], "dp", split_axis=0, concat_axis=0, tiled=True
    )
    pair = fetched.reshape(-1, width)
    down, upward = pair[:, :rank], pair[:, rank:]
    f32 = jnp.float32
    hidden_part = jnp.dot(inputs, down, preferred_element_type=f32)
    dhidden_part = scale * jnp.dot(grads_out, upward, preferred_element_type=f32)
    hidden, dhidden = lax.psum((hidden_part, dhidden_part), "tensor")
    hidden16, dhidden16 = hidden.astype(jnp.bfloat16), dhidden.astype(jnp.bfloat16)
    d_down = jnp.dot(inputs.T, dhidden16, preferred_element_type=f32)
    d_up = scale * jnp.dot(grads_out.T, hidden16, preferred_element_type=f32)
    sent = jnp.concatenate([d_down, d_up], axis=1).astype(jnp.bfloat16).reshape(owners, rows, width)
    received = lax.all_to_all(sent, "dp", split_axis=0, concat_axis=0, tiled=True).astype(f32)
    same = adapters[:, None] == adapters[None, :]
    total = jnp.sum(jnp.where(same, lengths[None, :], 0), axis=1).astype(f32)
    summed = jax.ops.segment_sum(received, adapters, num_segments=count)
    denom = jnp.ones((count,), f32).at[adapters].set(jnp.maximum(total, 1.0))
    gradient = (summed / denom[:, None, None]).astype(jnp.bfloat16)
    grad_input = jnp.dot(dhidden16, down.T, preferred_element_type=f32).astype(jnp.bfloat16)
    return grad_input, gradient[:, None]


def solution(mesh):
    owners, cores = mesh.shape["dp"], mesh.shape["tensor"]

    def on_device(activations, cotangent, adapter_weight_pair, *rest):
        rows = adapter_weight_pair.shape[2]
        fits = owners & (owners - 1) == 0 and owners >= 4 and cores == 2 and rows % 256 == 0
        body = with_kernels if fits else without_kernels
        return body(activations, cotangent, adapter_weight_pair, *rest)

    in_specs = (
        P(("group", "dp"), "tensor"),
        P(("group", "dp"), "tensor"),
        P(None, "tensor", "dp", None),
        P("group", None),
        P("group", None),
    )
    out_specs = (P(("group", "dp"), "tensor"), P("group", "tensor", "dp", None))
    return jax.shard_map(
        on_device, mesh=mesh, in_specs=in_specs, out_specs=out_specs, check_vma=False
    )
```

```python
import functools

import jax
import jax.numpy as jnp
from jax import lax
from jax.experimental import pallas as pl
from jax.experimental.pallas import tpu as pltpu
from jax.sharding import PartitionSpec as P

adapter_alpha = 128.0

in_vmem = pl.BlockSpec(memory_space=pltpu.VMEM)
in_smem = pl.BlockSpec(memory_space=pltpu.SMEM)
in_hbm = pl.BlockSpec(memory_space=pltpu.HBM)


def low_lanes(rows, width):
    return lax.broadcasted_iota(jnp.int32, (rows, width), 1) < width // 2


def call(kernel, out_shape, in_specs, out_specs, scratch=(), flops=0, moved=0, aliases=None, vmem=40):
    return pl.pallas_call(
        kernel,
        out_shape=out_shape,
        in_specs=in_specs,
        out_specs=out_specs,
        scratch_shapes=list(scratch),
        input_output_aliases=aliases or {},
        compiler_params=pltpu.CompilerParams(vmem_limit_bytes=vmem * 1024 * 1024),
        cost_estimate=pl.CostEstimate(flops=flops, bytes_accessed=moved, transcendentals=0),
    )


def swap_halves(value):
    return pltpu.roll(value, value.shape[-1] // 2, 1)


def gather_kernel(plan, ids, here, table, *refs):
    split, whole = plan
    parts = len(split)
    up, straight = refs[:parts], refs[parts : parts + len(whole)]
    down, (held, sems) = refs[parts + len(whole) : -2], refs[-2:]
    me = here[0]
    targets = [(k, held.at[n]) for n, k in enumerate(split)] + list(zip(whole, straight))
    copies = [
        pltpu.make_async_copy(table.at[ids[me ^ k]], target, sems.at[n])
        for n, (k, target) in enumerate(targets)
    ]
    for copy in copies:
        copy.start()
    half = held.shape[1] // 2
    low = low_lanes(half, held.shape[2])
    for n in range(parts):
        copies[n].wait()
        first = held[n, :half].astype(jnp.float32)
        second = held[n, half:].astype(jnp.float32)
        up[n][...] = jnp.where(low, swap_halves(first), second).astype(jnp.bfloat16)
        down[n][...] = jnp.where(low, first, swap_halves(second)).astype(jnp.bfloat16)
    for copy in copies[parts:]:
        copy.wait()


def prep_kernel(rows, after, x, y, turned, blank, zeros, sem):
    zeros[...] = jnp.zeros_like(zeros)
    step = zeros.shape[0]
    copies = [
        pltpu.make_async_copy(zeros, blank.at[pl.ds(s, step)], sem.at[s // step])
        for s in range(0, blank.shape[0], step)
    ]
    for copy in copies:
        copy.start()
    tokens = x.shape[0]

    @pl.loop(0, x.shape[1] // rows)
    def _(owner):
        columns = pl.ds(pl.multiple_of(owner * rows, rows), rows)
        turned[owner, :, pl.ds(0, tokens)] = x[:, columns].T
        turned[owner, :, pl.ds(tokens, tokens)] = y[:, columns].T

    for copy in copies:
        copy.wait()


def halves_product(values, packed, owner):
    half = packed.shape[0]
    first = pl.ds(pl.multiple_of(owner * 2 * half, half), half)
    second = pl.ds(pl.multiple_of(owner * 2 * half + half, half), half)
    one = jnp.dot(values[:, first], packed[...], preferred_element_type=jnp.float32)
    two = jnp.dot(values[:, second], packed[...], preferred_element_type=jnp.float32)
    return one, two


def rank_kernel(plan, here, x, y, *refs):
    split, whole = plan
    straight, up, dhidden, hidden = [*refs[:1], *refs[1 + len(split) : -2]], refs[1 : 1 + len(split)], *refs[-2:]
    rows, width = straight[0].shape
    tokens = x.shape[0]
    me = here[0]
    x_rank = jnp.zeros((tokens, width), jnp.float32)
    y_rank = jnp.zeros((tokens, width), jnp.float32)
    y_first = jnp.zeros((tokens, width), jnp.float32)
    for k, pair in zip(whole, straight):
        columns = pl.ds(pl.multiple_of((me ^ k) * rows, rows), rows)
        x_rank += jnp.dot(x[:, columns], pair[...], preferred_element_type=jnp.float32)
        y_rank += jnp.dot(y[:, columns], pair[...], preferred_element_type=jnp.float32)
    for n, k in enumerate(split):
        first, second = halves_product(y, up[n], me ^ k)
        y_first += first
        y_rank += second
    y_rank += swap_halves(y_first)
    half = tokens // 2
    low = low_lanes(half, width)
    dhidden[...] = jnp.where(low, swap_halves(y_rank[:half]), y_rank[half:])
    hidden[...] = jnp.where(low, x_rank[:half], swap_halves(x_rank[half:]))


def rank_rest_kernel(plan, here, x, partial, *refs):
    split, _ = plan
    down, out = refs[:-1], refs[-1]
    tokens, width = x.shape[0], partial.shape[1]
    x_first = jnp.zeros((tokens, width), jnp.float32)
    x_second = jnp.zeros((tokens, width), jnp.float32)
    for n, k in enumerate(split):
        first, second = halves_product(x, down[n], here[0] ^ k)
        x_first += first
        x_second += second
    x_rank = x_first + swap_halves(x_second)
    half = tokens // 2
    low = low_lanes(half, width)
    out[...] = partial[...] + jnp.where(low, x_rank[:half], swap_halves(x_rank[half:]))


def rounded(mine, other, length, scale):
    total = scale * (mine[...] + other[...])
    swapped = swap_halves(total)
    low = low_lanes(*total.shape)
    live = lax.broadcasted_iota(jnp.int32, (2 * total.shape[0], total.shape[1]), 0) < length
    left = [jnp.where(low, total, 0.0), jnp.where(low, swapped, 0.0)]
    right = [jnp.where(low, 0.0, swapped), jnp.where(low, 0.0, total)]
    return [jnp.where(live, jnp.concatenate(v, axis=0), 0.0).astype(jnp.bfloat16) for v in (left, right)]


def packed_piece(turned, owner, lanes, left, right):
    half = turned.shape[1] // 2
    first = jnp.dot(turned[owner, :half, lanes], left, preferred_element_type=jnp.float32)
    second = jnp.dot(turned[owner, half:, lanes], right, preferred_element_type=jnp.float32)
    return first + second


def down_piece_kernel(plan, scale, here, lengths, mine, other, turned, *out):
    split, _ = plan
    me = here[0]
    left, right = rounded(mine, other, lengths[me], scale)
    tokens = left.shape[0]
    for n, k in enumerate(split):
        out[n][...] = packed_piece(turned, me ^ k, slice(0, tokens), left, right).astype(jnp.bfloat16)


def piece_kernel(plan, scale, here, lengths, d_mine, d_other, mine, other, turned, *refs):
    split, whole = plan
    up, straight = refs[: len(split)], refs[len(split) :]
    me = here[0]
    dhidden, _ = rounded(d_mine, d_other, lengths[me], scale)
    left, right = rounded(mine, other, lengths[me], 1.0)
    tokens = left.shape[0]
    ranks = jnp.concatenate([dhidden, right], axis=0)

    def rows_for(owner):
        piece = jnp.dot(turned[owner], ranks, preferred_element_type=jnp.float32)
        return jnp.where(low_lanes(*piece.shape), piece, scale * piece).astype(jnp.bfloat16)

    for n, k in enumerate(split):
        piece = packed_piece(turned, me ^ k, slice(tokens, 2 * tokens), left, right)
        up[n][...] = (scale * piece).astype(jnp.bfloat16)
    for n, k in enumerate(whole):
        straight[n][...] = rows_for(me ^ k)


def input_kernel(plan, scale, here, lengths, mine, other, *refs):
    split, whole = plan
    down, straight, out = refs[: len(split)], refs[len(split) : -1], refs[-1]
    rows = straight[0].shape[0]
    half = rows // 2
    me = here[0]
    left, right = rounded(mine, other, lengths[me], scale)

    def product(ranks, columns):
        value = lax.dot_general(
            ranks, columns, (((1,), (1,)), ((), ())), preferred_element_type=jnp.float32
        )
        return value.astype(jnp.bfloat16)

    for k, pair in zip(whole, straight):
        out[:, pl.ds(pl.multiple_of((me ^ k) * rows, rows), rows)] = product(left, pair[...])
    for n, k in enumerate(split):
        start = (me ^ k) * rows
        out[:, pl.ds(pl.multiple_of(start, half), half)] = product(left, down[n][...])
        out[:, pl.ds(pl.multiple_of(start + half, half), half)] = product(right, down[n][...])


def merge_kernel(plan, ids, here, lengths, *refs):
    split, whole = plan
    parts = len(split)
    down, up, straight = refs[:parts], refs[parts : 2 * parts], refs[2 * parts : -5]
    out, total, held, sems = refs[-4:]
    me = here[0]
    rows, width = total.shape
    half = rows // 2
    low = low_lanes(half, width)

    def unpacked(n):
        d_down, d_up = down[n][...].astype(jnp.float32), up[n][...].astype(jnp.float32)
        first = jnp.where(low, d_down, swap_halves(d_up))
        second = jnp.where(low, swap_halves(d_down), d_up)
        return jnp.concatenate([first, second], axis=0)

    def read(ref):
        return lambda: ref[...].astype(jnp.float32)

    pieces = [(me ^ k, read(straight[n])) for n, k in enumerate(whole)]
    pieces += [(me ^ k, functools.partial(unpacked, n)) for n, k in enumerate(split)]
    owners = len(pieces)
    adapters = [ids[block] for block, _ in pieces]
    counts = [lengths[block] for block, _ in pieces]
    copies, firsts = [], []
    for k, (_, value) in enumerate(pieces):
        copies.append(pltpu.make_async_copy(held.at[k], out.at[adapters[k]], sems.at[k]))
        same = [adapters[other] == adapters[k] for other in range(owners)]
        earlier = functools.reduce(jnp.logical_or, same[:k], jnp.bool_(False))
        later = functools.reduce(jnp.logical_or, same[k + 1 :], jnp.bool_(False))
        firsts.append(jnp.logical_not(earlier))

        def store(sum_of, count):
            denom = jnp.maximum(count.astype(jnp.float32), 1.0)
            part = 1.0 / jnp.full((1, width), denom)
            held[k] = (sum_of * part).astype(jnp.bfloat16)
            copies[k].start()

        @pl.when(firsts[k] & jnp.logical_not(later))
        def _():
            store(value(), counts[k])

        @pl.when(firsts[k] & later)
        def _():
            total[...] = value()
            count = counts[k]
            for other in range(k + 1, owners):
                count += jnp.where(same[other], counts[other], 0)

                @pl.when(same[other])
                def _():
                    total[...] += pieces[other][1]()

            store(total[...], count)

    for k in range(owners):
        pl.when(firsts[k])(copies[k].wait)


def to_partner(pieces, partners, owners):
    return [
        lax.ppermute(piece, "dp", [(i, i ^ k) for i in range(owners)]) if k else piece
        for k, piece in zip(partners, pieces)
    ]


def after(value, *others):
    return lax.optimization_barrier((value, *others))[0]


def across_cores(value):
    cores = lax.axis_size("tensor")
    return lax.ppermute(value, "tensor", [(i, i ^ 1) for i in range(cores)])


def with_kernels(activations, cotangent, adapter_weight_pair, adapter_of_block, block_live_length):
    owners = lax.axis_size("dp")
    near, far = range(1, owners // 2), range(owners // 2, owners)
    plan = split, whole = tuple(far[-2:]), (1, *far[:-2], *near[1:], 0)
    here = lax.axis_index("dp").astype(jnp.int32).reshape(1)
    ids, lengths = adapter_of_block[:, 0], block_live_length[:, 0]
    count, _, rows, width = adapter_weight_pair.shape
    table = adapter_weight_pair.reshape(count, rows, width)
    tokens, features = activations.shape
    scale = adapter_alpha / (width // 2)
    bf16, f32 = jnp.bfloat16, jnp.float32
    packed = jax.ShapeDtypeStruct((rows // 2, width), bf16)
    straight = jax.ShapeDtypeStruct((rows, width), bf16)
    rank_space = jax.ShapeDtypeStruct((tokens // 2, width), f32)
    parts, wholes = len(split), len(whole)
    pair_bytes = owners * rows * width * 2
    token_bytes = tokens * features * 2

    sent = call(
        functools.partial(gather_kernel, plan),
        [packed] * parts + [straight] * wholes + [packed] * parts,
        [in_smem, in_smem, in_hbm],
        [in_vmem] * (2 * parts + wholes),
        [pltpu.VMEM((parts, rows, width), bf16), pltpu.SemaphoreType.DMA((owners,))],
        moved=2 * pair_bytes,
        vmem=53,
    )(ids, here, table)
    ups = to_partner(sent[:parts], split, owners)

    step = 8
    turned, blank = call(
        functools.partial(prep_kernel, rows),
        [
            jax.ShapeDtypeStruct((owners, rows, 2 * tokens), bf16),
            jax.ShapeDtypeStruct(table.shape, bf16),
        ],
        [in_hbm, in_vmem, in_vmem],
        [in_vmem, in_hbm],
        [pltpu.VMEM((step, rows, width), bf16), pltpu.SemaphoreType.DMA((count // step,))],
        moved=4 * token_bytes + 2 * count * rows * width,
    )(sent[0], activations, cotangent)
    sent = list(sent)
    held_back = whole.index(near[-1]) + parts
    sent[held_back] = after(sent[held_back], turned)
    pairs = to_partner(sent[parts : parts + wholes], whole, owners)
    downs = to_partner(sent[parts + wholes :], split, owners)

    dhidden, partial = call(
        functools.partial(rank_kernel, plan),
        [rank_space, rank_space],
        [in_smem] + [in_vmem] * (2 + parts + wholes),
        [in_vmem, in_vmem],
        moved=1024,
    )(here, activations, cotangent, pairs[0], *ups, *pairs[1:])
    dhidden_other = across_cores(dhidden)
    down_pieces = call(
        functools.partial(down_piece_kernel, plan, scale),
        [packed] * parts,
        [in_smem] * 2 + [in_vmem] * 3,
        [in_vmem] * parts,
        moved=1024,
    )(here, lengths, after(dhidden, downs[0]), dhidden_other, turned)
    d_downs = to_partner(down_pieces, split, owners)

    hidden = call(
        functools.partial(rank_rest_kernel, plan),
        rank_space,
        [in_smem] + [in_vmem] * (2 + parts),
        in_vmem,
        moved=1024,
    )(here, activations, after(partial, *down_pieces), *downs)
    hidden_other = across_cores(hidden)
    pieces = call(
        functools.partial(piece_kernel, plan, scale),
        [packed] * parts + [straight] * wholes,
        [in_smem] * 2 + [in_vmem] * 5,
        [in_vmem] * (parts + wholes),
        moved=1024,
    )(here, lengths, dhidden, dhidden_other, after(hidden, d_downs[0]), hidden_other, turned)
    d_ups = to_partner(pieces[:parts], split, owners)
    d_pairs = to_partner(pieces[parts:], whole, owners)

    grad_input = call(
        functools.partial(input_kernel, plan, scale),
        jax.ShapeDtypeStruct((tokens, features), bf16),
        [in_smem] * 2 + [in_vmem] * (2 + parts + wholes),
        in_vmem,
        flops=2 * tokens * features * width,
        moved=token_bytes + pair_bytes,
    )(here, lengths, after(dhidden, *pieces), dhidden_other, *downs, *pairs)

    gradient = call(
        functools.partial(merge_kernel, plan),
        jax.ShapeDtypeStruct(table.shape, bf16),
        [in_smem] * 3 + [in_vmem] * (2 * parts + wholes) + [in_hbm],
        in_hbm,
        [
            pltpu.VMEM((rows, width), f32),
            pltpu.VMEM((owners, rows, width), bf16),
            pltpu.SemaphoreType.DMA((owners,)),
        ],
        moved=2 * pair_bytes,
        aliases={3 + 2 * parts + wholes: 0},
    )(ids, here, lengths, *d_downs, *d_ups, *d_pairs, blank)
    return grad_input, gradient[:, None]


def without_kernels(activations, cotangent, adapter_weight_pair, adapter_of_block, block_live_length):
    owners = lax.axis_size("dp")
    here = lax.axis_index("dp")
    count, _, rows, width = adapter_weight_pair.shape
    rank = width // 2
    scale = adapter_alpha / rank
    adapters = adapter_of_block[:, 0]
    lengths = block_live_length[:, 0]
    keep = (jnp.arange(activations.shape[0], dtype=jnp.int32) < lengths[here])[:, None]
    inputs = jnp.where(keep, activations, jnp.zeros_like(activations))
    grads_out = jnp.where(keep, cotangent, jnp.zeros_like(cotangent))
    fetched = lax.all_to_all(
        adapter_weight_pair[:, 0][adapters], "dp", split_axis=0, concat_axis=0, tiled=True
    )
    pair = fetched.reshape(-1, width)
    down, upward = pair[:, :rank], pair[:, rank:]
    f32 = jnp.float32
    hidden_part = jnp.dot(inputs, down, preferred_element_type=f32)
    dhidden_part = scale * jnp.dot(grads_out, upward, preferred_element_type=f32)
    hidden, dhidden = lax.psum((hidden_part, dhidden_part), "tensor")
    hidden16, dhidden16 = hidden.astype(jnp.bfloat16), dhidden.astype(jnp.bfloat16)
    d_down = jnp.dot(inputs.T, dhidden16, preferred_element_type=f32)
    d_up = scale * jnp.dot(grads_out.T, hidden16, preferred_element_type=f32)
    sent = jnp.concatenate([d_down, d_up], axis=1).astype(jnp.bfloat16).reshape(owners, rows, width)
    received = lax.all_to_all(sent, "dp", split_axis=0, concat_axis=0, tiled=True).astype(f32)
    same = adapters[:, None] == adapters[None, :]
    total = jnp.sum(jnp.where(same, lengths[None, :], 0), axis=1).astype(f32)
    summed = jax.ops.segment_sum(received, adapters, num_segments=count)
    denom = jnp.ones((count,), f32).at[adapters].set(jnp.maximum(total, 1.0))
    gradient = (summed / denom[:, None, None]).astype(jnp.bfloat16)
    grad_input = jnp.dot(dhidden16, down.T, preferred_element_type=f32).astype(jnp.bfloat16)
    return grad_input, gradient[:, None]


def solution(mesh):
    owners, cores = mesh.shape["dp"], mesh.shape["tensor"]

    def on_device(activations, cotangent, adapter_weight_pair, *rest):
        rows = adapter_weight_pair.shape[2]
        fits = owners & (owners - 1) == 0 and owners >= 4 and cores == 2 and rows % 256 == 0
        body = with_kernels if fits else without_kernels
        return body(activations, cotangent, adapter_weight_pair, *rest)

    in_specs = (
        P(("group", "dp"), "tensor"),
        P(("group", "dp"), "tensor"),
        P(None, "tensor", "dp", None),
        P("group", None),
        P("group", None),
    )
    out_specs = (P(("group", "dp"), "tensor"), P("group", "tensor", "dp", None))
    return jax.shard_map(
        on_device, mesh=mesh, in_specs=in_specs, out_specs=out_specs, check_vma=False
    )
```

```python
import functools

import jax
import jax.numpy as jnp
from jax import lax
from jax.experimental import pallas as pl
from jax.experimental.pallas import tpu as pltpu
from jax.sharding import PartitionSpec as P

adapter_alpha = 128.0

in_vmem = pl.BlockSpec(memory_space=pltpu.VMEM)
in_smem = pl.BlockSpec(memory_space=pltpu.SMEM)
in_hbm = pl.BlockSpec(memory_space=pltpu.HBM)


def low_lanes(rows, width):
    return lax.broadcasted_iota(jnp.int32, (rows, width), 1) < width // 2


def call(kernel, out_shape, in_specs, out_specs, scratch=(), flops=0, moved=0, aliases=None, vmem=40):
    return pl.pallas_call(
        kernel,
        out_shape=out_shape,
        in_specs=in_specs,
        out_specs=out_specs,
        scratch_shapes=list(scratch),
        input_output_aliases=aliases or {},
        compiler_params=pltpu.CompilerParams(vmem_limit_bytes=vmem * 1024 * 1024),
        cost_estimate=pl.CostEstimate(flops=flops, bytes_accessed=moved, transcendentals=0),
    )


def gather_kernel(peers, ids, here, table, *refs):
    out, sems = refs[: len(peers)], refs[len(peers)]
    copies = [
        pltpu.make_async_copy(table.at[ids[here[0] ^ k]], out[n], sems.at[n])
        for n, k in enumerate(peers)
    ]
    for copy in copies:
        copy.start()
    for copy in copies:
        copy.wait()


def prep_kernel(rows, after, x, y, turned, blank, zeros, sem):
    zeros[...] = jnp.zeros_like(zeros)
    step = zeros.shape[0]
    copies = [
        pltpu.make_async_copy(zeros, blank.at[pl.ds(s, step)], sem.at[s // step])
        for s in range(0, blank.shape[0], step)
    ]
    for copy in copies:
        copy.start()
    tokens = x.shape[0]

    @pl.loop(0, x.shape[1] // rows)
    def _(owner):
        columns = pl.ds(pl.multiple_of(owner * rows, rows), rows)
        turned[owner, :, pl.ds(0, tokens)] = x[:, columns].T
        turned[owner, :, pl.ds(tokens, tokens)] = y[:, columns].T

    for copy in copies:
        copy.wait()


def arrived(ref, me, k):
    if len(ref.shape) == 2:
        return ref[...]
    top = 1 << (k.bit_length() - 1)
    return ref[jnp.where((me & top) > 0, 0, 1)]


def rank_kernel(peers, here, x, y, *refs):
    pairs, out = refs[: len(peers)], refs[len(peers)]
    rows, width = pairs[0].shape
    tokens = x.shape[0]
    x_rank = jnp.zeros((tokens, width), jnp.float32)
    y_rank = jnp.zeros((tokens, width), jnp.float32)
    for n, k in enumerate(peers):
        columns = pl.ds(pl.multiple_of((here[0] ^ k) * rows, rows), rows)
        pair = arrived(pairs[n], here[0], k)
        x_rank += jnp.dot(x[:, columns], pair, preferred_element_type=jnp.float32)
        y_rank += jnp.dot(y[:, columns], pair, preferred_element_type=jnp.float32)
    out[...] = jnp.where(low_lanes(tokens, width), x_rank, y_rank)


def rounded(mine, other, length, scale):
    total = mine[...] + other[...]
    rows, width = total.shape
    total = jnp.where(low_lanes(rows, width), total, scale * total)
    live = lax.broadcasted_iota(jnp.int32, (rows, width), 0) < length
    return jnp.where(live, total, 0.0)


def swap_halves(value):
    return pltpu.roll(value, value.shape[-1] // 2, 1)


def piece_kernel(peers, scale, here, lengths, mine, other, turned, *refs):
    me = here[0]
    both = swap_halves(rounded(mine, other, lengths[me], scale))
    low = low_lanes(*both.shape)
    top = jnp.where(low, both, 0.0).astype(jnp.bfloat16)
    bottom = jnp.where(low, 0.0, both).astype(jnp.bfloat16)
    ranks = jnp.concatenate([top, bottom], axis=0)
    for n, k in enumerate(peers):
        piece = jnp.dot(turned[me ^ k], ranks, preferred_element_type=jnp.float32)
        refs[n][...] = jnp.where(low_lanes(*piece.shape), piece, scale * piece).astype(jnp.bfloat16)


def input_kernel(peers, scale, here, lengths, mine, other, *refs):
    pairs, out = refs[: len(peers)], refs[len(peers)]
    me = here[0]
    both = swap_halves(rounded(mine, other, lengths[me], scale))
    ranks = jnp.where(low_lanes(*both.shape), both, 0.0).astype(jnp.bfloat16)
    rows = pairs[0].shape[0]
    for n, k in enumerate(peers):
        columns = pl.ds(pl.multiple_of((me ^ k) * rows, rows), rows)
        out[:, columns] = lax.dot_general(
            ranks, arrived(pairs[n], me, k), (((1,), (1,)), ((), ())), preferred_element_type=jnp.float32
        ).astype(jnp.bfloat16)


def merge_kernel(peers, ids, here, lengths, *refs):
    owners = len(peers)
    pieces = refs[:owners]
    out, total, held, sems = refs[owners + 1 :]
    blocks = [here[0] ^ k for k in peers]
    copies, firsts = [], []

    def value(n):
        return arrived(pieces[n], here[0], peers[n]).astype(jnp.float32)

    for k in range(owners):
        adapter = ids[blocks[k]]
        copies.append(pltpu.make_async_copy(held.at[k], out.at[adapter], sems.at[k]))
        same = [ids[blocks[other]] == adapter for other in range(owners)]
        earlier = functools.reduce(jnp.logical_or, same[:k], jnp.bool_(False))
        later = functools.reduce(jnp.logical_or, same[k + 1 :], jnp.bool_(False))
        firsts.append(jnp.logical_not(earlier))

        def store(value, count):
            denom = jnp.maximum(count.astype(jnp.float32), 1.0)
            part = 1.0 / jnp.full((1, value.shape[1]), denom)
            held[k] = (value * part).astype(jnp.bfloat16)
            copies[k].start()

        @pl.when(firsts[k] & jnp.logical_not(later))
        def _():
            store(value(k), lengths[blocks[k]])

        @pl.when(firsts[k] & later)
        def _():
            total[...] = value(k)
            count = lengths[blocks[k]]
            for other in range(k + 1, owners):
                count += jnp.where(same[other], lengths[blocks[other]], 0)

                @pl.when(same[other])
                def _():
                    total[...] += value(other)

            store(total[...], count)

    for k in range(owners):
        pl.when(firsts[k])(copies[k].wait)


def peer_order(owners):
    return (0, *range(owners // 2, owners), *range(1, owners // 2))


def exchange(pieces, peers):
    out = [pieces[0]]
    owners = len(peers)
    for k, piece in zip(peers[1:], pieces[1:]):
        pairs = [[i, i ^ k] for i in range(owners)]
        if k < owners // 2:
            groups = [pair for pair in pairs if pair[0] < pair[1]]
            out.append(lax.all_gather(piece, "dp", axis_index_groups=groups))
        else:
            out.append(lax.ppermute(piece, "dp", pairs))
    return out


def across_cores(value):
    cores = lax.axis_size("tensor")
    return lax.ppermute(value, "tensor", [(i, i ^ 1) for i in range(cores)])


def with_kernels(activations, cotangent, adapter_weight_pair, adapter_of_block, block_live_length):
    owners = lax.axis_size("dp")
    peers = peer_order(owners)
    here = lax.axis_index("dp").astype(jnp.int32).reshape(1)
    ids, lengths = adapter_of_block[:, 0], block_live_length[:, 0]
    count, _, rows, width = adapter_weight_pair.shape
    table = adapter_weight_pair.reshape(count, rows, width)
    tokens, features = activations.shape
    scale = adapter_alpha / (width // 2)
    bf16, f32 = jnp.bfloat16, jnp.float32
    pair_shapes = [jax.ShapeDtypeStruct((rows, width), bf16)] * owners
    pair_bytes = owners * rows * width * 2
    token_bytes = tokens * features * 2

    sent = call(
        functools.partial(gather_kernel, peers),
        pair_shapes,
        [in_smem, in_smem, in_hbm],
        [in_vmem] * owners,
        [pltpu.SemaphoreType.DMA((owners,))],
        moved=2 * pair_bytes,
        vmem=53,
    )(ids, here, table)
    pairs = exchange(sent, peers)

    step = 8
    turned, blank = call(
        functools.partial(prep_kernel, rows),
        [
            jax.ShapeDtypeStruct((owners, rows, 2 * tokens), bf16),
            jax.ShapeDtypeStruct(table.shape, bf16),
        ],
        [in_hbm, in_vmem, in_vmem],
        [in_vmem, in_hbm],
        [pltpu.VMEM((step, rows, width), bf16), pltpu.SemaphoreType.DMA((count // step,))],
        moved=4 * token_bytes + 2 * count * rows * width,
    )(sent[0], activations, cotangent)
    *pairs, turned, blank = lax.optimization_barrier((*pairs, turned, blank))

    mine = call(
        functools.partial(rank_kernel, peers),
        jax.ShapeDtypeStruct((tokens, width), f32),
        [in_smem] + [in_vmem] * (2 + owners),
        in_vmem,
        flops=4 * tokens * features * width,
        moved=2 * token_bytes + pair_bytes,
    )(here, activations, cotangent, *pairs)
    other = across_cores(mine)

    pieces = call(
        functools.partial(piece_kernel, peers, scale),
        pair_shapes,
        [in_smem] * 2 + [in_vmem] * 3,
        [in_vmem] * owners,
        flops=4 * tokens * features * width,
        moved=2 * token_bytes + pair_bytes,
    )(here, lengths, mine, other, turned)
    arrived = exchange(pieces, peers)

    grad_input = call(
        functools.partial(input_kernel, peers, scale),
        jax.ShapeDtypeStruct((tokens, features), bf16),
        [in_smem] * 2 + [in_vmem] * (2 + owners),
        in_vmem,
        flops=2 * tokens * features * width,
        moved=token_bytes + pair_bytes,
    )(here, lengths, mine, other, *pairs)

    gradient = call(
        functools.partial(merge_kernel, peers),
        jax.ShapeDtypeStruct(table.shape, bf16),
        [in_smem] * 3 + [in_vmem] * owners + [in_hbm],
        in_hbm,
        [
            pltpu.VMEM((rows, width), f32),
            pltpu.VMEM((owners, rows, width), bf16),
            pltpu.SemaphoreType.DMA((owners,)),
        ],
        moved=2 * pair_bytes,
        aliases={3 + owners: 0},
    )(ids, here, lengths, *arrived, blank)
    return grad_input, gradient[:, None]


def without_kernels(activations, cotangent, adapter_weight_pair, adapter_of_block, block_live_length):
    owners = lax.axis_size("dp")
    here = lax.axis_index("dp")
    count, _, rows, width = adapter_weight_pair.shape
    rank = width // 2
    scale = adapter_alpha / rank
    adapters = adapter_of_block[:, 0]
    lengths = block_live_length[:, 0]
    keep = (jnp.arange(activations.shape[0], dtype=jnp.int32) < lengths[here])[:, None]
    inputs = jnp.where(keep, activations, jnp.zeros_like(activations))
    grads_out = jnp.where(keep, cotangent, jnp.zeros_like(cotangent))
    fetched = lax.all_to_all(
        adapter_weight_pair[:, 0][adapters], "dp", split_axis=0, concat_axis=0, tiled=True
    )
    pair = fetched.reshape(-1, width)
    down, upward = pair[:, :rank], pair[:, rank:]
    f32 = jnp.float32
    hidden_part = jnp.dot(inputs, down, preferred_element_type=f32)
    dhidden_part = scale * jnp.dot(grads_out, upward, preferred_element_type=f32)
    hidden, dhidden = lax.psum((hidden_part, dhidden_part), "tensor")
    hidden16, dhidden16 = hidden.astype(jnp.bfloat16), dhidden.astype(jnp.bfloat16)
    d_down = jnp.dot(inputs.T, dhidden16, preferred_element_type=f32)
    d_up = scale * jnp.dot(grads_out.T, hidden16, preferred_element_type=f32)
    sent = jnp.concatenate([d_down, d_up], axis=1).astype(jnp.bfloat16).reshape(owners, rows, width)
    received = lax.all_to_all(sent, "dp", split_axis=0, concat_axis=0, tiled=True).astype(f32)
    same = adapters[:, None] == adapters[None, :]
    total = jnp.sum(jnp.where(same, lengths[None, :], 0), axis=1).astype(f32)
    summed = jax.ops.segment_sum(received, adapters, num_segments=count)
    denom = jnp.ones((count,), f32).at[adapters].set(jnp.maximum(total, 1.0))
    gradient = (summed / denom[:, None, None]).astype(jnp.bfloat16)
    grad_input = jnp.dot(dhidden16, down.T, preferred_element_type=f32).astype(jnp.bfloat16)
    return grad_input, gradient[:, None]


def solution(mesh):
    owners, cores = mesh.shape["dp"], mesh.shape["tensor"]

    def on_device(activations, cotangent, adapter_weight_pair, *rest):
        rows = adapter_weight_pair.shape[2]
        fits = owners & (owners - 1) == 0 and cores == 2 and rows % 256 == 0
        body = with_kernels if fits else without_kernels
        return body(activations, cotangent, adapter_weight_pair, *rest)

    in_specs = (
        P(("group", "dp"), "tensor"),
        P(("group", "dp"), "tensor"),
        P(None, "tensor", "dp", None),
        P("group", None),
        P("group", None),
    )
    out_specs = (P(("group", "dp"), "tensor"), P("group", "tensor", "dp", None))
    return jax.shard_map(
        on_device, mesh=mesh, in_specs=in_specs, out_specs=out_specs, check_vma=False
    )
```

```python
import functools

import jax
import jax.numpy as jnp
from jax import lax
from jax.experimental import pallas as pl
from jax.experimental.pallas import tpu as pltpu
from jax.sharding import PartitionSpec as P

adapter_alpha = 128.0
RANK_ORDER = ((False, 1), (False, 2), (True, 6), (True, 7), (False, 4), (False, 5))
MERGE_ORDER = (("both", 1), ("both", 2), ("both", 4), ("both", 5), ("both", 3))
PREP_AFTER = 0
TIES = ()
D_TIES = ()

in_vmem = pl.BlockSpec(memory_space=pltpu.VMEM)
in_smem = pl.BlockSpec(memory_space=pltpu.SMEM)
in_hbm = pl.BlockSpec(memory_space=pltpu.HBM)


def low_lanes(rows, width):
    return lax.broadcasted_iota(jnp.int32, (rows, width), 1) < width // 2


def call(kernel, out_shape, in_specs, out_specs, scratch=(), flops=0, moved=0, aliases=None, vmem=40):
    return pl.pallas_call(
        kernel,
        out_shape=out_shape,
        in_specs=in_specs,
        out_specs=out_specs,
        scratch_shapes=list(scratch),
        input_output_aliases=aliases or {},
        compiler_params=pltpu.CompilerParams(vmem_limit_bytes=vmem * 1024 * 1024),
        cost_estimate=pl.CostEstimate(flops=flops, bytes_accessed=moved, transcendentals=0),
    )


def swap_halves(value):
    return pltpu.roll(value, value.shape[-1] // 2, 1)


def gather_kernel(plan, ids, here, table, *refs):
    split, whole = plan
    parts = len(split)
    up, straight = refs[:parts], refs[parts : parts + len(whole)]
    down, (held, sems) = refs[parts + len(whole) : -2], refs[-2:]
    me = here[0]
    targets = [(k, held.at[n]) for n, k in enumerate(split)] + list(zip(whole, straight))
    copies = [
        pltpu.make_async_copy(table.at[ids[me ^ k]], target, sems.at[n])
        for n, (k, target) in enumerate(targets)
    ]
    for copy in copies:
        copy.start()
    half = held.shape[1] // 2
    low = low_lanes(half, held.shape[2])
    for n in range(parts):
        copies[n].wait()
        first = held[n, :half].astype(jnp.float32)
        second = held[n, half:].astype(jnp.float32)
        up[n][...] = jnp.where(low, swap_halves(first), second).astype(jnp.bfloat16)
        down[n][...] = jnp.where(low, first, swap_halves(second)).astype(jnp.bfloat16)
    for copy in copies[parts:]:
        copy.wait()


def prep_kernel(rows, after, x, y, turned, blank, zeros, sem):
    zeros[...] = jnp.zeros_like(zeros)
    step = zeros.shape[0]
    copies = [
        pltpu.make_async_copy(zeros, blank.at[pl.ds(s, step)], sem.at[s // step])
        for s in range(0, blank.shape[0], step)
    ]
    for copy in copies:
        copy.start()
    tokens = x.shape[0]

    @pl.loop(0, x.shape[1] // rows)
    def _(owner):
        columns = pl.ds(pl.multiple_of(owner * rows, rows), rows)
        turned[owner, :, pl.ds(0, tokens)] = x[:, columns].T
        turned[owner, :, pl.ds(tokens, tokens)] = y[:, columns].T

    for copy in copies:
        copy.wait()


def halves_product(values, packed, owner):
    half = packed.shape[0]
    first = pl.ds(pl.multiple_of(owner * 2 * half, half), half)
    second = pl.ds(pl.multiple_of(owner * 2 * half + half, half), half)
    one = jnp.dot(values[:, first], packed[...], preferred_element_type=jnp.float32)
    two = jnp.dot(values[:, second], packed[...], preferred_element_type=jnp.float32)
    return one, two


def rank_kernel(order, here, x, y, *refs):
    pieces, (dhidden, hidden) = refs[:-2], refs[-2:]
    width = dhidden.shape[1]
    tokens = x.shape[0]
    me = here[0]
    x_rank = jnp.zeros((tokens, width), jnp.float32)
    y_rank = jnp.zeros((tokens, width), jnp.float32)
    y_first = jnp.zeros((tokens, width), jnp.float32)
    for (packed, k), piece in zip(order, pieces):
        if packed:
            first, second = halves_product(y, piece, me ^ k)
            y_first += first
            y_rank += second
        else:
            rows = piece.shape[0]
            columns = pl.ds(pl.multiple_of((me ^ k) * rows, rows), rows)
            x_rank += jnp.dot(x[:, columns], piece[...], preferred_element_type=jnp.float32)
            y_rank += jnp.dot(y[:, columns], piece[...], preferred_element_type=jnp.float32)
    y_rank += swap_halves(y_first)
    half = tokens // 2
    low = low_lanes(half, width)
    dhidden[...] = jnp.where(low, swap_halves(y_rank[:half]), y_rank[half:])
    hidden[...] = jnp.where(low, x_rank[:half], swap_halves(x_rank[half:]))


def rank_rest_kernel(plan, here, x, partial, *refs):
    split, _ = plan
    down, out = refs[:-1], refs[-1]
    tokens, width = x.shape[0], partial.shape[1]
    x_first = jnp.zeros((tokens, width), jnp.float32)
    x_second = jnp.zeros((tokens, width), jnp.float32)
    for n, k in enumerate(split):
        first, second = halves_product(x, down[n], here[0] ^ k)
        x_first += first
        x_second += second
    x_rank = x_first + swap_halves(x_second)
    half = tokens // 2
    low = low_lanes(half, width)
    out[...] = partial[...] + jnp.where(low, x_rank[:half], swap_halves(x_rank[half:]))


def rounded(mine, other, length, scale):
    total = scale * (mine[...] + other[...])
    swapped = swap_halves(total)
    low = low_lanes(*total.shape)
    live = lax.broadcasted_iota(jnp.int32, (2 * total.shape[0], total.shape[1]), 0) < length
    left = [jnp.where(low, total, 0.0), jnp.where(low, swapped, 0.0)]
    right = [jnp.where(low, 0.0, swapped), jnp.where(low, 0.0, total)]
    return [jnp.where(live, jnp.concatenate(v, axis=0), 0.0).astype(jnp.bfloat16) for v in (left, right)]


def packed_piece(turned, owner, lanes, left, right):
    half = turned.shape[1] // 2
    first = jnp.dot(turned[owner, :half, lanes], left, preferred_element_type=jnp.float32)
    second = jnp.dot(turned[owner, half:, lanes], right, preferred_element_type=jnp.float32)
    return first + second


def down_piece_kernel(plan, scale, here, lengths, mine, other, turned, *out):
    split, _ = plan
    me = here[0]
    left, right = rounded(mine, other, lengths[me], scale)
    tokens = left.shape[0]
    for n, k in enumerate(split):
        out[n][...] = packed_piece(turned, me ^ k, slice(0, tokens), left, right).astype(jnp.bfloat16)


def piece_kernel(plan, scale, here, lengths, d_mine, d_other, mine, other, turned, *refs):
    split, whole = plan
    up, straight = refs[: len(split)], refs[len(split) :]
    me = here[0]
    dhidden, _ = rounded(d_mine, d_other, lengths[me], scale)
    left, right = rounded(mine, other, lengths[me], 1.0)
    tokens = left.shape[0]
    ranks = jnp.concatenate([dhidden, right], axis=0)

    def rows_for(owner):
        piece = jnp.dot(turned[owner], ranks, preferred_element_type=jnp.float32)
        return jnp.where(low_lanes(*piece.shape), piece, scale * piece).astype(jnp.bfloat16)

    for n, k in enumerate(split):
        piece = packed_piece(turned, me ^ k, slice(tokens, 2 * tokens), left, right)
        up[n][...] = (scale * piece).astype(jnp.bfloat16)
    for n, k in enumerate(whole):
        straight[n][...] = rows_for(me ^ k)


def input_kernel(plan, scale, here, lengths, mine, other, *refs):
    split, whole = plan
    down, straight, out = refs[: len(split)], refs[len(split) : -1], refs[-1]
    rows = straight[0].shape[0]
    half = rows // 2
    me = here[0]
    left, right = rounded(mine, other, lengths[me], scale)

    def product(ranks, columns):
        value = lax.dot_general(
            ranks, columns, (((1,), (1,)), ((), ())), preferred_element_type=jnp.float32
        )
        return value.astype(jnp.bfloat16)

    for k, pair in zip(whole, straight):
        out[:, pl.ds(pl.multiple_of((me ^ k) * rows, rows), rows)] = product(left, pair[...])
    for n, k in enumerate(split):
        start = (me ^ k) * rows
        out[:, pl.ds(pl.multiple_of(start, half), half)] = product(left, down[n][...])
        out[:, pl.ds(pl.multiple_of(start + half, half), half)] = product(right, down[n][...])


def merge_kernel(plan, order, ids, here, lengths, *refs):
    split, whole = plan
    by_key = dict(zip(order, refs[:-5]))
    down, up = [by_key["down", k] for k in split], [by_key["up", k] for k in split]
    straight = [by_key["both", k] for k in whole]
    out, total, held, sems = refs[-4:]
    me = here[0]
    rows, width = total.shape
    half = rows // 2
    low = low_lanes(half, width)

    def unpacked(n):
        d_down, d_up = down[n][...].astype(jnp.float32), up[n][...].astype(jnp.float32)
        first = jnp.where(low, d_down, swap_halves(d_up))
        second = jnp.where(low, swap_halves(d_down), d_up)
        return jnp.concatenate([first, second], axis=0)

    def read(ref):
        return lambda: ref[...].astype(jnp.float32)

    pieces = [(me ^ k, read(straight[n])) for n, k in enumerate(whole)]
    pieces += [(me ^ k, functools.partial(unpacked, n)) for n, k in enumerate(split)]
    owners = len(pieces)
    adapters = [ids[block] for block, _ in pieces]
    counts = [lengths[block] for block, _ in pieces]
    copies, firsts = [], []
    for k, (_, value) in enumerate(pieces):
        copies.append(pltpu.make_async_copy(held.at[k], out.at[adapters[k]], sems.at[k]))
        same = [adapters[other] == adapters[k] for other in range(owners)]
        earlier = functools.reduce(jnp.logical_or, same[:k], jnp.bool_(False))
        later = functools.reduce(jnp.logical_or, same[k + 1 :], jnp.bool_(False))
        firsts.append(jnp.logical_not(earlier))

        def store(sum_of, count):
            denom = jnp.maximum(count.astype(jnp.float32), 1.0)
            part = 1.0 / jnp.full((1, width), denom)
            held[k] = (sum_of * part).astype(jnp.bfloat16)
            copies[k].start()

        @pl.when(firsts[k] & jnp.logical_not(later))
        def _():
            store(value(), counts[k])

        @pl.when(firsts[k] & later)
        def _():
            total[...] = value()
            count = counts[k]
            for other in range(k + 1, owners):
                count += jnp.where(same[other], counts[other], 0)

                @pl.when(same[other])
                def _():
                    total[...] += pieces[other][1]()

            store(total[...], count)

    for k in range(owners):
        pl.when(firsts[k])(copies[k].wait)


def to_partner(pieces, partners, owners, ties=()):
    to_send, out = dict(zip(partners, pieces)), {}
    held = dict(ties)
    for k in sorted(partners, key=lambda k: k in held):
        piece = after(to_send[k], out[held[k]]) if k in held else to_send[k]
        out[k] = lax.ppermute(piece, "dp", [(i, i ^ k) for i in range(owners)]) if k else piece
    return [out[k] for k in partners]


def in_order(pieces, first):
    keys = [key for key in first if key in pieces]
    keys += [key for key in pieces if key not in keys]
    return [(key, pieces[key]) for key in keys]


def after(value, *others):
    return lax.optimization_barrier((value, *others))[0]


def across_cores(value):
    cores = lax.axis_size("tensor")
    return lax.ppermute(value, "tensor", [(i, i ^ 1) for i in range(cores)])


def with_kernels(activations, cotangent, adapter_weight_pair, adapter_of_block, block_live_length):
    owners = lax.axis_size("dp")
    near, far = range(1, owners // 2), range(owners // 2, owners)
    plan = split, whole = tuple(far[-2:]), (*near[:-1], *far[:-2], near[-1], 0)
    here = lax.axis_index("dp").astype(jnp.int32).reshape(1)
    ids, lengths = adapter_of_block[:, 0], block_live_length[:, 0]
    count, _, rows, width = adapter_weight_pair.shape
    table = adapter_weight_pair.reshape(count, rows, width)
    tokens, features = activations.shape
    scale = adapter_alpha / (width // 2)
    bf16, f32 = jnp.bfloat16, jnp.float32
    packed = jax.ShapeDtypeStruct((rows // 2, width), bf16)
    straight = jax.ShapeDtypeStruct((rows, width), bf16)
    rank_space = jax.ShapeDtypeStruct((tokens // 2, width), f32)
    parts, wholes = len(split), len(whole)
    pair_bytes = owners * rows * width * 2
    token_bytes = tokens * features * 2

    sent = call(
        functools.partial(gather_kernel, plan),
        [packed] * parts + [straight] * wholes + [packed] * parts,
        [in_smem, in_smem, in_hbm],
        [in_vmem] * (2 * parts + wholes),
        [pltpu.VMEM((parts, rows, width), bf16), pltpu.SemaphoreType.DMA((owners,))],
        moved=2 * pair_bytes,
        vmem=53,
    )(ids, here, table)
    ups = to_partner(sent[:parts], split, owners)

    pairs = to_partner(sent[parts : parts + wholes], whole, owners, TIES)
    downs = to_partner(sent[parts + wholes :], split, owners)

    step = 8
    turned, blank = call(
        functools.partial(prep_kernel, rows),
        [
            jax.ShapeDtypeStruct((owners, rows, 2 * tokens), bf16),
            jax.ShapeDtypeStruct(table.shape, bf16),
        ],
        [in_hbm, in_vmem, in_vmem],
        [in_vmem, in_hbm],
        [pltpu.VMEM((step, rows, width), bf16), pltpu.SemaphoreType.DMA((count // step,))],
        moved=4 * token_bytes + 2 * count * rows * width,
    )(ups[PREP_AFTER], activations, cotangent)
    from_whole = {(False, k): piece for k, piece in zip(whole, pairs)}
    from_split = {(True, k): piece for k, piece in zip(split, ups)}
    rank_order = in_order({**from_whole, **from_split}, RANK_ORDER)
    dhidden, partial = call(
        functools.partial(rank_kernel, tuple(key for key, _ in rank_order)),
        [rank_space, rank_space],
        [in_smem] + [in_vmem] * (2 + parts + wholes),
        [in_vmem, in_vmem],
        moved=1024,
    )(here, after(activations, turned), cotangent, *[piece for _, piece in rank_order])
    dhidden_other = across_cores(dhidden)
    down_pieces = call(
        functools.partial(down_piece_kernel, plan, scale),
        [packed] * parts,
        [in_smem] * 2 + [in_vmem] * 3,
        [in_vmem] * parts,
        moved=1024,
    )(here, lengths, after(dhidden, downs[0]), dhidden_other, turned)
    d_downs = to_partner(down_pieces, split, owners)

    hidden = call(
        functools.partial(rank_rest_kernel, plan),
        rank_space,
        [in_smem] + [in_vmem] * (2 + parts),
        in_vmem,
        moved=1024,
    )(here, activations, after(partial, *down_pieces), *downs)
    hidden_other = across_cores(hidden)
    pieces = call(
        functools.partial(piece_kernel, plan, scale),
        [packed] * parts + [straight] * wholes,
        [in_smem] * 2 + [in_vmem] * 5,
        [in_vmem] * (parts + wholes),
        moved=1024,
    )(here, lengths, dhidden, dhidden_other, after(hidden, d_downs[0]), hidden_other, turned)
    d_ups = to_partner(pieces[:parts], split, owners)
    d_pairs = to_partner(pieces[parts:], whole, owners, D_TIES)

    grad_input = call(
        functools.partial(input_kernel, plan, scale),
        jax.ShapeDtypeStruct((tokens, features), bf16),
        [in_smem] * 2 + [in_vmem] * (2 + parts + wholes),
        in_vmem,
        flops=2 * tokens * features * width,
        moved=token_bytes + pair_bytes,
    )(here, lengths, after(dhidden, *pieces), dhidden_other, *downs, *pairs)

    from_all = {("both", k): piece for k, piece in zip(whole, d_pairs)}
    from_all |= {("down", k): piece for k, piece in zip(split, d_downs)}
    from_all |= {("up", k): piece for k, piece in zip(split, d_ups)}
    merge_order = in_order(from_all, MERGE_ORDER)
    gradient = call(
        functools.partial(merge_kernel, plan, tuple(key for key, _ in merge_order)),
        jax.ShapeDtypeStruct(table.shape, bf16),
        [in_smem] * 3 + [in_vmem] * (2 * parts + wholes) + [in_hbm],
        in_hbm,
        [
            pltpu.VMEM((rows, width), f32),
            pltpu.VMEM((owners, rows, width), bf16),
            pltpu.SemaphoreType.DMA((owners,)),
        ],
        moved=2 * pair_bytes,
        aliases={3 + 2 * parts + wholes: 0},
    )(ids, here, lengths, *[piece for _, piece in merge_order], blank)
    return grad_input, gradient[:, None]


def without_kernels(activations, cotangent, adapter_weight_pair, adapter_of_block, block_live_length):
    owners = lax.axis_size("dp")
    here = lax.axis_index("dp")
    count, _, rows, width = adapter_weight_pair.shape
    rank = width // 2
    scale = adapter_alpha / rank
    adapters = adapter_of_block[:, 0]
    lengths = block_live_length[:, 0]
    keep = (jnp.arange(activations.shape[0], dtype=jnp.int32) < lengths[here])[:, None]
    inputs = jnp.where(keep, activations, jnp.zeros_like(activations))
    grads_out = jnp.where(keep, cotangent, jnp.zeros_like(cotangent))
    fetched = lax.all_to_all(
        adapter_weight_pair[:, 0][adapters], "dp", split_axis=0, concat_axis=0, tiled=True
    )
    pair = fetched.reshape(-1, width)
    down, upward = pair[:, :rank], pair[:, rank:]
    f32 = jnp.float32
    hidden_part = jnp.dot(inputs, down, preferred_element_type=f32)
    dhidden_part = scale * jnp.dot(grads_out, upward, preferred_element_type=f32)
    hidden, dhidden = lax.psum((hidden_part, dhidden_part), "tensor")
    hidden16, dhidden16 = hidden.astype(jnp.bfloat16), dhidden.astype(jnp.bfloat16)
    d_down = jnp.dot(inputs.T, dhidden16, preferred_element_type=f32)
    d_up = scale * jnp.dot(grads_out.T, hidden16, preferred_element_type=f32)
    sent = jnp.concatenate([d_down, d_up], axis=1).astype(jnp.bfloat16).reshape(owners, rows, width)
    received = lax.all_to_all(sent, "dp", split_axis=0, concat_axis=0, tiled=True).astype(f32)
    same = adapters[:, None] == adapters[None, :]
    total = jnp.sum(jnp.where(same, lengths[None, :], 0), axis=1).astype(f32)
    summed = jax.ops.segment_sum(received, adapters, num_segments=count)
    denom = jnp.ones((count,), f32).at[adapters].set(jnp.maximum(total, 1.0))
    gradient = (summed / denom[:, None, None]).astype(jnp.bfloat16)
    grad_input = jnp.dot(dhidden16, down.T, preferred_element_type=f32).astype(jnp.bfloat16)
    return grad_input, gradient[:, None]


def solution(mesh):
    owners, cores = mesh.shape["dp"], mesh.shape["tensor"]

    def on_device(activations, cotangent, adapter_weight_pair, *rest):
        rows = adapter_weight_pair.shape[2]
        fits = owners & (owners - 1) == 0 and owners >= 4 and cores == 2 and rows % 256 == 0
        body = with_kernels if fits else without_kernels
        return body(activations, cotangent, adapter_weight_pair, *rest)

    in_specs = (
        P(("group", "dp"), "tensor"),
        P(("group", "dp"), "tensor"),
        P(None, "tensor", "dp", None),
        P("group", None),
        P("group", None),
    )
    out_specs = (P(("group", "dp"), "tensor"), P("group", "tensor", "dp", None))
    return jax.shard_map(
        on_device, mesh=mesh, in_specs=in_specs, out_specs=out_specs, check_vma=False
    )
```

```python
import functools

import jax
import jax.numpy as jnp
from jax import lax
from jax.experimental import pallas as pl
from jax.experimental.pallas import tpu as pltpu
from jax.sharding import PartitionSpec as P

adapter_alpha = 128.0
RANK_ORDER = ((False, 1), (False, 2), (True, 4), (True, 5), (False, 6), (False, 7), (False, 3))
MERGE_ORDER = (("both", 6), ("both", 1), ("both", 7), ("both", 2), ("both", 3))
PREP_AFTER = 0
PREP_VMEM = 40
SPLIT = (4, 5)
WHOLE = (6, 1, 7, 2, 3)

in_vmem = pl.BlockSpec(memory_space=pltpu.VMEM)
in_smem = pl.BlockSpec(memory_space=pltpu.SMEM)
in_hbm = pl.BlockSpec(memory_space=pltpu.HBM)


def low_lanes(rows, width):
    return lax.broadcasted_iota(jnp.int32, (rows, width), 1) < width // 2


def call(kernel, out_shape, in_specs, out_specs, scratch=(), flops=0, moved=0, aliases=None, vmem=40):
    return pl.pallas_call(
        kernel,
        out_shape=out_shape,
        in_specs=in_specs,
        out_specs=out_specs,
        scratch_shapes=list(scratch),
        input_output_aliases=aliases or {},
        compiler_params=pltpu.CompilerParams(vmem_limit_bytes=vmem * 1024 * 1024),
        cost_estimate=pl.CostEstimate(flops=flops, bytes_accessed=moved, transcendentals=0),
    )


def swap_halves(value):
    return pltpu.roll(value, value.shape[-1] // 2, 1)


def gather_kernel(plan, ids, here, table, *refs):
    split, whole = plan
    parts = len(split)
    up, straight = refs[:parts], refs[parts : parts + len(whole)]
    down, (held, sems) = refs[parts + len(whole) : -2], refs[-2:]
    me = here[0]
    targets = [(k, held.at[n]) for n, k in enumerate(split)] + list(zip(whole, straight))
    copies = [
        pltpu.make_async_copy(table.at[ids[me ^ k]], target, sems.at[n])
        for n, (k, target) in enumerate(targets)
    ]
    for copy in copies:
        copy.start()
    half = held.shape[1] // 2
    low = low_lanes(half, held.shape[2])
    for n in range(parts):
        copies[n].wait()
        first = held[n, :half].astype(jnp.float32)
        second = held[n, half:].astype(jnp.float32)
        up[n][...] = jnp.where(low, swap_halves(first), second).astype(jnp.bfloat16)
        down[n][...] = jnp.where(low, first, swap_halves(second)).astype(jnp.bfloat16)
    for copy in copies[parts:]:
        copy.wait()


def prep_kernel(ids, here, table, after, x, y, turned, own, blank, zeros, sem, own_sem):
    own_copy = pltpu.make_async_copy(table.at[ids[here[0]]], own, own_sem)
    own_copy.start()
    rows = own.shape[0]
    zeros[...] = jnp.zeros_like(zeros)
    step = zeros.shape[0]
    copies = [
        pltpu.make_async_copy(zeros, blank.at[pl.ds(s, step)], sem.at[s // step])
        for s in range(0, blank.shape[0], step)
    ]
    for copy in copies:
        copy.start()
    tokens = x.shape[0]

    @pl.loop(0, x.shape[1] // rows)
    def _(owner):
        columns = pl.ds(pl.multiple_of(owner * rows, rows), rows)
        turned[owner, :, pl.ds(0, tokens)] = x[:, columns].T
        turned[owner, :, pl.ds(tokens, tokens)] = y[:, columns].T

    for copy in [own_copy, *copies]:
        copy.wait()


def halves_product(values, packed, owner):
    half = packed.shape[0]
    first = pl.ds(pl.multiple_of(owner * 2 * half, half), half)
    second = pl.ds(pl.multiple_of(owner * 2 * half + half, half), half)
    one = jnp.dot(values[:, first], packed[...], preferred_element_type=jnp.float32)
    two = jnp.dot(values[:, second], packed[...], preferred_element_type=jnp.float32)
    return one, two


def rank_kernel(order, here, x, y, *refs):
    pieces, (dhidden, hidden) = refs[:-2], refs[-2:]
    width = dhidden.shape[1]
    tokens = x.shape[0]
    me = here[0]
    x_rank = jnp.zeros((tokens, width), jnp.float32)
    y_rank = jnp.zeros((tokens, width), jnp.float32)
    y_first = jnp.zeros((tokens, width), jnp.float32)
    for (packed, k), piece in zip(order, pieces):
        if packed:
            first, second = halves_product(y, piece, me ^ k)
            y_first += first
            y_rank += second
        else:
            rows = piece.shape[0]
            columns = pl.ds(pl.multiple_of((me ^ k) * rows, rows), rows)
            x_rank += jnp.dot(x[:, columns], piece[...], preferred_element_type=jnp.float32)
            y_rank += jnp.dot(y[:, columns], piece[...], preferred_element_type=jnp.float32)
    y_rank += swap_halves(y_first)
    half = tokens // 2
    low = low_lanes(half, width)
    dhidden[...] = jnp.where(low, swap_halves(y_rank[:half]), y_rank[half:])
    hidden[...] = jnp.where(low, x_rank[:half], swap_halves(x_rank[half:]))


def rank_rest_kernel(plan, here, x, partial, *refs):
    split, _ = plan
    down, out = refs[:-1], refs[-1]
    tokens, width = x.shape[0], partial.shape[1]
    x_first = jnp.zeros((tokens, width), jnp.float32)
    x_second = jnp.zeros((tokens, width), jnp.float32)
    for n, k in enumerate(split):
        first, second = halves_product(x, down[n], here[0] ^ k)
        x_first += first
        x_second += second
    x_rank = x_first + swap_halves(x_second)
    half = tokens // 2
    low = low_lanes(half, width)
    out[...] = partial[...] + jnp.where(low, x_rank[:half], swap_halves(x_rank[half:]))


def rounded(mine, other, length, scale):
    total = scale * (mine[...] + other[...])
    swapped = swap_halves(total)
    low = low_lanes(*total.shape)
    live = lax.broadcasted_iota(jnp.int32, (2 * total.shape[0], total.shape[1]), 0) < length
    left = [jnp.where(low, total, 0.0), jnp.where(low, swapped, 0.0)]
    right = [jnp.where(low, 0.0, swapped), jnp.where(low, 0.0, total)]
    return [jnp.where(live, jnp.concatenate(v, axis=0), 0.0).astype(jnp.bfloat16) for v in (left, right)]


def packed_piece(turned, owner, lanes, left, right):
    half = turned.shape[1] // 2
    first = jnp.dot(turned[owner, :half, lanes], left, preferred_element_type=jnp.float32)
    second = jnp.dot(turned[owner, half:, lanes], right, preferred_element_type=jnp.float32)
    return first + second


def down_piece_kernel(plan, scale, here, lengths, mine, other, turned, *out):
    split, _ = plan
    me = here[0]
    left, right = rounded(mine, other, lengths[me], scale)
    tokens = left.shape[0]
    for n, k in enumerate(split):
        out[n][...] = packed_piece(turned, me ^ k, slice(0, tokens), left, right).astype(jnp.bfloat16)


def piece_kernel(plan, scale, here, lengths, d_mine, d_other, mine, other, turned, *refs):
    split, whole = plan
    straight, up = refs[: len(whole)], refs[len(whole) :]
    me = here[0]
    dhidden, _ = rounded(d_mine, d_other, lengths[me], scale)
    left, right = rounded(mine, other, lengths[me], 1.0)
    tokens = left.shape[0]
    ranks = jnp.concatenate([dhidden, right], axis=0)

    def rows_for(owner):
        piece = jnp.dot(turned[owner], ranks, preferred_element_type=jnp.float32)
        return jnp.where(low_lanes(*piece.shape), piece, scale * piece).astype(jnp.bfloat16)

    for n, k in enumerate(split):
        piece = packed_piece(turned, me ^ k, slice(tokens, 2 * tokens), left, right)
        up[n][...] = (scale * piece).astype(jnp.bfloat16)
    for n, k in enumerate(whole):
        straight[n][...] = rows_for(me ^ k)


def input_kernel(plan, scale, here, lengths, mine, other, *refs):
    split, whole = plan
    down, straight, out = refs[: len(split)], refs[len(split) : -1], refs[-1]
    rows = straight[0].shape[0]
    half = rows // 2
    me = here[0]
    left, right = rounded(mine, other, lengths[me], scale)

    def product(ranks, columns):
        value = lax.dot_general(
            ranks, columns, (((1,), (1,)), ((), ())), preferred_element_type=jnp.float32
        )
        return value.astype(jnp.bfloat16)

    for k, pair in zip(whole, straight):
        out[:, pl.ds(pl.multiple_of((me ^ k) * rows, rows), rows)] = product(left, pair[...])
    for n, k in enumerate(split):
        start = (me ^ k) * rows
        out[:, pl.ds(pl.multiple_of(start, half), half)] = product(left, down[n][...])
        out[:, pl.ds(pl.multiple_of(start + half, half), half)] = product(right, down[n][...])


def merge_kernel(plan, order, ids, here, lengths, *refs):
    split, whole = plan
    by_key = dict(zip(order, refs[:-5]))
    down, up = [by_key["down", k] for k in split], [by_key["up", k] for k in split]
    straight = [by_key["both", k] for k in whole]
    out, total, held, sems = refs[-4:]
    me = here[0]
    rows, width = total.shape
    half = rows // 2
    low = low_lanes(half, width)

    def unpacked(n):
        d_down, d_up = down[n][...].astype(jnp.float32), up[n][...].astype(jnp.float32)
        first = jnp.where(low, d_down, swap_halves(d_up))
        second = jnp.where(low, swap_halves(d_down), d_up)
        return jnp.concatenate([first, second], axis=0)

    def read(ref):
        return lambda: ref[...].astype(jnp.float32)

    pieces = [(me ^ k, read(straight[n])) for n, k in enumerate(whole)]
    pieces += [(me ^ k, functools.partial(unpacked, n)) for n, k in enumerate(split)]
    owners = len(pieces)
    adapters = [ids[block] for block, _ in pieces]
    counts = [lengths[block] for block, _ in pieces]
    copies, firsts = [], []
    for k, (_, value) in enumerate(pieces):
        copies.append(pltpu.make_async_copy(held.at[k], out.at[adapters[k]], sems.at[k]))
        same = [adapters[other] == adapters[k] for other in range(owners)]
        earlier = functools.reduce(jnp.logical_or, same[:k], jnp.bool_(False))
        later = functools.reduce(jnp.logical_or, same[k + 1 :], jnp.bool_(False))
        firsts.append(jnp.logical_not(earlier))

        def store(sum_of, count):
            denom = jnp.maximum(count.astype(jnp.float32), 1.0)
            part = 1.0 / jnp.full((1, width), denom)
            held[k] = (sum_of * part).astype(jnp.bfloat16)
            copies[k].start()

        @pl.when(firsts[k] & jnp.logical_not(later))
        def _():
            store(value(), counts[k])

        @pl.when(firsts[k] & later)
        def _():
            total[...] = value()
            count = counts[k]
            for other in range(k + 1, owners):
                count += jnp.where(same[other], counts[other], 0)

                @pl.when(same[other])
                def _():
                    total[...] += pieces[other][1]()

            store(total[...], count)

    for k in range(owners):
        pl.when(firsts[k])(copies[k].wait)


def to_partner(pieces, partners, owners):
    return [
        lax.ppermute(piece, "dp", [(i, i ^ k) for i in range(owners)]) if k else piece
        for k, piece in zip(partners, pieces)
    ]


def in_order(pieces, first):
    keys = [key for key in first if key in pieces]
    keys += [key for key in pieces if key not in keys]
    return [(key, pieces[key]) for key in keys]


def after(value, *others):
    return lax.optimization_barrier((value, *others))[0]


def across_cores(value):
    cores = lax.axis_size("tensor")
    return lax.ppermute(value, "tensor", [(i, i ^ 1) for i in range(cores)])


def with_kernels(activations, cotangent, adapter_weight_pair, adapter_of_block, block_live_length):
    owners = lax.axis_size("dp")
    plan = split, whole = SPLIT, WHOLE
    here = lax.axis_index("dp").astype(jnp.int32).reshape(1)
    ids, lengths = adapter_of_block[:, 0], block_live_length[:, 0]
    count, _, rows, width = adapter_weight_pair.shape
    table = adapter_weight_pair.reshape(count, rows, width)
    tokens, features = activations.shape
    scale = adapter_alpha / (width // 2)
    bf16, f32 = jnp.bfloat16, jnp.float32
    packed = jax.ShapeDtypeStruct((rows // 2, width), bf16)
    straight = jax.ShapeDtypeStruct((rows, width), bf16)
    rank_space = jax.ShapeDtypeStruct((tokens // 2, width), f32)
    parts, wholes = len(split), len(whole)
    pair_bytes = owners * rows * width * 2
    token_bytes = tokens * features * 2

    sent = call(
        functools.partial(gather_kernel, plan),
        [packed] * parts + [straight] * wholes + [packed] * parts,
        [in_smem, in_smem, in_hbm],
        [in_vmem] * (2 * parts + wholes),
        [pltpu.VMEM((parts, rows, width), bf16), pltpu.SemaphoreType.DMA((owners,))],
        moved=2 * pair_bytes,
        vmem=53,
    )(ids, here, table)
    ups = to_partner(sent[:parts], split, owners)

    pairs = to_partner(sent[parts : parts + wholes], whole, owners)
    downs = to_partner(sent[parts + wholes :], split, owners)

    step = 8
    turned, own, blank = call(
        prep_kernel,
        [
            jax.ShapeDtypeStruct((owners, rows, 2 * tokens), bf16),
            straight,
            jax.ShapeDtypeStruct(table.shape, bf16),
        ],
        [in_smem, in_smem, in_hbm, in_hbm, in_vmem, in_vmem],
        [in_vmem, in_vmem, in_hbm],
        [
            pltpu.VMEM((step, rows, width), bf16),
            pltpu.SemaphoreType.DMA((count // step,)),
            pltpu.SemaphoreType.DMA,
        ],
        moved=4 * token_bytes + 2 * count * rows * width,
        vmem=PREP_VMEM,
    )(ids, here, table, ups[PREP_AFTER], activations, cotangent)

    pairs.append(own)
    whole += (0,)
    wholes += 1
    plan = split, whole
    from_whole = {(False, k): piece for k, piece in zip(whole, pairs)}
    from_split = {(True, k): piece for k, piece in zip(split, ups)}
    rank_order = in_order({**from_whole, **from_split}, RANK_ORDER)
    dhidden, partial = call(
        functools.partial(rank_kernel, tuple(key for key, _ in rank_order)),
        [rank_space, rank_space],
        [in_smem] + [in_vmem] * (2 + parts + wholes),
        [in_vmem, in_vmem],
        moved=1024,
    )(here, after(activations, turned), cotangent, *[piece for _, piece in rank_order])
    dhidden_other = across_cores(dhidden)
    down_pieces = call(
        functools.partial(down_piece_kernel, plan, scale),
        [packed] * parts,
        [in_smem] * 2 + [in_vmem] * 3,
        [in_vmem] * parts,
        moved=1024,
    )(here, lengths, after(dhidden, *downs), dhidden_other, turned)
    d_downs = to_partner(down_pieces, split, owners)

    hidden = call(
        functools.partial(rank_rest_kernel, plan),
        rank_space,
        [in_smem] + [in_vmem] * (2 + parts),
        in_vmem,
        moved=1024,
    )(here, activations, after(partial, *down_pieces), *downs)
    hidden_other = across_cores(hidden)
    pieces = call(
        functools.partial(piece_kernel, plan, scale),
        [straight] * wholes + [packed] * parts,
        [in_smem] * 2 + [in_vmem] * 5,
        [in_vmem] * (parts + wholes),
        moved=1024,
    )(here, lengths, dhidden, dhidden_other, hidden, hidden_other, turned)
    d_pairs = to_partner(pieces[:wholes], whole, owners)
    d_ups = to_partner(pieces[wholes:], split, owners)

    grad_input = call(
        functools.partial(input_kernel, plan, scale),
        jax.ShapeDtypeStruct((tokens, features), bf16),
        [in_smem] * 2 + [in_vmem] * (2 + parts + wholes),
        in_vmem,
        flops=2 * tokens * features * width,
        moved=token_bytes + pair_bytes,
    )(here, lengths, after(dhidden, *pieces), dhidden_other, *downs, *pairs)

    from_all = {("both", k): piece for k, piece in zip(whole, d_pairs)}
    from_all |= {("down", k): piece for k, piece in zip(split, d_downs)}
    from_all |= {("up", k): piece for k, piece in zip(split, d_ups)}
    merge_order = in_order(from_all, MERGE_ORDER)
    gradient = call(
        functools.partial(merge_kernel, plan, tuple(key for key, _ in merge_order)),
        jax.ShapeDtypeStruct(table.shape, bf16),
        [in_smem] * 3 + [in_vmem] * (2 * parts + wholes) + [in_hbm],
        in_hbm,
        [
            pltpu.VMEM((rows, width), f32),
            pltpu.VMEM((owners, rows, width), bf16),
            pltpu.SemaphoreType.DMA((owners,)),
        ],
        moved=2 * pair_bytes,
        aliases={3 + 2 * parts + wholes: 0},
    )(ids, here, lengths, *[piece for _, piece in merge_order], blank)
    return grad_input, gradient[:, None]


def without_kernels(activations, cotangent, adapter_weight_pair, adapter_of_block, block_live_length):
    owners = lax.axis_size("dp")
    here = lax.axis_index("dp")
    count, _, rows, width = adapter_weight_pair.shape
    rank = width // 2
    scale = adapter_alpha / rank
    adapters = adapter_of_block[:, 0]
    lengths = block_live_length[:, 0]
    keep = (jnp.arange(activations.shape[0], dtype=jnp.int32) < lengths[here])[:, None]
    inputs = jnp.where(keep, activations, jnp.zeros_like(activations))
    grads_out = jnp.where(keep, cotangent, jnp.zeros_like(cotangent))
    fetched = lax.all_to_all(
        adapter_weight_pair[:, 0][adapters], "dp", split_axis=0, concat_axis=0, tiled=True
    )
    pair = fetched.reshape(-1, width)
    down, upward = pair[:, :rank], pair[:, rank:]
    f32 = jnp.float32
    hidden_part = jnp.dot(inputs, down, preferred_element_type=f32)
    dhidden_part = scale * jnp.dot(grads_out, upward, preferred_element_type=f32)
    hidden, dhidden = lax.psum((hidden_part, dhidden_part), "tensor")
    hidden16, dhidden16 = hidden.astype(jnp.bfloat16), dhidden.astype(jnp.bfloat16)
    d_down = jnp.dot(inputs.T, dhidden16, preferred_element_type=f32)
    d_up = scale * jnp.dot(grads_out.T, hidden16, preferred_element_type=f32)
    sent = jnp.concatenate([d_down, d_up], axis=1).astype(jnp.bfloat16).reshape(owners, rows, width)
    received = lax.all_to_all(sent, "dp", split_axis=0, concat_axis=0, tiled=True).astype(f32)
    same = adapters[:, None] == adapters[None, :]
    total = jnp.sum(jnp.where(same, lengths[None, :], 0), axis=1).astype(f32)
    summed = jax.ops.segment_sum(received, adapters, num_segments=count)
    denom = jnp.ones((count,), f32).at[adapters].set(jnp.maximum(total, 1.0))
    gradient = (summed / denom[:, None, None]).astype(jnp.bfloat16)
    grad_input = jnp.dot(dhidden16, down.T, preferred_element_type=f32).astype(jnp.bfloat16)
    return grad_input, gradient[:, None]


def solution(mesh):
    owners, cores = mesh.shape["dp"], mesh.shape["tensor"]

    def on_device(activations, cotangent, adapter_weight_pair, *rest):
        rows = adapter_weight_pair.shape[2]
        fits = owners == len(SPLIT) + len(WHOLE) + 1 and cores == 2 and rows % 256 == 0
        body = with_kernels if fits else without_kernels
        return body(activations, cotangent, adapter_weight_pair, *rest)

    in_specs = (
        P(("group", "dp"), "tensor"),
        P(("group", "dp"), "tensor"),
        P(None, "tensor", "dp", None),
        P("group", None),
        P("group", None),
    )
    out_specs = (P(("group", "dp"), "tensor"), P("group", "tensor", "dp", None))
    return jax.shard_map(
        on_device, mesh=mesh, in_specs=in_specs, out_specs=out_specs, check_vma=False
    )
```

```python
import functools

import jax
import jax.numpy as jnp
from jax import lax
from jax.experimental import pallas as pl
from jax.experimental.pallas import tpu as pltpu
from jax.sharding import PartitionSpec as P

adapter_alpha = 128.0
RANK_ORDER = ((False, 1), (False, 2), (True, 4), (True, 5), (False, 6), (False, 7), (False, 3))
MERGE_ORDER = (("both", 2), ("both", 6), ("both", 3), ("both", 7), ("both", 1))
PREP_AFTER = 0
PREP_VMEM = 40
SPLIT = (4, 5)
WHOLE = (2, 6, 3, 7, 1)

in_vmem = pl.BlockSpec(memory_space=pltpu.VMEM)
in_smem = pl.BlockSpec(memory_space=pltpu.SMEM)
in_hbm = pl.BlockSpec(memory_space=pltpu.HBM)


def low_lanes(rows, width):
    return lax.broadcasted_iota(jnp.int32, (rows, width), 1) < width // 2


def call(kernel, out_shape, in_specs, out_specs, scratch=(), flops=0, moved=0, aliases=None, vmem=40):
    return pl.pallas_call(
        kernel,
        out_shape=out_shape,
        in_specs=in_specs,
        out_specs=out_specs,
        scratch_shapes=list(scratch),
        input_output_aliases=aliases or {},
        compiler_params=pltpu.CompilerParams(vmem_limit_bytes=vmem * 1024 * 1024),
        cost_estimate=pl.CostEstimate(flops=flops, bytes_accessed=moved, transcendentals=0),
    )


def swap_halves(value):
    return pltpu.roll(value, value.shape[-1] // 2, 1)


def gather_kernel(plan, ids, here, table, *refs):
    split, whole = plan
    parts = len(split)
    up, straight = refs[:parts], refs[parts : parts + len(whole)]
    down, (held, sems) = refs[parts + len(whole) : -2], refs[-2:]
    me = here[0]
    targets = [(k, held.at[n]) for n, k in enumerate(split)] + list(zip(whole, straight))
    copies = [
        pltpu.make_async_copy(table.at[ids[me ^ k]], target, sems.at[n])
        for n, (k, target) in enumerate(targets)
    ]
    for copy in copies:
        copy.start()
    half = held.shape[1] // 2
    low = low_lanes(half, held.shape[2])
    for n in range(parts):
        copies[n].wait()
        first = held[n, :half].astype(jnp.float32)
        second = held[n, half:].astype(jnp.float32)
        up[n][...] = jnp.where(low, swap_halves(first), second).astype(jnp.bfloat16)
        down[n][...] = jnp.where(low, first, swap_halves(second)).astype(jnp.bfloat16)
    for copy in copies[parts:]:
        copy.wait()


def prep_kernel(ids, here, table, after, x, y, turned, own, blank, zeros, sem, own_sem):
    own_copy = pltpu.make_async_copy(table.at[ids[here[0]]], own, own_sem)
    own_copy.start()
    rows = own.shape[0]
    zeros[...] = jnp.zeros_like(zeros)
    step = zeros.shape[0]
    copies = [
        pltpu.make_async_copy(zeros, blank.at[pl.ds(s, step)], sem.at[s // step])
        for s in range(0, blank.shape[0], step)
    ]
    for copy in copies:
        copy.start()
    tokens = x.shape[0]

    @pl.loop(0, x.shape[1] // rows)
    def _(owner):
        columns = pl.ds(pl.multiple_of(owner * rows, rows), rows)
        turned[owner, :, pl.ds(0, tokens)] = x[:, columns].T
        turned[owner, :, pl.ds(tokens, tokens)] = y[:, columns].T

    for copy in [own_copy, *copies]:
        copy.wait()


def halves_product(values, packed, owner):
    half = packed.shape[0]
    first = pl.ds(pl.multiple_of(owner * 2 * half, half), half)
    second = pl.ds(pl.multiple_of(owner * 2 * half + half, half), half)
    one = jnp.dot(values[:, first], packed[...], preferred_element_type=jnp.float32)
    two = jnp.dot(values[:, second], packed[...], preferred_element_type=jnp.float32)
    return one, two


def rank_kernel(order, here, x, y, *refs):
    pieces, (dhidden, hidden) = refs[:-2], refs[-2:]
    width = dhidden.shape[1]
    tokens = x.shape[0]
    me = here[0]
    x_rank = jnp.zeros((tokens, width), jnp.float32)
    y_rank = jnp.zeros((tokens, width), jnp.float32)
    y_first = jnp.zeros((tokens, width), jnp.float32)
    for (packed, k), piece in zip(order, pieces):
        if packed:
            first, second = halves_product(y, piece, me ^ k)
            y_first += first
            y_rank += second
        else:
            rows = piece.shape[0]
            columns = pl.ds(pl.multiple_of((me ^ k) * rows, rows), rows)
            x_rank += jnp.dot(x[:, columns], piece[...], preferred_element_type=jnp.float32)
            y_rank += jnp.dot(y[:, columns], piece[...], preferred_element_type=jnp.float32)
    y_rank += swap_halves(y_first)
    half = tokens // 2
    low = low_lanes(half, width)
    dhidden[...] = jnp.where(low, swap_halves(y_rank[:half]), y_rank[half:])
    hidden[...] = jnp.where(low, x_rank[:half], swap_halves(x_rank[half:]))


def rank_rest_kernel(plan, here, x, partial, *refs):
    split, _ = plan
    down, out = refs[:-1], refs[-1]
    tokens, width = x.shape[0], partial.shape[1]
    x_first = jnp.zeros((tokens, width), jnp.float32)
    x_second = jnp.zeros((tokens, width), jnp.float32)
    for n, k in enumerate(split):
        first, second = halves_product(x, down[n], here[0] ^ k)
        x_first += first
        x_second += second
    x_rank = x_first + swap_halves(x_second)
    half = tokens // 2
    low = low_lanes(half, width)
    out[...] = partial[...] + jnp.where(low, x_rank[:half], swap_halves(x_rank[half:]))


def rounded(mine, other, length, scale):
    total = scale * (mine[...] + other[...])
    swapped = swap_halves(total)
    low = low_lanes(*total.shape)
    live = lax.broadcasted_iota(jnp.int32, (2 * total.shape[0], total.shape[1]), 0) < length
    left = [jnp.where(low, total, 0.0), jnp.where(low, swapped, 0.0)]
    right = [jnp.where(low, 0.0, swapped), jnp.where(low, 0.0, total)]
    return [jnp.where(live, jnp.concatenate(v, axis=0), 0.0).astype(jnp.bfloat16) for v in (left, right)]


def packed_piece(turned, owner, lanes, left, right):
    half = turned.shape[1] // 2
    first = jnp.dot(turned[owner, :half, lanes], left, preferred_element_type=jnp.float32)
    second = jnp.dot(turned[owner, half:, lanes], right, preferred_element_type=jnp.float32)
    return first + second


def down_piece_kernel(plan, scale, here, lengths, mine, other, turned, *out):
    split, _ = plan
    me = here[0]
    left, right = rounded(mine, other, lengths[me], scale)
    tokens = left.shape[0]
    for n, k in enumerate(split):
        out[n][...] = packed_piece(turned, me ^ k, slice(0, tokens), left, right).astype(jnp.bfloat16)


def piece_kernel(plan, scale, here, lengths, d_mine, d_other, mine, other, turned, *refs):
    split, whole = plan
    straight, up = refs[: len(whole)], refs[len(whole) :]
    me = here[0]
    dhidden, _ = rounded(d_mine, d_other, lengths[me], scale)
    left, right = rounded(mine, other, lengths[me], 1.0)
    tokens = left.shape[0]
    ranks = jnp.concatenate([dhidden, right], axis=0)

    def rows_for(owner):
        piece = jnp.dot(turned[owner], ranks, preferred_element_type=jnp.float32)
        return jnp.where(low_lanes(*piece.shape), piece, scale * piece).astype(jnp.bfloat16)

    for n, k in enumerate(split):
        piece = packed_piece(turned, me ^ k, slice(tokens, 2 * tokens), left, right)
        up[n][...] = (scale * piece).astype(jnp.bfloat16)
    for n, k in enumerate(whole):
        straight[n][...] = rows_for(me ^ k)


def input_kernel(plan, scale, here, lengths, mine, other, *refs):
    split, whole = plan
    down, straight, out = refs[: len(split)], refs[len(split) : -1], refs[-1]
    rows = straight[0].shape[0]
    half = rows // 2
    me = here[0]
    left, right = rounded(mine, other, lengths[me], scale)

    def product(ranks, columns):
        value = lax.dot_general(
            ranks, columns, (((1,), (1,)), ((), ())), preferred_element_type=jnp.float32
        )
        return value.astype(jnp.bfloat16)

    for k, pair in zip(whole, straight):
        out[:, pl.ds(pl.multiple_of((me ^ k) * rows, rows), rows)] = product(left, pair[...])
    for n, k in enumerate(split):
        start = (me ^ k) * rows
        out[:, pl.ds(pl.multiple_of(start, half), half)] = product(left, down[n][...])
        out[:, pl.ds(pl.multiple_of(start + half, half), half)] = product(right, down[n][...])


def merge_kernel(plan, order, ids, here, lengths, *refs):
    split, whole = plan
    by_key = dict(zip(order, refs[:-5]))
    down, up = [by_key["down", k] for k in split], [by_key["up", k] for k in split]
    straight = [by_key["both", k] for k in whole]
    out, total, held, sems = refs[-4:]
    me = here[0]
    rows, width = total.shape
    half = rows // 2
    low = low_lanes(half, width)

    def unpacked(n):
        d_down, d_up = down[n][...].astype(jnp.float32), up[n][...].astype(jnp.float32)
        first = jnp.where(low, d_down, swap_halves(d_up))
        second = jnp.where(low, swap_halves(d_down), d_up)
        return jnp.concatenate([first, second], axis=0)

    def read(ref):
        return lambda: ref[...].astype(jnp.float32)

    pieces = [(me ^ k, read(straight[n])) for n, k in enumerate(whole)]
    pieces += [(me ^ k, functools.partial(unpacked, n)) for n, k in enumerate(split)]
    owners = len(pieces)
    adapters = [ids[block] for block, _ in pieces]
    counts = [lengths[block] for block, _ in pieces]
    copies, firsts = [], []
    for k, (_, value) in enumerate(pieces):
        copies.append(pltpu.make_async_copy(held.at[k], out.at[adapters[k]], sems.at[k]))
        same = [adapters[other] == adapters[k] for other in range(owners)]
        earlier = functools.reduce(jnp.logical_or, same[:k], jnp.bool_(False))
        later = functools.reduce(jnp.logical_or, same[k + 1 :], jnp.bool_(False))
        firsts.append(jnp.logical_not(earlier))

        def store(sum_of, count):
            denom = jnp.maximum(count.astype(jnp.float32), 1.0)
            part = 1.0 / jnp.full((1, width), denom)
            held[k] = (sum_of * part).astype(jnp.bfloat16)
            copies[k].start()

        @pl.when(firsts[k] & jnp.logical_not(later))
        def _():
            store(value(), counts[k])

        @pl.when(firsts[k] & later)
        def _():
            total[...] = value()
            count = counts[k]
            for other in range(k + 1, owners):
                count += jnp.where(same[other], counts[other], 0)

                @pl.when(same[other])
                def _():
                    total[...] += pieces[other][1]()

            store(total[...], count)

    for k in range(owners):
        pl.when(firsts[k])(copies[k].wait)


def to_partner(pieces, partners, owners):
    return [
        lax.ppermute(piece, "dp", [(i, i ^ k) for i in range(owners)]) if k else piece
        for k, piece in zip(partners, pieces)
    ]


def in_order(pieces, first):
    keys = [key for key in first if key in pieces]
    keys += [key for key in pieces if key not in keys]
    return [(key, pieces[key]) for key in keys]


def after(value, *others):
    return lax.optimization_barrier((value, *others))[0]


def across_cores(value):
    cores = lax.axis_size("tensor")
    return lax.ppermute(value, "tensor", [(i, i ^ 1) for i in range(cores)])


def with_kernels(activations, cotangent, adapter_weight_pair, adapter_of_block, block_live_length):
    owners = lax.axis_size("dp")
    plan = split, whole = SPLIT, WHOLE
    here = lax.axis_index("dp").astype(jnp.int32).reshape(1)
    ids, lengths = adapter_of_block[:, 0], block_live_length[:, 0]
    count, _, rows, width = adapter_weight_pair.shape
    table = adapter_weight_pair.reshape(count, rows, width)
    tokens, features = activations.shape
    scale = adapter_alpha / (width // 2)
    bf16, f32 = jnp.bfloat16, jnp.float32
    packed = jax.ShapeDtypeStruct((rows // 2, width), bf16)
    straight = jax.ShapeDtypeStruct((rows, width), bf16)
    rank_space = jax.ShapeDtypeStruct((tokens // 2, width), f32)
    parts, wholes = len(split), len(whole)
    pair_bytes = owners * rows * width * 2
    token_bytes = tokens * features * 2

    sent = call(
        functools.partial(gather_kernel, plan),
        [packed] * parts + [straight] * wholes + [packed] * parts,
        [in_smem, in_smem, in_hbm],
        [in_vmem] * (2 * parts + wholes),
        [pltpu.VMEM((parts, rows, width), bf16), pltpu.SemaphoreType.DMA((owners,))],
        moved=2 * pair_bytes,
        vmem=53,
    )(ids, here, table)
    ups = to_partner(sent[:parts], split, owners)
    pairs = to_partner(sent[parts : parts + wholes], whole, owners)
    step = 8
    turned, own, blank = call(
        prep_kernel,
        [
            jax.ShapeDtypeStruct((owners, rows, 2 * tokens), bf16),
            straight,
            jax.ShapeDtypeStruct(table.shape, bf16),
        ],
        [in_smem, in_smem, in_hbm, in_hbm, in_vmem, in_vmem],
        [in_vmem, in_vmem, in_hbm],
        [
            pltpu.VMEM((step, rows, width), bf16),
            pltpu.SemaphoreType.DMA((count // step,)),
            pltpu.SemaphoreType.DMA,
        ],
        moved=4 * token_bytes + 2 * count * rows * width,
        vmem=PREP_VMEM,
    )(ids, here, table, ups[PREP_AFTER], activations, cotangent)

    held_back = list(sent[parts + wholes :])
    held_back[-1] = after(held_back[-1], turned)
    downs = to_partner(held_back, split, owners)
    pairs.append(own)
    whole += (0,)
    wholes += 1
    plan = split, whole
    from_whole = {(False, k): piece for k, piece in zip(whole, pairs)}
    from_split = {(True, k): piece for k, piece in zip(split, ups)}
    rank_order = in_order({**from_whole, **from_split}, RANK_ORDER)
    dhidden, partial = call(
        functools.partial(rank_kernel, tuple(key for key, _ in rank_order)),
        [rank_space, rank_space],
        [in_smem] + [in_vmem] * (2 + parts + wholes),
        [in_vmem, in_vmem],
        moved=1024,
    )(here, after(activations, turned), cotangent, *[piece for _, piece in rank_order])
    dhidden_other = across_cores(dhidden)
    down_pieces = call(
        functools.partial(down_piece_kernel, plan, scale),
        [packed] * parts,
        [in_smem] * 2 + [in_vmem] * 3,
        [in_vmem] * parts,
        moved=1024,
    )(here, lengths, after(dhidden, *downs), dhidden_other, turned)
    d_downs = to_partner(down_pieces, split, owners)

    hidden = call(
        functools.partial(rank_rest_kernel, plan),
        rank_space,
        [in_smem] + [in_vmem] * (2 + parts),
        in_vmem,
        moved=1024,
    )(here, activations, after(partial, *down_pieces), *downs)
    hidden_other = across_cores(hidden)
    pieces = call(
        functools.partial(piece_kernel, plan, scale),
        [straight] * wholes + [packed] * parts,
        [in_smem] * 2 + [in_vmem] * 5,
        [in_vmem] * (parts + wholes),
        moved=1024,
    )(here, lengths, dhidden, dhidden_other, hidden, hidden_other, turned)
    d_pairs = to_partner(pieces[:wholes], whole, owners)
    d_ups = to_partner(pieces[wholes:], split, owners)

    grad_input = call(
        functools.partial(input_kernel, plan, scale),
        jax.ShapeDtypeStruct((tokens, features), bf16),
        [in_smem] * 2 + [in_vmem] * (2 + parts + wholes),
        in_vmem,
        flops=2 * tokens * features * width,
        moved=token_bytes + pair_bytes,
    )(here, lengths, after(dhidden, *pieces), dhidden_other, *downs, *pairs)

    from_all = {("both", k): piece for k, piece in zip(whole, d_pairs)}
    from_all |= {("down", k): piece for k, piece in zip(split, d_downs)}
    from_all |= {("up", k): piece for k, piece in zip(split, d_ups)}
    merge_order = in_order(from_all, MERGE_ORDER)
    gradient = call(
        functools.partial(merge_kernel, plan, tuple(key for key, _ in merge_order)),
        jax.ShapeDtypeStruct(table.shape, bf16),
        [in_smem] * 3 + [in_vmem] * (2 * parts + wholes) + [in_hbm],
        in_hbm,
        [
            pltpu.VMEM((rows, width), f32),
            pltpu.VMEM((owners, rows, width), bf16),
            pltpu.SemaphoreType.DMA((owners,)),
        ],
        moved=2 * pair_bytes,
        aliases={3 + 2 * parts + wholes: 0},
    )(ids, here, lengths, *[piece for _, piece in merge_order], blank)
    return grad_input, gradient[:, None]


def without_kernels(activations, cotangent, adapter_weight_pair, adapter_of_block, block_live_length):
    owners = lax.axis_size("dp")
    here = lax.axis_index("dp")
    count, _, rows, width = adapter_weight_pair.shape
    rank = width // 2
    scale = adapter_alpha / rank
    adapters = adapter_of_block[:, 0]
    lengths = block_live_length[:, 0]
    keep = (jnp.arange(activations.shape[0], dtype=jnp.int32) < lengths[here])[:, None]
    inputs = jnp.where(keep, activations, jnp.zeros_like(activations))
    grads_out = jnp.where(keep, cotangent, jnp.zeros_like(cotangent))
    fetched = lax.all_to_all(
        adapter_weight_pair[:, 0][adapters], "dp", split_axis=0, concat_axis=0, tiled=True
    )
    pair = fetched.reshape(-1, width)
    down, upward = pair[:, :rank], pair[:, rank:]
    f32 = jnp.float32
    hidden_part = jnp.dot(inputs, down, preferred_element_type=f32)
    dhidden_part = scale * jnp.dot(grads_out, upward, preferred_element_type=f32)
    hidden, dhidden = lax.psum((hidden_part, dhidden_part), "tensor")
    hidden16, dhidden16 = hidden.astype(jnp.bfloat16), dhidden.astype(jnp.bfloat16)
    d_down = jnp.dot(inputs.T, dhidden16, preferred_element_type=f32)
    d_up = scale * jnp.dot(grads_out.T, hidden16, preferred_element_type=f32)
    sent = jnp.concatenate([d_down, d_up], axis=1).astype(jnp.bfloat16).reshape(owners, rows, width)
    received = lax.all_to_all(sent, "dp", split_axis=0, concat_axis=0, tiled=True).astype(f32)
    same = adapters[:, None] == adapters[None, :]
    total = jnp.sum(jnp.where(same, lengths[None, :], 0), axis=1).astype(f32)
    summed = jax.ops.segment_sum(received, adapters, num_segments=count)
    denom = jnp.ones((count,), f32).at[adapters].set(jnp.maximum(total, 1.0))
    gradient = (summed / denom[:, None, None]).astype(jnp.bfloat16)
    grad_input = jnp.dot(dhidden16, down.T, preferred_element_type=f32).astype(jnp.bfloat16)
    return grad_input, gradient[:, None]


def solution(mesh):
    owners, cores = mesh.shape["dp"], mesh.shape["tensor"]

    def on_device(activations, cotangent, adapter_weight_pair, *rest):
        rows = adapter_weight_pair.shape[2]
        fits = owners == len(SPLIT) + len(WHOLE) + 1 and cores == 2 and rows % 256 == 0
        body = with_kernels if fits else without_kernels
        return body(activations, cotangent, adapter_weight_pair, *rest)

    in_specs = (
        P(("group", "dp"), "tensor"),
        P(("group", "dp"), "tensor"),
        P(None, "tensor", "dp", None),
        P("group", None),
        P("group", None),
    )
    out_specs = (P(("group", "dp"), "tensor"), P("group", "tensor", "dp", None))
    return jax.shard_map(
        on_device, mesh=mesh, in_specs=in_specs, out_specs=out_specs, check_vma=False
    )
```

```python
import functools

import jax
import jax.numpy as jnp
from jax import lax
from jax.experimental import pallas as pl
from jax.experimental.pallas import tpu as pltpu
from jax.sharding import PartitionSpec as P

adapter_alpha = 128.0
RANK_ORDER = ((False, 1), (False, 2), (True, 4), (True, 5), (False, 6), (False, 7), (False, 3))
LATE = (3, 7, 1)
PREP_AFTER = 0
PREP_VMEM = 40
SPLIT = (4, 5)
WHOLE = (6, 2, 3, 7, 1)

in_vmem = pl.BlockSpec(memory_space=pltpu.VMEM)
in_smem = pl.BlockSpec(memory_space=pltpu.SMEM)
in_hbm = pl.BlockSpec(memory_space=pltpu.HBM)


def low_lanes(rows, width):
    return lax.broadcasted_iota(jnp.int32, (rows, width), 1) < width // 2


def call(kernel, out_shape, in_specs, out_specs, scratch=(), flops=0, moved=0, aliases=None, vmem=40):
    return pl.pallas_call(
        kernel,
        out_shape=out_shape,
        in_specs=in_specs,
        out_specs=out_specs,
        scratch_shapes=list(scratch),
        input_output_aliases=aliases or {},
        compiler_params=pltpu.CompilerParams(vmem_limit_bytes=vmem * 1024 * 1024),
        cost_estimate=pl.CostEstimate(flops=flops, bytes_accessed=moved, transcendentals=0),
    )


def swap_halves(value):
    return pltpu.roll(value, value.shape[-1] // 2, 1)


def gather_kernel(plan, ids, here, table, *refs):
    split, whole = plan
    parts = len(split)
    up, straight = refs[:parts], refs[parts : parts + len(whole)]
    down, (held, sems) = refs[parts + len(whole) : -2], refs[-2:]
    me = here[0]
    targets = [(k, held.at[n]) for n, k in enumerate(split)] + list(zip(whole, straight))
    copies = [
        pltpu.make_async_copy(table.at[ids[me ^ k]], target, sems.at[n])
        for n, (k, target) in enumerate(targets)
    ]
    for copy in copies:
        copy.start()
    half = held.shape[1] // 2
    low = low_lanes(half, held.shape[2])
    for n in range(parts):
        copies[n].wait()
        first = held[n, :half].astype(jnp.float32)
        second = held[n, half:].astype(jnp.float32)
        up[n][...] = jnp.where(low, swap_halves(first), second).astype(jnp.bfloat16)
        down[n][...] = jnp.where(low, first, swap_halves(second)).astype(jnp.bfloat16)
    for copy in copies[parts:]:
        copy.wait()


def prep_kernel(ids, here, table, after, x, y, turned, own, blank, zeros, sem, own_sem):
    own_copy = pltpu.make_async_copy(table.at[ids[here[0]]], own, own_sem)
    own_copy.start()
    rows = own.shape[0]
    zeros[...] = jnp.zeros_like(zeros)
    step = zeros.shape[0]
    copies = [
        pltpu.make_async_copy(zeros, blank.at[pl.ds(s, step)], sem.at[s // step])
        for s in range(0, blank.shape[0], step)
    ]
    for copy in copies:
        copy.start()
    tokens = x.shape[0]

    @pl.loop(0, x.shape[1] // rows)
    def _(owner):
        columns = pl.ds(pl.multiple_of(owner * rows, rows), rows)
        turned[owner, :, pl.ds(0, tokens)] = x[:, columns].T
        turned[owner, :, pl.ds(tokens, tokens)] = y[:, columns].T

    for copy in [own_copy, *copies]:
        copy.wait()


def halves_product(values, packed, owner):
    half = packed.shape[0]
    first = pl.ds(pl.multiple_of(owner * 2 * half, half), half)
    second = pl.ds(pl.multiple_of(owner * 2 * half + half, half), half)
    one = jnp.dot(values[:, first], packed[...], preferred_element_type=jnp.float32)
    two = jnp.dot(values[:, second], packed[...], preferred_element_type=jnp.float32)
    return one, two


def rank_kernel(order, here, x, y, *refs):
    pieces, (dhidden, hidden) = refs[:-2], refs[-2:]
    width = dhidden.shape[1]
    tokens = x.shape[0]
    me = here[0]
    x_rank = jnp.zeros((tokens, width), jnp.float32)
    y_rank = jnp.zeros((tokens, width), jnp.float32)
    y_first = jnp.zeros((tokens, width), jnp.float32)
    for (packed, k), piece in zip(order, pieces):
        if packed:
            first, second = halves_product(y, piece, me ^ k)
            y_first += first
            y_rank += second
        else:
            rows = piece.shape[0]
            columns = pl.ds(pl.multiple_of((me ^ k) * rows, rows), rows)
            x_rank += jnp.dot(x[:, columns], piece[...], preferred_element_type=jnp.float32)
            y_rank += jnp.dot(y[:, columns], piece[...], preferred_element_type=jnp.float32)
    y_rank += swap_halves(y_first)
    half = tokens // 2
    low = low_lanes(half, width)
    dhidden[...] = jnp.where(low, swap_halves(y_rank[:half]), y_rank[half:])
    hidden[...] = jnp.where(low, x_rank[:half], swap_halves(x_rank[half:]))


def rank_rest_kernel(plan, here, x, partial, *refs):
    split, _ = plan
    down, out = refs[:-1], refs[-1]
    tokens, width = x.shape[0], partial.shape[1]
    x_first = jnp.zeros((tokens, width), jnp.float32)
    x_second = jnp.zeros((tokens, width), jnp.float32)
    for n, k in enumerate(split):
        first, second = halves_product(x, down[n], here[0] ^ k)
        x_first += first
        x_second += second
    x_rank = x_first + swap_halves(x_second)
    half = tokens // 2
    low = low_lanes(half, width)
    out[...] = partial[...] + jnp.where(low, x_rank[:half], swap_halves(x_rank[half:]))


def rounded(mine, other, length, scale):
    total = scale * (mine[...] + other[...])
    swapped = swap_halves(total)
    low = low_lanes(*total.shape)
    live = lax.broadcasted_iota(jnp.int32, (2 * total.shape[0], total.shape[1]), 0) < length
    left = [jnp.where(low, total, 0.0), jnp.where(low, swapped, 0.0)]
    right = [jnp.where(low, 0.0, swapped), jnp.where(low, 0.0, total)]
    return [jnp.where(live, jnp.concatenate(v, axis=0), 0.0).astype(jnp.bfloat16) for v in (left, right)]


def packed_piece(turned, owner, lanes, left, right):
    half = turned.shape[1] // 2
    first = jnp.dot(turned[owner, :half, lanes], left, preferred_element_type=jnp.float32)
    second = jnp.dot(turned[owner, half:, lanes], right, preferred_element_type=jnp.float32)
    return first + second


def down_piece_kernel(plan, scale, here, lengths, mine, other, turned, *out):
    split, _ = plan
    me = here[0]
    left, right = rounded(mine, other, lengths[me], scale)
    tokens = left.shape[0]
    for n, k in enumerate(split):
        out[n][...] = packed_piece(turned, me ^ k, slice(0, tokens), left, right).astype(jnp.bfloat16)


def piece_kernel(plan, scale, here, lengths, d_mine, d_other, mine, other, turned, *refs):
    split, whole = plan
    straight, up = refs[: len(whole)], refs[len(whole) :]
    me = here[0]
    dhidden, _ = rounded(d_mine, d_other, lengths[me], scale)
    left, right = rounded(mine, other, lengths[me], 1.0)
    tokens = left.shape[0]
    ranks = jnp.concatenate([dhidden, right], axis=0)

    def rows_for(owner):
        piece = jnp.dot(turned[owner], ranks, preferred_element_type=jnp.float32)
        return jnp.where(low_lanes(*piece.shape), piece, scale * piece).astype(jnp.bfloat16)

    for n, k in enumerate(split):
        piece = packed_piece(turned, me ^ k, slice(tokens, 2 * tokens), left, right)
        up[n][...] = (scale * piece).astype(jnp.bfloat16)
    for n, k in enumerate(whole):
        straight[n][...] = rows_for(me ^ k)


def input_kernel(plan, scale, here, lengths, mine, other, *refs):
    split, whole = plan
    down, straight, out = refs[: len(split)], refs[len(split) : -1], refs[-1]
    rows = straight[0].shape[0]
    half = rows // 2
    me = here[0]
    left, right = rounded(mine, other, lengths[me], scale)

    def product(ranks, columns):
        value = lax.dot_general(
            ranks, columns, (((1,), (1,)), ((), ())), preferred_element_type=jnp.float32
        )
        return value.astype(jnp.bfloat16)

    for k, pair in zip(whole, straight):
        out[:, pl.ds(pl.multiple_of((me ^ k) * rows, rows), rows)] = product(left, pair[...])
    for n, k in enumerate(split):
        start = (me ^ k) * rows
        out[:, pl.ds(pl.multiple_of(start, half), half)] = product(left, down[n][...])
        out[:, pl.ds(pl.multiple_of(start + half, half), half)] = product(right, down[n][...])


def merge_kernel(order, handled, others, ids, here, lengths, *refs):
    by_key = dict(zip(order, refs[:-5]))
    out, total, held, sems = refs[-4:]
    me = here[0]
    rows, width = total.shape
    half = rows // 2
    low = low_lanes(half, width)
    others_here = ("both", others[0]) in by_key or ("up", others[0]) in by_key

    def value(k):
        if ("both", k) in by_key:
            return by_key["both", k][...].astype(jnp.float32)
        d_down = by_key["down", k][...].astype(jnp.float32)
        d_up = by_key["up", k][...].astype(jnp.float32)
        first = jnp.where(low, d_down, swap_halves(d_up))
        second = jnp.where(low, swap_halves(d_down), d_up)
        return jnp.concatenate([first, second], axis=0)

    def either(conditions):
        return functools.reduce(jnp.logical_or, conditions, jnp.bool_(False))

    copies, chosen = [], []
    for n, k in enumerate(handled):
        adapter = ids[me ^ k]
        copies.append(pltpu.make_async_copy(held.at[n], out.at[adapter], sems.at[n]))
        same = {other: ids[me ^ other] == adapter for other in (*handled, *others) if other != k}
        skip = either([same[other] for other in handled[:n]])
        adding = list(handled[n + 1 :])
        if others_here:
            adding += others
        else:
            skip |= either([same[other] for other in others])
        more = either([same[other] for other in adding])
        chosen.append(jnp.logical_not(skip))

        def store(sum_of, count):
            denom = jnp.maximum(count.astype(jnp.float32), 1.0)
            part = 1.0 / jnp.full((1, width), denom)
            held[n] = (sum_of * part).astype(jnp.bfloat16)
            copies[n].start()

        @pl.when(chosen[n] & jnp.logical_not(more))
        def _():
            store(value(k), lengths[me ^ k])

        @pl.when(chosen[n] & more)
        def _():
            total[...] = value(k)
            count = lengths[me ^ k]
            for other in adding:
                count += jnp.where(same[other], lengths[me ^ other], 0)

                @pl.when(same[other])
                def _():
                    total[...] += value(other)

            store(total[...], count)

    for n in range(len(handled)):
        pl.when(chosen[n])(copies[n].wait)


def to_partner(pieces, partners, owners):
    return [
        lax.ppermute(piece, "dp", [(i, i ^ k) for i in range(owners)]) if k else piece
        for k, piece in zip(partners, pieces)
    ]


def in_order(pieces, first):
    keys = [key for key in first if key in pieces]
    keys += [key for key in pieces if key not in keys]
    return [(key, pieces[key]) for key in keys]


def after(value, *others):
    return lax.optimization_barrier((value, *others))[0]


def across_cores(value):
    cores = lax.axis_size("tensor")
    return lax.ppermute(value, "tensor", [(i, i ^ 1) for i in range(cores)])


def with_kernels(activations, cotangent, adapter_weight_pair, adapter_of_block, block_live_length):
    owners = lax.axis_size("dp")
    plan = split, whole = SPLIT, WHOLE
    here = lax.axis_index("dp").astype(jnp.int32).reshape(1)
    ids, lengths = adapter_of_block[:, 0], block_live_length[:, 0]
    count, _, rows, width = adapter_weight_pair.shape
    table = adapter_weight_pair.reshape(count, rows, width)
    tokens, features = activations.shape
    scale = adapter_alpha / (width // 2)
    bf16, f32 = jnp.bfloat16, jnp.float32
    packed = jax.ShapeDtypeStruct((rows // 2, width), bf16)
    straight = jax.ShapeDtypeStruct((rows, width), bf16)
    rank_space = jax.ShapeDtypeStruct((tokens // 2, width), f32)
    parts, wholes = len(split), len(whole)
    pair_bytes = owners * rows * width * 2
    token_bytes = tokens * features * 2

    sent = call(
        functools.partial(gather_kernel, plan),
        [packed] * parts + [straight] * wholes + [packed] * parts,
        [in_smem, in_smem, in_hbm],
        [in_vmem] * (2 * parts + wholes),
        [pltpu.VMEM((parts, rows, width), bf16), pltpu.SemaphoreType.DMA((owners,))],
        moved=2 * pair_bytes,
        vmem=53,
    )(ids, here, table)
    ups = to_partner(sent[:parts], split, owners)
    pairs = to_partner(sent[parts : parts + wholes], whole, owners)
    step = 8
    turned, own, blank = call(
        prep_kernel,
        [
            jax.ShapeDtypeStruct((owners, rows, 2 * tokens), bf16),
            straight,
            jax.ShapeDtypeStruct(table.shape, bf16),
        ],
        [in_smem, in_smem, in_hbm, in_hbm, in_vmem, in_vmem],
        [in_vmem, in_vmem, in_hbm],
        [
            pltpu.VMEM((step, rows, width), bf16),
            pltpu.SemaphoreType.DMA((count // step,)),
            pltpu.SemaphoreType.DMA,
        ],
        moved=4 * token_bytes + 2 * count * rows * width,
        vmem=PREP_VMEM,
    )(ids, here, table, ups[PREP_AFTER], activations, cotangent)

    held_back = list(sent[parts + wholes :])
    held_back[-1] = after(held_back[-1], turned)
    downs = to_partner(held_back, split, owners)
    pairs.append(own)
    whole += (0,)
    wholes += 1
    plan = split, whole
    from_whole = {(False, k): piece for k, piece in zip(whole, pairs)}
    from_split = {(True, k): piece for k, piece in zip(split, ups)}
    rank_order = in_order({**from_whole, **from_split}, RANK_ORDER)
    dhidden, partial = call(
        functools.partial(rank_kernel, tuple(key for key, _ in rank_order)),
        [rank_space, rank_space],
        [in_smem] + [in_vmem] * (2 + parts + wholes),
        [in_vmem, in_vmem],
        moved=1024,
    )(here, after(activations, turned), cotangent, *[piece for _, piece in rank_order])
    dhidden_other = across_cores(dhidden)
    down_pieces = call(
        functools.partial(down_piece_kernel, plan, scale),
        [packed] * parts,
        [in_smem] * 2 + [in_vmem] * 3,
        [in_vmem] * parts,
        moved=1024,
    )(here, lengths, after(dhidden, *downs), dhidden_other, turned)
    d_downs = to_partner(down_pieces, split, owners)

    hidden = call(
        functools.partial(rank_rest_kernel, plan),
        rank_space,
        [in_smem] + [in_vmem] * (2 + parts),
        in_vmem,
        moved=1024,
    )(here, activations, after(partial, *down_pieces), *downs)
    hidden_other = across_cores(hidden)
    pieces = call(
        functools.partial(piece_kernel, plan, scale),
        [straight] * wholes + [packed] * parts,
        [in_smem] * 2 + [in_vmem] * 5,
        [in_vmem] * (parts + wholes),
        moved=1024,
    )(here, lengths, dhidden, dhidden_other, hidden, hidden_other, turned)
    d_pairs = to_partner(pieces[:wholes], whole, owners)
    d_ups = [after(piece, down) for piece, down in zip(pieces[wholes:], d_downs)]
    d_ups = to_partner(d_ups, split, owners)

    grad_input = call(
        functools.partial(input_kernel, plan, scale),
        jax.ShapeDtypeStruct((tokens, features), bf16),
        [in_smem] * 2 + [in_vmem] * (2 + parts + wholes),
        in_vmem,
        flops=2 * tokens * features * width,
        moved=token_bytes + pair_bytes,
    )(here, lengths, after(dhidden, *pieces), dhidden_other, *downs, *pairs)

    arrived = {("both", k): piece for k, piece in zip(whole, d_pairs)}
    arrived |= {("down", k): piece for k, piece in zip(split, d_downs)}
    arrived |= {("up", k): piece for k, piece in zip(split, d_ups)}
    late = tuple(k for k in whole if k in LATE)
    early = tuple(k for k in (*split, *whole) if k not in LATE)

    def merge(handled, others, pieces, so_far):
        return call(
            functools.partial(merge_kernel, tuple(pieces), handled, others),
            jax.ShapeDtypeStruct(table.shape, bf16),
            [in_smem] * 3 + [in_vmem] * len(pieces) + [in_hbm],
            in_hbm,
            [
                pltpu.VMEM((rows, width), f32),
                pltpu.VMEM((len(handled), rows, width), bf16),
                pltpu.SemaphoreType.DMA((len(handled),)),
            ],
            moved=2 * pair_bytes,
            aliases={3 + len(pieces): 0},
        )(ids, here, lengths, *pieces.values(), so_far)

    early_pieces = {key: piece for key, piece in arrived.items() if key[1] in early}
    gradient = merge(late, early, arrived, merge(early, late, early_pieces, blank))
    return grad_input, gradient[:, None]


def without_kernels(activations, cotangent, adapter_weight_pair, adapter_of_block, block_live_length):
    owners = lax.axis_size("dp")
    here = lax.axis_index("dp")
    count, _, rows, width = adapter_weight_pair.shape
    rank = width // 2
    scale = adapter_alpha / rank
    adapters = adapter_of_block[:, 0]
    lengths = block_live_length[:, 0]
    keep = (jnp.arange(activations.shape[0], dtype=jnp.int32) < lengths[here])[:, None]
    inputs = jnp.where(keep, activations, jnp.zeros_like(activations))
    grads_out = jnp.where(keep, cotangent, jnp.zeros_like(cotangent))
    fetched = lax.all_to_all(
        adapter_weight_pair[:, 0][adapters], "dp", split_axis=0, concat_axis=0, tiled=True
    )
    pair = fetched.reshape(-1, width)
    down, upward = pair[:, :rank], pair[:, rank:]
    f32 = jnp.float32
    hidden_part = jnp.dot(inputs, down, preferred_element_type=f32)
    dhidden_part = scale * jnp.dot(grads_out, upward, preferred_element_type=f32)
    hidden, dhidden = lax.psum((hidden_part, dhidden_part), "tensor")
    hidden16, dhidden16 = hidden.astype(jnp.bfloat16), dhidden.astype(jnp.bfloat16)
    d_down = jnp.dot(inputs.T, dhidden16, preferred_element_type=f32)
    d_up = scale * jnp.dot(grads_out.T, hidden16, preferred_element_type=f32)
    sent = jnp.concatenate([d_down, d_up], axis=1).astype(jnp.bfloat16).reshape(owners, rows, width)
    received = lax.all_to_all(sent, "dp", split_axis=0, concat_axis=0, tiled=True).astype(f32)
    same = adapters[:, None] == adapters[None, :]
    total = jnp.sum(jnp.where(same, lengths[None, :], 0), axis=1).astype(f32)
    summed = jax.ops.segment_sum(received, adapters, num_segments=count)
    denom = jnp.ones((count,), f32).at[adapters].set(jnp.maximum(total, 1.0))
    gradient = (summed / denom[:, None, None]).astype(jnp.bfloat16)
    grad_input = jnp.dot(dhidden16, down.T, preferred_element_type=f32).astype(jnp.bfloat16)
    return grad_input, gradient[:, None]


def solution(mesh):
    owners, cores = mesh.shape["dp"], mesh.shape["tensor"]

    def on_device(activations, cotangent, adapter_weight_pair, *rest):
        rows = adapter_weight_pair.shape[2]
        fits = owners == len(SPLIT) + len(WHOLE) + 1 and cores == 2 and rows % 256 == 0
        body = with_kernels if fits else without_kernels
        return body(activations, cotangent, adapter_weight_pair, *rest)

    in_specs = (
        P(("group", "dp"), "tensor"),
        P(("group", "dp"), "tensor"),
        P(None, "tensor", "dp", None),
        P("group", None),
        P("group", None),
    )
    out_specs = (P(("group", "dp"), "tensor"), P("group", "tensor", "dp", None))
    return jax.shard_map(
        on_device, mesh=mesh, in_specs=in_specs, out_specs=out_specs, check_vma=False
    )
```

```python
import functools

import jax
import jax.numpy as jnp
from jax import lax
from jax.experimental import pallas as pl
from jax.experimental.pallas import tpu as pltpu
from jax.sharding import PartitionSpec as P

adapter_alpha = 128.0
FETCH = (1, 4, 2, 5, 6, 3, 7)
FETCH_TIES = {}
SEND = (1, 4, 2, 5, 6, 3, 7)
SEND_TIES = {}
PREP_AFTER = 1
LATE = (3, 7)

in_vmem = pl.BlockSpec(memory_space=pltpu.VMEM)
in_smem = pl.BlockSpec(memory_space=pltpu.SMEM)
in_hbm = pl.BlockSpec(memory_space=pltpu.HBM)


def low_lanes(rows, width):
    return lax.broadcasted_iota(jnp.int32, (rows, width), 1) < width // 2


def call(kernel, out_shape, in_specs, out_specs, scratch=(), flops=0, moved=0, aliases=None, vmem=40):
    return pl.pallas_call(
        kernel,
        out_shape=out_shape,
        in_specs=in_specs,
        out_specs=out_specs,
        scratch_shapes=list(scratch),
        input_output_aliases=aliases or {},
        compiler_params=pltpu.CompilerParams(vmem_limit_bytes=vmem * 1024 * 1024),
        cost_estimate=pl.CostEstimate(flops=flops, bytes_accessed=moved, transcendentals=0),
    )


def gather_kernel(peers, ids, here, table, *refs):
    out, sems = refs[: len(peers)], refs[len(peers)]
    copies = [
        pltpu.make_async_copy(table.at[ids[here[0] ^ k]], out[n], sems.at[n])
        for n, k in enumerate(peers)
    ]
    for copy in copies:
        copy.start()
    for copy in copies:
        copy.wait()


def prep_kernel(ids, here, table, after, x, y, turned, own, blank, zeros, sem, own_sem):
    own_copy = pltpu.make_async_copy(table.at[ids[here[0]]], own, own_sem)
    own_copy.start()
    rows = own.shape[0]
    zeros[...] = jnp.zeros_like(zeros)
    step = zeros.shape[0]
    copies = [
        pltpu.make_async_copy(zeros, blank.at[pl.ds(s, step)], sem.at[s // step])
        for s in range(0, blank.shape[0], step)
    ]
    for copy in copies:
        copy.start()
    tokens = x.shape[0]

    @pl.loop(0, x.shape[1] // rows)
    def _(owner):
        columns = pl.ds(pl.multiple_of(owner * rows, rows), rows)
        turned[owner, :, pl.ds(0, tokens)] = x[:, columns].T
        turned[owner, :, pl.ds(tokens, tokens)] = y[:, columns].T

    for copy in [own_copy, *copies]:
        copy.wait()


def rank_kernel(peers, here, x, y, *refs):
    pairs, out = refs[: len(peers)], refs[len(peers)]
    rows, width = pairs[0].shape
    tokens = x.shape[0]
    x_rank = jnp.zeros((tokens, width), jnp.float32)
    y_rank = jnp.zeros((tokens, width), jnp.float32)
    for n, k in enumerate(peers):
        columns = pl.ds(pl.multiple_of((here[0] ^ k) * rows, rows), rows)
        x_rank += jnp.dot(x[:, columns], pairs[n][...], preferred_element_type=jnp.float32)
        y_rank += jnp.dot(y[:, columns], pairs[n][...], preferred_element_type=jnp.float32)
    out[...] = jnp.where(low_lanes(tokens, width), x_rank, y_rank)


def rounded(mine, other, length, scale):
    total = mine[...] + other[...]
    rows, width = total.shape
    total = jnp.where(low_lanes(rows, width), total, scale * total)
    live = lax.broadcasted_iota(jnp.int32, (rows, width), 0) < length
    return jnp.where(live, total, 0.0)


def swap_halves(value):
    return pltpu.roll(value, value.shape[-1] // 2, 1)


def piece_kernel(peers, scale, here, lengths, mine, other, turned, *refs):
    me = here[0]
    both = swap_halves(rounded(mine, other, lengths[me], scale))
    low = low_lanes(*both.shape)
    top = jnp.where(low, both, 0.0).astype(jnp.bfloat16)
    bottom = jnp.where(low, 0.0, both).astype(jnp.bfloat16)
    ranks = jnp.concatenate([top, bottom], axis=0)
    for n, k in enumerate(peers):
        piece = jnp.dot(turned[me ^ k], ranks, preferred_element_type=jnp.float32)
        refs[n][...] = jnp.where(low_lanes(*piece.shape), piece, scale * piece).astype(jnp.bfloat16)


def input_kernel(peers, scale, here, lengths, mine, other, *refs):
    pairs, out = refs[: len(peers)], refs[len(peers)]
    me = here[0]
    both = swap_halves(rounded(mine, other, lengths[me], scale))
    ranks = jnp.where(low_lanes(*both.shape), both, 0.0).astype(jnp.bfloat16)
    rows = pairs[0].shape[0]
    for n, k in enumerate(peers):
        columns = pl.ds(pl.multiple_of((me ^ k) * rows, rows), rows)
        out[:, columns] = lax.dot_general(
            ranks, pairs[n][...], (((1,), (1,)), ((), ())), preferred_element_type=jnp.float32
        ).astype(jnp.bfloat16)


def merge_kernel(peers, handled, others, ids, here, lengths, *refs):
    pieces = dict(zip(peers, refs[:-5]))
    out, total, held, sems = refs[-4:]
    me = here[0]
    width = total.shape[1]
    others_here = all(k in pieces for k in others)

    def value(k):
        return pieces[k][...].astype(jnp.float32)

    def either(conditions):
        return functools.reduce(jnp.logical_or, conditions, jnp.bool_(False))

    copies, chosen = [], []
    for n, k in enumerate(handled):
        adapter = ids[me ^ k]
        copies.append(pltpu.make_async_copy(held.at[n], out.at[adapter], sems.at[n]))
        same = {other: ids[me ^ other] == adapter for other in (*handled, *others) if other != k}
        skip = either([same[other] for other in handled[:n]])
        adding = list(handled[n + 1 :])
        if others_here:
            adding += others
        else:
            skip |= either([same[other] for other in others])
        more = either([same[other] for other in adding])
        chosen.append(jnp.logical_not(skip))

        def store(sum_of, count):
            denom = jnp.maximum(count.astype(jnp.float32), 1.0)
            part = 1.0 / jnp.full((1, width), denom)
            held[n] = (sum_of * part).astype(jnp.bfloat16)
            copies[n].start()

        @pl.when(chosen[n] & jnp.logical_not(more))
        def _():
            store(value(k), lengths[me ^ k])

        @pl.when(chosen[n] & more)
        def _():
            total[...] = value(k)
            count = lengths[me ^ k]
            for other in adding:
                count += jnp.where(same[other], lengths[me ^ other], 0)

                @pl.when(same[other])
                def _():
                    total[...] += value(other)

            store(total[...], count)

    for n in range(len(handled)):
        pl.when(chosen[n])(copies[n].wait)


def exchange(pieces, ties):
    owners = lax.axis_size("dp")
    out = {}
    for k in sorted(pieces, key=lambda k: k in ties):
        piece = lax.optimization_barrier((pieces[k], out[ties[k]]))[0] if k in ties else pieces[k]
        out[k] = lax.ppermute(piece, "dp", [(i, i ^ k) for i in range(owners)])
    return {k: out[k] for k in pieces}


def across_cores(value):
    cores = lax.axis_size("tensor")
    return lax.ppermute(value, "tensor", [(i, i ^ 1) for i in range(cores)])


def with_kernels(activations, cotangent, adapter_weight_pair, adapter_of_block, block_live_length):
    owners = lax.axis_size("dp")
    here = lax.axis_index("dp").astype(jnp.int32).reshape(1)
    ids, lengths = adapter_of_block[:, 0], block_live_length[:, 0]
    count, _, rows, width = adapter_weight_pair.shape
    table = adapter_weight_pair.reshape(count, rows, width)
    tokens, features = activations.shape
    scale = adapter_alpha / (width // 2)
    bf16, f32 = jnp.bfloat16, jnp.float32
    straight = jax.ShapeDtypeStruct((rows, width), bf16)
    pair_bytes = owners * rows * width * 2
    token_bytes = tokens * features * 2
    partners = len(FETCH)

    sent = call(
        functools.partial(gather_kernel, FETCH),
        [straight] * partners,
        [in_smem, in_smem, in_hbm],
        [in_vmem] * partners,
        [pltpu.SemaphoreType.DMA((partners,))],
        moved=2 * pair_bytes,
        vmem=53,
    )(ids, here, table)
    pairs = exchange(dict(zip(FETCH, sent)), FETCH_TIES)

    step = 8
    turned, own, blank = call(
        prep_kernel,
        [
            jax.ShapeDtypeStruct((owners, rows, 2 * tokens), bf16),
            straight,
            jax.ShapeDtypeStruct(table.shape, bf16),
        ],
        [in_smem, in_smem, in_hbm, in_hbm, in_vmem, in_vmem],
        [in_vmem, in_vmem, in_hbm],
        [
            pltpu.VMEM((step, rows, width), bf16),
            pltpu.SemaphoreType.DMA((count // step,)),
            pltpu.SemaphoreType.DMA,
        ],
        moved=4 * token_bytes + 2 * count * rows * width,
    )(ids, here, table, pairs[PREP_AFTER], activations, cotangent)
    pairs[0] = own

    mine = call(
        functools.partial(rank_kernel, tuple(pairs)),
        jax.ShapeDtypeStruct((tokens, width), f32),
        [in_smem] + [in_vmem] * (2 + owners),
        in_vmem,
        moved=1024,
    )(here, lax.optimization_barrier((activations, turned))[0], cotangent, *pairs.values())
    other = across_cores(mine)

    peers = (*SEND, 0)
    pieces = call(
        functools.partial(piece_kernel, peers, scale),
        [straight] * owners,
        [in_smem] * 2 + [in_vmem] * 3,
        [in_vmem] * owners,
        moved=1024,
    )(here, lengths, mine, other, turned)
    arrived = exchange(dict(zip(SEND, pieces)), SEND_TIES)
    arrived[0] = pieces[-1]

    grad_input = call(
        functools.partial(input_kernel, tuple(pairs), scale),
        jax.ShapeDtypeStruct((tokens, features), bf16),
        [in_smem] * 2 + [in_vmem] * (2 + owners),
        in_vmem,
        flops=2 * tokens * features * width,
        moved=token_bytes + pair_bytes,
    )(here, lengths, lax.optimization_barrier((mine, *pieces))[0], other, *pairs.values())

    late = tuple(k for k in peers if k in LATE)
    early = tuple(k for k in peers if k not in LATE)

    def merge(handled, others, merged, so_far):
        return call(
            functools.partial(merge_kernel, tuple(merged), handled, others),
            jax.ShapeDtypeStruct(table.shape, bf16),
            [in_smem] * 3 + [in_vmem] * len(merged) + [in_hbm],
            in_hbm,
            [
                pltpu.VMEM((rows, width), f32),
                pltpu.VMEM((len(handled), rows, width), bf16),
                pltpu.SemaphoreType.DMA((len(handled),)),
            ],
            moved=2 * pair_bytes,
            aliases={3 + len(merged): 0},
        )(ids, here, lengths, *merged.values(), so_far)

    early_pieces = {k: arrived[k] for k in early}
    gradient = merge(late, early, arrived, merge(early, late, early_pieces, blank))
    return grad_input, gradient[:, None]


def without_kernels(activations, cotangent, adapter_weight_pair, adapter_of_block, block_live_length):
    owners = lax.axis_size("dp")
    here = lax.axis_index("dp")
    count, _, rows, width = adapter_weight_pair.shape
    rank = width // 2
    scale = adapter_alpha / rank
    adapters = adapter_of_block[:, 0]
    lengths = block_live_length[:, 0]
    keep = (jnp.arange(activations.shape[0], dtype=jnp.int32) < lengths[here])[:, None]
    inputs = jnp.where(keep, activations, jnp.zeros_like(activations))
    grads_out = jnp.where(keep, cotangent, jnp.zeros_like(cotangent))
    fetched = lax.all_to_all(
        adapter_weight_pair[:, 0][adapters], "dp", split_axis=0, concat_axis=0, tiled=True
    )
    pair = fetched.reshape(-1, width)
    down, upward = pair[:, :rank], pair[:, rank:]
    f32 = jnp.float32
    hidden_part = jnp.dot(inputs, down, preferred_element_type=f32)
    dhidden_part = scale * jnp.dot(grads_out, upward, preferred_element_type=f32)
    hidden, dhidden = lax.psum((hidden_part, dhidden_part), "tensor")
    hidden16, dhidden16 = hidden.astype(jnp.bfloat16), dhidden.astype(jnp.bfloat16)
    d_down = jnp.dot(inputs.T, dhidden16, preferred_element_type=f32)
    d_up = scale * jnp.dot(grads_out.T, hidden16, preferred_element_type=f32)
    sent = jnp.concatenate([d_down, d_up], axis=1).astype(jnp.bfloat16).reshape(owners, rows, width)
    received = lax.all_to_all(sent, "dp", split_axis=0, concat_axis=0, tiled=True).astype(f32)
    same = adapters[:, None] == adapters[None, :]
    total = jnp.sum(jnp.where(same, lengths[None, :], 0), axis=1).astype(f32)
    summed = jax.ops.segment_sum(received, adapters, num_segments=count)
    denom = jnp.ones((count,), f32).at[adapters].set(jnp.maximum(total, 1.0))
    gradient = (summed / denom[:, None, None]).astype(jnp.bfloat16)
    grad_input = jnp.dot(dhidden16, down.T, preferred_element_type=f32).astype(jnp.bfloat16)
    return grad_input, gradient[:, None]


def solution(mesh):
    owners, cores = mesh.shape["dp"], mesh.shape["tensor"]

    def on_device(activations, cotangent, adapter_weight_pair, *rest):
        rows = adapter_weight_pair.shape[2]
        fits = owners == len(FETCH) + 1 and cores == 2 and rows % 256 == 0
        body = with_kernels if fits else without_kernels
        return body(activations, cotangent, adapter_weight_pair, *rest)

    in_specs = (
        P(("group", "dp"), "tensor"),
        P(("group", "dp"), "tensor"),
        P(None, "tensor", "dp", None),
        P("group", None),
        P("group", None),
    )
    out_specs = (P(("group", "dp"), "tensor"), P("group", "tensor", "dp", None))
    return jax.shard_map(
        on_device, mesh=mesh, in_specs=in_specs, out_specs=out_specs, check_vma=False
    )
```

```python
import functools

import jax
import jax.numpy as jnp
from jax import lax
from jax.experimental import pallas as pl
from jax.experimental.pallas import tpu as pltpu
from jax.sharding import PartitionSpec as P

adapter_alpha = 128.0
FETCH = (1, 6, 2, 7, 4, 3, 5)
FETCH_TIES = {}
SEND = (1, 6, 2, 7, 4, 3, 5)
SEND_TIES = {}
PREP_AFTER = 1
LATE = (4, 3, 5)

in_vmem = pl.BlockSpec(memory_space=pltpu.VMEM)
in_smem = pl.BlockSpec(memory_space=pltpu.SMEM)
in_hbm = pl.BlockSpec(memory_space=pltpu.HBM)


def low_lanes(rows, width):
    return lax.broadcasted_iota(jnp.int32, (rows, width), 1) < width // 2


def call(kernel, out_shape, in_specs, out_specs, scratch=(), flops=0, moved=0, aliases=None, vmem=40):
    return pl.pallas_call(
        kernel,
        out_shape=out_shape,
        in_specs=in_specs,
        out_specs=out_specs,
        scratch_shapes=list(scratch),
        input_output_aliases=aliases or {},
        compiler_params=pltpu.CompilerParams(vmem_limit_bytes=vmem * 1024 * 1024),
        cost_estimate=pl.CostEstimate(flops=flops, bytes_accessed=moved, transcendentals=0),
    )


def gather_kernel(peers, ids, here, table, *refs):
    out, sems = refs[: len(peers)], refs[len(peers)]
    copies = [
        pltpu.make_async_copy(table.at[ids[here[0] ^ k]], out[n], sems.at[n])
        for n, k in enumerate(peers)
    ]
    for copy in copies:
        copy.start()
    for copy in copies:
        copy.wait()


def prep_kernel(ids, here, table, after, x, y, turned, own, blank, zeros, sem, own_sem):
    own_copy = pltpu.make_async_copy(table.at[ids[here[0]]], own, own_sem)
    own_copy.start()
    rows = own.shape[0]
    zeros[...] = jnp.zeros_like(zeros)
    step = zeros.shape[0]
    copies = [
        pltpu.make_async_copy(zeros, blank.at[pl.ds(s, step)], sem.at[s // step])
        for s in range(0, blank.shape[0], step)
    ]
    for copy in copies:
        copy.start()
    tokens = x.shape[0]

    @pl.loop(0, x.shape[1] // rows)
    def _(owner):
        columns = pl.ds(pl.multiple_of(owner * rows, rows), rows)
        turned[owner, :, pl.ds(0, tokens)] = x[:, columns].T
        turned[owner, :, pl.ds(tokens, tokens)] = y[:, columns].T

    for copy in [own_copy, *copies]:
        copy.wait()


def rank_kernel(peers, here, x, y, *refs):
    pairs, out = refs[: len(peers)], refs[len(peers)]
    rows, width = pairs[0].shape
    tokens = x.shape[0]
    x_rank = jnp.zeros((tokens, width), jnp.float32)
    y_rank = jnp.zeros((tokens, width), jnp.float32)
    for n, k in enumerate(peers):
        columns = pl.ds(pl.multiple_of((here[0] ^ k) * rows, rows), rows)
        x_rank += jnp.dot(x[:, columns], pairs[n][...], preferred_element_type=jnp.float32)
        y_rank += jnp.dot(y[:, columns], pairs[n][...], preferred_element_type=jnp.float32)
    out[...] = jnp.where(low_lanes(tokens, width), x_rank, y_rank)


def rounded(mine, other, length, scale):
    total = mine[...] + other[...]
    rows, width = total.shape
    total = jnp.where(low_lanes(rows, width), total, scale * total)
    live = lax.broadcasted_iota(jnp.int32, (rows, width), 0) < length
    return jnp.where(live, total, 0.0)


def swap_halves(value):
    return pltpu.roll(value, value.shape[-1] // 2, 1)


def piece_kernel(peers, scale, here, lengths, mine, other, turned, *refs):
    me = here[0]
    both = swap_halves(rounded(mine, other, lengths[me], scale))
    low = low_lanes(*both.shape)
    top = jnp.where(low, both, 0.0).astype(jnp.bfloat16)
    bottom = jnp.where(low, 0.0, both).astype(jnp.bfloat16)
    ranks = jnp.concatenate([top, bottom], axis=0)
    for n, k in enumerate(peers):
        piece = jnp.dot(turned[me ^ k], ranks, preferred_element_type=jnp.float32)
        refs[n][...] = jnp.where(low_lanes(*piece.shape), piece, scale * piece).astype(jnp.bfloat16)


def input_kernel(peers, scale, here, lengths, mine, other, *refs):
    pairs, out = refs[: len(peers)], refs[len(peers)]
    me = here[0]
    both = swap_halves(rounded(mine, other, lengths[me], scale))
    ranks = jnp.where(low_lanes(*both.shape), both, 0.0).astype(jnp.bfloat16)
    rows = pairs[0].shape[0]
    for n, k in enumerate(peers):
        columns = pl.ds(pl.multiple_of((me ^ k) * rows, rows), rows)
        out[:, columns] = lax.dot_general(
            ranks, pairs[n][...], (((1,), (1,)), ((), ())), preferred_element_type=jnp.float32
        ).astype(jnp.bfloat16)


def merge_kernel(peers, handled, others, ids, here, lengths, *refs):
    pieces = dict(zip(peers, refs[:-5]))
    out, total, held, sems = refs[-4:]
    me = here[0]
    width = total.shape[1]
    others_here = all(k in pieces for k in others)

    def value(k):
        return pieces[k][...].astype(jnp.float32)

    def either(conditions):
        return functools.reduce(jnp.logical_or, conditions, jnp.bool_(False))

    copies, chosen = [], []
    for n, k in enumerate(handled):
        adapter = ids[me ^ k]
        copies.append(pltpu.make_async_copy(held.at[n], out.at[adapter], sems.at[n]))
        same = {other: ids[me ^ other] == adapter for other in (*handled, *others) if other != k}
        skip = either([same[other] for other in handled[:n]])
        adding = list(handled[n + 1 :])
        if others_here:
            adding += others
        else:
            skip |= either([same[other] for other in others])
        more = either([same[other] for other in adding])
        chosen.append(jnp.logical_not(skip))

        def store(sum_of, count):
            denom = jnp.maximum(count.astype(jnp.float32), 1.0)
            part = 1.0 / jnp.full((1, width), denom)
            held[n] = (sum_of * part).astype(jnp.bfloat16)
            copies[n].start()

        @pl.when(chosen[n] & jnp.logical_not(more))
        def _():
            store(value(k), lengths[me ^ k])

        @pl.when(chosen[n] & more)
        def _():
            total[...] = value(k)
            count = lengths[me ^ k]
            for other in adding:
                count += jnp.where(same[other], lengths[me ^ other], 0)

                @pl.when(same[other])
                def _():
                    total[...] += value(other)

            store(total[...], count)

    for n in range(len(handled)):
        pl.when(chosen[n])(copies[n].wait)


def exchange(pieces, ties):
    owners = lax.axis_size("dp")
    out = {}
    for k in sorted(pieces, key=lambda k: k in ties):
        piece = lax.optimization_barrier((pieces[k], out[ties[k]]))[0] if k in ties else pieces[k]
        out[k] = lax.ppermute(piece, "dp", [(i, i ^ k) for i in range(owners)])
    return {k: out[k] for k in pieces}


def across_cores(value):
    cores = lax.axis_size("tensor")
    return lax.ppermute(value, "tensor", [(i, i ^ 1) for i in range(cores)])


def with_kernels(activations, cotangent, adapter_weight_pair, adapter_of_block, block_live_length):
    owners = lax.axis_size("dp")
    here = lax.axis_index("dp").astype(jnp.int32).reshape(1)
    ids, lengths = adapter_of_block[:, 0], block_live_length[:, 0]
    count, _, rows, width = adapter_weight_pair.shape
    table = adapter_weight_pair.reshape(count, rows, width)
    tokens, features = activations.shape
    scale = adapter_alpha / (width // 2)
    bf16, f32 = jnp.bfloat16, jnp.float32
    straight = jax.ShapeDtypeStruct((rows, width), bf16)
    pair_bytes = owners * rows * width * 2
    token_bytes = tokens * features * 2
    partners = len(FETCH)

    sent = call(
        functools.partial(gather_kernel, FETCH),
        [straight] * partners,
        [in_smem, in_smem, in_hbm],
        [in_vmem] * partners,
        [pltpu.SemaphoreType.DMA((partners,))],
        moved=2 * pair_bytes,
        vmem=53,
    )(ids, here, table)
    pairs = exchange(dict(zip(FETCH, sent)), FETCH_TIES)

    step = 8
    turned, own, blank = call(
        prep_kernel,
        [
            jax.ShapeDtypeStruct((owners, rows, 2 * tokens), bf16),
            straight,
            jax.ShapeDtypeStruct(table.shape, bf16),
        ],
        [in_smem, in_smem, in_hbm, in_hbm, in_vmem, in_vmem],
        [in_vmem, in_vmem, in_hbm],
        [
            pltpu.VMEM((step, rows, width), bf16),
            pltpu.SemaphoreType.DMA((count // step,)),
            pltpu.SemaphoreType.DMA,
        ],
        moved=4 * token_bytes + 2 * count * rows * width,
    )(ids, here, table, pairs[PREP_AFTER], activations, cotangent)
    pairs[0] = own

    mine = call(
        functools.partial(rank_kernel, tuple(pairs)),
        jax.ShapeDtypeStruct((tokens, width), f32),
        [in_smem] + [in_vmem] * (2 + owners),
        in_vmem,
        moved=1024,
    )(here, lax.optimization_barrier((activations, turned))[0], cotangent, *pairs.values())
    other = across_cores(mine)

    peers = (*SEND, 0)
    pieces = call(
        functools.partial(piece_kernel, peers, scale),
        [straight] * owners,
        [in_smem] * 2 + [in_vmem] * 3,
        [in_vmem] * owners,
        moved=1024,
    )(here, lengths, mine, other, turned)
    arrived = exchange(dict(zip(SEND, pieces)), SEND_TIES)
    arrived[0] = pieces[-1]

    grad_input = call(
        functools.partial(input_kernel, tuple(pairs), scale),
        jax.ShapeDtypeStruct((tokens, features), bf16),
        [in_smem] * 2 + [in_vmem] * (2 + owners),
        in_vmem,
        flops=2 * tokens * features * width,
        moved=token_bytes + pair_bytes,
    )(here, lengths, lax.optimization_barrier((mine, *pieces))[0], other, *pairs.values())

    late = tuple(k for k in peers if k in LATE)
    early = tuple(k for k in peers if k not in LATE)

    def merge(handled, others, merged, so_far):
        return call(
            functools.partial(merge_kernel, tuple(merged), handled, others),
            jax.ShapeDtypeStruct(table.shape, bf16),
            [in_smem] * 3 + [in_vmem] * len(merged) + [in_hbm],
            in_hbm,
            [
                pltpu.VMEM((rows, width), f32),
                pltpu.VMEM((len(handled), rows, width), bf16),
                pltpu.SemaphoreType.DMA((len(handled),)),
            ],
            moved=2 * pair_bytes,
            aliases={3 + len(merged): 0},
        )(ids, here, lengths, *merged.values(), so_far)

    early_pieces = {k: arrived[k] for k in early}
    gradient = merge(late, early, arrived, merge(early, late, early_pieces, blank))
    return grad_input, gradient[:, None]


def without_kernels(activations, cotangent, adapter_weight_pair, adapter_of_block, block_live_length):
    owners = lax.axis_size("dp")
    here = lax.axis_index("dp")
    count, _, rows, width = adapter_weight_pair.shape
    rank = width // 2
    scale = adapter_alpha / rank
    adapters = adapter_of_block[:, 0]
    lengths = block_live_length[:, 0]
    keep = (jnp.arange(activations.shape[0], dtype=jnp.int32) < lengths[here])[:, None]
    inputs = jnp.where(keep, activations, jnp.zeros_like(activations))
    grads_out = jnp.where(keep, cotangent, jnp.zeros_like(cotangent))
    fetched = lax.all_to_all(
        adapter_weight_pair[:, 0][adapters], "dp", split_axis=0, concat_axis=0, tiled=True
    )
    pair = fetched.reshape(-1, width)
    down, upward = pair[:, :rank], pair[:, rank:]
    f32 = jnp.float32
    hidden_part = jnp.dot(inputs, down, preferred_element_type=f32)
    dhidden_part = scale * jnp.dot(grads_out, upward, preferred_element_type=f32)
    hidden, dhidden = lax.psum((hidden_part, dhidden_part), "tensor")
    hidden16, dhidden16 = hidden.astype(jnp.bfloat16), dhidden.astype(jnp.bfloat16)
    d_down = jnp.dot(inputs.T, dhidden16, preferred_element_type=f32)
    d_up = scale * jnp.dot(grads_out.T, hidden16, preferred_element_type=f32)
    sent = jnp.concatenate([d_down, d_up], axis=1).astype(jnp.bfloat16).reshape(owners, rows, width)
    received = lax.all_to_all(sent, "dp", split_axis=0, concat_axis=0, tiled=True).astype(f32)
    same = adapters[:, None] == adapters[None, :]
    total = jnp.sum(jnp.where(same, lengths[None, :], 0), axis=1).astype(f32)
    summed = jax.ops.segment_sum(received, adapters, num_segments=count)
    denom = jnp.ones((count,), f32).at[adapters].set(jnp.maximum(total, 1.0))
    gradient = (summed / denom[:, None, None]).astype(jnp.bfloat16)
    grad_input = jnp.dot(dhidden16, down.T, preferred_element_type=f32).astype(jnp.bfloat16)
    return grad_input, gradient[:, None]


def solution(mesh):
    owners, cores = mesh.shape["dp"], mesh.shape["tensor"]

    def on_device(activations, cotangent, adapter_weight_pair, *rest):
        rows = adapter_weight_pair.shape[2]
        fits = owners == len(FETCH) + 1 and cores == 2 and rows % 256 == 0
        body = with_kernels if fits else without_kernels
        return body(activations, cotangent, adapter_weight_pair, *rest)

    in_specs = (
        P(("group", "dp"), "tensor"),
        P(("group", "dp"), "tensor"),
        P(None, "tensor", "dp", None),
        P("group", None),
        P("group", None),
    )
    out_specs = (P(("group", "dp"), "tensor"), P("group", "tensor", "dp", None))
    return jax.shard_map(
        on_device, mesh=mesh, in_specs=in_specs, out_specs=out_specs, check_vma=False
    )
```

```python
import functools

import jax
import jax.numpy as jnp
from jax import lax
from jax.experimental import pallas as pl
from jax.experimental.pallas import tpu as pltpu
from jax.sharding import PartitionSpec as P

adapter_alpha = 128.0
FETCH = (1, 4, 2, 5, 6, 3, 7)
FETCH_TIES = {}
SEND = (1, 4, 2, 5, 6, 3, 7)
SEND_TIES = {}
PREP_AFTER = 1
LATE = (6, 3, 7)
RANK_LAST = (3, 7)
SEND_FIRST = 2

in_vmem = pl.BlockSpec(memory_space=pltpu.VMEM)
in_smem = pl.BlockSpec(memory_space=pltpu.SMEM)
in_hbm = pl.BlockSpec(memory_space=pltpu.HBM)


def low_lanes(rows, width):
    return lax.broadcasted_iota(jnp.int32, (rows, width), 1) < width // 2


def call(kernel, out_shape, in_specs, out_specs, scratch=(), flops=0, moved=0, aliases=None, vmem=40):
    return pl.pallas_call(
        kernel,
        out_shape=out_shape,
        in_specs=in_specs,
        out_specs=out_specs,
        scratch_shapes=list(scratch),
        input_output_aliases=aliases or {},
        compiler_params=pltpu.CompilerParams(vmem_limit_bytes=vmem * 1024 * 1024),
        cost_estimate=pl.CostEstimate(flops=flops, bytes_accessed=moved, transcendentals=0),
    )


def gather_kernel(peers, ids, here, table, *refs):
    out, sems = refs[: len(peers)], refs[len(peers)]
    copies = [
        pltpu.make_async_copy(table.at[ids[here[0] ^ k]], out[n], sems.at[n])
        for n, k in enumerate(peers)
    ]
    for copy in copies:
        copy.start()
    for copy in copies:
        copy.wait()


def prep_kernel(ids, here, table, after, x, y, turned, own, blank, zeros, sem, own_sem):
    own_copy = pltpu.make_async_copy(table.at[ids[here[0]]], own, own_sem)
    own_copy.start()
    rows = own.shape[0]
    zeros[...] = jnp.zeros_like(zeros)
    step = zeros.shape[0]
    copies = [
        pltpu.make_async_copy(zeros, blank.at[pl.ds(s, step)], sem.at[s // step])
        for s in range(0, blank.shape[0], step)
    ]
    for copy in copies:
        copy.start()
    tokens = x.shape[0]

    @pl.loop(0, x.shape[1] // rows)
    def _(owner):
        columns = pl.ds(pl.multiple_of(owner * rows, rows), rows)
        turned[owner, :, pl.ds(0, tokens)] = x[:, columns].T
        turned[owner, :, pl.ds(tokens, tokens)] = y[:, columns].T

    for copy in [own_copy, *copies]:
        copy.wait()


def rank_kernel(peers, here, x, y, so_far, *refs):
    pairs, out = refs[: len(peers)], refs[len(peers)]
    rows, width = pairs[0].shape
    tokens = x.shape[0]
    x_rank = so_far[...]
    y_rank = x_rank
    for n, k in enumerate(peers):
        columns = pl.ds(pl.multiple_of((here[0] ^ k) * rows, rows), rows)
        x_rank += jnp.dot(x[:, columns], pairs[n][...], preferred_element_type=jnp.float32)
        y_rank += jnp.dot(y[:, columns], pairs[n][...], preferred_element_type=jnp.float32)
    out[...] = jnp.where(low_lanes(tokens, width), x_rank, y_rank)


def rounded(mine, other, length, scale):
    total = mine[...] + other[...]
    rows, width = total.shape
    total = jnp.where(low_lanes(rows, width), total, scale * total)
    live = lax.broadcasted_iota(jnp.int32, (rows, width), 0) < length
    return jnp.where(live, total, 0.0)


def swap_halves(value):
    return pltpu.roll(value, value.shape[-1] // 2, 1)


def piece_kernel(peers, scale, here, lengths, mine, other, turned, *refs):
    me = here[0]
    both = swap_halves(rounded(mine, other, lengths[me], scale))
    low = low_lanes(*both.shape)
    top = jnp.where(low, both, 0.0).astype(jnp.bfloat16)
    bottom = jnp.where(low, 0.0, both).astype(jnp.bfloat16)
    ranks = jnp.concatenate([top, bottom], axis=0)
    for n, k in enumerate(peers):
        piece = jnp.dot(turned[me ^ k], ranks, preferred_element_type=jnp.float32)
        refs[n][...] = jnp.where(low_lanes(*piece.shape), piece, scale * piece).astype(jnp.bfloat16)


def input_kernel(peers, scale, here, lengths, mine, other, *refs):
    pairs, out = refs[: len(peers)], refs[len(peers)]
    me = here[0]
    both = swap_halves(rounded(mine, other, lengths[me], scale))
    ranks = jnp.where(low_lanes(*both.shape), both, 0.0).astype(jnp.bfloat16)
    rows = pairs[0].shape[0]
    for n, k in enumerate(peers):
        columns = pl.ds(pl.multiple_of((me ^ k) * rows, rows), rows)
        out[:, columns] = lax.dot_general(
            ranks, pairs[n][...], (((1,), (1,)), ((), ())), preferred_element_type=jnp.float32
        ).astype(jnp.bfloat16)


def merge_kernel(peers, handled, others, ids, here, lengths, *refs):
    pieces = dict(zip(peers, refs[:-5]))
    out, total, held, sems = refs[-4:]
    me = here[0]
    width = total.shape[1]
    others_here = all(k in pieces for k in others)

    def value(k):
        return pieces[k][...].astype(jnp.float32)

    def either(conditions):
        return functools.reduce(jnp.logical_or, conditions, jnp.bool_(False))

    copies, chosen = [], []
    for n, k in enumerate(handled):
        adapter = ids[me ^ k]
        copies.append(pltpu.make_async_copy(held.at[n], out.at[adapter], sems.at[n]))
        same = {other: ids[me ^ other] == adapter for other in (*handled, *others) if other != k}
        skip = either([same[other] for other in handled[:n]])
        adding = list(handled[n + 1 :])
        if others_here:
            adding += others
        else:
            skip |= either([same[other] for other in others])
        more = either([same[other] for other in adding])
        chosen.append(jnp.logical_not(skip))

        def store(sum_of, count):
            denom = jnp.maximum(count.astype(jnp.float32), 1.0)
            part = 1.0 / jnp.full((1, width), denom)
            held[n] = (sum_of * part).astype(jnp.bfloat16)
            copies[n].start()

        @pl.when(chosen[n] & jnp.logical_not(more))
        def _():
            store(value(k), lengths[me ^ k])

        @pl.when(chosen[n] & more)
        def _():
            total[...] = value(k)
            count = lengths[me ^ k]
            for other in adding:
                count += jnp.where(same[other], lengths[me ^ other], 0)

                @pl.when(same[other])
                def _():
                    total[...] += value(other)

            store(total[...], count)

    for n in range(len(handled)):
        pl.when(chosen[n])(copies[n].wait)


def exchange(pieces, ties):
    owners = lax.axis_size("dp")
    out = {}
    for k in sorted(pieces, key=lambda k: k in ties):
        piece = lax.optimization_barrier((pieces[k], out[ties[k]]))[0] if k in ties else pieces[k]
        out[k] = lax.ppermute(piece, "dp", [(i, i ^ k) for i in range(owners)])
    return {k: out[k] for k in pieces}


def across_cores(value):
    cores = lax.axis_size("tensor")
    return lax.ppermute(value, "tensor", [(i, i ^ 1) for i in range(cores)])


def with_kernels(activations, cotangent, adapter_weight_pair, adapter_of_block, block_live_length):
    owners = lax.axis_size("dp")
    here = lax.axis_index("dp").astype(jnp.int32).reshape(1)
    ids, lengths = adapter_of_block[:, 0], block_live_length[:, 0]
    count, _, rows, width = adapter_weight_pair.shape
    table = adapter_weight_pair.reshape(count, rows, width)
    tokens, features = activations.shape
    scale = adapter_alpha / (width // 2)
    bf16, f32 = jnp.bfloat16, jnp.float32
    straight = jax.ShapeDtypeStruct((rows, width), bf16)
    pair_bytes = owners * rows * width * 2
    token_bytes = tokens * features * 2
    partners = len(FETCH)

    sent = call(
        functools.partial(gather_kernel, FETCH),
        [straight] * partners,
        [in_smem, in_smem, in_hbm],
        [in_vmem] * partners,
        [pltpu.SemaphoreType.DMA((partners,))],
        moved=2 * pair_bytes,
        vmem=53,
    )(ids, here, table)
    pairs = exchange(dict(zip(FETCH, sent)), FETCH_TIES)

    step = 8
    turned, own, blank = call(
        prep_kernel,
        [
            jax.ShapeDtypeStruct((owners, rows, 2 * tokens), bf16),
            straight,
            jax.ShapeDtypeStruct(table.shape, bf16),
        ],
        [in_smem, in_smem, in_hbm, in_hbm, in_vmem, in_vmem],
        [in_vmem, in_vmem, in_hbm],
        [
            pltpu.VMEM((step, rows, width), bf16),
            pltpu.SemaphoreType.DMA((count // step,)),
            pltpu.SemaphoreType.DMA,
        ],
        moved=4 * token_bytes + 2 * count * rows * width,
    )(ids, here, table, pairs[PREP_AFTER], activations, cotangent)
    pairs[0] = own

    mine = jnp.zeros((tokens, width), f32)
    for part in ([k for k in pairs if k not in RANK_LAST], RANK_LAST):
        mine = call(
            functools.partial(rank_kernel, tuple(part)),
            jax.ShapeDtypeStruct((tokens, width), f32),
            [in_smem] + [in_vmem] * (3 + len(part)),
            in_vmem,
            moved=1024,
        )(here, lax.optimization_barrier((activations, turned))[0], cotangent, mine, *[pairs[k] for k in part])
    other = across_cores(mine)

    peers = (*SEND, 0)
    pieces = []
    for part in (peers[:SEND_FIRST], peers[SEND_FIRST:]):
        pieces += call(
            functools.partial(piece_kernel, part, scale),
            [straight] * len(part),
            [in_smem] * 2 + [in_vmem] * 3,
            [in_vmem] * len(part),
            moved=1024,
        )(here, lengths, mine, other, turned)
    arrived = exchange(dict(zip(SEND, pieces)), SEND_TIES)
    arrived[0] = pieces[-1]

    grad_input = call(
        functools.partial(input_kernel, tuple(pairs), scale),
        jax.ShapeDtypeStruct((tokens, features), bf16),
        [in_smem] * 2 + [in_vmem] * (2 + owners),
        in_vmem,
        flops=2 * tokens * features * width,
        moved=token_bytes + pair_bytes,
    )(here, lengths, lax.optimization_barrier((mine, *pieces))[0], other, *pairs.values())

    late = tuple(k for k in peers if k in LATE)
    early = tuple(k for k in peers if k not in LATE)

    def merge(handled, others, merged, so_far):
        return call(
            functools.partial(merge_kernel, tuple(merged), handled, others),
            jax.ShapeDtypeStruct(table.shape, bf16),
            [in_smem] * 3 + [in_vmem] * len(merged) + [in_hbm],
            in_hbm,
            [
                pltpu.VMEM((rows, width), f32),
                pltpu.VMEM((len(handled), rows, width), bf16),
                pltpu.SemaphoreType.DMA((len(handled),)),
            ],
            moved=2 * pair_bytes,
            aliases={3 + len(merged): 0},
        )(ids, here, lengths, *merged.values(), so_far)

    early_pieces = {k: arrived[k] for k in early}
    gradient = merge(late, early, arrived, merge(early, late, early_pieces, blank))
    return grad_input, gradient[:, None]


def without_kernels(activations, cotangent, adapter_weight_pair, adapter_of_block, block_live_length):
    owners = lax.axis_size("dp")
    here = lax.axis_index("dp")
    count, _, rows, width = adapter_weight_pair.shape
    rank = width // 2
    scale = adapter_alpha / rank
    adapters = adapter_of_block[:, 0]
    lengths = block_live_length[:, 0]
    keep = (jnp.arange(activations.shape[0], dtype=jnp.int32) < lengths[here])[:, None]
    inputs = jnp.where(keep, activations, jnp.zeros_like(activations))
    grads_out = jnp.where(keep, cotangent, jnp.zeros_like(cotangent))
    fetched = lax.all_to_all(
        adapter_weight_pair[:, 0][adapters], "dp", split_axis=0, concat_axis=0, tiled=True
    )
    pair = fetched.reshape(-1, width)
    down, upward = pair[:, :rank], pair[:, rank:]
    f32 = jnp.float32
    hidden_part = jnp.dot(inputs, down, preferred_element_type=f32)
    dhidden_part = scale * jnp.dot(grads_out, upward, preferred_element_type=f32)
    hidden, dhidden = lax.psum((hidden_part, dhidden_part), "tensor")
    hidden16, dhidden16 = hidden.astype(jnp.bfloat16), dhidden.astype(jnp.bfloat16)
    d_down = jnp.dot(inputs.T, dhidden16, preferred_element_type=f32)
    d_up = scale * jnp.dot(grads_out.T, hidden16, preferred_element_type=f32)
    sent = jnp.concatenate([d_down, d_up], axis=1).astype(jnp.bfloat16).reshape(owners, rows, width)
    received = lax.all_to_all(sent, "dp", split_axis=0, concat_axis=0, tiled=True).astype(f32)
    same = adapters[:, None] == adapters[None, :]
    total = jnp.sum(jnp.where(same, lengths[None, :], 0), axis=1).astype(f32)
    summed = jax.ops.segment_sum(received, adapters, num_segments=count)
    denom = jnp.ones((count,), f32).at[adapters].set(jnp.maximum(total, 1.0))
    gradient = (summed / denom[:, None, None]).astype(jnp.bfloat16)
    grad_input = jnp.dot(dhidden16, down.T, preferred_element_type=f32).astype(jnp.bfloat16)
    return grad_input, gradient[:, None]


def solution(mesh):
    owners, cores = mesh.shape["dp"], mesh.shape["tensor"]

    def on_device(activations, cotangent, adapter_weight_pair, *rest):
        rows = adapter_weight_pair.shape[2]
        fits = owners == len(FETCH) + 1 and cores == 2 and rows % 256 == 0
        body = with_kernels if fits else without_kernels
        return body(activations, cotangent, adapter_weight_pair, *rest)

    in_specs = (
        P(("group", "dp"), "tensor"),
        P(("group", "dp"), "tensor"),
        P(None, "tensor", "dp", None),
        P("group", None),
        P("group", None),
    )
    out_specs = (P(("group", "dp"), "tensor"), P("group", "tensor", "dp", None))
    return jax.shard_map(
        on_device, mesh=mesh, in_specs=in_specs, out_specs=out_specs, check_vma=False
    )
```

```python
import functools

import jax
import jax.numpy as jnp
from jax import lax
from jax.experimental import pallas as pl
from jax.experimental.pallas import tpu as pltpu
from jax.sharding import PartitionSpec as P

adapter_alpha = 128.0
FETCH = (1, 2, 4, 5, 6, 7, 3)
FETCH_TIES = {7: 1, 3: 2}
SEND = (1, 2, 4, 5, 6, 7, 3)
SEND_TIES = {7: 1, 3: 2}
PREP_AFTER = 1
LATE = (6, 7, 3)
RANK_LAST = (3, 7)
SEND_FIRST = 2

in_vmem = pl.BlockSpec(memory_space=pltpu.VMEM)
in_smem = pl.BlockSpec(memory_space=pltpu.SMEM)
in_hbm = pl.BlockSpec(memory_space=pltpu.HBM)


def low_lanes(rows, width):
    return lax.broadcasted_iota(jnp.int32, (rows, width), 1) < width // 2


def call(kernel, out_shape, in_specs, out_specs, scratch=(), flops=0, moved=0, aliases=None, vmem=40):
    return pl.pallas_call(
        kernel,
        out_shape=out_shape,
        in_specs=in_specs,
        out_specs=out_specs,
        scratch_shapes=list(scratch),
        input_output_aliases=aliases or {},
        compiler_params=pltpu.CompilerParams(vmem_limit_bytes=vmem * 1024 * 1024),
        cost_estimate=pl.CostEstimate(flops=flops, bytes_accessed=moved, transcendentals=0),
    )


def gather_kernel(peers, ids, here, table, *refs):
    out, sems = refs[: len(peers)], refs[len(peers)]
    copies = [
        pltpu.make_async_copy(table.at[ids[here[0] ^ k]], out[n], sems.at[n])
        for n, k in enumerate(peers)
    ]
    for copy in copies:
        copy.start()
    for copy in copies:
        copy.wait()


def prep_kernel(ids, here, table, after, x, y, turned, own, blank, zeros, sem, own_sem):
    own_copy = pltpu.make_async_copy(table.at[ids[here[0]]], own, own_sem)
    own_copy.start()
    rows = own.shape[0]
    zeros[...] = jnp.zeros_like(zeros)
    step = zeros.shape[0]
    copies = [
        pltpu.make_async_copy(zeros, blank.at[pl.ds(s, step)], sem.at[s // step])
        for s in range(0, blank.shape[0], step)
    ]
    for copy in copies:
        copy.start()
    tokens = x.shape[0]

    @pl.loop(0, x.shape[1] // rows)
    def _(owner):
        columns = pl.ds(pl.multiple_of(owner * rows, rows), rows)
        turned[owner, :, pl.ds(0, tokens)] = x[:, columns].T
        turned[owner, :, pl.ds(tokens, tokens)] = y[:, columns].T

    for copy in [own_copy, *copies]:
        copy.wait()


def rank_kernel(peers, here, x, y, so_far, *refs):
    pairs, out = refs[: len(peers)], refs[len(peers)]
    rows, width = pairs[0].shape
    tokens = x.shape[0]
    x_rank = so_far[...]
    y_rank = x_rank
    for n, k in enumerate(peers):
        columns = pl.ds(pl.multiple_of((here[0] ^ k) * rows, rows), rows)
        x_rank += jnp.dot(x[:, columns], pairs[n][...], preferred_element_type=jnp.float32)
        y_rank += jnp.dot(y[:, columns], pairs[n][...], preferred_element_type=jnp.float32)
    out[...] = jnp.where(low_lanes(tokens, width), x_rank, y_rank)


def rounded(mine, other, length, scale):
    total = mine[...] + other[...]
    rows, width = total.shape
    total = jnp.where(low_lanes(rows, width), total, scale * total)
    live = lax.broadcasted_iota(jnp.int32, (rows, width), 0) < length
    return jnp.where(live, total, 0.0)


def swap_halves(value):
    return pltpu.roll(value, value.shape[-1] // 2, 1)


def piece_kernel(peers, scale, here, lengths, mine, other, turned, *refs):
    me = here[0]
    both = swap_halves(rounded(mine, other, lengths[me], scale))
    low = low_lanes(*both.shape)
    top = jnp.where(low, both, 0.0).astype(jnp.bfloat16)
    bottom = jnp.where(low, 0.0, both).astype(jnp.bfloat16)
    ranks = jnp.concatenate([top, bottom], axis=0)
    for n, k in enumerate(peers):
        piece = jnp.dot(turned[me ^ k], ranks, preferred_element_type=jnp.float32)
        refs[n][...] = jnp.where(low_lanes(*piece.shape), piece, scale * piece).astype(jnp.bfloat16)


def input_kernel(peers, scale, here, lengths, mine, other, *refs):
    pairs, out = refs[: len(peers)], refs[len(peers)]
    me = here[0]
    both = swap_halves(rounded(mine, other, lengths[me], scale))
    ranks = jnp.where(low_lanes(*both.shape), both, 0.0).astype(jnp.bfloat16)
    rows = pairs[0].shape[0]
    for n, k in enumerate(peers):
        columns = pl.ds(pl.multiple_of((me ^ k) * rows, rows), rows)
        out[:, columns] = lax.dot_general(
            ranks, pairs[n][...], (((1,), (1,)), ((), ())), preferred_element_type=jnp.float32
        ).astype(jnp.bfloat16)


def merge_kernel(peers, handled, others, ids, here, lengths, *refs):
    pieces = dict(zip(peers, refs[:-5]))
    out, total, held, sems = refs[-4:]
    me = here[0]
    width = total.shape[1]
    others_here = all(k in pieces for k in others)

    def value(k):
        return pieces[k][...].astype(jnp.float32)

    def either(conditions):
        return functools.reduce(jnp.logical_or, conditions, jnp.bool_(False))

    copies, chosen = [], []
    for n, k in enumerate(handled):
        adapter = ids[me ^ k]
        copies.append(pltpu.make_async_copy(held.at[n], out.at[adapter], sems.at[n]))
        same = {other: ids[me ^ other] == adapter for other in (*handled, *others) if other != k}
        skip = either([same[other] for other in handled[:n]])
        adding = list(handled[n + 1 :])
        if others_here:
            adding += others
        else:
            skip |= either([same[other] for other in others])
        more = either([same[other] for other in adding])
        chosen.append(jnp.logical_not(skip))

        def store(sum_of, count):
            denom = jnp.maximum(count.astype(jnp.float32), 1.0)
            part = 1.0 / jnp.full((1, width), denom)
            held[n] = (sum_of * part).astype(jnp.bfloat16)
            copies[n].start()

        @pl.when(chosen[n] & jnp.logical_not(more))
        def _():
            store(value(k), lengths[me ^ k])

        @pl.when(chosen[n] & more)
        def _():
            total[...] = value(k)
            count = lengths[me ^ k]
            for other in adding:
                count += jnp.where(same[other], lengths[me ^ other], 0)

                @pl.when(same[other])
                def _():
                    total[...] += value(other)

            store(total[...], count)

    for n in range(len(handled)):
        pl.when(chosen[n])(copies[n].wait)


def exchange(pieces, ties):
    owners = lax.axis_size("dp")
    out = {}
    for k in sorted(pieces, key=lambda k: k in ties):
        piece = lax.optimization_barrier((pieces[k], out[ties[k]]))[0] if k in ties else pieces[k]
        out[k] = lax.ppermute(piece, "dp", [(i, i ^ k) for i in range(owners)])
    return {k: out[k] for k in pieces}


def across_cores(value):
    cores = lax.axis_size("tensor")
    return lax.ppermute(value, "tensor", [(i, i ^ 1) for i in range(cores)])


def with_kernels(activations, cotangent, adapter_weight_pair, adapter_of_block, block_live_length):
    owners = lax.axis_size("dp")
    here = lax.axis_index("dp").astype(jnp.int32).reshape(1)
    ids, lengths = adapter_of_block[:, 0], block_live_length[:, 0]
    count, _, rows, width = adapter_weight_pair.shape
    table = adapter_weight_pair.reshape(count, rows, width)
    tokens, features = activations.shape
    scale = adapter_alpha / (width // 2)
    bf16, f32 = jnp.bfloat16, jnp.float32
    straight = jax.ShapeDtypeStruct((rows, width), bf16)
    pair_bytes = owners * rows * width * 2
    token_bytes = tokens * features * 2
    partners = len(FETCH)

    sent = call(
        functools.partial(gather_kernel, FETCH),
        [straight] * partners,
        [in_smem, in_smem, in_hbm],
        [in_vmem] * partners,
        [pltpu.SemaphoreType.DMA((partners,))],
        moved=2 * pair_bytes,
        vmem=53,
    )(ids, here, table)
    pairs = exchange(dict(zip(FETCH, sent)), FETCH_TIES)

    step = 8
    turned, own, blank = call(
        prep_kernel,
        [
            jax.ShapeDtypeStruct((owners, rows, 2 * tokens), bf16),
            straight,
            jax.ShapeDtypeStruct(table.shape, bf16),
        ],
        [in_smem, in_smem, in_hbm, in_hbm, in_vmem, in_vmem],
        [in_vmem, in_vmem, in_hbm],
        [
            pltpu.VMEM((step, rows, width), bf16),
            pltpu.SemaphoreType.DMA((count // step,)),
            pltpu.SemaphoreType.DMA,
        ],
        moved=4 * token_bytes + 2 * count * rows * width,
    )(ids, here, table, pairs[PREP_AFTER], activations, cotangent)
    pairs[0] = own

    mine = jnp.zeros((tokens, width), f32)
    for part in ([k for k in pairs if k not in RANK_LAST], RANK_LAST):
        mine = call(
            functools.partial(rank_kernel, tuple(part)),
            jax.ShapeDtypeStruct((tokens, width), f32),
            [in_smem] + [in_vmem] * (3 + len(part)),
            in_vmem,
            moved=1024,
        )(here, lax.optimization_barrier((activations, turned))[0], cotangent, mine, *[pairs[k] for k in part])
    other = across_cores(mine)

    peers = (*SEND, 0)
    pieces = []
    for part in (peers[:SEND_FIRST], peers[SEND_FIRST:]):
        pieces += call(
            functools.partial(piece_kernel, part, scale),
            [straight] * len(part),
            [in_smem] * 2 + [in_vmem] * 3,
            [in_vmem] * len(part),
            moved=1024,
        )(here, lengths, mine, other, turned)
    arrived = exchange(dict(zip(SEND, pieces)), SEND_TIES)
    arrived[0] = pieces[-1]

    grad_input = call(
        functools.partial(input_kernel, tuple(pairs), scale),
        jax.ShapeDtypeStruct((tokens, features), bf16),
        [in_smem] * 2 + [in_vmem] * (2 + owners),
        in_vmem,
        flops=2 * tokens * features * width,
        moved=token_bytes + pair_bytes,
    )(here, lengths, lax.optimization_barrier((mine, *pieces))[0], other, *pairs.values())

    late = tuple(k for k in peers if k in LATE)
    early = tuple(k for k in peers if k not in LATE)

    def merge(handled, others, merged, so_far):
        return call(
            functools.partial(merge_kernel, tuple(merged), handled, others),
            jax.ShapeDtypeStruct(table.shape, bf16),
            [in_smem] * 3 + [in_vmem] * len(merged) + [in_hbm],
            in_hbm,
            [
                pltpu.VMEM((rows, width), f32),
                pltpu.VMEM((len(handled), rows, width), bf16),
                pltpu.SemaphoreType.DMA((len(handled),)),
            ],
            moved=2 * pair_bytes,
            aliases={3 + len(merged): 0},
        )(ids, here, lengths, *merged.values(), so_far)

    early_pieces = {k: arrived[k] for k in early}
    gradient = merge(late, early, arrived, merge(early, late, early_pieces, blank))
    return grad_input, gradient[:, None]


def without_kernels(activations, cotangent, adapter_weight_pair, adapter_of_block, block_live_length):
    owners = lax.axis_size("dp")
    here = lax.axis_index("dp")
    count, _, rows, width = adapter_weight_pair.shape
    rank = width // 2
    scale = adapter_alpha / rank
    adapters = adapter_of_block[:, 0]
    lengths = block_live_length[:, 0]
    keep = (jnp.arange(activations.shape[0], dtype=jnp.int32) < lengths[here])[:, None]
    inputs = jnp.where(keep, activations, jnp.zeros_like(activations))
    grads_out = jnp.where(keep, cotangent, jnp.zeros_like(cotangent))
    fetched = lax.all_to_all(
        adapter_weight_pair[:, 0][adapters], "dp", split_axis=0, concat_axis=0, tiled=True
    )
    pair = fetched.reshape(-1, width)
    down, upward = pair[:, :rank], pair[:, rank:]
    f32 = jnp.float32
    hidden_part = jnp.dot(inputs, down, preferred_element_type=f32)
    dhidden_part = scale * jnp.dot(grads_out, upward, preferred_element_type=f32)
    hidden, dhidden = lax.psum((hidden_part, dhidden_part), "tensor")
    hidden16, dhidden16 = hidden.astype(jnp.bfloat16), dhidden.astype(jnp.bfloat16)
    d_down = jnp.dot(inputs.T, dhidden16, preferred_element_type=f32)
    d_up = scale * jnp.dot(grads_out.T, hidden16, preferred_element_type=f32)
    sent = jnp.concatenate([d_down, d_up], axis=1).astype(jnp.bfloat16).reshape(owners, rows, width)
    received = lax.all_to_all(sent, "dp", split_axis=0, concat_axis=0, tiled=True).astype(f32)
    same = adapters[:, None] == adapters[None, :]
    total = jnp.sum(jnp.where(same, lengths[None, :], 0), axis=1).astype(f32)
    summed = jax.ops.segment_sum(received, adapters, num_segments=count)
    denom = jnp.ones((count,), f32).at[adapters].set(jnp.maximum(total, 1.0))
    gradient = (summed / denom[:, None, None]).astype(jnp.bfloat16)
    grad_input = jnp.dot(dhidden16, down.T, preferred_element_type=f32).astype(jnp.bfloat16)
    return grad_input, gradient[:, None]


def solution(mesh):
    owners, cores = mesh.shape["dp"], mesh.shape["tensor"]

    def on_device(activations, cotangent, adapter_weight_pair, *rest):
        rows = adapter_weight_pair.shape[2]
        fits = owners == len(FETCH) + 1 and cores == 2 and rows % 256 == 0
        body = with_kernels if fits else without_kernels
        return body(activations, cotangent, adapter_weight_pair, *rest)

    in_specs = (
        P(("group", "dp"), "tensor"),
        P(("group", "dp"), "tensor"),
        P(None, "tensor", "dp", None),
        P("group", None),
        P("group", None),
    )
    out_specs = (P(("group", "dp"), "tensor"), P("group", "tensor", "dp", None))
    return jax.shard_map(
        on_device, mesh=mesh, in_specs=in_specs, out_specs=out_specs, check_vma=False
    )
```

```python
import functools

import jax
import jax.numpy as jnp
from jax import lax
from jax.experimental import pallas as pl
from jax.experimental.pallas import tpu as pltpu
from jax.sharding import PartitionSpec as P

adapter_alpha = 128.0
FETCH = (1, 4, 2, 5, 6, 3, 7)
FETCH_TIES = {}
SEND = (1, 6, 2, 7, 4, 5, 3)
SEND_TIES = {}
PREP_AFTER = 1
LATE = (4, 5, 3)
RANK_LAST = (3, 7)
SEND_FIRST = 2

in_vmem = pl.BlockSpec(memory_space=pltpu.VMEM)
in_smem = pl.BlockSpec(memory_space=pltpu.SMEM)
in_hbm = pl.BlockSpec(memory_space=pltpu.HBM)


def low_lanes(rows, width):
    return lax.broadcasted_iota(jnp.int32, (rows, width), 1) < width // 2


def call(kernel, out_shape, in_specs, out_specs, scratch=(), flops=0, moved=0, aliases=None, vmem=40):
    return pl.pallas_call(
        kernel,
        out_shape=out_shape,
        in_specs=in_specs,
        out_specs=out_specs,
        scratch_shapes=list(scratch),
        input_output_aliases=aliases or {},
        compiler_params=pltpu.CompilerParams(vmem_limit_bytes=vmem * 1024 * 1024),
        cost_estimate=pl.CostEstimate(flops=flops, bytes_accessed=moved, transcendentals=0),
    )


def gather_kernel(peers, ids, here, table, *refs):
    out, sems = refs[: len(peers)], refs[len(peers)]
    copies = [
        pltpu.make_async_copy(table.at[ids[here[0] ^ k]], out[n], sems.at[n])
        for n, k in enumerate(peers)
    ]
    for copy in copies:
        copy.start()
    for copy in copies:
        copy.wait()


def prep_kernel(ids, here, table, after, x, y, turned, own, blank, zeros, sem, own_sem):
    own_copy = pltpu.make_async_copy(table.at[ids[here[0]]], own, own_sem)
    own_copy.start()
    rows = own.shape[0]
    zeros[...] = jnp.zeros_like(zeros)
    step = zeros.shape[0]
    copies = [
        pltpu.make_async_copy(zeros, blank.at[pl.ds(s, step)], sem.at[s // step])
        for s in range(0, blank.shape[0], step)
    ]
    for copy in copies:
        copy.start()
    tokens = x.shape[0]

    @pl.loop(0, x.shape[1] // rows)
    def _(owner):
        columns = pl.ds(pl.multiple_of(owner * rows, rows), rows)
        turned[owner, :, pl.ds(0, tokens)] = x[:, columns].T
        turned[owner, :, pl.ds(tokens, tokens)] = y[:, columns].T

    for copy in [own_copy, *copies]:
        copy.wait()


def rank_kernel(peers, here, x, y, so_far, *refs):
    pairs, out = refs[: len(peers)], refs[len(peers)]
    rows, width = pairs[0].shape
    tokens = x.shape[0]
    x_rank = so_far[...]
    y_rank = x_rank
    for n, k in enumerate(peers):
        columns = pl.ds(pl.multiple_of((here[0] ^ k) * rows, rows), rows)
        x_rank += jnp.dot(x[:, columns], pairs[n][...], preferred_element_type=jnp.float32)
        y_rank += jnp.dot(y[:, columns], pairs[n][...], preferred_element_type=jnp.float32)
    out[...] = jnp.where(low_lanes(tokens, width), x_rank, y_rank)


def rounded(mine, other, length, scale):
    total = mine[...] + other[...]
    rows, width = total.shape
    total = jnp.where(low_lanes(rows, width), total, scale * total)
    live = lax.broadcasted_iota(jnp.int32, (rows, width), 0) < length
    return jnp.where(live, total, 0.0)


def swap_halves(value):
    return pltpu.roll(value, value.shape[-1] // 2, 1)


def piece_kernel(peers, scale, here, lengths, mine, other, turned, *refs):
    me = here[0]
    both = swap_halves(rounded(mine, other, lengths[me], scale))
    low = low_lanes(*both.shape)
    top = jnp.where(low, both, 0.0).astype(jnp.bfloat16)
    bottom = jnp.where(low, 0.0, both).astype(jnp.bfloat16)
    ranks = jnp.concatenate([top, bottom], axis=0)
    for n, k in enumerate(peers):
        piece = jnp.dot(turned[me ^ k], ranks, preferred_element_type=jnp.float32)
        refs[n][...] = jnp.where(low_lanes(*piece.shape), piece, scale * piece).astype(jnp.bfloat16)


def input_kernel(peers, scale, here, lengths, mine, other, *refs):
    pairs, out = refs[: len(peers)], refs[len(peers)]
    me = here[0]
    both = swap_halves(rounded(mine, other, lengths[me], scale))
    ranks = jnp.where(low_lanes(*both.shape), both, 0.0).astype(jnp.bfloat16)
    rows = pairs[0].shape[0]
    for n, k in enumerate(peers):
        columns = pl.ds(pl.multiple_of((me ^ k) * rows, rows), rows)
        out[:, columns] = lax.dot_general(
            ranks, pairs[n][...], (((1,), (1,)), ((), ())), preferred_element_type=jnp.float32
        ).astype(jnp.bfloat16)


def merge_kernel(peers, handled, others, ids, here, lengths, *refs):
    pieces = dict(zip(peers, refs[:-5]))
    out, total, held, sems = refs[-4:]
    me = here[0]
    width = total.shape[1]
    others_here = all(k in pieces for k in others)

    def value(k):
        return pieces[k][...].astype(jnp.float32)

    def either(conditions):
        return functools.reduce(jnp.logical_or, conditions, jnp.bool_(False))

    copies, chosen = [], []
    for n, k in enumerate(handled):
        adapter = ids[me ^ k]
        copies.append(pltpu.make_async_copy(held.at[n], out.at[adapter], sems.at[n]))
        same = {other: ids[me ^ other] == adapter for other in (*handled, *others) if other != k}
        skip = either([same[other] for other in handled[:n]])
        adding = list(handled[n + 1 :])
        if others_here:
            adding += others
        else:
            skip |= either([same[other] for other in others])
        more = either([same[other] for other in adding])
        chosen.append(jnp.logical_not(skip))

        def store(sum_of, count):
            denom = jnp.maximum(count.astype(jnp.float32), 1.0)
            part = 1.0 / jnp.full((1, width), denom)
            held[n] = (sum_of * part).astype(jnp.bfloat16)
            copies[n].start()

        @pl.when(chosen[n] & jnp.logical_not(more))
        def _():
            store(value(k), lengths[me ^ k])

        @pl.when(chosen[n] & more)
        def _():
            total[...] = value(k)
            count = lengths[me ^ k]
            for other in adding:
                count += jnp.where(same[other], lengths[me ^ other], 0)

                @pl.when(same[other])
                def _():
                    total[...] += value(other)

            store(total[...], count)

    for n in range(len(handled)):
        pl.when(chosen[n])(copies[n].wait)


def exchange(pieces, ties):
    owners = lax.axis_size("dp")
    out = {}
    for k in sorted(pieces, key=lambda k: k in ties):
        piece = lax.optimization_barrier((pieces[k], out[ties[k]]))[0] if k in ties else pieces[k]
        out[k] = lax.ppermute(piece, "dp", [(i, i ^ k) for i in range(owners)])
    return {k: out[k] for k in pieces}


def across_cores(value):
    cores = lax.axis_size("tensor")
    return lax.ppermute(value, "tensor", [(i, i ^ 1) for i in range(cores)])


def with_kernels(activations, cotangent, adapter_weight_pair, adapter_of_block, block_live_length):
    owners = lax.axis_size("dp")
    here = lax.axis_index("dp").astype(jnp.int32).reshape(1)
    ids, lengths = adapter_of_block[:, 0], block_live_length[:, 0]
    count, _, rows, width = adapter_weight_pair.shape
    table = adapter_weight_pair.reshape(count, rows, width)
    tokens, features = activations.shape
    scale = adapter_alpha / (width // 2)
    bf16, f32 = jnp.bfloat16, jnp.float32
    straight = jax.ShapeDtypeStruct((rows, width), bf16)
    pair_bytes = owners * rows * width * 2
    token_bytes = tokens * features * 2
    partners = len(FETCH)

    sent = call(
        functools.partial(gather_kernel, FETCH),
        [straight] * partners,
        [in_smem, in_smem, in_hbm],
        [in_vmem] * partners,
        [pltpu.SemaphoreType.DMA((partners,))],
        moved=2 * pair_bytes,
        vmem=53,
    )(ids, here, table)
    pairs = exchange(dict(zip(FETCH, sent)), FETCH_TIES)

    step = 8
    turned, own, blank = call(
        prep_kernel,
        [
            jax.ShapeDtypeStruct((owners, rows, 2 * tokens), bf16),
            straight,
            jax.ShapeDtypeStruct(table.shape, bf16),
        ],
        [in_smem, in_smem, in_hbm, in_hbm, in_vmem, in_vmem],
        [in_vmem, in_vmem, in_hbm],
        [
            pltpu.VMEM((step, rows, width), bf16),
            pltpu.SemaphoreType.DMA((count // step,)),
            pltpu.SemaphoreType.DMA,
        ],
        moved=4 * token_bytes + 2 * count * rows * width,
    )(ids, here, table, pairs[PREP_AFTER], activations, cotangent)
    pairs[0] = own

    mine = jnp.zeros((tokens, width), f32)
    for part in ([k for k in pairs if k not in RANK_LAST], RANK_LAST):
        mine = call(
            functools.partial(rank_kernel, tuple(part)),
            jax.ShapeDtypeStruct((tokens, width), f32),
            [in_smem] + [in_vmem] * (3 + len(part)),
            in_vmem,
            moved=1024,
        )(here, lax.optimization_barrier((activations, turned))[0], cotangent, mine, *[pairs[k] for k in part])
    other = across_cores(mine)

    peers = (*SEND, 0)
    pieces = []
    for part in (peers[:SEND_FIRST], peers[SEND_FIRST:]):
        pieces += call(
            functools.partial(piece_kernel, part, scale),
            [straight] * len(part),
            [in_smem] * 2 + [in_vmem] * 3,
            [in_vmem] * len(part),
            moved=1024,
        )(here, lengths, mine, other, turned)
    arrived = exchange(dict(zip(SEND, pieces)), SEND_TIES)
    arrived[0] = pieces[-1]

    grad_input = call(
        functools.partial(input_kernel, tuple(pairs), scale),
        jax.ShapeDtypeStruct((tokens, features), bf16),
        [in_smem] * 2 + [in_vmem] * (2 + owners),
        in_vmem,
        flops=2 * tokens * features * width,
        moved=token_bytes + pair_bytes,
    )(here, lengths, lax.optimization_barrier((mine, *pieces))[0], other, *pairs.values())

    late = tuple(k for k in peers if k in LATE)
    early = tuple(k for k in peers if k not in LATE)

    def merge(handled, others, merged, so_far):
        return call(
            functools.partial(merge_kernel, tuple(merged), handled, others),
            jax.ShapeDtypeStruct(table.shape, bf16),
            [in_smem] * 3 + [in_vmem] * len(merged) + [in_hbm],
            in_hbm,
            [
                pltpu.VMEM((rows, width), f32),
                pltpu.VMEM((len(handled), rows, width), bf16),
                pltpu.SemaphoreType.DMA((len(handled),)),
            ],
            moved=2 * pair_bytes,
            aliases={3 + len(merged): 0},
        )(ids, here, lengths, *merged.values(), so_far)

    early_pieces = {k: arrived[k] for k in early}
    gradient = merge(late, early, arrived, merge(early, late, early_pieces, blank))
    return grad_input, gradient[:, None]


def without_kernels(activations, cotangent, adapter_weight_pair, adapter_of_block, block_live_length):
    owners = lax.axis_size("dp")
    here = lax.axis_index("dp")
    count, _, rows, width = adapter_weight_pair.shape
    rank = width // 2
    scale = adapter_alpha / rank
    adapters = adapter_of_block[:, 0]
    lengths = block_live_length[:, 0]
    keep = (jnp.arange(activations.shape[0], dtype=jnp.int32) < lengths[here])[:, None]
    inputs = jnp.where(keep, activations, jnp.zeros_like(activations))
    grads_out = jnp.where(keep, cotangent, jnp.zeros_like(cotangent))
    fetched = lax.all_to_all(
        adapter_weight_pair[:, 0][adapters], "dp", split_axis=0, concat_axis=0, tiled=True
    )
    pair = fetched.reshape(-1, width)
    down, upward = pair[:, :rank], pair[:, rank:]
    f32 = jnp.float32
    hidden_part = jnp.dot(inputs, down, preferred_element_type=f32)
    dhidden_part = scale * jnp.dot(grads_out, upward, preferred_element_type=f32)
    hidden, dhidden = lax.psum((hidden_part, dhidden_part), "tensor")
    hidden16, dhidden16 = hidden.astype(jnp.bfloat16), dhidden.astype(jnp.bfloat16)
    d_down = jnp.dot(inputs.T, dhidden16, preferred_element_type=f32)
    d_up = scale * jnp.dot(grads_out.T, hidden16, preferred_element_type=f32)
    sent = jnp.concatenate([d_down, d_up], axis=1).astype(jnp.bfloat16).reshape(owners, rows, width)
    received = lax.all_to_all(sent, "dp", split_axis=0, concat_axis=0, tiled=True).astype(f32)
    same = adapters[:, None] == adapters[None, :]
    total = jnp.sum(jnp.where(same, lengths[None, :], 0), axis=1).astype(f32)
    summed = jax.ops.segment_sum(received, adapters, num_segments=count)
    denom = jnp.ones((count,), f32).at[adapters].set(jnp.maximum(total, 1.0))
    gradient = (summed / denom[:, None, None]).astype(jnp.bfloat16)
    grad_input = jnp.dot(dhidden16, down.T, preferred_element_type=f32).astype(jnp.bfloat16)
    return grad_input, gradient[:, None]


def solution(mesh):
    owners, cores = mesh.shape["dp"], mesh.shape["tensor"]

    def on_device(activations, cotangent, adapter_weight_pair, *rest):
        rows = adapter_weight_pair.shape[2]
        fits = owners == len(FETCH) + 1 and cores == 2 and rows % 256 == 0
        body = with_kernels if fits else without_kernels
        return body(activations, cotangent, adapter_weight_pair, *rest)

    in_specs = (
        P(("group", "dp"), "tensor"),
        P(("group", "dp"), "tensor"),
        P(None, "tensor", "dp", None),
        P("group", None),
        P("group", None),
    )
    out_specs = (P(("group", "dp"), "tensor"), P("group", "tensor", "dp", None))
    return jax.shard_map(
        on_device, mesh=mesh, in_specs=in_specs, out_specs=out_specs, check_vma=False
    )
```

```python
import functools

import jax
import jax.numpy as jnp
from jax import lax
from jax.experimental import pallas as pl
from jax.experimental.pallas import tpu as pltpu
from jax.sharding import PartitionSpec as P

adapter_alpha = 128.0
FETCH = (4, 1, 2, 5, 6, 3, 7)
FETCH_TIES = {}
SEND = (1, 6, 2, 4, 5, 3, 7)
SEND_TIES = {}
PREP_AFTER = 1
LATE = (5, 3, 7)
RANK_LAST = (3, 7)
SEND_FIRST = 2
FETCH_FIRST = 1

in_vmem = pl.BlockSpec(memory_space=pltpu.VMEM)
in_smem = pl.BlockSpec(memory_space=pltpu.SMEM)
in_hbm = pl.BlockSpec(memory_space=pltpu.HBM)


def low_lanes(rows, width):
    return lax.broadcasted_iota(jnp.int32, (rows, width), 1) < width // 2


def call(kernel, out_shape, in_specs, out_specs, scratch=(), flops=0, moved=0, aliases=None, vmem=40):
    return pl.pallas_call(
        kernel,
        out_shape=out_shape,
        in_specs=in_specs,
        out_specs=out_specs,
        scratch_shapes=list(scratch),
        input_output_aliases=aliases or {},
        compiler_params=pltpu.CompilerParams(vmem_limit_bytes=vmem * 1024 * 1024),
        cost_estimate=pl.CostEstimate(flops=flops, bytes_accessed=moved, transcendentals=0),
    )


def gather_kernel(peers, ids, here, table, *refs):
    out, sems = refs[: len(peers)], refs[len(peers)]
    copies = [
        pltpu.make_async_copy(table.at[ids[here[0] ^ k]], out[n], sems.at[n])
        for n, k in enumerate(peers)
    ]
    for copy in copies:
        copy.start()
    for copy in copies:
        copy.wait()


def prep_kernel(ids, here, table, after, x, y, turned, own, blank, zeros, sem, own_sem):
    own_copy = pltpu.make_async_copy(table.at[ids[here[0]]], own, own_sem)
    own_copy.start()
    rows = own.shape[0]
    zeros[...] = jnp.zeros_like(zeros)
    step = zeros.shape[0]
    copies = [
        pltpu.make_async_copy(zeros, blank.at[pl.ds(s, step)], sem.at[s // step])
        for s in range(0, blank.shape[0], step)
    ]
    for copy in copies:
        copy.start()
    tokens = x.shape[0]

    @pl.loop(0, x.shape[1] // rows)
    def _(owner):
        columns = pl.ds(pl.multiple_of(owner * rows, rows), rows)
        turned[owner, :, pl.ds(0, tokens)] = x[:, columns].T
        turned[owner, :, pl.ds(tokens, tokens)] = y[:, columns].T

    for copy in [own_copy, *copies]:
        copy.wait()


def rank_kernel(peers, here, x, y, so_far, *refs):
    pairs, out = refs[: len(peers)], refs[len(peers)]
    rows, width = pairs[0].shape
    tokens = x.shape[0]
    x_rank = so_far[...]
    y_rank = x_rank
    for n, k in enumerate(peers):
        columns = pl.ds(pl.multiple_of((here[0] ^ k) * rows, rows), rows)
        x_rank += jnp.dot(x[:, columns], pairs[n][...], preferred_element_type=jnp.float32)
        y_rank += jnp.dot(y[:, columns], pairs[n][...], preferred_element_type=jnp.float32)
    out[...] = jnp.where(low_lanes(tokens, width), x_rank, y_rank)


def rounded(mine, other, length, scale):
    total = mine[...] + other[...]
    rows, width = total.shape
    total = jnp.where(low_lanes(rows, width), total, scale * total)
    live = lax.broadcasted_iota(jnp.int32, (rows, width), 0) < length
    return jnp.where(live, total, 0.0)


def swap_halves(value):
    return pltpu.roll(value, value.shape[-1] // 2, 1)


def piece_kernel(peers, scale, here, lengths, mine, other, turned, *refs):
    me = here[0]
    both = swap_halves(rounded(mine, other, lengths[me], scale))
    low = low_lanes(*both.shape)
    top = jnp.where(low, both, 0.0).astype(jnp.bfloat16)
    bottom = jnp.where(low, 0.0, both).astype(jnp.bfloat16)
    ranks = jnp.concatenate([top, bottom], axis=0)
    for n, k in enumerate(peers):
        piece = jnp.dot(turned[me ^ k], ranks, preferred_element_type=jnp.float32)
        refs[n][...] = jnp.where(low_lanes(*piece.shape), piece, scale * piece).astype(jnp.bfloat16)


def input_kernel(peers, scale, here, lengths, mine, other, *refs):
    pairs, out = refs[: len(peers)], refs[len(peers)]
    me = here[0]
    both = swap_halves(rounded(mine, other, lengths[me], scale))
    ranks = jnp.where(low_lanes(*both.shape), both, 0.0).astype(jnp.bfloat16)
    rows = pairs[0].shape[0]
    for n, k in enumerate(peers):
        columns = pl.ds(pl.multiple_of((me ^ k) * rows, rows), rows)
        out[:, columns] = lax.dot_general(
            ranks, pairs[n][...], (((1,), (1,)), ((), ())), preferred_element_type=jnp.float32
        ).astype(jnp.bfloat16)


def merge_kernel(peers, handled, others, ids, here, lengths, *refs):
    pieces = dict(zip(peers, refs[:-5]))
    out, total, held, sems = refs[-4:]
    me = here[0]
    width = total.shape[1]
    others_here = all(k in pieces for k in others)

    def value(k):
        return pieces[k][...].astype(jnp.float32)

    def either(conditions):
        return functools.reduce(jnp.logical_or, conditions, jnp.bool_(False))

    copies, chosen = [], []
    for n, k in enumerate(handled):
        adapter = ids[me ^ k]
        copies.append(pltpu.make_async_copy(held.at[n], out.at[adapter], sems.at[n]))
        same = {other: ids[me ^ other] == adapter for other in (*handled, *others) if other != k}
        skip = either([same[other] for other in handled[:n]])
        adding = list(handled[n + 1 :])
        if others_here:
            adding += others
        else:
            skip |= either([same[other] for other in others])
        more = either([same[other] for other in adding])
        chosen.append(jnp.logical_not(skip))

        def store(sum_of, count):
            denom = jnp.maximum(count.astype(jnp.float32), 1.0)
            part = 1.0 / jnp.full((1, width), denom)
            held[n] = (sum_of * part).astype(jnp.bfloat16)
            copies[n].start()

        @pl.when(chosen[n] & jnp.logical_not(more))
        def _():
            store(value(k), lengths[me ^ k])

        @pl.when(chosen[n] & more)
        def _():
            total[...] = value(k)
            count = lengths[me ^ k]
            for other in adding:
                count += jnp.where(same[other], lengths[me ^ other], 0)

                @pl.when(same[other])
                def _():
                    total[...] += value(other)

            store(total[...], count)

    for n in range(len(handled)):
        pl.when(chosen[n])(copies[n].wait)


def exchange(pieces, ties):
    owners = lax.axis_size("dp")
    out = {}
    for k in sorted(pieces, key=lambda k: k in ties):
        piece = lax.optimization_barrier((pieces[k], out[ties[k]]))[0] if k in ties else pieces[k]
        out[k] = lax.ppermute(piece, "dp", [(i, i ^ k) for i in range(owners)])
    return {k: out[k] for k in pieces}


def across_cores(value):
    cores = lax.axis_size("tensor")
    return lax.ppermute(value, "tensor", [(i, i ^ 1) for i in range(cores)])


def with_kernels(activations, cotangent, adapter_weight_pair, adapter_of_block, block_live_length):
    owners = lax.axis_size("dp")
    here = lax.axis_index("dp").astype(jnp.int32).reshape(1)
    ids, lengths = adapter_of_block[:, 0], block_live_length[:, 0]
    count, _, rows, width = adapter_weight_pair.shape
    table = adapter_weight_pair.reshape(count, rows, width)
    tokens, features = activations.shape
    scale = adapter_alpha / (width // 2)
    bf16, f32 = jnp.bfloat16, jnp.float32
    straight = jax.ShapeDtypeStruct((rows, width), bf16)
    pair_bytes = owners * rows * width * 2
    token_bytes = tokens * features * 2

    sent, me = [], here
    for part in (FETCH[:FETCH_FIRST], FETCH[FETCH_FIRST:]):
        sent += call(
            functools.partial(gather_kernel, part),
            [straight] * len(part),
            [in_smem, in_smem, in_hbm],
            [in_vmem] * len(part),
            [pltpu.SemaphoreType.DMA((len(part),))],
            moved=1024,
            vmem=53,
        )(ids, me, table)
        me = lax.optimization_barrier((here, *sent))[0]
    pairs = exchange(dict(zip(FETCH, sent)), FETCH_TIES)

    step = 8
    turned, own, blank = call(
        prep_kernel,
        [
            jax.ShapeDtypeStruct((owners, rows, 2 * tokens), bf16),
            straight,
            jax.ShapeDtypeStruct(table.shape, bf16),
        ],
        [in_smem, in_smem, in_hbm, in_hbm, in_vmem, in_vmem],
        [in_vmem, in_vmem, in_hbm],
        [
            pltpu.VMEM((step, rows, width), bf16),
            pltpu.SemaphoreType.DMA((count // step,)),
            pltpu.SemaphoreType.DMA,
        ],
        moved=4 * token_bytes + 2 * count * rows * width,
    )(ids, here, table, pairs[PREP_AFTER], activations, cotangent)
    pairs[0] = own

    mine = jnp.zeros((tokens, width), f32)
    for part in ([k for k in pairs if k not in RANK_LAST], RANK_LAST):
        mine = call(
            functools.partial(rank_kernel, tuple(part)),
            jax.ShapeDtypeStruct((tokens, width), f32),
            [in_smem] + [in_vmem] * (3 + len(part)),
            in_vmem,
            moved=1024,
        )(here, lax.optimization_barrier((activations, turned))[0], cotangent, mine, *[pairs[k] for k in part])
    other = across_cores(mine)

    peers = (*SEND, 0)
    pieces = []
    for part in (peers[:SEND_FIRST], peers[SEND_FIRST:]):
        pieces += call(
            functools.partial(piece_kernel, part, scale),
            [straight] * len(part),
            [in_smem] * 2 + [in_vmem] * 3,
            [in_vmem] * len(part),
            moved=1024,
        )(here, lengths, mine, other, turned)
    arrived = exchange(dict(zip(SEND, pieces)), SEND_TIES)
    arrived[0] = pieces[-1]

    grad_input = call(
        functools.partial(input_kernel, tuple(pairs), scale),
        jax.ShapeDtypeStruct((tokens, features), bf16),
        [in_smem] * 2 + [in_vmem] * (2 + owners),
        in_vmem,
        flops=2 * tokens * features * width,
        moved=token_bytes + pair_bytes,
    )(here, lengths, lax.optimization_barrier((mine, *pieces))[0], other, *pairs.values())

    late = tuple(k for k in peers if k in LATE)
    early = tuple(k for k in peers if k not in LATE)

    def merge(handled, others, merged, so_far):
        return call(
            functools.partial(merge_kernel, tuple(merged), handled, others),
            jax.ShapeDtypeStruct(table.shape, bf16),
            [in_smem] * 3 + [in_vmem] * len(merged) + [in_hbm],
            in_hbm,
            [
                pltpu.VMEM((rows, width), f32),
                pltpu.VMEM((len(handled), rows, width), bf16),
                pltpu.SemaphoreType.DMA((len(handled),)),
            ],
            moved=2 * pair_bytes,
            aliases={3 + len(merged): 0},
        )(ids, here, lengths, *merged.values(), so_far)

    early_pieces = {k: arrived[k] for k in early}
    gradient = merge(late, early, arrived, merge(early, late, early_pieces, blank))
    return grad_input, gradient[:, None]


def without_kernels(activations, cotangent, adapter_weight_pair, adapter_of_block, block_live_length):
    owners = lax.axis_size("dp")
    here = lax.axis_index("dp")
    count, _, rows, width = adapter_weight_pair.shape
    rank = width // 2
    scale = adapter_alpha / rank
    adapters = adapter_of_block[:, 0]
    lengths = block_live_length[:, 0]
    keep = (jnp.arange(activations.shape[0], dtype=jnp.int32) < lengths[here])[:, None]
    inputs = jnp.where(keep, activations, jnp.zeros_like(activations))
    grads_out = jnp.where(keep, cotangent, jnp.zeros_like(cotangent))
    fetched = lax.all_to_all(
        adapter_weight_pair[:, 0][adapters], "dp", split_axis=0, concat_axis=0, tiled=True
    )
    pair = fetched.reshape(-1, width)
    down, upward = pair[:, :rank], pair[:, rank:]
    f32 = jnp.float32
    hidden_part = jnp.dot(inputs, down, preferred_element_type=f32)
    dhidden_part = scale * jnp.dot(grads_out, upward, preferred_element_type=f32)
    hidden, dhidden = lax.psum((hidden_part, dhidden_part), "tensor")
    hidden16, dhidden16 = hidden.astype(jnp.bfloat16), dhidden.astype(jnp.bfloat16)
    d_down = jnp.dot(inputs.T, dhidden16, preferred_element_type=f32)
    d_up = scale * jnp.dot(grads_out.T, hidden16, preferred_element_type=f32)
    sent = jnp.concatenate([d_down, d_up], axis=1).astype(jnp.bfloat16).reshape(owners, rows, width)
    received = lax.all_to_all(sent, "dp", split_axis=0, concat_axis=0, tiled=True).astype(f32)
    same = adapters[:, None] == adapters[None, :]
    total = jnp.sum(jnp.where(same, lengths[None, :], 0), axis=1).astype(f32)
    summed = jax.ops.segment_sum(received, adapters, num_segments=count)
    denom = jnp.ones((count,), f32).at[adapters].set(jnp.maximum(total, 1.0))
    gradient = (summed / denom[:, None, None]).astype(jnp.bfloat16)
    grad_input = jnp.dot(dhidden16, down.T, preferred_element_type=f32).astype(jnp.bfloat16)
    return grad_input, gradient[:, None]


def solution(mesh):
    owners, cores = mesh.shape["dp"], mesh.shape["tensor"]

    def on_device(activations, cotangent, adapter_weight_pair, *rest):
        rows = adapter_weight_pair.shape[2]
        fits = owners == len(FETCH) + 1 and cores == 2 and rows % 256 == 0
        body = with_kernels if fits else without_kernels
        return body(activations, cotangent, adapter_weight_pair, *rest)

    in_specs = (
        P(("group", "dp"), "tensor"),
        P(("group", "dp"), "tensor"),
        P(None, "tensor", "dp", None),
        P("group", None),
        P("group", None),
    )
    out_specs = (P(("group", "dp"), "tensor"), P("group", "tensor", "dp", None))
    return jax.shard_map(
        on_device, mesh=mesh, in_specs=in_specs, out_specs=out_specs, check_vma=False
    )
```

```python
import functools

import jax
import jax.numpy as jnp
from jax import lax
from jax.experimental import pallas as pl
from jax.experimental.pallas import tpu as pltpu
from jax.sharding import PartitionSpec as P

adapter_alpha = 128.0
FETCH = (4, 1, 2, 5, 6, 3, 7)
FETCH_TIES = {}
SEND = (6, 1, 2, 4, 5, 3, 7)
SEND_TIES = {7: 6}
PREP_AFTER = 1
LATE = (5, 3, 7)
RANK_LAST = (3, 7)
SEND_FIRST = 1
FETCH_FIRST = 1

in_vmem = pl.BlockSpec(memory_space=pltpu.VMEM)
in_smem = pl.BlockSpec(memory_space=pltpu.SMEM)
in_hbm = pl.BlockSpec(memory_space=pltpu.HBM)


def low_lanes(rows, width):
    return lax.broadcasted_iota(jnp.int32, (rows, width), 1) < width // 2


def call(kernel, out_shape, in_specs, out_specs, scratch=(), flops=0, moved=0, aliases=None, vmem=40):
    return pl.pallas_call(
        kernel,
        out_shape=out_shape,
        in_specs=in_specs,
        out_specs=out_specs,
        scratch_shapes=list(scratch),
        input_output_aliases=aliases or {},
        compiler_params=pltpu.CompilerParams(vmem_limit_bytes=vmem * 1024 * 1024),
        cost_estimate=pl.CostEstimate(flops=flops, bytes_accessed=moved, transcendentals=0),
    )


def gather_kernel(peers, ids, here, table, *refs):
    out, sems = refs[: len(peers)], refs[len(peers)]
    copies = [
        pltpu.make_async_copy(table.at[ids[here[0] ^ k]], out[n], sems.at[n])
        for n, k in enumerate(peers)
    ]
    for copy in copies:
        copy.start()
    for copy in copies:
        copy.wait()


def prep_kernel(ids, here, table, after, x, y, turned, own, blank, zeros, sem, own_sem):
    own_copy = pltpu.make_async_copy(table.at[ids[here[0]]], own, own_sem)
    own_copy.start()
    rows = own.shape[0]
    zeros[...] = jnp.zeros_like(zeros)
    step = zeros.shape[0]
    copies = [
        pltpu.make_async_copy(zeros, blank.at[pl.ds(s, step)], sem.at[s // step])
        for s in range(0, blank.shape[0], step)
    ]
    for copy in copies:
        copy.start()
    tokens = x.shape[0]

    @pl.loop(0, x.shape[1] // rows)
    def _(owner):
        columns = pl.ds(pl.multiple_of(owner * rows, rows), rows)
        turned[owner, :, pl.ds(0, tokens)] = x[:, columns].T
        turned[owner, :, pl.ds(tokens, tokens)] = y[:, columns].T

    for copy in [own_copy, *copies]:
        copy.wait()


def rank_kernel(peers, here, x, y, so_far, *refs):
    pairs, out = refs[: len(peers)], refs[len(peers)]
    rows, width = pairs[0].shape
    tokens = x.shape[0]
    x_rank = so_far[...]
    y_rank = x_rank
    for n, k in enumerate(peers):
        columns = pl.ds(pl.multiple_of((here[0] ^ k) * rows, rows), rows)
        x_rank += jnp.dot(x[:, columns], pairs[n][...], preferred_element_type=jnp.float32)
        y_rank += jnp.dot(y[:, columns], pairs[n][...], preferred_element_type=jnp.float32)
    out[...] = jnp.where(low_lanes(tokens, width), x_rank, y_rank)


def rounded(mine, other, length, scale):
    total = mine[...] + other[...]
    rows, width = total.shape
    total = jnp.where(low_lanes(rows, width), total, scale * total)
    live = lax.broadcasted_iota(jnp.int32, (rows, width), 0) < length
    return jnp.where(live, total, 0.0)


def swap_halves(value):
    return pltpu.roll(value, value.shape[-1] // 2, 1)


def piece_kernel(peers, scale, here, lengths, mine, other, turned, *refs):
    me = here[0]
    both = swap_halves(rounded(mine, other, lengths[me], scale))
    low = low_lanes(*both.shape)
    top = jnp.where(low, both, 0.0).astype(jnp.bfloat16)
    bottom = jnp.where(low, 0.0, both).astype(jnp.bfloat16)
    ranks = jnp.concatenate([top, bottom], axis=0)
    for n, k in enumerate(peers):
        piece = jnp.dot(turned[me ^ k], ranks, preferred_element_type=jnp.float32)
        refs[n][...] = jnp.where(low_lanes(*piece.shape), piece, scale * piece).astype(jnp.bfloat16)


def input_kernel(peers, scale, here, lengths, mine, other, *refs):
    pairs, out = refs[: len(peers)], refs[len(peers)]
    me = here[0]
    both = swap_halves(rounded(mine, other, lengths[me], scale))
    ranks = jnp.where(low_lanes(*both.shape), both, 0.0).astype(jnp.bfloat16)
    rows = pairs[0].shape[0]
    for n, k in enumerate(peers):
        columns = pl.ds(pl.multiple_of((me ^ k) * rows, rows), rows)
        out[:, columns] = lax.dot_general(
            ranks, pairs[n][...], (((1,), (1,)), ((), ())), preferred_element_type=jnp.float32
        ).astype(jnp.bfloat16)


def merge_kernel(peers, handled, others, ids, here, lengths, *refs):
    pieces = dict(zip(peers, refs[:-5]))
    out, total, held, sems = refs[-4:]
    me = here[0]
    width = total.shape[1]
    others_here = all(k in pieces for k in others)

    def value(k):
        return pieces[k][...].astype(jnp.float32)

    def either(conditions):
        return functools.reduce(jnp.logical_or, conditions, jnp.bool_(False))

    copies, chosen = [], []
    for n, k in enumerate(handled):
        adapter = ids[me ^ k]
        copies.append(pltpu.make_async_copy(held.at[n], out.at[adapter], sems.at[n]))
        same = {other: ids[me ^ other] == adapter for other in (*handled, *others) if other != k}
        skip = either([same[other] for other in handled[:n]])
        adding = list(handled[n + 1 :])
        if others_here:
            adding += others
        else:
            skip |= either([same[other] for other in others])
        more = either([same[other] for other in adding])
        chosen.append(jnp.logical_not(skip))

        def store(sum_of, count):
            denom = jnp.maximum(count.astype(jnp.float32), 1.0)
            part = 1.0 / jnp.full((1, width), denom)
            held[n] = (sum_of * part).astype(jnp.bfloat16)
            copies[n].start()

        @pl.when(chosen[n] & jnp.logical_not(more))
        def _():
            store(value(k), lengths[me ^ k])

        @pl.when(chosen[n] & more)
        def _():
            total[...] = value(k)
            count = lengths[me ^ k]
            for other in adding:
                count += jnp.where(same[other], lengths[me ^ other], 0)

                @pl.when(same[other])
                def _():
                    total[...] += value(other)

            store(total[...], count)

    for n in range(len(handled)):
        pl.when(chosen[n])(copies[n].wait)


def exchange(pieces, ties):
    owners = lax.axis_size("dp")
    out = {}
    for k in sorted(pieces, key=lambda k: k in ties):
        piece = lax.optimization_barrier((pieces[k], out[ties[k]]))[0] if k in ties else pieces[k]
        out[k] = lax.ppermute(piece, "dp", [(i, i ^ k) for i in range(owners)])
    return {k: out[k] for k in pieces}


def across_cores(value):
    cores = lax.axis_size("tensor")
    return lax.ppermute(value, "tensor", [(i, i ^ 1) for i in range(cores)])


def with_kernels(activations, cotangent, adapter_weight_pair, adapter_of_block, block_live_length):
    owners = lax.axis_size("dp")
    here = lax.axis_index("dp").astype(jnp.int32).reshape(1)
    ids, lengths = adapter_of_block[:, 0], block_live_length[:, 0]
    count, _, rows, width = adapter_weight_pair.shape
    table = adapter_weight_pair.reshape(count, rows, width)
    tokens, features = activations.shape
    scale = adapter_alpha / (width // 2)
    bf16, f32 = jnp.bfloat16, jnp.float32
    straight = jax.ShapeDtypeStruct((rows, width), bf16)
    pair_bytes = owners * rows * width * 2
    token_bytes = tokens * features * 2

    sent, me = [], here
    for part in (FETCH[:FETCH_FIRST], FETCH[FETCH_FIRST:]):
        sent += call(
            functools.partial(gather_kernel, part),
            [straight] * len(part),
            [in_smem, in_smem, in_hbm],
            [in_vmem] * len(part),
            [pltpu.SemaphoreType.DMA((len(part),))],
            moved=1024,
            vmem=53,
        )(ids, me, table)
        me = lax.optimization_barrier((here, *sent))[0]
    pairs = exchange(dict(zip(FETCH, sent)), FETCH_TIES)

    step = 8
    turned, own, blank = call(
        prep_kernel,
        [
            jax.ShapeDtypeStruct((owners, rows, 2 * tokens), bf16),
            straight,
            jax.ShapeDtypeStruct(table.shape, bf16),
        ],
        [in_smem, in_smem, in_hbm, in_hbm, in_vmem, in_vmem],
        [in_vmem, in_vmem, in_hbm],
        [
            pltpu.VMEM((step, rows, width), bf16),
            pltpu.SemaphoreType.DMA((count // step,)),
            pltpu.SemaphoreType.DMA,
        ],
        moved=4 * token_bytes + 2 * count * rows * width,
    )(ids, here, table, pairs[PREP_AFTER], activations, cotangent)
    pairs[0] = own

    mine = jnp.zeros((tokens, width), f32)
    for part in ([k for k in pairs if k not in RANK_LAST], RANK_LAST):
        mine = call(
            functools.partial(rank_kernel, tuple(part)),
            jax.ShapeDtypeStruct((tokens, width), f32),
            [in_smem] + [in_vmem] * (3 + len(part)),
            in_vmem,
            moved=1024,
        )(here, lax.optimization_barrier((activations, turned))[0], cotangent, mine, *[pairs[k] for k in part])
    other = across_cores(mine)

    peers = (*SEND, 0)
    pieces = []
    for part in (peers[:SEND_FIRST], peers[SEND_FIRST:]):
        pieces += call(
            functools.partial(piece_kernel, part, scale),
            [straight] * len(part),
            [in_smem] * 2 + [in_vmem] * 3,
            [in_vmem] * len(part),
            moved=1024,
        )(here, lengths, mine, other, turned)
    arrived = exchange(dict(zip(SEND, pieces)), SEND_TIES)
    arrived[0] = pieces[-1]

    grad_input = call(
        functools.partial(input_kernel, tuple(pairs), scale),
        jax.ShapeDtypeStruct((tokens, features), bf16),
        [in_smem] * 2 + [in_vmem] * (2 + owners),
        in_vmem,
        flops=2 * tokens * features * width,
        moved=token_bytes + pair_bytes,
    )(here, lengths, lax.optimization_barrier((mine, *pieces))[0], other, *pairs.values())

    late = tuple(k for k in peers if k in LATE)
    early = tuple(k for k in peers if k not in LATE)

    def merge(handled, others, merged, so_far):
        return call(
            functools.partial(merge_kernel, tuple(merged), handled, others),
            jax.ShapeDtypeStruct(table.shape, bf16),
            [in_smem] * 3 + [in_vmem] * len(merged) + [in_hbm],
            in_hbm,
            [
                pltpu.VMEM((rows, width), f32),
                pltpu.VMEM((len(handled), rows, width), bf16),
                pltpu.SemaphoreType.DMA((len(handled),)),
            ],
            moved=2 * pair_bytes,
            aliases={3 + len(merged): 0},
        )(ids, here, lengths, *merged.values(), so_far)

    early_pieces = {k: arrived[k] for k in early}
    gradient = merge(late, early, arrived, merge(early, late, early_pieces, blank))
    return grad_input, gradient[:, None]


def without_kernels(activations, cotangent, adapter_weight_pair, adapter_of_block, block_live_length):
    owners = lax.axis_size("dp")
    here = lax.axis_index("dp")
    count, _, rows, width = adapter_weight_pair.shape
    rank = width // 2
    scale = adapter_alpha / rank
    adapters = adapter_of_block[:, 0]
    lengths = block_live_length[:, 0]
    keep = (jnp.arange(activations.shape[0], dtype=jnp.int32) < lengths[here])[:, None]
    inputs = jnp.where(keep, activations, jnp.zeros_like(activations))
    grads_out = jnp.where(keep, cotangent, jnp.zeros_like(cotangent))
    fetched = lax.all_to_all(
        adapter_weight_pair[:, 0][adapters], "dp", split_axis=0, concat_axis=0, tiled=True
    )
    pair = fetched.reshape(-1, width)
    down, upward = pair[:, :rank], pair[:, rank:]
    f32 = jnp.float32
    hidden_part = jnp.dot(inputs, down, preferred_element_type=f32)
    dhidden_part = scale * jnp.dot(grads_out, upward, preferred_element_type=f32)
    hidden, dhidden = lax.psum((hidden_part, dhidden_part), "tensor")
    hidden16, dhidden16 = hidden.astype(jnp.bfloat16), dhidden.astype(jnp.bfloat16)
    d_down = jnp.dot(inputs.T, dhidden16, preferred_element_type=f32)
    d_up = scale * jnp.dot(grads_out.T, hidden16, preferred_element_type=f32)
    sent = jnp.concatenate([d_down, d_up], axis=1).astype(jnp.bfloat16).reshape(owners, rows, width)
    received = lax.all_to_all(sent, "dp", split_axis=0, concat_axis=0, tiled=True).astype(f32)
    same = adapters[:, None] == adapters[None, :]
    total = jnp.sum(jnp.where(same, lengths[None, :], 0), axis=1).astype(f32)
    summed = jax.ops.segment_sum(received, adapters, num_segments=count)
    denom = jnp.ones((count,), f32).at[adapters].set(jnp.maximum(total, 1.0))
    gradient = (summed / denom[:, None, None]).astype(jnp.bfloat16)
    grad_input = jnp.dot(dhidden16, down.T, preferred_element_type=f32).astype(jnp.bfloat16)
    return grad_input, gradient[:, None]


def solution(mesh):
    owners, cores = mesh.shape["dp"], mesh.shape["tensor"]

    def on_device(activations, cotangent, adapter_weight_pair, *rest):
        rows = adapter_weight_pair.shape[2]
        fits = owners == len(FETCH) + 1 and cores == 2 and rows % 256 == 0
        body = with_kernels if fits else without_kernels
        return body(activations, cotangent, adapter_weight_pair, *rest)

    in_specs = (
        P(("group", "dp"), "tensor"),
        P(("group", "dp"), "tensor"),
        P(None, "tensor", "dp", None),
        P("group", None),
        P("group", None),
    )
    out_specs = (P(("group", "dp"), "tensor"), P("group", "tensor", "dp", None))
    return jax.shard_map(
        on_device, mesh=mesh, in_specs=in_specs, out_specs=out_specs, check_vma=False
    )
```

```python
import functools

import jax
import jax.numpy as jnp
from jax import lax
from jax.experimental import pallas as pl
from jax.experimental.pallas import tpu as pltpu
from jax.sharding import PartitionSpec as P

adapter_alpha = 128.0
FETCH = (4, 1, 2, 5, 6, 3, 7)
FETCH_TIES = {}
SEND = (6, 1, 2, 4, 5, 3, 7)
SEND_TIES = {7: 6}
PREP_AFTER = 1
LATE = (5, 3, 7)
RANK_LAST = (3, 7)
SEND_FIRST = 1
FETCH_FIRST = 1

in_vmem = pl.BlockSpec(memory_space=pltpu.VMEM)
in_smem = pl.BlockSpec(memory_space=pltpu.SMEM)
in_hbm = pl.BlockSpec(memory_space=pltpu.HBM)


def low_lanes(rows, width):
    return lax.broadcasted_iota(jnp.int32, (rows, width), 1) < width // 2


def call(kernel, out_shape, in_specs, out_specs, scratch=(), flops=0, moved=0, aliases=None, vmem=40):
    return pl.pallas_call(
        kernel,
        out_shape=out_shape,
        in_specs=in_specs,
        out_specs=out_specs,
        scratch_shapes=list(scratch),
        input_output_aliases=aliases or {},
        compiler_params=pltpu.CompilerParams(vmem_limit_bytes=vmem * 1024 * 1024),
        cost_estimate=pl.CostEstimate(flops=flops, bytes_accessed=moved, transcendentals=0),
    )


def gather_kernel(peers, ids, here, table, *refs):
    out, sems = refs[: len(peers)], refs[len(peers)]
    copies = [
        pltpu.make_async_copy(table.at[ids[here[0] ^ k]], out[n], sems.at[n])
        for n, k in enumerate(peers)
    ]
    for copy in copies:
        copy.start()
    for copy in copies:
        copy.wait()


def prep_kernel(ids, here, lengths, table, after, x, y, turned, own, live, blocks, blank, zeros, sem, own_sem):
    own_copy = pltpu.make_async_copy(table.at[ids[here[0]]], own, own_sem)
    own_copy.start()
    rows = own.shape[0]
    marked = lax.broadcasted_iota(jnp.int32, live.shape, 0) < lengths[here[0]]
    live[...] = jnp.where(marked, 1.0, 0.0)
    for n in range(ids.shape[0]):
        blocks[0, n] = ids[n]
        blocks[1, n] = lengths[n]
    zeros[...] = jnp.zeros_like(zeros)
    step = zeros.shape[0]
    copies = [
        pltpu.make_async_copy(zeros, blank.at[pl.ds(s, step)], sem.at[s // step])
        for s in range(0, blank.shape[0], step)
    ]
    for copy in copies:
        copy.start()
    tokens = x.shape[0]

    @pl.loop(0, x.shape[1] // rows)
    def _(owner):
        columns = pl.ds(pl.multiple_of(owner * rows, rows), rows)
        turned[owner, :, pl.ds(0, tokens)] = x[:, columns].T
        turned[owner, :, pl.ds(tokens, tokens)] = y[:, columns].T

    for copy in [own_copy, *copies]:
        copy.wait()


def rank_kernel(peers, here, x, y, so_far, *refs):
    pairs, out = refs[: len(peers)], refs[len(peers)]
    rows, width = pairs[0].shape
    tokens = x.shape[0]
    x_rank = so_far[...]
    y_rank = x_rank
    for n, k in enumerate(peers):
        columns = pl.ds(pl.multiple_of((here[0] ^ k) * rows, rows), rows)
        x_rank += jnp.dot(x[:, columns], pairs[n][...], preferred_element_type=jnp.float32)
        y_rank += jnp.dot(y[:, columns], pairs[n][...], preferred_element_type=jnp.float32)
    out[...] = jnp.where(low_lanes(tokens, width), x_rank, y_rank)


def rounded(mine, other, live, scale):
    total = mine[...] + other[...]
    total = jnp.where(low_lanes(*total.shape), total, scale * total)
    return jnp.where(live[...] > 0.0, total, 0.0)


def swap_halves(value):
    return pltpu.roll(value, value.shape[-1] // 2, 1)


def piece_kernel(peers, scale, here, live, mine, other, turned, *refs):
    me = here[0]
    both = swap_halves(rounded(mine, other, live, scale))
    low = low_lanes(*both.shape)
    top = jnp.where(low, both, 0.0).astype(jnp.bfloat16)
    bottom = jnp.where(low, 0.0, both).astype(jnp.bfloat16)
    ranks = jnp.concatenate([top, bottom], axis=0)
    for n, k in enumerate(peers):
        piece = jnp.dot(turned[me ^ k], ranks, preferred_element_type=jnp.float32)
        refs[n][...] = jnp.where(low_lanes(*piece.shape), piece, scale * piece).astype(jnp.bfloat16)


def input_kernel(peers, scale, here, live, mine, other, *refs):
    pairs, out = refs[: len(peers)], refs[len(peers)]
    me = here[0]
    both = swap_halves(rounded(mine, other, live, scale))
    ranks = jnp.where(low_lanes(*both.shape), both, 0.0).astype(jnp.bfloat16)
    rows = pairs[0].shape[0]
    for n, k in enumerate(peers):
        columns = pl.ds(pl.multiple_of((me ^ k) * rows, rows), rows)
        out[:, columns] = lax.dot_general(
            ranks, pairs[n][...], (((1,), (1,)), ((), ())), preferred_element_type=jnp.float32
        ).astype(jnp.bfloat16)


def merge_kernel(peers, handled, others, blocks, here, *refs):
    pieces = dict(zip(peers, refs[:-5]))
    out, total, held, sems = refs[-4:]
    me = here[0]
    width = total.shape[1]
    others_here = all(k in pieces for k in others)

    def value(k):
        return pieces[k][...].astype(jnp.float32)

    def either(conditions):
        return functools.reduce(jnp.logical_or, conditions, jnp.bool_(False))

    copies, chosen = [], []
    for n, k in enumerate(handled):
        adapter = blocks[0, me ^ k]
        copies.append(pltpu.make_async_copy(held.at[n], out.at[adapter], sems.at[n]))
        same = {other: blocks[0, me ^ other] == adapter for other in (*handled, *others) if other != k}
        skip = either([same[other] for other in handled[:n]])
        adding = list(handled[n + 1 :])
        if others_here:
            adding += others
        else:
            skip |= either([same[other] for other in others])
        more = either([same[other] for other in adding])
        chosen.append(jnp.logical_not(skip))

        def store(sum_of, count):
            denom = jnp.maximum(count.astype(jnp.float32), 1.0)
            part = 1.0 / jnp.full((1, width), denom)
            held[n] = (sum_of * part).astype(jnp.bfloat16)
            copies[n].start()

        @pl.when(chosen[n] & jnp.logical_not(more))
        def _():
            store(value(k), blocks[1, me ^ k])

        @pl.when(chosen[n] & more)
        def _():
            total[...] = value(k)
            count = blocks[1, me ^ k]
            for other in adding:
                count += jnp.where(same[other], blocks[1, me ^ other], 0)

                @pl.when(same[other])
                def _():
                    total[...] += value(other)

            store(total[...], count)

    for n in range(len(handled)):
        pl.when(chosen[n])(copies[n].wait)


def exchange(pieces, ties):
    owners = lax.axis_size("dp")
    out = {}
    for k in sorted(pieces, key=lambda k: k in ties):
        piece = lax.optimization_barrier((pieces[k], out[ties[k]]))[0] if k in ties else pieces[k]
        out[k] = lax.ppermute(piece, "dp", [(i, i ^ k) for i in range(owners)])
    return {k: out[k] for k in pieces}


def across_cores(value):
    cores = lax.axis_size("tensor")
    return lax.ppermute(value, "tensor", [(i, i ^ 1) for i in range(cores)])


def with_kernels(activations, cotangent, adapter_weight_pair, adapter_of_block, block_live_length):
    owners = lax.axis_size("dp")
    here = lax.axis_index("dp").astype(jnp.int32).reshape(1)
    ids, lengths = adapter_of_block[:, 0], block_live_length[:, 0]
    count, _, rows, width = adapter_weight_pair.shape
    table = adapter_weight_pair.reshape(count, rows, width)
    tokens, features = activations.shape
    scale = adapter_alpha / (width // 2)
    bf16, f32 = jnp.bfloat16, jnp.float32
    straight = jax.ShapeDtypeStruct((rows, width), bf16)
    pair_bytes = owners * rows * width * 2
    token_bytes = tokens * features * 2

    sent, me = [], here
    for part in (FETCH[:FETCH_FIRST], FETCH[FETCH_FIRST:]):
        sent += call(
            functools.partial(gather_kernel, part),
            [straight] * len(part),
            [in_smem, in_smem, in_hbm],
            [in_vmem] * len(part),
            [pltpu.SemaphoreType.DMA((len(part),))],
            moved=1024,
            vmem=53,
        )(ids, me, table)
        me = lax.optimization_barrier((here, *sent))[0]
    pairs = exchange(dict(zip(FETCH, sent)), FETCH_TIES)

    step = 8
    turned, own, live, blocks, blank = call(
        prep_kernel,
        [
            jax.ShapeDtypeStruct((owners, rows, 2 * tokens), bf16),
            straight,
            jax.ShapeDtypeStruct((tokens, width), f32),
            jax.ShapeDtypeStruct((2, owners), jnp.int32),
            jax.ShapeDtypeStruct(table.shape, bf16),
        ],
        [in_smem, in_smem, in_smem, in_hbm, in_hbm, in_vmem, in_vmem],
        [in_vmem, in_vmem, in_vmem, in_smem, in_hbm],
        [
            pltpu.VMEM((step, rows, width), bf16),
            pltpu.SemaphoreType.DMA((count // step,)),
            pltpu.SemaphoreType.DMA,
        ],
        moved=4 * token_bytes + 2 * count * rows * width,
    )(ids, here, lengths, table, pairs[PREP_AFTER], activations, cotangent)
    pairs[0] = own

    mine = jnp.zeros((tokens, width), f32)
    for part in ([k for k in pairs if k not in RANK_LAST], RANK_LAST):
        mine = call(
            functools.partial(rank_kernel, tuple(part)),
            jax.ShapeDtypeStruct((tokens, width), f32),
            [in_smem] + [in_vmem] * (3 + len(part)),
            in_vmem,
            moved=1024,
        )(here, lax.optimization_barrier((activations, turned))[0], cotangent, mine, *[pairs[k] for k in part])
    other = across_cores(mine)

    peers = (*SEND, 0)
    pieces = []
    for part in (peers[:SEND_FIRST], peers[SEND_FIRST:]):
        pieces += call(
            functools.partial(piece_kernel, part, scale),
            [straight] * len(part),
            [in_smem] + [in_vmem] * 4,
            [in_vmem] * len(part),
            moved=1024,
        )(here, live, mine, other, turned)
    arrived = exchange(dict(zip(SEND, pieces)), SEND_TIES)
    arrived[0] = pieces[-1]

    grad_input = call(
        functools.partial(input_kernel, tuple(pairs), scale),
        jax.ShapeDtypeStruct((tokens, features), bf16),
        [in_smem] + [in_vmem] * (3 + owners),
        in_vmem,
        flops=2 * tokens * features * width,
        moved=token_bytes + pair_bytes,
    )(here, live, lax.optimization_barrier((mine, *pieces))[0], other, *pairs.values())

    late = tuple(k for k in peers if k in LATE)
    early = tuple(k for k in peers if k not in LATE)

    def merge(handled, others, merged, so_far):
        return call(
            functools.partial(merge_kernel, tuple(merged), handled, others),
            jax.ShapeDtypeStruct(table.shape, bf16),
            [in_smem] * 2 + [in_vmem] * len(merged) + [in_hbm],
            in_hbm,
            [
                pltpu.VMEM((rows, width), f32),
                pltpu.VMEM((len(handled), rows, width), bf16),
                pltpu.SemaphoreType.DMA((len(handled),)),
            ],
            moved=2 * pair_bytes,
            aliases={2 + len(merged): 0},
        )(blocks, here, *merged.values(), so_far)

    early_pieces = {k: arrived[k] for k in early}
    gradient = merge(late, early, arrived, merge(early, late, early_pieces, blank))
    return grad_input, gradient[:, None]


def without_kernels(activations, cotangent, adapter_weight_pair, adapter_of_block, block_live_length):
    owners = lax.axis_size("dp")
    here = lax.axis_index("dp")
    count, _, rows, width = adapter_weight_pair.shape
    rank = width // 2
    scale = adapter_alpha / rank
    adapters = adapter_of_block[:, 0]
    lengths = block_live_length[:, 0]
    keep = (jnp.arange(activations.shape[0], dtype=jnp.int32) < lengths[here])[:, None]
    inputs = jnp.where(keep, activations, jnp.zeros_like(activations))
    grads_out = jnp.where(keep, cotangent, jnp.zeros_like(cotangent))
    fetched = lax.all_to_all(
        adapter_weight_pair[:, 0][adapters], "dp", split_axis=0, concat_axis=0, tiled=True
    )
    pair = fetched.reshape(-1, width)
    down, upward = pair[:, :rank], pair[:, rank:]
    f32 = jnp.float32
    hidden_part = jnp.dot(inputs, down, preferred_element_type=f32)
    dhidden_part = scale * jnp.dot(grads_out, upward, preferred_element_type=f32)
    hidden, dhidden = lax.psum((hidden_part, dhidden_part), "tensor")
    hidden16, dhidden16 = hidden.astype(jnp.bfloat16), dhidden.astype(jnp.bfloat16)
    d_down = jnp.dot(inputs.T, dhidden16, preferred_element_type=f32)
    d_up = scale * jnp.dot(grads_out.T, hidden16, preferred_element_type=f32)
    sent = jnp.concatenate([d_down, d_up], axis=1).astype(jnp.bfloat16).reshape(owners, rows, width)
    received = lax.all_to_all(sent, "dp", split_axis=0, concat_axis=0, tiled=True).astype(f32)
    same = adapters[:, None] == adapters[None, :]
    total = jnp.sum(jnp.where(same, lengths[None, :], 0), axis=1).astype(f32)
    summed = jax.ops.segment_sum(received, adapters, num_segments=count)
    denom = jnp.ones((count,), f32).at[adapters].set(jnp.maximum(total, 1.0))
    gradient = (summed / denom[:, None, None]).astype(jnp.bfloat16)
    grad_input = jnp.dot(dhidden16, down.T, preferred_element_type=f32).astype(jnp.bfloat16)
    return grad_input, gradient[:, None]


def solution(mesh):
    owners, cores = mesh.shape["dp"], mesh.shape["tensor"]

    def on_device(activations, cotangent, adapter_weight_pair, *rest):
        rows = adapter_weight_pair.shape[2]
        fits = owners == len(FETCH) + 1 and cores == 2 and rows % 256 == 0
        body = with_kernels if fits else without_kernels
        return body(activations, cotangent, adapter_weight_pair, *rest)

    in_specs = (
        P(("group", "dp"), "tensor"),
        P(("group", "dp"), "tensor"),
        P(None, "tensor", "dp", None),
        P("group", None),
        P("group", None),
    )
    out_specs = (P(("group", "dp"), "tensor"), P("group", "tensor", "dp", None))
    return jax.shard_map(
        on_device, mesh=mesh, in_specs=in_specs, out_specs=out_specs, check_vma=False
    )
```

```python
import functools

import jax
import jax.numpy as jnp
from jax import lax
from jax.experimental import pallas as pl
from jax.experimental.pallas import tpu as pltpu
from jax.sharding import PartitionSpec as P

adapter_alpha = 128.0
FETCH = (4, 1, 2, 6, 5, 3, 7)
FETCH_TIES = {}
SEND = (6, 1, 2, 4, 5, 3, 7)
SEND_TIES = {7: 6}
PREP_AFTER = 1
LATE = (5, 3, 7)
RANK_LAST = (3, 7)
SEND_FIRST = 1
FETCH_FIRST = 1

in_vmem = pl.BlockSpec(memory_space=pltpu.VMEM)
in_smem = pl.BlockSpec(memory_space=pltpu.SMEM)
in_hbm = pl.BlockSpec(memory_space=pltpu.HBM)


def low_lanes(rows, width):
    return lax.broadcasted_iota(jnp.int32, (rows, width), 1) < width // 2


def call(kernel, out_shape, in_specs, out_specs, scratch=(), flops=0, moved=0, aliases=None, vmem=40):
    return pl.pallas_call(
        kernel,
        out_shape=out_shape,
        in_specs=in_specs,
        out_specs=out_specs,
        scratch_shapes=list(scratch),
        input_output_aliases=aliases or {},
        compiler_params=pltpu.CompilerParams(vmem_limit_bytes=vmem * 1024 * 1024),
        cost_estimate=pl.CostEstimate(flops=flops, bytes_accessed=moved, transcendentals=0),
    )


def gather_kernel(peers, ids, here, table, *refs):
    out, sems = refs[: len(peers)], refs[len(peers)]
    copies = [
        pltpu.make_async_copy(table.at[ids[here[0] ^ k]], out[n], sems.at[n])
        for n, k in enumerate(peers)
    ]
    for copy in copies:
        copy.start()
    for copy in copies:
        copy.wait()


def prep_kernel(ids, here, lengths, table, after, x, y, turned, own, live, parts, blocks, blank, zeros, sem, own_sem):
    own_copy = pltpu.make_async_copy(table.at[ids[here[0]]], own, own_sem)
    own_copy.start()
    rows = own.shape[0]
    marked = lax.broadcasted_iota(jnp.int32, live.shape, 0) < lengths[here[0]]
    live[...] = jnp.where(marked, 1.0, 0.0)
    for n in range(ids.shape[0]):
        blocks[n] = ids[n]
        count = jnp.int32(0)
        for other in range(ids.shape[0]):
            count += jnp.where(ids[other] == ids[n], lengths[other], 0)
        denom = jnp.maximum(count.astype(jnp.float32), 1.0)
        parts[n : n + 1] = 1.0 / jnp.full((1, parts.shape[1]), denom)
    zeros[...] = jnp.zeros_like(zeros)
    step = zeros.shape[0]
    copies = [
        pltpu.make_async_copy(zeros, blank.at[pl.ds(s, step)], sem.at[s // step])
        for s in range(0, blank.shape[0], step)
    ]
    for copy in copies:
        copy.start()
    tokens = x.shape[0]

    @pl.loop(0, x.shape[1] // rows)
    def _(owner):
        columns = pl.ds(pl.multiple_of(owner * rows, rows), rows)
        turned[owner, :, pl.ds(0, tokens)] = x[:, columns].T
        turned[owner, :, pl.ds(tokens, tokens)] = y[:, columns].T

    for copy in [own_copy, *copies]:
        copy.wait()


def rank_kernel(peers, here, x, y, so_far, *refs):
    pairs, out = refs[: len(peers)], refs[len(peers)]
    rows, width = pairs[0].shape
    tokens = x.shape[0]
    x_rank = so_far[...]
    y_rank = x_rank
    for n, k in enumerate(peers):
        columns = pl.ds(pl.multiple_of((here[0] ^ k) * rows, rows), rows)
        x_rank += jnp.dot(x[:, columns], pairs[n][...], preferred_element_type=jnp.float32)
        y_rank += jnp.dot(y[:, columns], pairs[n][...], preferred_element_type=jnp.float32)
    out[...] = jnp.where(low_lanes(tokens, width), x_rank, y_rank)


def rounded(mine, other, live, scale):
    total = mine[...] + other[...]
    total = jnp.where(low_lanes(*total.shape), total, scale * total)
    return jnp.where(live[...] > 0.0, total, 0.0)


def swap_halves(value):
    return pltpu.roll(value, value.shape[-1] // 2, 1)


def piece_kernel(peers, scale, here, live, mine, other, turned, *refs):
    me = here[0]
    both = swap_halves(rounded(mine, other, live, scale))
    low = low_lanes(*both.shape)
    top = jnp.where(low, both, 0.0).astype(jnp.bfloat16)
    bottom = jnp.where(low, 0.0, both).astype(jnp.bfloat16)
    ranks = jnp.concatenate([top, bottom], axis=0)
    for n, k in enumerate(peers):
        piece = jnp.dot(turned[me ^ k], ranks, preferred_element_type=jnp.float32)
        refs[n][...] = jnp.where(low_lanes(*piece.shape), piece, scale * piece).astype(jnp.bfloat16)


def input_kernel(peers, scale, here, live, mine, other, *refs):
    pairs, out = refs[: len(peers)], refs[len(peers)]
    me = here[0]
    both = swap_halves(rounded(mine, other, live, scale))
    ranks = jnp.where(low_lanes(*both.shape), both, 0.0).astype(jnp.bfloat16)
    rows = pairs[0].shape[0]
    for n, k in enumerate(peers):
        columns = pl.ds(pl.multiple_of((me ^ k) * rows, rows), rows)
        out[:, columns] = lax.dot_general(
            ranks, pairs[n][...], (((1,), (1,)), ((), ())), preferred_element_type=jnp.float32
        ).astype(jnp.bfloat16)


def merge_kernel(peers, handled, others, blocks, here, parts, *refs):
    pieces = dict(zip(peers, refs[:-7]))
    out, total, held, sems, ids, ids_sem = refs[-6:]
    me = here[0]
    others_here = all(k in pieces for k in others)
    ids_copy = pltpu.make_async_copy(blocks, ids, ids_sem)
    ids_copy.start()

    def value(k):
        return pieces[k][...].astype(jnp.float32)

    def store(n, sum_of):
        held[n] = (sum_of * parts[pl.ds(me ^ handled[n], 1), :]).astype(jnp.bfloat16)

    def either(conditions):
        return functools.reduce(jnp.logical_or, conditions, jnp.bool_(False))

    for n, k in enumerate(handled):
        store(n, value(k))
    ids_copy.wait()
    copies, chosen = [], []
    for n, k in enumerate(handled):
        adapter = ids[me ^ k]
        copies.append(pltpu.make_async_copy(held.at[n], out.at[adapter], sems.at[n]))
        same = {other: ids[me ^ other] == adapter for other in (*handled, *others) if other != k}
        skip = either([same[other] for other in handled[:n]])
        adding = list(handled[n + 1 :])
        if others_here:
            adding += others
        else:
            skip |= either([same[other] for other in others])
        more = either([same[other] for other in adding])
        chosen.append(jnp.logical_not(skip))

        @pl.when(chosen[n] & more)
        def _():
            total[...] = value(k)
            for other in adding:

                @pl.when(same[other])
                def _():
                    total[...] += value(other)

            store(n, total[...])

        pl.when(chosen[n])(copies[n].start)

    for n in range(len(handled)):
        pl.when(chosen[n])(copies[n].wait)


def exchange(pieces, ties):
    owners = lax.axis_size("dp")
    out = {}
    for k in sorted(pieces, key=lambda k: k in ties):
        piece = lax.optimization_barrier((pieces[k], out[ties[k]]))[0] if k in ties else pieces[k]
        out[k] = lax.ppermute(piece, "dp", [(i, i ^ k) for i in range(owners)])
    return {k: out[k] for k in pieces}


def across_cores(value):
    cores = lax.axis_size("tensor")
    return lax.ppermute(value, "tensor", [(i, i ^ 1) for i in range(cores)])


def with_kernels(activations, cotangent, adapter_weight_pair, adapter_of_block, block_live_length):
    owners = lax.axis_size("dp")
    here = lax.axis_index("dp").astype(jnp.int32).reshape(1)
    ids, lengths = adapter_of_block[:, 0], block_live_length[:, 0]
    count, _, rows, width = adapter_weight_pair.shape
    table = adapter_weight_pair.reshape(count, rows, width)
    tokens, features = activations.shape
    scale = adapter_alpha / (width // 2)
    bf16, f32 = jnp.bfloat16, jnp.float32
    straight = jax.ShapeDtypeStruct((rows, width), bf16)
    pair_bytes = owners * rows * width * 2
    token_bytes = tokens * features * 2

    sent, me = [], here
    for part in (FETCH[:FETCH_FIRST], FETCH[FETCH_FIRST:]):
        sent += call(
            functools.partial(gather_kernel, part),
            [straight] * len(part),
            [in_smem, in_smem, in_hbm],
            [in_vmem] * len(part),
            [pltpu.SemaphoreType.DMA((len(part),))],
            moved=1024,
            vmem=53,
        )(ids, me, table)
        me = lax.optimization_barrier((here, *sent))[0]
    pairs = exchange(dict(zip(FETCH, sent)), FETCH_TIES)

    step = 8
    turned, own, live, parts, blocks, blank = call(
        prep_kernel,
        [
            jax.ShapeDtypeStruct((owners, rows, 2 * tokens), bf16),
            straight,
            jax.ShapeDtypeStruct((tokens, width), f32),
            jax.ShapeDtypeStruct((owners, width), f32),
            jax.ShapeDtypeStruct((owners,), jnp.int32),
            jax.ShapeDtypeStruct(table.shape, bf16),
        ],
        [in_smem, in_smem, in_smem, in_hbm, in_hbm, in_vmem, in_vmem],
        [in_vmem, in_vmem, in_vmem, in_vmem, in_smem, in_hbm],
        [
            pltpu.VMEM((step, rows, width), bf16),
            pltpu.SemaphoreType.DMA((count // step,)),
            pltpu.SemaphoreType.DMA,
        ],
        moved=4 * token_bytes + 2 * count * rows * width,
    )(ids, here, lengths, table, pairs[PREP_AFTER], activations, cotangent)
    pairs[0] = own

    mine = jnp.zeros((tokens, width), f32)
    for part in ([k for k in pairs if k not in RANK_LAST], RANK_LAST):
        mine = call(
            functools.partial(rank_kernel, tuple(part)),
            jax.ShapeDtypeStruct((tokens, width), f32),
            [in_smem] + [in_vmem] * (3 + len(part)),
            in_vmem,
            moved=1024,
        )(here, lax.optimization_barrier((activations, turned))[0], cotangent, mine, *[pairs[k] for k in part])
    other = across_cores(mine)

    peers = (*SEND, 0)
    pieces = []
    for part in (peers[:SEND_FIRST], peers[SEND_FIRST:]):
        pieces += call(
            functools.partial(piece_kernel, part, scale),
            [straight] * len(part),
            [in_smem] + [in_vmem] * 4,
            [in_vmem] * len(part),
            moved=1024,
        )(here, live, mine, other, turned)
    arrived = exchange(dict(zip(SEND, pieces)), SEND_TIES)
    arrived[0] = pieces[-1]

    grad_input = call(
        functools.partial(input_kernel, tuple(pairs), scale),
        jax.ShapeDtypeStruct((tokens, features), bf16),
        [in_smem] + [in_vmem] * (3 + owners),
        in_vmem,
        flops=2 * tokens * features * width,
        moved=token_bytes + pair_bytes,
    )(here, live, lax.optimization_barrier((mine, *pieces))[0], other, *pairs.values())

    late = tuple(k for k in peers if k in LATE)
    early = tuple(k for k in peers if k not in LATE)

    def merge(handled, others, merged, so_far):
        return call(
            functools.partial(merge_kernel, tuple(merged), handled, others),
            jax.ShapeDtypeStruct(table.shape, bf16),
            [in_hbm, in_smem, in_vmem] + [in_vmem] * len(merged) + [in_hbm],
            in_hbm,
            [
                pltpu.VMEM((rows, width), f32),
                pltpu.VMEM((len(handled), rows, width), bf16),
                pltpu.SemaphoreType.DMA((len(handled),)),
                pltpu.SMEM((owners,), jnp.int32),
                pltpu.SemaphoreType.DMA,
            ],
            moved=2 * pair_bytes,
            aliases={3 + len(merged): 0},
        )(blocks, here, parts, *merged.values(), so_far)

    early_pieces = {k: arrived[k] for k in early}
    gradient = merge(late, early, arrived, merge(early, late, early_pieces, blank))
    return grad_input, gradient[:, None]


def without_kernels(activations, cotangent, adapter_weight_pair, adapter_of_block, block_live_length):
    owners = lax.axis_size("dp")
    here = lax.axis_index("dp")
    count, _, rows, width = adapter_weight_pair.shape
    rank = width // 2
    scale = adapter_alpha / rank
    adapters = adapter_of_block[:, 0]
    lengths = block_live_length[:, 0]
    keep = (jnp.arange(activations.shape[0], dtype=jnp.int32) < lengths[here])[:, None]
    inputs = jnp.where(keep, activations, jnp.zeros_like(activations))
    grads_out = jnp.where(keep, cotangent, jnp.zeros_like(cotangent))
    fetched = lax.all_to_all(
        adapter_weight_pair[:, 0][adapters], "dp", split_axis=0, concat_axis=0, tiled=True
    )
    pair = fetched.reshape(-1, width)
    down, upward = pair[:, :rank], pair[:, rank:]
    f32 = jnp.float32
    hidden_part = jnp.dot(inputs, down, preferred_element_type=f32)
    dhidden_part = scale * jnp.dot(grads_out, upward, preferred_element_type=f32)
    hidden, dhidden = lax.psum((hidden_part, dhidden_part), "tensor")
    hidden16, dhidden16 = hidden.astype(jnp.bfloat16), dhidden.astype(jnp.bfloat16)
    d_down = jnp.dot(inputs.T, dhidden16, preferred_element_type=f32)
    d_up = scale * jnp.dot(grads_out.T, hidden16, preferred_element_type=f32)
    sent = jnp.concatenate([d_down, d_up], axis=1).astype(jnp.bfloat16).reshape(owners, rows, width)
    received = lax.all_to_all(sent, "dp", split_axis=0, concat_axis=0, tiled=True).astype(f32)
    same = adapters[:, None] == adapters[None, :]
    total = jnp.sum(jnp.where(same, lengths[None, :], 0), axis=1).astype(f32)
    summed = jax.ops.segment_sum(received, adapters, num_segments=count)
    denom = jnp.ones((count,), f32).at[adapters].set(jnp.maximum(total, 1.0))
    gradient = (summed / denom[:, None, None]).astype(jnp.bfloat16)
    grad_input = jnp.dot(dhidden16, down.T, preferred_element_type=f32).astype(jnp.bfloat16)
    return grad_input, gradient[:, None]


def solution(mesh):
    owners, cores = mesh.shape["dp"], mesh.shape["tensor"]

    def on_device(activations, cotangent, adapter_weight_pair, *rest):
        rows = adapter_weight_pair.shape[2]
        fits = owners == len(FETCH) + 1 and cores == 2 and rows % 256 == 0
        body = with_kernels if fits else without_kernels
        return body(activations, cotangent, adapter_weight_pair, *rest)

    in_specs = (
        P(("group", "dp"), "tensor"),
        P(("group", "dp"), "tensor"),
        P(None, "tensor", "dp", None),
        P("group", None),
        P("group", None),
    )
    out_specs = (P(("group", "dp"), "tensor"), P("group", "tensor", "dp", None))
    return jax.shard_map(
        on_device, mesh=mesh, in_specs=in_specs, out_specs=out_specs, check_vma=False
    )
```

```python
import functools

import jax
import jax.numpy as jnp
from jax import lax
from jax.experimental import pallas as pl
from jax.experimental.pallas import tpu as pltpu
from jax.sharding import PartitionSpec as P

adapter_alpha = 128.0
FETCH = (4, 1, 2, 5, 6, 3, 7)
FETCH_TIES = {}
SEND = (6, 1, 2, 4, 5, 3, 7)
SEND_TIES = {3: 6}
PREP_AFTER = 1
LATE = (5, 3, 7)
RANK_LAST = (3, 7)
SEND_FIRST = 1
FETCH_FIRST = 1

in_vmem = pl.BlockSpec(memory_space=pltpu.VMEM)
in_smem = pl.BlockSpec(memory_space=pltpu.SMEM)
in_hbm = pl.BlockSpec(memory_space=pltpu.HBM)


def low_lanes(rows, width):
    return lax.broadcasted_iota(jnp.int32, (rows, width), 1) < width // 2


def call(kernel, out_shape, in_specs, out_specs, scratch=(), flops=0, moved=0, aliases=None, vmem=40):
    return pl.pallas_call(
        kernel,
        out_shape=out_shape,
        in_specs=in_specs,
        out_specs=out_specs,
        scratch_shapes=list(scratch),
        input_output_aliases=aliases or {},
        compiler_params=pltpu.CompilerParams(vmem_limit_bytes=vmem * 1024 * 1024),
        cost_estimate=pl.CostEstimate(flops=flops, bytes_accessed=moved, transcendentals=0),
    )


def gather_kernel(peers, ids, here, table, *refs):
    out, sems = refs[: len(peers)], refs[len(peers)]
    copies = [
        pltpu.make_async_copy(table.at[ids[here[0] ^ k]], out[n], sems.at[n])
        for n, k in enumerate(peers)
    ]
    for copy in copies:
        copy.start()
    for copy in copies:
        copy.wait()


def prep_kernel(ids, here, lengths, table, after, x, y, turned, own, live, parts, blocks, blank, zeros, sem, own_sem):
    own_copy = pltpu.make_async_copy(table.at[ids[here[0]]], own, own_sem)
    own_copy.start()
    rows = own.shape[0]
    marked = lax.broadcasted_iota(jnp.int32, live.shape, 0) < lengths[here[0]]
    live[...] = jnp.where(marked, 1.0, 0.0)
    for n in range(ids.shape[0]):
        blocks[n] = ids[n]
        count = jnp.int32(0)
        for other in range(ids.shape[0]):
            count += jnp.where(ids[other] == ids[n], lengths[other], 0)
        denom = jnp.maximum(count.astype(jnp.float32), 1.0)
        parts[n : n + 1] = 1.0 / jnp.full((1, parts.shape[1]), denom)
    zeros[...] = jnp.zeros_like(zeros)
    step = zeros.shape[0]
    copies = [
        pltpu.make_async_copy(zeros, blank.at[pl.ds(s, step)], sem.at[s // step])
        for s in range(0, blank.shape[0], step)
    ]
    for copy in copies:
        copy.start()
    tokens = x.shape[0]

    @pl.loop(0, x.shape[1] // rows)
    def _(owner):
        columns = pl.ds(pl.multiple_of(owner * rows, rows), rows)
        turned[owner, :, pl.ds(0, tokens)] = x[:, columns].T
        turned[owner, :, pl.ds(tokens, tokens)] = y[:, columns].T

    for copy in [own_copy, *copies]:
        copy.wait()


def rank_kernel(peers, here, x, y, so_far, *refs):
    pairs, out = refs[: len(peers)], refs[len(peers)]
    rows, width = pairs[0].shape
    tokens = x.shape[0]
    x_rank = so_far[...]
    y_rank = x_rank
    for n, k in enumerate(peers):
        columns = pl.ds(pl.multiple_of((here[0] ^ k) * rows, rows), rows)
        x_rank += jnp.dot(x[:, columns], pairs[n][...], preferred_element_type=jnp.float32)
        y_rank += jnp.dot(y[:, columns], pairs[n][...], preferred_element_type=jnp.float32)
    out[...] = jnp.where(low_lanes(tokens, width), x_rank, y_rank)


def rounded(mine, other, live, scale):
    total = mine[...] + other[...]
    total = jnp.where(low_lanes(*total.shape), total, scale * total)
    return jnp.where(live[...] > 0.0, total, 0.0)


def swap_halves(value):
    return pltpu.roll(value, value.shape[-1] // 2, 1)


def piece_kernel(peers, scale, here, live, mine, other, turned, *refs):
    me = here[0]
    both = swap_halves(rounded(mine, other, live, scale))
    low = low_lanes(*both.shape)
    top = jnp.where(low, both, 0.0).astype(jnp.bfloat16)
    bottom = jnp.where(low, 0.0, both).astype(jnp.bfloat16)
    ranks = jnp.concatenate([top, bottom], axis=0)
    for n, k in enumerate(peers):
        piece = jnp.dot(turned[me ^ k], ranks, preferred_element_type=jnp.float32)
        refs[n][...] = jnp.where(low_lanes(*piece.shape), piece, scale * piece).astype(jnp.bfloat16)


def input_kernel(peers, scale, here, live, mine, other, *refs):
    pairs, out = refs[: len(peers)], refs[len(peers)]
    me = here[0]
    both = swap_halves(rounded(mine, other, live, scale))
    ranks = jnp.where(low_lanes(*both.shape), both, 0.0).astype(jnp.bfloat16)
    rows = pairs[0].shape[0]
    for n, k in enumerate(peers):
        columns = pl.ds(pl.multiple_of((me ^ k) * rows, rows), rows)
        out[:, columns] = lax.dot_general(
            ranks, pairs[n][...], (((1,), (1,)), ((), ())), preferred_element_type=jnp.float32
        ).astype(jnp.bfloat16)


def merge_kernel(peers, handled, others, blocks, here, parts, *refs):
    pieces = dict(zip(peers, refs[:-7]))
    out, total, held, sems, ids, ids_sem = refs[-6:]
    me = here[0]
    others_here = all(k in pieces for k in others)
    ids_copy = pltpu.make_async_copy(blocks, ids, ids_sem)
    ids_copy.start()

    def value(k):
        return pieces[k][...].astype(jnp.float32)

    def store(n, sum_of):
        held[n] = (sum_of * parts[pl.ds(me ^ handled[n], 1), :]).astype(jnp.bfloat16)

    def either(conditions):
        return functools.reduce(jnp.logical_or, conditions, jnp.bool_(False))

    for n, k in enumerate(handled):
        store(n, value(k))
    ids_copy.wait()
    copies, chosen = [], []
    for n, k in enumerate(handled):
        adapter = ids[me ^ k]
        copies.append(pltpu.make_async_copy(held.at[n], out.at[adapter], sems.at[n]))
        same = {other: ids[me ^ other] == adapter for other in (*handled, *others) if other != k}
        skip = either([same[other] for other in handled[:n]])
        adding = list(handled[n + 1 :])
        if others_here:
            adding += others
        else:
            skip |= either([same[other] for other in others])
        more = either([same[other] for other in adding])
        chosen.append(jnp.logical_not(skip))

        @pl.when(chosen[n] & more)
        def _():
            total[...] = value(k)
            for other in adding:

                @pl.when(same[other])
                def _():
                    total[...] += value(other)

            store(n, total[...])

        pl.when(chosen[n])(copies[n].start)

    for n in range(len(handled)):
        pl.when(chosen[n])(copies[n].wait)


def exchange(pieces, ties):
    owners = lax.axis_size("dp")
    out = {}
    for k in sorted(pieces, key=lambda k: k in ties):
        piece = lax.optimization_barrier((pieces[k], out[ties[k]]))[0] if k in ties else pieces[k]
        out[k] = lax.ppermute(piece, "dp", [(i, i ^ k) for i in range(owners)])
    return {k: out[k] for k in pieces}


def across_cores(value):
    cores = lax.axis_size("tensor")
    return lax.ppermute(value, "tensor", [(i, i ^ 1) for i in range(cores)])


def with_kernels(activations, cotangent, adapter_weight_pair, adapter_of_block, block_live_length):
    owners = lax.axis_size("dp")
    here = lax.axis_index("dp").astype(jnp.int32).reshape(1)
    ids, lengths = adapter_of_block[:, 0], block_live_length[:, 0]
    count, _, rows, width = adapter_weight_pair.shape
    table = adapter_weight_pair.reshape(count, rows, width)
    tokens, features = activations.shape
    scale = adapter_alpha / (width // 2)
    bf16, f32 = jnp.bfloat16, jnp.float32
    straight = jax.ShapeDtypeStruct((rows, width), bf16)
    pair_bytes = owners * rows * width * 2
    token_bytes = tokens * features * 2

    sent, me = [], here
    for part in (FETCH[:FETCH_FIRST], FETCH[FETCH_FIRST:]):
        sent += call(
            functools.partial(gather_kernel, part),
            [straight] * len(part),
            [in_smem, in_smem, in_hbm],
            [in_vmem] * len(part),
            [pltpu.SemaphoreType.DMA((len(part),))],
            moved=1024,
            vmem=53,
        )(ids, me, table)
        me = lax.optimization_barrier((here, *sent))[0]
    pairs = exchange(dict(zip(FETCH, sent)), FETCH_TIES)

    step = 8
    turned, own, live, parts, blocks, blank = call(
        prep_kernel,
        [
            jax.ShapeDtypeStruct((owners, rows, 2 * tokens), bf16),
            straight,
            jax.ShapeDtypeStruct((tokens, width), f32),
            jax.ShapeDtypeStruct((owners, width), f32),
            jax.ShapeDtypeStruct((owners,), jnp.int32),
            jax.ShapeDtypeStruct(table.shape, bf16),
        ],
        [in_smem, in_smem, in_smem, in_hbm, in_hbm, in_vmem, in_vmem],
        [in_vmem, in_vmem, in_vmem, in_vmem, in_smem, in_hbm],
        [
            pltpu.VMEM((step, rows, width), bf16),
            pltpu.SemaphoreType.DMA((count // step,)),
            pltpu.SemaphoreType.DMA,
        ],
        moved=4 * token_bytes + 2 * count * rows * width,
    )(ids, here, lengths, table, pairs[PREP_AFTER], activations, cotangent)
    pairs[0] = own

    mine = jnp.zeros((tokens, width), f32)
    for part in ([k for k in pairs if k not in RANK_LAST], RANK_LAST):
        mine = call(
            functools.partial(rank_kernel, tuple(part)),
            jax.ShapeDtypeStruct((tokens, width), f32),
            [in_smem] + [in_vmem] * (3 + len(part)),
            in_vmem,
            moved=1024,
        )(here, lax.optimization_barrier((activations, turned))[0], cotangent, mine, *[pairs[k] for k in part])
    other = across_cores(mine)

    peers = (*SEND, 0)
    pieces = []
    for part in (peers[:SEND_FIRST], peers[SEND_FIRST:]):
        pieces += call(
            functools.partial(piece_kernel, part, scale),
            [straight] * len(part),
            [in_smem] + [in_vmem] * 4,
            [in_vmem] * len(part),
            moved=1024,
        )(here, live, mine, other, turned)
    arrived = exchange(dict(zip(SEND, pieces)), SEND_TIES)
    arrived[0] = pieces[-1]

    grad_input = call(
        functools.partial(input_kernel, tuple(pairs), scale),
        jax.ShapeDtypeStruct((tokens, features), bf16),
        [in_smem] + [in_vmem] * (3 + owners),
        in_vmem,
        flops=2 * tokens * features * width,
        moved=token_bytes + pair_bytes,
    )(here, live, lax.optimization_barrier((mine, *pieces))[0], other, *pairs.values())

    late = tuple(k for k in peers if k in LATE)
    early = tuple(k for k in peers if k not in LATE)

    def merge(handled, others, merged, so_far):
        return call(
            functools.partial(merge_kernel, tuple(merged), handled, others),
            jax.ShapeDtypeStruct(table.shape, bf16),
            [in_hbm, in_smem, in_vmem] + [in_vmem] * len(merged) + [in_hbm],
            in_hbm,
            [
                pltpu.VMEM((rows, width), f32),
                pltpu.VMEM((len(handled), rows, width), bf16),
                pltpu.SemaphoreType.DMA((len(handled),)),
                pltpu.SMEM((owners,), jnp.int32),
                pltpu.SemaphoreType.DMA,
            ],
            moved=2 * pair_bytes,
            aliases={3 + len(merged): 0},
        )(blocks, here, parts, *merged.values(), so_far)

    early_pieces = {k: arrived[k] for k in early}
    gradient = merge(late, early, arrived, merge(early, late, early_pieces, blank))
    return grad_input, gradient[:, None]


def without_kernels(activations, cotangent, adapter_weight_pair, adapter_of_block, block_live_length):
    owners = lax.axis_size("dp")
    here = lax.axis_index("dp")
    count, _, rows, width = adapter_weight_pair.shape
    rank = width // 2
    scale = adapter_alpha / rank
    adapters = adapter_of_block[:, 0]
    lengths = block_live_length[:, 0]
    keep = (jnp.arange(activations.shape[0], dtype=jnp.int32) < lengths[here])[:, None]
    inputs = jnp.where(keep, activations, jnp.zeros_like(activations))
    grads_out = jnp.where(keep, cotangent, jnp.zeros_like(cotangent))
    fetched = lax.all_to_all(
        adapter_weight_pair[:, 0][adapters], "dp", split_axis=0, concat_axis=0, tiled=True
    )
    pair = fetched.reshape(-1, width)
    down, upward = pair[:, :rank], pair[:, rank:]
    f32 = jnp.float32
    hidden_part = jnp.dot(inputs, down, preferred_element_type=f32)
    dhidden_part = scale * jnp.dot(grads_out, upward, preferred_element_type=f32)
    hidden, dhidden = lax.psum((hidden_part, dhidden_part), "tensor")
    hidden16, dhidden16 = hidden.astype(jnp.bfloat16), dhidden.astype(jnp.bfloat16)
    d_down = jnp.dot(inputs.T, dhidden16, preferred_element_type=f32)
    d_up = scale * jnp.dot(grads_out.T, hidden16, preferred_element_type=f32)
    sent = jnp.concatenate([d_down, d_up], axis=1).astype(jnp.bfloat16).reshape(owners, rows, width)
    received = lax.all_to_all(sent, "dp", split_axis=0, concat_axis=0, tiled=True).astype(f32)
    same = adapters[:, None] == adapters[None, :]
    total = jnp.sum(jnp.where(same, lengths[None, :], 0), axis=1).astype(f32)
    summed = jax.ops.segment_sum(received, adapters, num_segments=count)
    denom = jnp.ones((count,), f32).at[adapters].set(jnp.maximum(total, 1.0))
    gradient = (summed / denom[:, None, None]).astype(jnp.bfloat16)
    grad_input = jnp.dot(dhidden16, down.T, preferred_element_type=f32).astype(jnp.bfloat16)
    return grad_input, gradient[:, None]


def solution(mesh):
    owners, cores = mesh.shape["dp"], mesh.shape["tensor"]

    def on_device(activations, cotangent, adapter_weight_pair, *rest):
        rows = adapter_weight_pair.shape[2]
        fits = owners == len(FETCH) + 1 and cores == 2 and rows % 256 == 0
        body = with_kernels if fits else without_kernels
        return body(activations, cotangent, adapter_weight_pair, *rest)

    in_specs = (
        P(("group", "dp"), "tensor"),
        P(("group", "dp"), "tensor"),
        P(None, "tensor", "dp", None),
        P("group", None),
        P("group", None),
    )
    out_specs = (P(("group", "dp"), "tensor"), P("group", "tensor", "dp", None))
    return jax.shard_map(
        on_device, mesh=mesh, in_specs=in_specs, out_specs=out_specs, check_vma=False
    )
```

```python
import functools

import jax
import jax.numpy as jnp
from jax import lax
from jax.experimental import pallas as pl
from jax.experimental.pallas import tpu as pltpu
from jax.sharding import PartitionSpec as P

adapter_alpha = 128.0
FETCH = (4, 1, 2, 5, 7, 3, 6)
FETCH_TIES = {}
SEND = (6, 1, 2, 4, 5, 3, 7)
SEND_TIES = {3: 6}
PREP_AFTER = 1
LATE = (5, 3, 7)
RANK_LAST = (3, 6)
SEND_FIRST = 1
FIRST_VMEM = 63
FETCH_FIRST = 1

in_vmem = pl.BlockSpec(memory_space=pltpu.VMEM)
in_smem = pl.BlockSpec(memory_space=pltpu.SMEM)
in_hbm = pl.BlockSpec(memory_space=pltpu.HBM)


def low_lanes(rows, width):
    return lax.broadcasted_iota(jnp.int32, (rows, width), 1) < width // 2


def call(kernel, out_shape, in_specs, out_specs, scratch=(), flops=0, moved=0, aliases=None, vmem=40):
    return pl.pallas_call(
        kernel,
        out_shape=out_shape,
        in_specs=in_specs,
        out_specs=out_specs,
        scratch_shapes=list(scratch),
        input_output_aliases=aliases or {},
        compiler_params=pltpu.CompilerParams(vmem_limit_bytes=vmem * 1024 * 1024),
        cost_estimate=pl.CostEstimate(flops=flops, bytes_accessed=moved, transcendentals=0),
    )


def gather_kernel(peers, ids, here, table, *refs):
    out, sems = refs[: len(peers)], refs[len(peers)]
    copies = [
        pltpu.make_async_copy(table.at[ids[here[0] ^ k]], out[n], sems.at[n])
        for n, k in enumerate(peers)
    ]
    for copy in copies:
        copy.start()
    for copy in copies:
        copy.wait()


def prep_kernel(ids, here, lengths, table, after, x, y, turned, own, live, parts, blocks, blank, zeros, sem, own_sem):
    own_copy = pltpu.make_async_copy(table.at[ids[here[0]]], own, own_sem)
    own_copy.start()
    rows = own.shape[0]
    marked = lax.broadcasted_iota(jnp.int32, live.shape, 0) < lengths[here[0]]
    live[...] = jnp.where(marked, 1.0, 0.0)
    for n in range(ids.shape[0]):
        blocks[n] = ids[n]
        count = jnp.int32(0)
        for other in range(ids.shape[0]):
            count += jnp.where(ids[other] == ids[n], lengths[other], 0)
        denom = jnp.maximum(count.astype(jnp.float32), 1.0)
        parts[n : n + 1] = 1.0 / jnp.full((1, parts.shape[1]), denom)
    zeros[...] = jnp.zeros_like(zeros)
    step = zeros.shape[0]
    copies = [
        pltpu.make_async_copy(zeros, blank.at[pl.ds(s, step)], sem.at[s // step])
        for s in range(0, blank.shape[0], step)
    ]
    for copy in copies:
        copy.start()
    tokens = x.shape[0]

    @pl.loop(0, x.shape[1] // rows)
    def _(owner):
        columns = pl.ds(pl.multiple_of(owner * rows, rows), rows)
        turned[owner, :, pl.ds(0, tokens)] = x[:, columns].T
        turned[owner, :, pl.ds(tokens, tokens)] = y[:, columns].T

    for copy in [own_copy, *copies]:
        copy.wait()


def rank_kernel(peers, here, x, y, so_far, *refs):
    pairs, out = refs[: len(peers)], refs[len(peers)]
    rows, width = pairs[0].shape
    tokens = x.shape[0]
    x_rank = so_far[...]
    y_rank = x_rank
    for n, k in enumerate(peers):
        columns = pl.ds(pl.multiple_of((here[0] ^ k) * rows, rows), rows)
        x_rank += jnp.dot(x[:, columns], pairs[n][...], preferred_element_type=jnp.float32)
        y_rank += jnp.dot(y[:, columns], pairs[n][...], preferred_element_type=jnp.float32)
    out[...] = jnp.where(low_lanes(tokens, width), x_rank, y_rank)


def rounded(mine, other, live, scale):
    total = mine[...] + other[...]
    total = jnp.where(low_lanes(*total.shape), total, scale * total)
    return jnp.where(live[...] > 0.0, total, 0.0)


def swap_halves(value):
    return pltpu.roll(value, value.shape[-1] // 2, 1)


def piece_kernel(peers, scale, here, live, mine, other, turned, *refs):
    me = here[0]
    both = swap_halves(rounded(mine, other, live, scale))
    low = low_lanes(*both.shape)
    top = jnp.where(low, both, 0.0).astype(jnp.bfloat16)
    bottom = jnp.where(low, 0.0, both).astype(jnp.bfloat16)
    ranks = jnp.concatenate([top, bottom], axis=0)
    for n, k in enumerate(peers):
        piece = jnp.dot(turned[me ^ k], ranks, preferred_element_type=jnp.float32)
        refs[n][...] = jnp.where(low_lanes(*piece.shape), piece, scale * piece).astype(jnp.bfloat16)


def input_kernel(peers, scale, here, live, mine, other, *refs):
    pairs, out = refs[: len(peers)], refs[len(peers)]
    me = here[0]
    both = swap_halves(rounded(mine, other, live, scale))
    ranks = jnp.where(low_lanes(*both.shape), both, 0.0).astype(jnp.bfloat16)
    rows = pairs[0].shape[0]
    for n, k in enumerate(peers):
        columns = pl.ds(pl.multiple_of((me ^ k) * rows, rows), rows)
        out[:, columns] = lax.dot_general(
            ranks, pairs[n][...], (((1,), (1,)), ((), ())), preferred_element_type=jnp.float32
        ).astype(jnp.bfloat16)


def merge_kernel(peers, handled, others, blocks, here, parts, *refs):
    pieces = dict(zip(peers, refs[:-7]))
    out, total, held, sems, ids, ids_sem = refs[-6:]
    me = here[0]
    others_here = all(k in pieces for k in others)
    ids_copy = pltpu.make_async_copy(blocks, ids, ids_sem)
    ids_copy.start()

    def value(k):
        return pieces[k][...].astype(jnp.float32)

    def store(n, sum_of):
        held[n] = (sum_of * parts[pl.ds(me ^ handled[n], 1), :]).astype(jnp.bfloat16)

    def either(conditions):
        return functools.reduce(jnp.logical_or, conditions, jnp.bool_(False))

    for n, k in enumerate(handled):
        store(n, value(k))
    ids_copy.wait()
    copies, chosen = [], []
    for n, k in enumerate(handled):
        adapter = ids[me ^ k]
        copies.append(pltpu.make_async_copy(held.at[n], out.at[adapter], sems.at[n]))
        same = {other: ids[me ^ other] == adapter for other in (*handled, *others) if other != k}
        skip = either([same[other] for other in handled[:n]])
        adding = list(handled[n + 1 :])
        if others_here:
            adding += others
        else:
            skip |= either([same[other] for other in others])
        more = either([same[other] for other in adding])
        chosen.append(jnp.logical_not(skip))

        @pl.when(chosen[n] & more)
        def _():
            total[...] = value(k)
            for other in adding:

                @pl.when(same[other])
                def _():
                    total[...] += value(other)

            store(n, total[...])

        pl.when(chosen[n])(copies[n].start)

    for n in range(len(handled)):
        pl.when(chosen[n])(copies[n].wait)


def exchange(pieces, ties):
    owners = lax.axis_size("dp")
    out = {}
    for k in sorted(pieces, key=lambda k: k in ties):
        piece = lax.optimization_barrier((pieces[k], out[ties[k]]))[0] if k in ties else pieces[k]
        out[k] = lax.ppermute(piece, "dp", [(i, i ^ k) for i in range(owners)])
    return {k: out[k] for k in pieces}


def across_cores(value):
    cores = lax.axis_size("tensor")
    return lax.ppermute(value, "tensor", [(i, i ^ 1) for i in range(cores)])


def with_kernels(activations, cotangent, adapter_weight_pair, adapter_of_block, block_live_length):
    owners = lax.axis_size("dp")
    here = lax.axis_index("dp").astype(jnp.int32).reshape(1)
    ids, lengths = adapter_of_block[:, 0], block_live_length[:, 0]
    count, _, rows, width = adapter_weight_pair.shape
    table = adapter_weight_pair.reshape(count, rows, width)
    tokens, features = activations.shape
    scale = adapter_alpha / (width // 2)
    bf16, f32 = jnp.bfloat16, jnp.float32
    straight = jax.ShapeDtypeStruct((rows, width), bf16)
    pair_bytes = owners * rows * width * 2
    token_bytes = tokens * features * 2

    sent, me = [], here
    for part in (FETCH[:FETCH_FIRST], FETCH[FETCH_FIRST:]):
        sent += call(
            functools.partial(gather_kernel, part),
            [straight] * len(part),
            [in_smem, in_smem, in_hbm],
            [in_vmem if sent else in_hbm] * len(part),
            [pltpu.SemaphoreType.DMA((len(part),))],
            moved=1024,
            vmem=53 if sent else FIRST_VMEM,
        )(ids, me, table)
        me = lax.optimization_barrier((here, *sent))[0]
    pairs = exchange(dict(zip(FETCH, sent)), FETCH_TIES)

    step = 8
    turned, own, live, parts, blocks, blank = call(
        prep_kernel,
        [
            jax.ShapeDtypeStruct((owners, rows, 2 * tokens), bf16),
            straight,
            jax.ShapeDtypeStruct((tokens, width), f32),
            jax.ShapeDtypeStruct((owners, width), f32),
            jax.ShapeDtypeStruct((owners,), jnp.int32),
            jax.ShapeDtypeStruct(table.shape, bf16),
        ],
        [in_smem, in_smem, in_smem, in_hbm, in_hbm, in_vmem, in_vmem],
        [in_vmem, in_vmem, in_vmem, in_vmem, in_smem, in_hbm],
        [
            pltpu.VMEM((step, rows, width), bf16),
            pltpu.SemaphoreType.DMA((count // step,)),
            pltpu.SemaphoreType.DMA,
        ],
        moved=4 * token_bytes + 2 * count * rows * width,
    )(ids, here, lengths, table, pairs[PREP_AFTER], activations, cotangent)
    pairs[0] = own

    mine = jnp.zeros((tokens, width), f32)
    for part in ([k for k in pairs if k not in RANK_LAST], RANK_LAST):
        mine = call(
            functools.partial(rank_kernel, tuple(part)),
            jax.ShapeDtypeStruct((tokens, width), f32),
            [in_smem] + [in_vmem] * (3 + len(part)),
            in_vmem,
            moved=1024,
        )(here, lax.optimization_barrier((activations, turned))[0], cotangent, mine, *[pairs[k] for k in part])
    other = across_cores(mine)

    peers = (*SEND, 0)
    pieces = []
    for part in (peers[:SEND_FIRST], peers[SEND_FIRST:]):
        pieces += call(
            functools.partial(piece_kernel, part, scale),
            [straight] * len(part),
            [in_smem] + [in_vmem] * 4,
            [in_vmem] * len(part),
            moved=1024,
        )(here, live, mine, other, turned)
    arrived = exchange(dict(zip(SEND, pieces)), SEND_TIES)
    arrived[0] = pieces[-1]

    grad_input = call(
        functools.partial(input_kernel, tuple(pairs), scale),
        jax.ShapeDtypeStruct((tokens, features), bf16),
        [in_smem] + [in_vmem] * (3 + owners),
        in_vmem,
        flops=2 * tokens * features * width,
        moved=token_bytes + pair_bytes,
    )(here, live, lax.optimization_barrier((mine, *pieces))[0], other, *pairs.values())

    late = tuple(k for k in peers if k in LATE)
    early = tuple(k for k in peers if k not in LATE)

    def merge(handled, others, merged, so_far):
        return call(
            functools.partial(merge_kernel, tuple(merged), handled, others),
            jax.ShapeDtypeStruct(table.shape, bf16),
            [in_hbm, in_smem, in_vmem] + [in_vmem] * len(merged) + [in_hbm],
            in_hbm,
            [
                pltpu.VMEM((rows, width), f32),
                pltpu.VMEM((len(handled), rows, width), bf16),
                pltpu.SemaphoreType.DMA((len(handled),)),
                pltpu.SMEM((owners,), jnp.int32),
                pltpu.SemaphoreType.DMA,
            ],
            moved=2 * pair_bytes,
            aliases={3 + len(merged): 0},
        )(blocks, here, parts, *merged.values(), so_far)

    early_pieces = {k: arrived[k] for k in early}
    gradient = merge(late, early, arrived, merge(early, late, early_pieces, blank))
    return grad_input, gradient[:, None]


def without_kernels(activations, cotangent, adapter_weight_pair, adapter_of_block, block_live_length):
    owners = lax.axis_size("dp")
    here = lax.axis_index("dp")
    count, _, rows, width = adapter_weight_pair.shape
    rank = width // 2
    scale = adapter_alpha / rank
    adapters = adapter_of_block[:, 0]
    lengths = block_live_length[:, 0]
    keep = (jnp.arange(activations.shape[0], dtype=jnp.int32) < lengths[here])[:, None]
    inputs = jnp.where(keep, activations, jnp.zeros_like(activations))
    grads_out = jnp.where(keep, cotangent, jnp.zeros_like(cotangent))
    fetched = lax.all_to_all(
        adapter_weight_pair[:, 0][adapters], "dp", split_axis=0, concat_axis=0, tiled=True
    )
    pair = fetched.reshape(-1, width)
    down, upward = pair[:, :rank], pair[:, rank:]
    f32 = jnp.float32
    hidden_part = jnp.dot(inputs, down, preferred_element_type=f32)
    dhidden_part = scale * jnp.dot(grads_out, upward, preferred_element_type=f32)
    hidden, dhidden = lax.psum((hidden_part, dhidden_part), "tensor")
    hidden16, dhidden16 = hidden.astype(jnp.bfloat16), dhidden.astype(jnp.bfloat16)
    d_down = jnp.dot(inputs.T, dhidden16, preferred_element_type=f32)
    d_up = scale * jnp.dot(grads_out.T, hidden16, preferred_element_type=f32)
    sent = jnp.concatenate([d_down, d_up], axis=1).astype(jnp.bfloat16).reshape(owners, rows, width)
    received = lax.all_to_all(sent, "dp", split_axis=0, concat_axis=0, tiled=True).astype(f32)
    same = adapters[:, None] == adapters[None, :]
    total = jnp.sum(jnp.where(same, lengths[None, :], 0), axis=1).astype(f32)
    summed = jax.ops.segment_sum(received, adapters, num_segments=count)
    denom = jnp.ones((count,), f32).at[adapters].set(jnp.maximum(total, 1.0))
    gradient = (summed / denom[:, None, None]).astype(jnp.bfloat16)
    grad_input = jnp.dot(dhidden16, down.T, preferred_element_type=f32).astype(jnp.bfloat16)
    return grad_input, gradient[:, None]


def solution(mesh):
    owners, cores = mesh.shape["dp"], mesh.shape["tensor"]

    def on_device(activations, cotangent, adapter_weight_pair, *rest):
        rows = adapter_weight_pair.shape[2]
        fits = owners == len(FETCH) + 1 and cores == 2 and rows % 256 == 0
        body = with_kernels if fits else without_kernels
        return body(activations, cotangent, adapter_weight_pair, *rest)

    in_specs = (
        P(("group", "dp"), "tensor"),
        P(("group", "dp"), "tensor"),
        P(None, "tensor", "dp", None),
        P("group", None),
        P("group", None),
    )
    out_specs = (P(("group", "dp"), "tensor"), P("group", "tensor", "dp", None))
    return jax.shard_map(
        on_device, mesh=mesh, in_specs=in_specs, out_specs=out_specs, check_vma=False
    )
```

```python
import functools

import jax
import jax.numpy as jnp
from jax import lax
from jax.experimental import pallas as pl
from jax.experimental.pallas import tpu as pltpu
from jax.sharding import PartitionSpec as P

adapter_alpha = 128.0
FETCH = (4, 1, 2, 5, 6, 3, 7)
FETCH_TIES = {}
SEND = (6, 1, 2, 4, 5, 3, 7)
SEND_TIES = {3: 6}
PREP_AFTER = 1
LATE = (5, 3, 7)
RANK_LAST = (3, 7)
SEND_FIRST = 1
FETCH_FIRST = 1

in_vmem = pl.BlockSpec(memory_space=pltpu.VMEM)
in_smem = pl.BlockSpec(memory_space=pltpu.SMEM)
in_hbm = pl.BlockSpec(memory_space=pltpu.HBM)


def low_lanes(rows, width):
    return lax.broadcasted_iota(jnp.int32, (rows, width), 1) < width // 2


def call(kernel, out_shape, in_specs, out_specs, scratch=(), flops=0, moved=0, aliases=None, vmem=40):
    return pl.pallas_call(
        kernel,
        out_shape=out_shape,
        in_specs=in_specs,
        out_specs=out_specs,
        scratch_shapes=list(scratch),
        input_output_aliases=aliases or {},
        compiler_params=pltpu.CompilerParams(vmem_limit_bytes=vmem * 1024 * 1024),
        cost_estimate=pl.CostEstimate(flops=flops, bytes_accessed=moved, transcendentals=0),
    )


def gather_kernel(peers, ids, here, table, *refs):
    out, sems = refs[: len(peers)], refs[len(peers)]
    copies = [
        pltpu.make_async_copy(table.at[ids[here[0] ^ k]], out[n], sems.at[n])
        for n, k in enumerate(peers)
    ]
    for copy in copies:
        copy.start()
    for copy in copies:
        copy.wait()


def prep_kernel(ids, here, lengths, table, after, x, y, turned, own, live, parts, blank, zeros, sem, own_sem):
    own_copy = pltpu.make_async_copy(table.at[ids[here[0]]], own, own_sem)
    own_copy.start()
    rows = own.shape[0]
    marked = lax.broadcasted_iota(jnp.int32, live.shape, 0) < lengths[here[0]]
    live[...] = jnp.where(marked, 1.0, 0.0)
    for n in range(ids.shape[0]):
        count = jnp.int32(0)
        for other in range(ids.shape[0]):
            count += jnp.where(ids[other] == ids[n], lengths[other], 0)
        denom = jnp.maximum(count.astype(jnp.float32), 1.0)
        parts[n : n + 1] = 1.0 / jnp.full((1, parts.shape[1]), denom)
    zeros[...] = jnp.zeros_like(zeros)
    step = zeros.shape[0]
    copies = [
        pltpu.make_async_copy(zeros, blank.at[pl.ds(s, step)], sem.at[s // step])
        for s in range(0, blank.shape[0], step)
    ]
    for copy in copies:
        copy.start()
    tokens = x.shape[0]

    @pl.loop(0, x.shape[1] // rows)
    def _(owner):
        columns = pl.ds(pl.multiple_of(owner * rows, rows), rows)
        turned[owner, :, pl.ds(0, tokens)] = x[:, columns].T
        turned[owner, :, pl.ds(tokens, tokens)] = y[:, columns].T

    for copy in [own_copy, *copies]:
        copy.wait()


def rank_kernel(peers, here, x, y, so_far, *refs):
    pairs, out = refs[: len(peers)], refs[len(peers)]
    rows, width = pairs[0].shape
    tokens = x.shape[0]
    x_rank = so_far[...]
    y_rank = x_rank
    for n, k in enumerate(peers):
        columns = pl.ds(pl.multiple_of((here[0] ^ k) * rows, rows), rows)
        x_rank += jnp.dot(x[:, columns], pairs[n][...], preferred_element_type=jnp.float32)
        y_rank += jnp.dot(y[:, columns], pairs[n][...], preferred_element_type=jnp.float32)
    out[...] = jnp.where(low_lanes(tokens, width), x_rank, y_rank)


def rounded(mine, other, live, scale):
    total = mine[...] + other[...]
    total = jnp.where(low_lanes(*total.shape), total, scale * total)
    return jnp.where(live[...] > 0.0, total, 0.0)


def swap_halves(value):
    return pltpu.roll(value, value.shape[-1] // 2, 1)


def piece_kernel(peers, scale, here, live, mine, other, turned, *refs):
    me = here[0]
    both = swap_halves(rounded(mine, other, live, scale))
    low = low_lanes(*both.shape)
    top = jnp.where(low, both, 0.0).astype(jnp.bfloat16)
    bottom = jnp.where(low, 0.0, both).astype(jnp.bfloat16)
    ranks = jnp.concatenate([top, bottom], axis=0)
    for n, k in enumerate(peers):
        piece = jnp.dot(turned[me ^ k], ranks, preferred_element_type=jnp.float32)
        refs[n][...] = jnp.where(low_lanes(*piece.shape), piece, scale * piece).astype(jnp.bfloat16)


def input_kernel(peers, scale, here, live, mine, other, *refs):
    pairs, out = refs[: len(peers)], refs[len(peers)]
    me = here[0]
    both = swap_halves(rounded(mine, other, live, scale))
    ranks = jnp.where(low_lanes(*both.shape), both, 0.0).astype(jnp.bfloat16)
    rows = pairs[0].shape[0]
    for n, k in enumerate(peers):
        columns = pl.ds(pl.multiple_of((me ^ k) * rows, rows), rows)
        out[:, columns] = lax.dot_general(
            ranks, pairs[n][...], (((1,), (1,)), ((), ())), preferred_element_type=jnp.float32
        ).astype(jnp.bfloat16)


def adapter_words(ids, bits):
    per_word = 31 // bits
    words = []
    for start in range(0, ids.shape[0], per_word):
        group = ids[start : start + per_word]
        words.append(jnp.sum(group << (bits * jnp.arange(group.shape[0], dtype=jnp.int32))))
    return words


def adapter_from(words, bits, block):
    per_word = 31 // bits
    word = words[0][0]
    for n in range(1, len(words)):
        word = jnp.where(block >= n * per_word, words[n][0], word)
    return (word >> (bits * lax.rem(block, per_word))) & (2**bits - 1)


def merge_kernel(peers, handled, others, bits, n_words, *refs):
    words, (here, parts), refs = refs[:n_words], refs[n_words : n_words + 2], refs[n_words + 2 :]
    pieces = dict(zip(peers, refs[:-5]))
    out, total, held, sems = refs[-4:]
    me = here[0]
    others_here = all(k in pieces for k in others)
    ids = {k: adapter_from(words, bits, me ^ k) for k in (*handled, *others)}

    def value(k):
        return pieces[k][...].astype(jnp.float32)

    def store(n, sum_of):
        held[n] = (sum_of * parts[pl.ds(me ^ handled[n], 1), :]).astype(jnp.bfloat16)

    def either(conditions):
        return functools.reduce(jnp.logical_or, conditions, jnp.bool_(False))

    for n, k in enumerate(handled):
        store(n, value(k))
    copies, chosen = [], []
    for n, k in enumerate(handled):
        adapter = ids[k]
        copies.append(pltpu.make_async_copy(held.at[n], out.at[adapter], sems.at[n]))
        same = {other: ids[other] == adapter for other in (*handled, *others) if other != k}
        skip = either([same[other] for other in handled[:n]])
        adding = list(handled[n + 1 :])
        if others_here:
            adding += others
        else:
            skip |= either([same[other] for other in others])
        more = either([same[other] for other in adding])
        chosen.append(jnp.logical_not(skip))

        @pl.when(chosen[n] & more)
        def _():
            total[...] = value(k)
            for other in adding:

                @pl.when(same[other])
                def _():
                    total[...] += value(other)

            store(n, total[...])

        pl.when(chosen[n])(copies[n].start)

    for n in range(len(handled)):
        pl.when(chosen[n])(copies[n].wait)


def exchange(pieces, ties):
    owners = lax.axis_size("dp")
    out = {}
    for k in sorted(pieces, key=lambda k: k in ties):
        piece = lax.optimization_barrier((pieces[k], out[ties[k]]))[0] if k in ties else pieces[k]
        out[k] = lax.ppermute(piece, "dp", [(i, i ^ k) for i in range(owners)])
    return {k: out[k] for k in pieces}


def across_cores(value):
    cores = lax.axis_size("tensor")
    return lax.ppermute(value, "tensor", [(i, i ^ 1) for i in range(cores)])


def with_kernels(activations, cotangent, adapter_weight_pair, adapter_of_block, block_live_length):
    owners = lax.axis_size("dp")
    here = lax.axis_index("dp").astype(jnp.int32).reshape(1)
    ids, lengths = adapter_of_block[:, 0], block_live_length[:, 0]
    count, _, rows, width = adapter_weight_pair.shape
    table = adapter_weight_pair.reshape(count, rows, width)
    tokens, features = activations.shape
    scale = adapter_alpha / (width // 2)
    bf16, f32 = jnp.bfloat16, jnp.float32
    straight = jax.ShapeDtypeStruct((rows, width), bf16)
    pair_bytes = owners * rows * width * 2
    token_bytes = tokens * features * 2

    sent, me = [], here
    for part in (FETCH[:FETCH_FIRST], FETCH[FETCH_FIRST:]):
        sent += call(
            functools.partial(gather_kernel, part),
            [straight] * len(part),
            [in_smem, in_smem, in_hbm],
            [in_vmem] * len(part),
            [pltpu.SemaphoreType.DMA((len(part),))],
            moved=1024,
            vmem=53,
        )(ids, me, table)
        me = lax.optimization_barrier((here, *sent))[0]
    pairs = exchange(dict(zip(FETCH, sent)), FETCH_TIES)

    step = 8
    turned, own, live, parts, blank = call(
        prep_kernel,
        [
            jax.ShapeDtypeStruct((owners, rows, 2 * tokens), bf16),
            straight,
            jax.ShapeDtypeStruct((tokens, width), f32),
            jax.ShapeDtypeStruct((owners, width), f32),
            jax.ShapeDtypeStruct(table.shape, bf16),
        ],
        [in_smem, in_smem, in_smem, in_hbm, in_hbm, in_vmem, in_vmem],
        [in_vmem, in_vmem, in_vmem, in_vmem, in_hbm],
        [
            pltpu.VMEM((step, rows, width), bf16),
            pltpu.SemaphoreType.DMA((count // step,)),
            pltpu.SemaphoreType.DMA,
        ],
        moved=4 * token_bytes + 2 * count * rows * width,
    )(ids, here, lengths, table, pairs[PREP_AFTER], activations, cotangent)
    pairs[0] = own

    mine = jnp.zeros((tokens, width), f32)
    for part in ([k for k in pairs if k not in RANK_LAST], RANK_LAST):
        mine = call(
            functools.partial(rank_kernel, tuple(part)),
            jax.ShapeDtypeStruct((tokens, width), f32),
            [in_smem] + [in_vmem] * (3 + len(part)),
            in_vmem,
            moved=1024,
        )(here, lax.optimization_barrier((activations, turned))[0], cotangent, mine, *[pairs[k] for k in part])
    other = across_cores(mine)

    peers = (*SEND, 0)
    pieces = []
    for part in (peers[:SEND_FIRST], peers[SEND_FIRST:]):
        pieces += call(
            functools.partial(piece_kernel, part, scale),
            [straight] * len(part),
            [in_smem] + [in_vmem] * 4,
            [in_vmem] * len(part),
            moved=1024,
        )(here, live, mine, other, turned)
    arrived = exchange(dict(zip(SEND, pieces)), SEND_TIES)
    arrived[0] = pieces[-1]

    grad_input = call(
        functools.partial(input_kernel, tuple(pairs), scale),
        jax.ShapeDtypeStruct((tokens, features), bf16),
        [in_smem] + [in_vmem] * (3 + owners),
        in_vmem,
        flops=2 * tokens * features * width,
        moved=token_bytes + pair_bytes,
    )(here, live, lax.optimization_barrier((mine, *pieces))[0], other, *pairs.values())

    bits = (count - 1).bit_length()
    words = [word.reshape(1) for word in adapter_words(ids, bits)]
    late = tuple(k for k in peers if k in LATE)
    early = tuple(k for k in peers if k not in LATE)

    def merge(handled, others, merged, so_far):
        return call(
            functools.partial(merge_kernel, tuple(merged), handled, others, bits, len(words)),
            jax.ShapeDtypeStruct(table.shape, bf16),
            [in_smem] * (len(words) + 1) + [in_vmem] * (1 + len(merged)) + [in_hbm],
            in_hbm,
            [
                pltpu.VMEM((rows, width), f32),
                pltpu.VMEM((len(handled), rows, width), bf16),
                pltpu.SemaphoreType.DMA((len(handled),)),
            ],
            moved=2 * pair_bytes,
            aliases={2 + len(words) + len(merged): 0},
        )(*words, here, parts, *merged.values(), so_far)

    early_pieces = {k: arrived[k] for k in early}
    gradient = merge(late, early, arrived, merge(early, late, early_pieces, blank))
    return grad_input, gradient[:, None]


def without_kernels(activations, cotangent, adapter_weight_pair, adapter_of_block, block_live_length):
    owners = lax.axis_size("dp")
    here = lax.axis_index("dp")
    count, _, rows, width = adapter_weight_pair.shape
    rank = width // 2
    scale = adapter_alpha / rank
    adapters = adapter_of_block[:, 0]
    lengths = block_live_length[:, 0]
    keep = (jnp.arange(activations.shape[0], dtype=jnp.int32) < lengths[here])[:, None]
    inputs = jnp.where(keep, activations, jnp.zeros_like(activations))
    grads_out = jnp.where(keep, cotangent, jnp.zeros_like(cotangent))
    fetched = lax.all_to_all(
        adapter_weight_pair[:, 0][adapters], "dp", split_axis=0, concat_axis=0, tiled=True
    )
    pair = fetched.reshape(-1, width)
    down, upward = pair[:, :rank], pair[:, rank:]
    f32 = jnp.float32
    hidden_part = jnp.dot(inputs, down, preferred_element_type=f32)
    dhidden_part = scale * jnp.dot(grads_out, upward, preferred_element_type=f32)
    hidden, dhidden = lax.psum((hidden_part, dhidden_part), "tensor")
    hidden16, dhidden16 = hidden.astype(jnp.bfloat16), dhidden.astype(jnp.bfloat16)
    d_down = jnp.dot(inputs.T, dhidden16, preferred_element_type=f32)
    d_up = scale * jnp.dot(grads_out.T, hidden16, preferred_element_type=f32)
    sent = jnp.concatenate([d_down, d_up], axis=1).astype(jnp.bfloat16).reshape(owners, rows, width)
    received = lax.all_to_all(sent, "dp", split_axis=0, concat_axis=0, tiled=True).astype(f32)
    same = adapters[:, None] == adapters[None, :]
    total = jnp.sum(jnp.where(same, lengths[None, :], 0), axis=1).astype(f32)
    summed = jax.ops.segment_sum(received, adapters, num_segments=count)
    denom = jnp.ones((count,), f32).at[adapters].set(jnp.maximum(total, 1.0))
    gradient = (summed / denom[:, None, None]).astype(jnp.bfloat16)
    grad_input = jnp.dot(dhidden16, down.T, preferred_element_type=f32).astype(jnp.bfloat16)
    return grad_input, gradient[:, None]


def solution(mesh):
    owners, cores = mesh.shape["dp"], mesh.shape["tensor"]

    def on_device(activations, cotangent, adapter_weight_pair, *rest):
        rows = adapter_weight_pair.shape[2]
        fits = owners == len(FETCH) + 1 and cores == 2 and rows % 256 == 0
        body = with_kernels if fits else without_kernels
        return body(activations, cotangent, adapter_weight_pair, *rest)

    in_specs = (
        P(("group", "dp"), "tensor"),
        P(("group", "dp"), "tensor"),
        P(None, "tensor", "dp", None),
        P("group", None),
        P("group", None),
    )
    out_specs = (P(("group", "dp"), "tensor"), P("group", "tensor", "dp", None))
    return jax.shard_map(
        on_device, mesh=mesh, in_specs=in_specs, out_specs=out_specs, check_vma=False
    )
```

```python
import functools

import jax
import jax.numpy as jnp
from jax import lax
from jax.experimental import pallas as pl
from jax.experimental.pallas import tpu as pltpu
from jax.sharding import PartitionSpec as P

adapter_alpha = 128.0
FETCH = (4, 1, 2, 5, 6, 3, 7)
FETCH_TIES = {}
SEND = (6, 1, 2, 4, 5, 3, 7)
SEND_TIES = {3: 6}
PREP_AFTER = 1
LATE = (5, 3, 7)
RANK_LAST = (3, 7)
SEND_FIRST = 1
FETCH_FIRST = 1

in_vmem = pl.BlockSpec(memory_space=pltpu.VMEM)
in_smem = pl.BlockSpec(memory_space=pltpu.SMEM)
in_hbm = pl.BlockSpec(memory_space=pltpu.HBM)


def low_lanes(rows, width):
    return lax.broadcasted_iota(jnp.int32, (rows, width), 1) < width // 2


def call(kernel, out_shape, in_specs, out_specs, scratch=(), flops=0, moved=0, aliases=None, vmem=40):
    return pl.pallas_call(
        kernel,
        out_shape=out_shape,
        in_specs=in_specs,
        out_specs=out_specs,
        scratch_shapes=list(scratch),
        input_output_aliases=aliases or {},
        compiler_params=pltpu.CompilerParams(vmem_limit_bytes=vmem * 1024 * 1024),
        cost_estimate=pl.CostEstimate(flops=flops, bytes_accessed=moved, transcendentals=0),
    )


def gather_kernel(peers, ids, here, table, *refs):
    out, sems = refs[: len(peers)], refs[len(peers)]
    copies = [
        pltpu.make_async_copy(table.at[ids[here[0] ^ k]], out[n], sems.at[n])
        for n, k in enumerate(peers)
    ]
    for copy in copies:
        copy.start()
    for copy in copies:
        copy.wait()


def either(conditions):
    return functools.reduce(jnp.logical_or, conditions, jnp.bool_(False))


def prep_kernel(groups, ids, here, lengths, table, after, x, y, turned, own, live, parts, words, blocks, blank, zeros, sem, own_sem):
    own_copy = pltpu.make_async_copy(table.at[ids[here[0]]], own, own_sem)
    own_copy.start()
    rows = own.shape[0]
    marked = lax.broadcasted_iota(jnp.int32, live.shape, 0) < lengths[here[0]]
    live[...] = jnp.where(marked, 1.0, 0.0)
    for n in range(ids.shape[0]):
        blocks[n] = ids[n]
        count = jnp.int32(0)
        for other in range(ids.shape[0]):
            count += jnp.where(ids[other] == ids[n], lengths[other], 0)
        denom = jnp.maximum(count.astype(jnp.float32), 1.0)
        parts[n : n + 1] = 1.0 / jnp.full((1, parts.shape[1]), denom)
    me = here[0]
    early, late = groups
    for k in range(ids.shape[0]):
        same = {other: ids[me ^ other] == ids[me ^ k] for other in range(ids.shape[0]) if other != k}
        group, others = (late, early) if k in late else (early, late)
        place = group.index(k)
        skip = either([same[other] for other in group[:place]])
        adding = list(group[place + 1 :])
        if k in late:
            adding += others
        else:
            skip |= either([same[other] for other in others])
        more = either([same[other] for other in adding])
        word = ids[me ^ k] + jnp.where(skip, 2**16, 0) + jnp.where(more, 2**17, 0)
        words[k : k + 1] = jnp.full((1, words.shape[1]), word)
    zeros[...] = jnp.zeros_like(zeros)
    step = zeros.shape[0]
    copies = [
        pltpu.make_async_copy(zeros, blank.at[pl.ds(s, step)], sem.at[s // step])
        for s in range(0, blank.shape[0], step)
    ]
    for copy in copies:
        copy.start()
    tokens = x.shape[0]

    @pl.loop(0, x.shape[1] // rows)
    def _(owner):
        columns = pl.ds(pl.multiple_of(owner * rows, rows), rows)
        turned[owner, :, pl.ds(0, tokens)] = x[:, columns].T
        turned[owner, :, pl.ds(tokens, tokens)] = y[:, columns].T

    for copy in [own_copy, *copies]:
        copy.wait()


def rank_kernel(peers, here, x, y, so_far, *refs):
    pairs, out = refs[: len(peers)], refs[len(peers)]
    rows, width = pairs[0].shape
    tokens = x.shape[0]
    x_rank = so_far[...]
    y_rank = x_rank
    for n, k in enumerate(peers):
        columns = pl.ds(pl.multiple_of((here[0] ^ k) * rows, rows), rows)
        x_rank += jnp.dot(x[:, columns], pairs[n][...], preferred_element_type=jnp.float32)
        y_rank += jnp.dot(y[:, columns], pairs[n][...], preferred_element_type=jnp.float32)
    out[...] = jnp.where(low_lanes(tokens, width), x_rank, y_rank)


def rounded(mine, other, live, scale):
    total = mine[...] + other[...]
    total = jnp.where(low_lanes(*total.shape), total, scale * total)
    return jnp.where(live[...] > 0.0, total, 0.0)


def swap_halves(value):
    return pltpu.roll(value, value.shape[-1] // 2, 1)


def piece_kernel(peers, scale, here, live, mine, other, turned, *refs):
    me = here[0]
    both = swap_halves(rounded(mine, other, live, scale))
    low = low_lanes(*both.shape)
    top = jnp.where(low, both, 0.0).astype(jnp.bfloat16)
    bottom = jnp.where(low, 0.0, both).astype(jnp.bfloat16)
    ranks = jnp.concatenate([top, bottom], axis=0)
    for n, k in enumerate(peers):
        piece = jnp.dot(turned[me ^ k], ranks, preferred_element_type=jnp.float32)
        refs[n][...] = jnp.where(low_lanes(*piece.shape), piece, scale * piece).astype(jnp.bfloat16)


def input_kernel(peers, scale, here, live, mine, other, *refs):
    pairs, out = refs[: len(peers)], refs[len(peers)]
    me = here[0]
    both = swap_halves(rounded(mine, other, live, scale))
    ranks = jnp.where(low_lanes(*both.shape), both, 0.0).astype(jnp.bfloat16)
    rows = pairs[0].shape[0]
    for n, k in enumerate(peers):
        columns = pl.ds(pl.multiple_of((me ^ k) * rows, rows), rows)
        out[:, columns] = lax.dot_general(
            ranks, pairs[n][...], (((1,), (1,)), ((), ())), preferred_element_type=jnp.float32
        ).astype(jnp.bfloat16)


def merge_kernel(peers, handled, others, blocks, here, parts, words, *refs):
    pieces = dict(zip(peers, refs[:-7]))
    out, total, held, sems, ids, ids_sem = refs[-6:]
    me = here[0]
    others_here = all(k in pieces for k in others)

    def value(k):
        return pieces[k][...].astype(jnp.float32)

    def store(n, sum_of):
        held[n] = (sum_of * parts[pl.ds(me ^ handled[n], 1), :]).astype(jnp.bfloat16)

    copies, chosen = [], []
    for n, k in enumerate(handled):
        word = jnp.max(words[k : k + 1, :])
        adapter = word & (2**16 - 1)
        more = (word >> 17) == 1
        copies.append(pltpu.make_async_copy(held.at[n], out.at[adapter], sems.at[n]))
        chosen.append(((word >> 16) & 1) == 0)
        store(n, value(k))

        @pl.when(chosen[n] & more)
        def _():
            ids_copy = pltpu.make_async_copy(blocks, ids, ids_sem)
            ids_copy.start()
            ids_copy.wait()
            total[...] = value(k)
            for other in (*handled[n + 1 :], *(others if others_here else ())):

                @pl.when(ids[me ^ other] == adapter)
                def _():
                    total[...] += value(other)

            store(n, total[...])

        pl.when(chosen[n])(copies[n].start)

    for n in range(len(handled)):
        pl.when(chosen[n])(copies[n].wait)


def exchange(pieces, ties):
    owners = lax.axis_size("dp")
    out = {}
    for k in sorted(pieces, key=lambda k: k in ties):
        piece = lax.optimization_barrier((pieces[k], out[ties[k]]))[0] if k in ties else pieces[k]
        out[k] = lax.ppermute(piece, "dp", [(i, i ^ k) for i in range(owners)])
    return {k: out[k] for k in pieces}


def across_cores(value):
    cores = lax.axis_size("tensor")
    return lax.ppermute(value, "tensor", [(i, i ^ 1) for i in range(cores)])


def with_kernels(activations, cotangent, adapter_weight_pair, adapter_of_block, block_live_length):
    owners = lax.axis_size("dp")
    here = lax.axis_index("dp").astype(jnp.int32).reshape(1)
    ids, lengths = adapter_of_block[:, 0], block_live_length[:, 0]
    count, _, rows, width = adapter_weight_pair.shape
    table = adapter_weight_pair.reshape(count, rows, width)
    tokens, features = activations.shape
    scale = adapter_alpha / (width // 2)
    bf16, f32 = jnp.bfloat16, jnp.float32
    straight = jax.ShapeDtypeStruct((rows, width), bf16)
    pair_bytes = owners * rows * width * 2
    token_bytes = tokens * features * 2

    sent, me = [], here
    for part in (FETCH[:FETCH_FIRST], FETCH[FETCH_FIRST:]):
        sent += call(
            functools.partial(gather_kernel, part),
            [straight] * len(part),
            [in_smem, in_smem, in_hbm],
            [in_vmem] * len(part),
            [pltpu.SemaphoreType.DMA((len(part),))],
            moved=1024,
            vmem=53,
        )(ids, me, table)
        me = lax.optimization_barrier((here, *sent))[0]
    pairs = exchange(dict(zip(FETCH, sent)), FETCH_TIES)

    peers = (*SEND, 0)
    late = tuple(k for k in peers if k in LATE)
    early = tuple(k for k in peers if k not in LATE)
    step = 8
    turned, own, live, parts, words, blocks, blank = call(
        functools.partial(prep_kernel, (early, late)),
        [
            jax.ShapeDtypeStruct((owners, rows, 2 * tokens), bf16),
            straight,
            jax.ShapeDtypeStruct((tokens, width), f32),
            jax.ShapeDtypeStruct((owners, width), f32),
            jax.ShapeDtypeStruct((owners, width), jnp.int32),
            jax.ShapeDtypeStruct((owners,), jnp.int32),
            jax.ShapeDtypeStruct(table.shape, bf16),
        ],
        [in_smem, in_smem, in_smem, in_hbm, in_hbm, in_vmem, in_vmem],
        [in_vmem, in_vmem, in_vmem, in_vmem, in_vmem, in_smem, in_hbm],
        [
            pltpu.VMEM((step, rows, width), bf16),
            pltpu.SemaphoreType.DMA((count // step,)),
            pltpu.SemaphoreType.DMA,
        ],
        moved=4 * token_bytes + 2 * count * rows * width,
    )(ids, here, lengths, table, pairs[PREP_AFTER], activations, cotangent)
    pairs[0] = own

    mine = jnp.zeros((tokens, width), f32)
    for part in ([k for k in pairs if k not in RANK_LAST], RANK_LAST):
        mine = call(
            functools.partial(rank_kernel, tuple(part)),
            jax.ShapeDtypeStruct((tokens, width), f32),
            [in_smem] + [in_vmem] * (3 + len(part)),
            in_vmem,
            moved=1024,
        )(here, lax.optimization_barrier((activations, turned))[0], cotangent, mine, *[pairs[k] for k in part])
    other = across_cores(mine)

    pieces = []
    for part in (peers[:SEND_FIRST], peers[SEND_FIRST:]):
        pieces += call(
            functools.partial(piece_kernel, part, scale),
            [straight] * len(part),
            [in_smem] + [in_vmem] * 4,
            [in_vmem] * len(part),
            moved=1024,
        )(here, live, mine, other, turned)
    arrived = exchange(dict(zip(SEND, pieces)), SEND_TIES)
    arrived[0] = pieces[-1]

    grad_input = call(
        functools.partial(input_kernel, tuple(pairs), scale),
        jax.ShapeDtypeStruct((tokens, features), bf16),
        [in_smem] + [in_vmem] * (3 + owners),
        in_vmem,
        flops=2 * tokens * features * width,
        moved=token_bytes + pair_bytes,
    )(here, live, lax.optimization_barrier((mine, *pieces))[0], other, *pairs.values())


    def merge(handled, others, merged, so_far):
        return call(
            functools.partial(merge_kernel, tuple(merged), handled, others),
            jax.ShapeDtypeStruct(table.shape, bf16),
            [in_hbm, in_smem] + [in_vmem] * (2 + len(merged)) + [in_hbm],
            in_hbm,
            [
                pltpu.VMEM((rows, width), f32),
                pltpu.VMEM((len(handled), rows, width), bf16),
                pltpu.SemaphoreType.DMA((len(handled),)),
                pltpu.SMEM((owners,), jnp.int32),
                pltpu.SemaphoreType.DMA,
            ],
            moved=2 * pair_bytes,
            aliases={4 + len(merged): 0},
        )(blocks, here, parts, words, *merged.values(), so_far)

    early_pieces = {k: arrived[k] for k in early}
    gradient = merge(late, early, arrived, merge(early, late, early_pieces, blank))
    return grad_input, gradient[:, None]


def without_kernels(activations, cotangent, adapter_weight_pair, adapter_of_block, block_live_length):
    owners = lax.axis_size("dp")
    here = lax.axis_index("dp")
    count, _, rows, width = adapter_weight_pair.shape
    rank = width // 2
    scale = adapter_alpha / rank
    adapters = adapter_of_block[:, 0]
    lengths = block_live_length[:, 0]
    keep = (jnp.arange(activations.shape[0], dtype=jnp.int32) < lengths[here])[:, None]
    inputs = jnp.where(keep, activations, jnp.zeros_like(activations))
    grads_out = jnp.where(keep, cotangent, jnp.zeros_like(cotangent))
    fetched = lax.all_to_all(
        adapter_weight_pair[:, 0][adapters], "dp", split_axis=0, concat_axis=0, tiled=True
    )
    pair = fetched.reshape(-1, width)
    down, upward = pair[:, :rank], pair[:, rank:]
    f32 = jnp.float32
    hidden_part = jnp.dot(inputs, down, preferred_element_type=f32)
    dhidden_part = scale * jnp.dot(grads_out, upward, preferred_element_type=f32)
    hidden, dhidden = lax.psum((hidden_part, dhidden_part), "tensor")
    hidden16, dhidden16 = hidden.astype(jnp.bfloat16), dhidden.astype(jnp.bfloat16)
    d_down = jnp.dot(inputs.T, dhidden16, preferred_element_type=f32)
    d_up = scale * jnp.dot(grads_out.T, hidden16, preferred_element_type=f32)
    sent = jnp.concatenate([d_down, d_up], axis=1).astype(jnp.bfloat16).reshape(owners, rows, width)
    received = lax.all_to_all(sent, "dp", split_axis=0, concat_axis=0, tiled=True).astype(f32)
    same = adapters[:, None] == adapters[None, :]
    total = jnp.sum(jnp.where(same, lengths[None, :], 0), axis=1).astype(f32)
    summed = jax.ops.segment_sum(received, adapters, num_segments=count)
    denom = jnp.ones((count,), f32).at[adapters].set(jnp.maximum(total, 1.0))
    gradient = (summed / denom[:, None, None]).astype(jnp.bfloat16)
    grad_input = jnp.dot(dhidden16, down.T, preferred_element_type=f32).astype(jnp.bfloat16)
    return grad_input, gradient[:, None]


def solution(mesh):
    owners, cores = mesh.shape["dp"], mesh.shape["tensor"]

    def on_device(activations, cotangent, adapter_weight_pair, *rest):
        rows = adapter_weight_pair.shape[2]
        fits = owners == len(FETCH) + 1 and cores == 2 and rows % 256 == 0
        body = with_kernels if fits else without_kernels
        return body(activations, cotangent, adapter_weight_pair, *rest)

    in_specs = (
        P(("group", "dp"), "tensor"),
        P(("group", "dp"), "tensor"),
        P(None, "tensor", "dp", None),
        P("group", None),
        P("group", None),
    )
    out_specs = (P(("group", "dp"), "tensor"), P("group", "tensor", "dp", None))
    return jax.shard_map(
        on_device, mesh=mesh, in_specs=in_specs, out_specs=out_specs, check_vma=False
    )
```

```python
import functools

import jax
import jax.numpy as jnp
from jax import lax
from jax.experimental import pallas as pl
from jax.experimental.pallas import tpu as pltpu
from jax.sharding import PartitionSpec as P

adapter_alpha = 128.0
FETCH = (4, 1, 2, 5, 6, 3, 7)
FETCH_TIES = {3: 4}
SEND = (6, 1, 2, 4, 5, 3, 7)
SEND_TIES = {3: 6}
PREP_AFTER = 1
LATE = (5, 3, 7)
RANK_LAST = (3, 7)
SEND_FIRST = 1
FETCH_FIRST = 1

in_vmem = pl.BlockSpec(memory_space=pltpu.VMEM)
in_smem = pl.BlockSpec(memory_space=pltpu.SMEM)
in_hbm = pl.BlockSpec(memory_space=pltpu.HBM)


def low_lanes(rows, width):
    return lax.broadcasted_iota(jnp.int32, (rows, width), 1) < width // 2


def call(kernel, out_shape, in_specs, out_specs, scratch=(), flops=0, moved=0, aliases=None, vmem=40):
    return pl.pallas_call(
        kernel,
        out_shape=out_shape,
        in_specs=in_specs,
        out_specs=out_specs,
        scratch_shapes=list(scratch),
        input_output_aliases=aliases or {},
        compiler_params=pltpu.CompilerParams(vmem_limit_bytes=vmem * 1024 * 1024),
        cost_estimate=pl.CostEstimate(flops=flops, bytes_accessed=moved, transcendentals=0),
    )


def gather_kernel(peers, ids, here, table, *refs):
    out, sems = refs[: len(peers)], refs[len(peers)]
    copies = [
        pltpu.make_async_copy(table.at[ids[here[0] ^ k]], out[n], sems.at[n])
        for n, k in enumerate(peers)
    ]
    for copy in copies:
        copy.start()
    for copy in copies:
        copy.wait()


def prep_kernel(ids, here, lengths, table, after, x, y, turned, own, live, parts, blocks, blank, zeros, sem, own_sem):
    own_copy = pltpu.make_async_copy(table.at[ids[here[0]]], own, own_sem)
    own_copy.start()
    rows = own.shape[0]
    marked = lax.broadcasted_iota(jnp.int32, live.shape, 0) < lengths[here[0]]
    live[...] = jnp.where(marked, 1.0, 0.0)
    for n in range(ids.shape[0]):
        blocks[n] = ids[n]
        count = jnp.int32(0)
        for other in range(ids.shape[0]):
            count += jnp.where(ids[other] == ids[n], lengths[other], 0)
        denom = jnp.maximum(count.astype(jnp.float32), 1.0)
        parts[n : n + 1] = 1.0 / jnp.full((1, parts.shape[1]), denom)
    zeros[...] = jnp.zeros_like(zeros)
    step = zeros.shape[0]
    copies = [
        pltpu.make_async_copy(zeros, blank.at[pl.ds(s, step)], sem.at[s // step])
        for s in range(0, blank.shape[0], step)
    ]
    for copy in copies:
        copy.start()
    tokens = x.shape[0]

    @pl.loop(0, x.shape[1] // rows)
    def _(owner):
        columns = pl.ds(pl.multiple_of(owner * rows, rows), rows)
        turned[owner, :, pl.ds(0, tokens)] = x[:, columns].T
        turned[owner, :, pl.ds(tokens, tokens)] = y[:, columns].T

    for copy in [own_copy, *copies]:
        copy.wait()


def rank_kernel(peers, here, x, y, so_far, *refs):
    pairs, out = refs[: len(peers)], refs[len(peers)]
    rows, width = pairs[0].shape
    tokens = x.shape[0]
    x_rank = so_far[...]
    y_rank = x_rank
    for n, k in enumerate(peers):
        columns = pl.ds(pl.multiple_of((here[0] ^ k) * rows, rows), rows)
        x_rank += jnp.dot(x[:, columns], pairs[n][...], preferred_element_type=jnp.float32)
        y_rank += jnp.dot(y[:, columns], pairs[n][...], preferred_element_type=jnp.float32)
    out[...] = jnp.where(low_lanes(tokens, width), x_rank, y_rank)


def rounded(mine, other, live, scale):
    total = mine[...] + other[...]
    total = jnp.where(low_lanes(*total.shape), total, scale * total)
    return jnp.where(live[...] > 0.0, total, 0.0)


def swap_halves(value):
    return pltpu.roll(value, value.shape[-1] // 2, 1)


def piece_kernel(peers, scale, here, live, mine, other, turned, *refs):
    me = here[0]
    both = swap_halves(rounded(mine, other, live, scale))
    low = low_lanes(*both.shape)
    top = jnp.where(low, both, 0.0).astype(jnp.bfloat16)
    bottom = jnp.where(low, 0.0, both).astype(jnp.bfloat16)
    ranks = jnp.concatenate([top, bottom], axis=0)
    for n, k in enumerate(peers):
        piece = jnp.dot(turned[me ^ k], ranks, preferred_element_type=jnp.float32)
        refs[n][...] = jnp.where(low_lanes(*piece.shape), piece, scale * piece).astype(jnp.bfloat16)


def input_kernel(peers, scale, here, live, mine, other, *refs):
    pairs, out = refs[: len(peers)], refs[len(peers)]
    me = here[0]
    both = swap_halves(rounded(mine, other, live, scale))
    ranks = jnp.where(low_lanes(*both.shape), both, 0.0).astype(jnp.bfloat16)
    rows = pairs[0].shape[0]
    for n, k in enumerate(peers):
        columns = pl.ds(pl.multiple_of((me ^ k) * rows, rows), rows)
        out[:, columns] = lax.dot_general(
            ranks, pairs[n][...], (((1,), (1,)), ((), ())), preferred_element_type=jnp.float32
        ).astype(jnp.bfloat16)


def merge_kernel(peers, handled, others, blocks, here, parts, *refs):
    pieces = dict(zip(peers, refs[:-7]))
    out, total, held, sems, ids, ids_sem = refs[-6:]
    me = here[0]
    others_here = all(k in pieces for k in others)
    ids_copy = pltpu.make_async_copy(blocks, ids, ids_sem)
    ids_copy.start()

    def value(k):
        return pieces[k][...].astype(jnp.float32)

    def store(n, sum_of):
        held[n] = (sum_of * parts[pl.ds(me ^ handled[n], 1), :]).astype(jnp.bfloat16)

    def either(conditions):
        return functools.reduce(jnp.logical_or, conditions, jnp.bool_(False))

    for n, k in enumerate(handled):
        store(n, value(k))
    ids_copy.wait()
    copies, chosen = [], []
    for n, k in enumerate(handled):
        adapter = ids[me ^ k]
        copies.append(pltpu.make_async_copy(held.at[n], out.at[adapter], sems.at[n]))
        same = {other: ids[me ^ other] == adapter for other in (*handled, *others) if other != k}
        skip = either([same[other] for other in handled[:n]])
        adding = list(handled[n + 1 :])
        if others_here:
            adding += others
        else:
            skip |= either([same[other] for other in others])
        more = either([same[other] for other in adding])
        chosen.append(jnp.logical_not(skip))

        @pl.when(chosen[n] & more)
        def _():
            total[...] = value(k)
            for other in adding:

                @pl.when(same[other])
                def _():
                    total[...] += value(other)

            store(n, total[...])

        pl.when(chosen[n])(copies[n].start)

    for n in range(len(handled)):
        pl.when(chosen[n])(copies[n].wait)


def exchange(pieces, ties):
    owners = lax.axis_size("dp")
    out = {}
    for k in sorted(pieces, key=lambda k: k in ties):
        piece = lax.optimization_barrier((pieces[k], out[ties[k]]))[0] if k in ties else pieces[k]
        out[k] = lax.ppermute(piece, "dp", [(i, i ^ k) for i in range(owners)])
    return {k: out[k] for k in pieces}


def across_cores(value):
    cores = lax.axis_size("tensor")
    return lax.ppermute(value, "tensor", [(i, i ^ 1) for i in range(cores)])


def with_kernels(activations, cotangent, adapter_weight_pair, adapter_of_block, block_live_length):
    owners = lax.axis_size("dp")
    here = lax.axis_index("dp").astype(jnp.int32).reshape(1)
    ids, lengths = adapter_of_block[:, 0], block_live_length[:, 0]
    count, _, rows, width = adapter_weight_pair.shape
    table = adapter_weight_pair.reshape(count, rows, width)
    tokens, features = activations.shape
    scale = adapter_alpha / (width // 2)
    bf16, f32 = jnp.bfloat16, jnp.float32
    straight = jax.ShapeDtypeStruct((rows, width), bf16)
    pair_bytes = owners * rows * width * 2
    token_bytes = tokens * features * 2

    sent, me = [], here
    for part in (FETCH[:FETCH_FIRST], FETCH[FETCH_FIRST:]):
        sent += call(
            functools.partial(gather_kernel, part),
            [straight] * len(part),
            [in_smem, in_smem, in_hbm],
            [in_vmem] * len(part),
            [pltpu.SemaphoreType.DMA((len(part),))],
            moved=1024,
            vmem=53,
        )(ids, me, table)
        me = lax.optimization_barrier((here, *sent))[0]
    pairs = exchange(dict(zip(FETCH, sent)), FETCH_TIES)

    step = 8
    turned, own, live, parts, blocks, blank = call(
        prep_kernel,
        [
            jax.ShapeDtypeStruct((owners, rows, 2 * tokens), bf16),
            straight,
            jax.ShapeDtypeStruct((tokens, width), f32),
            jax.ShapeDtypeStruct((owners, width), f32),
            jax.ShapeDtypeStruct((owners,), jnp.int32),
            jax.ShapeDtypeStruct(table.shape, bf16),
        ],
        [in_smem, in_smem, in_smem, in_hbm, in_hbm, in_vmem, in_vmem],
        [in_vmem, in_vmem, in_vmem, in_vmem, in_smem, in_hbm],
        [
            pltpu.VMEM((step, rows, width), bf16),
            pltpu.SemaphoreType.DMA((count // step,)),
            pltpu.SemaphoreType.DMA,
        ],
        moved=4 * token_bytes + 2 * count * rows * width,
    )(ids, here, lengths, table, pairs[PREP_AFTER], activations, cotangent)
    pairs[0] = own

    mine = jnp.zeros((tokens, width), f32)
    for part in ([k for k in pairs if k not in RANK_LAST], RANK_LAST):
        mine = call(
            functools.partial(rank_kernel, tuple(part)),
            jax.ShapeDtypeStruct((tokens, width), f32),
            [in_smem] + [in_vmem] * (3 + len(part)),
            in_vmem,
            moved=1024,
        )(here, lax.optimization_barrier((activations, turned))[0], cotangent, mine, *[pairs[k] for k in part])
    other = across_cores(mine)

    peers = (*SEND, 0)
    pieces = []
    for part in (peers[:SEND_FIRST], peers[SEND_FIRST:]):
        pieces += call(
            functools.partial(piece_kernel, part, scale),
            [straight] * len(part),
            [in_smem] + [in_vmem] * 4,
            [in_vmem] * len(part),
            moved=1024,
        )(here, live, mine, other, turned)
    arrived = exchange(dict(zip(SEND, pieces)), SEND_TIES)
    arrived[0] = pieces[-1]

    grad_input = call(
        functools.partial(input_kernel, tuple(pairs), scale),
        jax.ShapeDtypeStruct((tokens, features), bf16),
        [in_smem] + [in_vmem] * (3 + owners),
        in_vmem,
        flops=2 * tokens * features * width,
        moved=token_bytes + pair_bytes,
    )(here, live, lax.optimization_barrier((mine, *pieces))[0], other, *pairs.values())

    late = tuple(k for k in peers if k in LATE)
    early = tuple(k for k in peers if k not in LATE)

    def merge(handled, others, merged, so_far):
        return call(
            functools.partial(merge_kernel, tuple(merged), handled, others),
            jax.ShapeDtypeStruct(table.shape, bf16),
            [in_hbm, in_smem, in_vmem] + [in_vmem] * len(merged) + [in_hbm],
            in_hbm,
            [
                pltpu.VMEM((rows, width), f32),
                pltpu.VMEM((len(handled), rows, width), bf16),
                pltpu.SemaphoreType.DMA((len(handled),)),
                pltpu.SMEM((owners,), jnp.int32),
                pltpu.SemaphoreType.DMA,
            ],
            moved=2 * pair_bytes,
            aliases={3 + len(merged): 0},
        )(blocks, here, parts, *merged.values(), so_far)

    early_pieces = {k: arrived[k] for k in early}
    gradient = merge(late, early, arrived, merge(early, late, early_pieces, blank))
    return grad_input, gradient[:, None]


def without_kernels(activations, cotangent, adapter_weight_pair, adapter_of_block, block_live_length):
    owners = lax.axis_size("dp")
    here = lax.axis_index("dp")
    count, _, rows, width = adapter_weight_pair.shape
    rank = width // 2
    scale = adapter_alpha / rank
    adapters = adapter_of_block[:, 0]
    lengths = block_live_length[:, 0]
    keep = (jnp.arange(activations.shape[0], dtype=jnp.int32) < lengths[here])[:, None]
    inputs = jnp.where(keep, activations, jnp.zeros_like(activations))
    grads_out = jnp.where(keep, cotangent, jnp.zeros_like(cotangent))
    fetched = lax.all_to_all(
        adapter_weight_pair[:, 0][adapters], "dp", split_axis=0, concat_axis=0, tiled=True
    )
    pair = fetched.reshape(-1, width)
    down, upward = pair[:, :rank], pair[:, rank:]
    f32 = jnp.float32
    hidden_part = jnp.dot(inputs, down, preferred_element_type=f32)
    dhidden_part = scale * jnp.dot(grads_out, upward, preferred_element_type=f32)
    hidden, dhidden = lax.psum((hidden_part, dhidden_part), "tensor")
    hidden16, dhidden16 = hidden.astype(jnp.bfloat16), dhidden.astype(jnp.bfloat16)
    d_down = jnp.dot(inputs.T, dhidden16, preferred_element_type=f32)
    d_up = scale * jnp.dot(grads_out.T, hidden16, preferred_element_type=f32)
    sent = jnp.concatenate([d_down, d_up], axis=1).astype(jnp.bfloat16).reshape(owners, rows, width)
    received = lax.all_to_all(sent, "dp", split_axis=0, concat_axis=0, tiled=True).astype(f32)
    same = adapters[:, None] == adapters[None, :]
    total = jnp.sum(jnp.where(same, lengths[None, :], 0), axis=1).astype(f32)
    summed = jax.ops.segment_sum(received, adapters, num_segments=count)
    denom = jnp.ones((count,), f32).at[adapters].set(jnp.maximum(total, 1.0))
    gradient = (summed / denom[:, None, None]).astype(jnp.bfloat16)
    grad_input = jnp.dot(dhidden16, down.T, preferred_element_type=f32).astype(jnp.bfloat16)
    return grad_input, gradient[:, None]


def solution(mesh):
    owners, cores = mesh.shape["dp"], mesh.shape["tensor"]

    def on_device(activations, cotangent, adapter_weight_pair, *rest):
        rows = adapter_weight_pair.shape[2]
        fits = owners == len(FETCH) + 1 and cores == 2 and rows % 256 == 0
        body = with_kernels if fits else without_kernels
        return body(activations, cotangent, adapter_weight_pair, *rest)

    in_specs = (
        P(("group", "dp"), "tensor"),
        P(("group", "dp"), "tensor"),
        P(None, "tensor", "dp", None),
        P("group", None),
        P("group", None),
    )
    out_specs = (P(("group", "dp"), "tensor"), P("group", "tensor", "dp", None))
    return jax.shard_map(
        on_device, mesh=mesh, in_specs=in_specs, out_specs=out_specs, check_vma=False
    )
```

```python
import functools

import jax
import jax.numpy as jnp
from jax import lax
from jax.experimental import pallas as pl
from jax.experimental.pallas import tpu as pltpu
from jax.sharding import PartitionSpec as P

adapter_alpha = 128.0
FETCH = (4, 1, 2, 5, 6, 3, 7)
FETCH_TIES = {}
SEND = (6, 1, 2, 7, 4, 3, 5)
SEND_TIES = {3: 6}
PREP_AFTER = 1
LATE = (4, 3, 5)
RANK_LAST = (3, 7)
SEND_FIRST = 1
FETCH_FIRST = 1

in_vmem = pl.BlockSpec(memory_space=pltpu.VMEM)
in_smem = pl.BlockSpec(memory_space=pltpu.SMEM)
in_hbm = pl.BlockSpec(memory_space=pltpu.HBM)


def low_lanes(rows, width):
    return lax.broadcasted_iota(jnp.int32, (rows, width), 1) < width // 2


def call(kernel, out_shape, in_specs, out_specs, scratch=(), flops=0, moved=0, aliases=None, vmem=40):
    return pl.pallas_call(
        kernel,
        out_shape=out_shape,
        in_specs=in_specs,
        out_specs=out_specs,
        scratch_shapes=list(scratch),
        input_output_aliases=aliases or {},
        compiler_params=pltpu.CompilerParams(vmem_limit_bytes=vmem * 1024 * 1024),
        cost_estimate=pl.CostEstimate(flops=flops, bytes_accessed=moved, transcendentals=0),
    )


def gather_kernel(peers, ids, here, table, *refs):
    out, sems = refs[: len(peers)], refs[len(peers)]
    copies = [
        pltpu.make_async_copy(table.at[ids[here[0] ^ k]], out[n], sems.at[n])
        for n, k in enumerate(peers)
    ]
    for copy in copies:
        copy.start()
    for copy in copies:
        copy.wait()


def prep_kernel(ids, here, lengths, table, after, x, y, turned, own, live, parts, blocks, blank, zeros, sem, own_sem):
    own_copy = pltpu.make_async_copy(table.at[ids[here[0]]], own, own_sem)
    own_copy.start()
    rows = own.shape[0]
    marked = lax.broadcasted_iota(jnp.int32, live.shape, 0) < lengths[here[0]]
    live[...] = jnp.where(marked, 1.0, 0.0)
    for n in range(ids.shape[0]):
        blocks[n] = ids[n]
        count = jnp.int32(0)
        for other in range(ids.shape[0]):
            count += jnp.where(ids[other] == ids[n], lengths[other], 0)
        denom = jnp.maximum(count.astype(jnp.float32), 1.0)
        parts[n : n + 1] = 1.0 / jnp.full((1, parts.shape[1]), denom)
    zeros[...] = jnp.zeros_like(zeros)
    step = zeros.shape[0]
    copies = [
        pltpu.make_async_copy(zeros, blank.at[pl.ds(s, step)], sem.at[s // step])
        for s in range(0, blank.shape[0], step)
    ]
    for copy in copies:
        copy.start()
    tokens = x.shape[0]

    @pl.loop(0, x.shape[1] // rows)
    def _(owner):
        columns = pl.ds(pl.multiple_of(owner * rows, rows), rows)
        turned[owner, :, pl.ds(0, tokens)] = x[:, columns].T
        turned[owner, :, pl.ds(tokens, tokens)] = y[:, columns].T

    for copy in [own_copy, *copies]:
        copy.wait()


def rank_kernel(peers, here, x, y, so_far, *refs):
    pairs, out = refs[: len(peers)], refs[len(peers)]
    rows, width = pairs[0].shape
    tokens = x.shape[0]
    x_rank = so_far[...]
    y_rank = x_rank
    for n, k in enumerate(peers):
        columns = pl.ds(pl.multiple_of((here[0] ^ k) * rows, rows), rows)
        x_rank += jnp.dot(x[:, columns], pairs[n][...], preferred_element_type=jnp.float32)
        y_rank += jnp.dot(y[:, columns], pairs[n][...], preferred_element_type=jnp.float32)
    out[...] = jnp.where(low_lanes(tokens, width), x_rank, y_rank)


def rounded(mine, other, live, scale):
    total = mine[...] + other[...]
    total = jnp.where(low_lanes(*total.shape), total, scale * total)
    return jnp.where(live[...] > 0.0, total, 0.0)


def swap_halves(value):
    return pltpu.roll(value, value.shape[-1] // 2, 1)


def piece_kernel(peers, scale, here, live, mine, other, turned, *refs):
    me = here[0]
    both = swap_halves(rounded(mine, other, live, scale))
    low = low_lanes(*both.shape)
    top = jnp.where(low, both, 0.0).astype(jnp.bfloat16)
    bottom = jnp.where(low, 0.0, both).astype(jnp.bfloat16)
    ranks = jnp.concatenate([top, bottom], axis=0)
    for n, k in enumerate(peers):
        piece = jnp.dot(turned[me ^ k], ranks, preferred_element_type=jnp.float32)
        refs[n][...] = jnp.where(low_lanes(*piece.shape), piece, scale * piece).astype(jnp.bfloat16)


def input_kernel(peers, scale, here, live, mine, other, *refs):
    pairs, out = refs[: len(peers)], refs[len(peers)]
    me = here[0]
    both = swap_halves(rounded(mine, other, live, scale))
    ranks = jnp.where(low_lanes(*both.shape), both, 0.0).astype(jnp.bfloat16)
    rows = pairs[0].shape[0]
    for n, k in enumerate(peers):
        columns = pl.ds(pl.multiple_of((me ^ k) * rows, rows), rows)
        out[:, columns] = lax.dot_general(
            ranks, pairs[n][...], (((1,), (1,)), ((), ())), preferred_element_type=jnp.float32
        ).astype(jnp.bfloat16)


def merge_kernel(peers, handled, others, blocks, here, parts, *refs):
    pieces = dict(zip(peers, refs[:-7]))
    out, total, held, sems, ids, ids_sem = refs[-6:]
    me = here[0]
    others_here = all(k in pieces for k in others)
    ids_copy = pltpu.make_async_copy(blocks, ids, ids_sem)
    ids_copy.start()

    def value(k):
        return pieces[k][...].astype(jnp.float32)

    def store(n, sum_of):
        held[n] = (sum_of * parts[pl.ds(me ^ handled[n], 1), :]).astype(jnp.bfloat16)

    def either(conditions):
        return functools.reduce(jnp.logical_or, conditions, jnp.bool_(False))

    for n, k in enumerate(handled):
        store(n, value(k))
    ids_copy.wait()
    copies, chosen = [], []
    for n, k in enumerate(handled):
        adapter = ids[me ^ k]
        copies.append(pltpu.make_async_copy(held.at[n], out.at[adapter], sems.at[n]))
        same = {other: ids[me ^ other] == adapter for other in (*handled, *others) if other != k}
        skip = either([same[other] for other in handled[:n]])
        adding = list(handled[n + 1 :])
        if others_here:
            adding += others
        else:
            skip |= either([same[other] for other in others])
        more = either([same[other] for other in adding])
        chosen.append(jnp.logical_not(skip))

        @pl.when(chosen[n] & more)
        def _():
            total[...] = value(k)
            for other in adding:

                @pl.when(same[other])
                def _():
                    total[...] += value(other)

            store(n, total[...])

        pl.when(chosen[n])(copies[n].start)

    for n in range(len(handled)):
        pl.when(chosen[n])(copies[n].wait)


def exchange(pieces, ties):
    owners = lax.axis_size("dp")
    out = {}
    for k in sorted(pieces, key=lambda k: k in ties):
        piece = lax.optimization_barrier((pieces[k], out[ties[k]]))[0] if k in ties else pieces[k]
        out[k] = lax.ppermute(piece, "dp", [(i, i ^ k) for i in range(owners)])
    return {k: out[k] for k in pieces}


def across_cores(value):
    cores = lax.axis_size("tensor")
    return lax.ppermute(value, "tensor", [(i, i ^ 1) for i in range(cores)])


def with_kernels(activations, cotangent, adapter_weight_pair, adapter_of_block, block_live_length):
    owners = lax.axis_size("dp")
    here = lax.axis_index("dp").astype(jnp.int32).reshape(1)
    ids, lengths = adapter_of_block[:, 0], block_live_length[:, 0]
    count, _, rows, width = adapter_weight_pair.shape
    table = adapter_weight_pair.reshape(count, rows, width)
    tokens, features = activations.shape
    scale = adapter_alpha / (width // 2)
    bf16, f32 = jnp.bfloat16, jnp.float32
    straight = jax.ShapeDtypeStruct((rows, width), bf16)
    pair_bytes = owners * rows * width * 2
    token_bytes = tokens * features * 2

    sent, me = [], here
    for part in (FETCH[:FETCH_FIRST], FETCH[FETCH_FIRST:]):
        sent += call(
            functools.partial(gather_kernel, part),
            [straight] * len(part),
            [in_smem, in_smem, in_hbm],
            [in_vmem] * len(part),
            [pltpu.SemaphoreType.DMA((len(part),))],
            moved=1024,
            vmem=53,
        )(ids, me, table)
        me = lax.optimization_barrier((here, *sent))[0]
    pairs = exchange(dict(zip(FETCH, sent)), FETCH_TIES)

    step = 8
    turned, own, live, parts, blocks, blank = call(
        prep_kernel,
        [
            jax.ShapeDtypeStruct((owners, rows, 2 * tokens), bf16),
            straight,
            jax.ShapeDtypeStruct((tokens, width), f32),
            jax.ShapeDtypeStruct((owners, width), f32),
            jax.ShapeDtypeStruct((owners,), jnp.int32),
            jax.ShapeDtypeStruct(table.shape, bf16),
        ],
        [in_smem, in_smem, in_smem, in_hbm, in_hbm, in_vmem, in_vmem],
        [in_vmem, in_vmem, in_vmem, in_vmem, in_smem, in_hbm],
        [
            pltpu.VMEM((step, rows, width), bf16),
            pltpu.SemaphoreType.DMA((count // step,)),
            pltpu.SemaphoreType.DMA,
        ],
        moved=4 * token_bytes + 2 * count * rows * width,
    )(ids, here, lengths, table, pairs[PREP_AFTER], activations, cotangent)
    pairs[0] = own

    mine = jnp.zeros((tokens, width), f32)
    for part in ([k for k in pairs if k not in RANK_LAST], RANK_LAST):
        mine = call(
            functools.partial(rank_kernel, tuple(part)),
            jax.ShapeDtypeStruct((tokens, width), f32),
            [in_smem] + [in_vmem] * (3 + len(part)),
            in_vmem,
            moved=1024,
        )(here, lax.optimization_barrier((activations, turned))[0], cotangent, mine, *[pairs[k] for k in part])
    other = across_cores(mine)

    peers = (*SEND, 0)
    pieces = []
    for part in (peers[:SEND_FIRST], peers[SEND_FIRST:]):
        pieces += call(
            functools.partial(piece_kernel, part, scale),
            [straight] * len(part),
            [in_smem] + [in_vmem] * 4,
            [in_vmem] * len(part),
            moved=1024,
        )(here, live, mine, other, turned)
    arrived = exchange(dict(zip(SEND, pieces)), SEND_TIES)
    arrived[0] = pieces[-1]

    grad_input = call(
        functools.partial(input_kernel, tuple(pairs), scale),
        jax.ShapeDtypeStruct((tokens, features), bf16),
        [in_smem] + [in_vmem] * (3 + owners),
        in_vmem,
        flops=2 * tokens * features * width,
        moved=token_bytes + pair_bytes,
    )(here, live, lax.optimization_barrier((mine, *pieces))[0], other, *pairs.values())

    late = tuple(k for k in peers if k in LATE)
    early = tuple(k for k in peers if k not in LATE)

    def merge(handled, others, merged, so_far):
        return call(
            functools.partial(merge_kernel, tuple(merged), handled, others),
            jax.ShapeDtypeStruct(table.shape, bf16),
            [in_hbm, in_smem, in_vmem] + [in_vmem] * len(merged) + [in_hbm],
            in_hbm,
            [
                pltpu.VMEM((rows, width), f32),
                pltpu.VMEM((len(handled), rows, width), bf16),
                pltpu.SemaphoreType.DMA((len(handled),)),
                pltpu.SMEM((owners,), jnp.int32),
                pltpu.SemaphoreType.DMA,
            ],
            moved=2 * pair_bytes,
            aliases={3 + len(merged): 0},
        )(blocks, here, parts, *merged.values(), so_far)

    early_pieces = {k: arrived[k] for k in early}
    gradient = merge(late, early, arrived, merge(early, late, early_pieces, blank))
    return grad_input, gradient[:, None]


def without_kernels(activations, cotangent, adapter_weight_pair, adapter_of_block, block_live_length):
    owners = lax.axis_size("dp")
    here = lax.axis_index("dp")
    count, _, rows, width = adapter_weight_pair.shape
    rank = width // 2
    scale = adapter_alpha / rank
    adapters = adapter_of_block[:, 0]
    lengths = block_live_length[:, 0]
    keep = (jnp.arange(activations.shape[0], dtype=jnp.int32) < lengths[here])[:, None]
    inputs = jnp.where(keep, activations, jnp.zeros_like(activations))
    grads_out = jnp.where(keep, cotangent, jnp.zeros_like(cotangent))
    fetched = lax.all_to_all(
        adapter_weight_pair[:, 0][adapters], "dp", split_axis=0, concat_axis=0, tiled=True
    )
    pair = fetched.reshape(-1, width)
    down, upward = pair[:, :rank], pair[:, rank:]
    f32 = jnp.float32
    hidden_part = jnp.dot(inputs, down, preferred_element_type=f32)
    dhidden_part = scale * jnp.dot(grads_out, upward, preferred_element_type=f32)
    hidden, dhidden = lax.psum((hidden_part, dhidden_part), "tensor")
    hidden16, dhidden16 = hidden.astype(jnp.bfloat16), dhidden.astype(jnp.bfloat16)
    d_down = jnp.dot(inputs.T, dhidden16, preferred_element_type=f32)
    d_up = scale * jnp.dot(grads_out.T, hidden16, preferred_element_type=f32)
    sent = jnp.concatenate([d_down, d_up], axis=1).astype(jnp.bfloat16).reshape(owners, rows, width)
    received = lax.all_to_all(sent, "dp", split_axis=0, concat_axis=0, tiled=True).astype(f32)
    same = adapters[:, None] == adapters[None, :]
    total = jnp.sum(jnp.where(same, lengths[None, :], 0), axis=1).astype(f32)
    summed = jax.ops.segment_sum(received, adapters, num_segments=count)
    denom = jnp.ones((count,), f32).at[adapters].set(jnp.maximum(total, 1.0))
    gradient = (summed / denom[:, None, None]).astype(jnp.bfloat16)
    grad_input = jnp.dot(dhidden16, down.T, preferred_element_type=f32).astype(jnp.bfloat16)
    return grad_input, gradient[:, None]


def solution(mesh):
    owners, cores = mesh.shape["dp"], mesh.shape["tensor"]

    def on_device(activations, cotangent, adapter_weight_pair, *rest):
        rows = adapter_weight_pair.shape[2]
        fits = owners == len(FETCH) + 1 and cores == 2 and rows % 256 == 0
        body = with_kernels if fits else without_kernels
        return body(activations, cotangent, adapter_weight_pair, *rest)

    in_specs = (
        P(("group", "dp"), "tensor"),
        P(("group", "dp"), "tensor"),
        P(None, "tensor", "dp", None),
        P("group", None),
        P("group", None),
    )
    out_specs = (P(("group", "dp"), "tensor"), P("group", "tensor", "dp", None))
    return jax.shard_map(
        on_device, mesh=mesh, in_specs=in_specs, out_specs=out_specs, check_vma=False
    )
```

```python
import functools

import jax
import jax.numpy as jnp
from jax import lax
from jax.experimental import pallas as pl
from jax.experimental.pallas import tpu as pltpu
from jax.sharding import PartitionSpec as P

adapter_alpha = 128.0
FETCH = (4, 1, 2, 5, 6, 3, 7)
FETCH_TIES = {3: 4}
SEND = (6, 1, 4, 2, 5, 3, 7)
SEND_TIES = {3: 6}
PREP_AFTER = 1
LATE = (5, 3, 7)
RANK_LAST = (3, 7)
SEND_FIRST = 1
FETCH_FIRST = 1

in_vmem = pl.BlockSpec(memory_space=pltpu.VMEM)
in_smem = pl.BlockSpec(memory_space=pltpu.SMEM)
in_hbm = pl.BlockSpec(memory_space=pltpu.HBM)


def low_lanes(rows, width):
    return lax.broadcasted_iota(jnp.int32, (rows, width), 1) < width // 2


def call(kernel, out_shape, in_specs, out_specs, scratch=(), flops=0, moved=0, aliases=None, vmem=40):
    return pl.pallas_call(
        kernel,
        out_shape=out_shape,
        in_specs=in_specs,
        out_specs=out_specs,
        scratch_shapes=list(scratch),
        input_output_aliases=aliases or {},
        compiler_params=pltpu.CompilerParams(vmem_limit_bytes=vmem * 1024 * 1024),
        cost_estimate=pl.CostEstimate(flops=flops, bytes_accessed=moved, transcendentals=0),
    )


def gather_kernel(peers, ids, here, table, *refs):
    out, sems = refs[: len(peers)], refs[len(peers)]
    copies = [
        pltpu.make_async_copy(table.at[ids[here[0] ^ k]], out[n], sems.at[n])
        for n, k in enumerate(peers)
    ]
    for copy in copies:
        copy.start()
    for copy in copies:
        copy.wait()


def prep_kernel(ids, here, lengths, table, after, x, y, turned, own, live, parts, blocks, blank, zeros, sem, own_sem):
    own_copy = pltpu.make_async_copy(table.at[ids[here[0]]], own, own_sem)
    own_copy.start()
    rows = own.shape[0]
    marked = lax.broadcasted_iota(jnp.int32, live.shape, 0) < lengths[here[0]]
    live[...] = jnp.where(marked, 1.0, 0.0)
    for n in range(ids.shape[0]):
        blocks[n] = ids[n]
        count = jnp.int32(0)
        for other in range(ids.shape[0]):
            count += jnp.where(ids[other] == ids[n], lengths[other], 0)
        denom = jnp.maximum(count.astype(jnp.float32), 1.0)
        parts[n : n + 1] = 1.0 / jnp.full((1, parts.shape[1]), denom)
    zeros[...] = jnp.zeros_like(zeros)
    step = zeros.shape[0]
    copies = [
        pltpu.make_async_copy(zeros, blank.at[pl.ds(s, step)], sem.at[s // step])
        for s in range(0, blank.shape[0], step)
    ]
    for copy in copies:
        copy.start()
    tokens = x.shape[0]

    @pl.loop(0, x.shape[1] // rows)
    def _(owner):
        columns = pl.ds(pl.multiple_of(owner * rows, rows), rows)
        turned[owner, :, pl.ds(0, tokens)] = x[:, columns].T
        turned[owner, :, pl.ds(tokens, tokens)] = y[:, columns].T

    for copy in [own_copy, *copies]:
        copy.wait()


def rank_kernel(peers, here, x, y, so_far, *refs):
    pairs, out = refs[: len(peers)], refs[len(peers)]
    rows, width = pairs[0].shape
    tokens = x.shape[0]
    x_rank = so_far[...]
    y_rank = x_rank
    for n, k in enumerate(peers):
        columns = pl.ds(pl.multiple_of((here[0] ^ k) * rows, rows), rows)
        x_rank += jnp.dot(x[:, columns], pairs[n][...], preferred_element_type=jnp.float32)
        y_rank += jnp.dot(y[:, columns], pairs[n][...], preferred_element_type=jnp.float32)
    out[...] = jnp.where(low_lanes(tokens, width), x_rank, y_rank)


def rounded(mine, other, live, scale):
    total = mine[...] + other[...]
    total = jnp.where(low_lanes(*total.shape), total, scale * total)
    return jnp.where(live[...] > 0.0, total, 0.0)


def swap_halves(value):
    return pltpu.roll(value, value.shape[-1] // 2, 1)


def piece_kernel(peers, scale, here, live, mine, other, turned, *refs):
    me = here[0]
    both = swap_halves(rounded(mine, other, live, scale))
    low = low_lanes(*both.shape)
    top = jnp.where(low, both, 0.0).astype(jnp.bfloat16)
    bottom = jnp.where(low, 0.0, both).astype(jnp.bfloat16)
    ranks = jnp.concatenate([top, bottom], axis=0)
    for n, k in enumerate(peers):
        piece = jnp.dot(turned[me ^ k], ranks, preferred_element_type=jnp.float32)
        refs[n][...] = jnp.where(low_lanes(*piece.shape), piece, scale * piece).astype(jnp.bfloat16)


def input_kernel(peers, scale, here, live, mine, other, *refs):
    pairs, out = refs[: len(peers)], refs[len(peers)]
    me = here[0]
    both = swap_halves(rounded(mine, other, live, scale))
    ranks = jnp.where(low_lanes(*both.shape), both, 0.0).astype(jnp.bfloat16)
    rows = pairs[0].shape[0]
    for n, k in enumerate(peers):
        columns = pl.ds(pl.multiple_of((me ^ k) * rows, rows), rows)
        out[:, columns] = lax.dot_general(
            ranks, pairs[n][...], (((1,), (1,)), ((), ())), preferred_element_type=jnp.float32
        ).astype(jnp.bfloat16)


def merge_kernel(peers, handled, others, blocks, here, parts, *refs):
    pieces = dict(zip(peers, refs[:-7]))
    out, total, held, sems, ids, ids_sem = refs[-6:]
    me = here[0]
    others_here = all(k in pieces for k in others)
    ids_copy = pltpu.make_async_copy(blocks, ids, ids_sem)
    ids_copy.start()

    def value(k):
        return pieces[k][...].astype(jnp.float32)

    def store(n, sum_of):
        held[n] = (sum_of * parts[pl.ds(me ^ handled[n], 1), :]).astype(jnp.bfloat16)

    def either(conditions):
        return functools.reduce(jnp.logical_or, conditions, jnp.bool_(False))

    for n, k in enumerate(handled):
        store(n, value(k))
    ids_copy.wait()
    copies, chosen = [], []
    for n, k in enumerate(handled):
        adapter = ids[me ^ k]
        copies.append(pltpu.make_async_copy(held.at[n], out.at[adapter], sems.at[n]))
        same = {other: ids[me ^ other] == adapter for other in (*handled, *others) if other != k}
        skip = either([same[other] for other in handled[:n]])
        adding = list(handled[n + 1 :])
        if others_here:
            adding += others
        else:
            skip |= either([same[other] for other in others])
        more = either([same[other] for other in adding])
        chosen.append(jnp.logical_not(skip))

        @pl.when(chosen[n] & more)
        def _():
            total[...] = value(k)
            for other in adding:

                @pl.when(same[other])
                def _():
                    total[...] += value(other)

            store(n, total[...])

        pl.when(chosen[n])(copies[n].start)

    for n in range(len(handled)):
        pl.when(chosen[n])(copies[n].wait)


def exchange(pieces, ties):
    owners = lax.axis_size("dp")
    out = {}
    for k in sorted(pieces, key=lambda k: k in ties):
        piece = lax.optimization_barrier((pieces[k], out[ties[k]]))[0] if k in ties else pieces[k]
        out[k] = lax.ppermute(piece, "dp", [(i, i ^ k) for i in range(owners)])
    return {k: out[k] for k in pieces}


def across_cores(value):
    cores = lax.axis_size("tensor")
    return lax.ppermute(value, "tensor", [(i, i ^ 1) for i in range(cores)])


def with_kernels(activations, cotangent, adapter_weight_pair, adapter_of_block, block_live_length):
    owners = lax.axis_size("dp")
    here = lax.axis_index("dp").astype(jnp.int32).reshape(1)
    ids, lengths = adapter_of_block[:, 0], block_live_length[:, 0]
    count, _, rows, width = adapter_weight_pair.shape
    table = adapter_weight_pair.reshape(count, rows, width)
    tokens, features = activations.shape
    scale = adapter_alpha / (width // 2)
    bf16, f32 = jnp.bfloat16, jnp.float32
    straight = jax.ShapeDtypeStruct((rows, width), bf16)
    pair_bytes = owners * rows * width * 2
    token_bytes = tokens * features * 2

    sent, me = [], here
    for part in (FETCH[:FETCH_FIRST], FETCH[FETCH_FIRST:]):
        sent += call(
            functools.partial(gather_kernel, part),
            [straight] * len(part),
            [in_smem, in_smem, in_hbm],
            [in_vmem] * len(part),
            [pltpu.SemaphoreType.DMA((len(part),))],
            moved=1024,
            vmem=53,
        )(ids, me, table)
        me = lax.optimization_barrier((here, *sent))[0]
    pairs = exchange(dict(zip(FETCH, sent)), FETCH_TIES)

    step = 8
    turned, own, live, parts, blocks, blank = call(
        prep_kernel,
        [
            jax.ShapeDtypeStruct((owners, rows, 2 * tokens), bf16),
            straight,
            jax.ShapeDtypeStruct((tokens, width), f32),
            jax.ShapeDtypeStruct((owners, width), f32),
            jax.ShapeDtypeStruct((owners,), jnp.int32),
            jax.ShapeDtypeStruct(table.shape, bf16),
        ],
        [in_smem, in_smem, in_smem, in_hbm, in_hbm, in_vmem, in_vmem],
        [in_vmem, in_vmem, in_vmem, in_vmem, in_smem, in_hbm],
        [
            pltpu.VMEM((step, rows, width), bf16),
            pltpu.SemaphoreType.DMA((count // step,)),
            pltpu.SemaphoreType.DMA,
        ],
        moved=4 * token_bytes + 2 * count * rows * width,
    )(ids, here, lengths, table, pairs[PREP_AFTER], activations, cotangent)
    pairs[0] = own

    mine = jnp.zeros((tokens, width), f32)
    for part in ([k for k in pairs if k not in RANK_LAST], RANK_LAST):
        mine = call(
            functools.partial(rank_kernel, tuple(part)),
            jax.ShapeDtypeStruct((tokens, width), f32),
            [in_smem] + [in_vmem] * (3 + len(part)),
            in_vmem,
            moved=1024,
        )(here, lax.optimization_barrier((activations, turned))[0], cotangent, mine, *[pairs[k] for k in part])
    other = across_cores(mine)

    peers = (*SEND, 0)
    pieces = []
    for part in (peers[:SEND_FIRST], peers[SEND_FIRST:]):
        pieces += call(
            functools.partial(piece_kernel, part, scale),
            [straight] * len(part),
            [in_smem] + [in_vmem] * 4,
            [in_vmem] * len(part),
            moved=1024,
        )(here, live, mine, other, turned)
    arrived = exchange(dict(zip(SEND, pieces)), SEND_TIES)
    arrived[0] = pieces[-1]

    grad_input = call(
        functools.partial(input_kernel, tuple(pairs), scale),
        jax.ShapeDtypeStruct((tokens, features), bf16),
        [in_smem] + [in_vmem] * (3 + owners),
        in_vmem,
        flops=2 * tokens * features * width,
        moved=token_bytes + pair_bytes,
    )(here, live, lax.optimization_barrier((mine, *pieces))[0], other, *pairs.values())

    late = tuple(k for k in peers if k in LATE)
    early = tuple(k for k in peers if k not in LATE)

    def merge(handled, others, merged, so_far):
        return call(
            functools.partial(merge_kernel, tuple(merged), handled, others),
            jax.ShapeDtypeStruct(table.shape, bf16),
            [in_hbm, in_smem, in_vmem] + [in_vmem] * len(merged) + [in_hbm],
            in_hbm,
            [
                pltpu.VMEM((rows, width), f32),
                pltpu.VMEM((len(handled), rows, width), bf16),
                pltpu.SemaphoreType.DMA((len(handled),)),
                pltpu.SMEM((owners,), jnp.int32),
                pltpu.SemaphoreType.DMA,
            ],
            moved=2 * pair_bytes,
            aliases={3 + len(merged): 0},
        )(blocks, here, parts, *merged.values(), so_far)

    early_pieces = {k: arrived[k] for k in early}
    gradient = merge(late, early, arrived, merge(early, late, early_pieces, blank))
    return grad_input, gradient[:, None]


def without_kernels(activations, cotangent, adapter_weight_pair, adapter_of_block, block_live_length):
    owners = lax.axis_size("dp")
    here = lax.axis_index("dp")
    count, _, rows, width = adapter_weight_pair.shape
    rank = width // 2
    scale = adapter_alpha / rank
    adapters = adapter_of_block[:, 0]
    lengths = block_live_length[:, 0]
    keep = (jnp.arange(activations.shape[0], dtype=jnp.int32) < lengths[here])[:, None]
    inputs = jnp.where(keep, activations, jnp.zeros_like(activations))
    grads_out = jnp.where(keep, cotangent, jnp.zeros_like(cotangent))
    fetched = lax.all_to_all(
        adapter_weight_pair[:, 0][adapters], "dp", split_axis=0, concat_axis=0, tiled=True
    )
    pair = fetched.reshape(-1, width)
    down, upward = pair[:, :rank], pair[:, rank:]
    f32 = jnp.float32
    hidden_part = jnp.dot(inputs, down, preferred_element_type=f32)
    dhidden_part = scale * jnp.dot(grads_out, upward, preferred_element_type=f32)
    hidden, dhidden = lax.psum((hidden_part, dhidden_part), "tensor")
    hidden16, dhidden16 = hidden.astype(jnp.bfloat16), dhidden.astype(jnp.bfloat16)
    d_down = jnp.dot(inputs.T, dhidden16, preferred_element_type=f32)
    d_up = scale * jnp.dot(grads_out.T, hidden16, preferred_element_type=f32)
    sent = jnp.concatenate([d_down, d_up], axis=1).astype(jnp.bfloat16).reshape(owners, rows, width)
    received = lax.all_to_all(sent, "dp", split_axis=0, concat_axis=0, tiled=True).astype(f32)
    same = adapters[:, None] == adapters[None, :]
    total = jnp.sum(jnp.where(same, lengths[None, :], 0), axis=1).astype(f32)
    summed = jax.ops.segment_sum(received, adapters, num_segments=count)
    denom = jnp.ones((count,), f32).at[adapters].set(jnp.maximum(total, 1.0))
    gradient = (summed / denom[:, None, None]).astype(jnp.bfloat16)
    grad_input = jnp.dot(dhidden16, down.T, preferred_element_type=f32).astype(jnp.bfloat16)
    return grad_input, gradient[:, None]


def solution(mesh):
    owners, cores = mesh.shape["dp"], mesh.shape["tensor"]

    def on_device(activations, cotangent, adapter_weight_pair, *rest):
        rows = adapter_weight_pair.shape[2]
        fits = owners == len(FETCH) + 1 and cores == 2 and rows % 256 == 0
        body = with_kernels if fits else without_kernels
        return body(activations, cotangent, adapter_weight_pair, *rest)

    in_specs = (
        P(("group", "dp"), "tensor"),
        P(("group", "dp"), "tensor"),
        P(None, "tensor", "dp", None),
        P("group", None),
        P("group", None),
    )
    out_specs = (P(("group", "dp"), "tensor"), P("group", "tensor", "dp", None))
    return jax.shard_map(
        on_device, mesh=mesh, in_specs=in_specs, out_specs=out_specs, check_vma=False
    )
```

```python
import functools

import jax
import jax.numpy as jnp
from jax import lax
from jax.experimental import pallas as pl
from jax.experimental.pallas import tpu as pltpu
from jax.sharding import PartitionSpec as P

adapter_alpha = 128.0
FETCH = (4, 1, 2, 5, 6, 3, 7)
FETCH_TIES = {}
SEND = (6, 1, 4, 2, 5, 3, 7)
SEND_TIES = {3: 6}
PREP_AFTER = 1
LATE = (5, 3, 7)
RANK_LAST = (3, 7)
SEND_FIRST = 1
FETCH_FIRST = 1

in_vmem = pl.BlockSpec(memory_space=pltpu.VMEM)
in_smem = pl.BlockSpec(memory_space=pltpu.SMEM)
in_hbm = pl.BlockSpec(memory_space=pltpu.HBM)


def low_lanes(rows, width):
    return lax.broadcasted_iota(jnp.int32, (rows, width), 1) < width // 2


def call(kernel, out_shape, in_specs, out_specs, scratch=(), flops=0, moved=0, aliases=None, vmem=40):
    return pl.pallas_call(
        kernel,
        out_shape=out_shape,
        in_specs=in_specs,
        out_specs=out_specs,
        scratch_shapes=list(scratch),
        input_output_aliases=aliases or {},
        compiler_params=pltpu.CompilerParams(vmem_limit_bytes=vmem * 1024 * 1024),
        cost_estimate=pl.CostEstimate(flops=flops, bytes_accessed=moved, transcendentals=0),
    )


def gather_kernel(peers, ids, here, table, *refs):
    out, sems = refs[: len(peers)], refs[len(peers)]
    copies = [
        pltpu.make_async_copy(table.at[ids[here[0] ^ k]], out[n], sems.at[n])
        for n, k in enumerate(peers)
    ]
    for copy in copies:
        copy.start()
    for copy in copies:
        copy.wait()


def prep_kernel(ids, here, lengths, table, after, x, y, turned, own, live, parts, blocks, blank, zeros, sem, own_sem):
    own_copy = pltpu.make_async_copy(table.at[ids[here[0]]], own, own_sem)
    own_copy.start()
    rows = own.shape[0]
    marked = lax.broadcasted_iota(jnp.int32, live.shape, 0) < lengths[here[0]]
    live[...] = jnp.where(marked, 1.0, 0.0)
    for n in range(ids.shape[0]):
        blocks[n] = ids[n]
        count = jnp.int32(0)
        for other in range(ids.shape[0]):
            count += jnp.where(ids[other] == ids[n], lengths[other], 0)
        denom = jnp.maximum(count.astype(jnp.float32), 1.0)
        parts[n : n + 1] = 1.0 / jnp.full((1, parts.shape[1]), denom)
    zeros[...] = jnp.zeros_like(zeros)
    step = zeros.shape[0]
    copies = [
        pltpu.make_async_copy(zeros, blank.at[pl.ds(s, step)], sem.at[s // step])
        for s in range(0, blank.shape[0], step)
    ]
    for copy in copies:
        copy.start()
    tokens = x.shape[0]

    @pl.loop(0, x.shape[1] // rows)
    def _(owner):
        columns = pl.ds(pl.multiple_of(owner * rows, rows), rows)
        turned[owner, :, pl.ds(0, tokens)] = x[:, columns].T
        turned[owner, :, pl.ds(tokens, tokens)] = y[:, columns].T

    for copy in [own_copy, *copies]:
        copy.wait()


def rank_kernel(peers, here, x, y, so_far, *refs):
    pairs, out = refs[: len(peers)], refs[len(peers)]
    rows, width = pairs[0].shape
    tokens = x.shape[0]
    x_rank = so_far[...]
    y_rank = x_rank
    for n, k in enumerate(peers):
        columns = pl.ds(pl.multiple_of((here[0] ^ k) * rows, rows), rows)
        x_rank += jnp.dot(x[:, columns], pairs[n][...], preferred_element_type=jnp.float32)
        y_rank += jnp.dot(y[:, columns], pairs[n][...], preferred_element_type=jnp.float32)
    out[...] = jnp.where(low_lanes(tokens, width), x_rank, y_rank)


def rounded(mine, other, live, scale):
    total = mine[...] + other[...]
    total = jnp.where(low_lanes(*total.shape), total, scale * total)
    return jnp.where(live[...] > 0.0, total, 0.0)


def swap_halves(value):
    return pltpu.roll(value, value.shape[-1] // 2, 1)


def piece_kernel(peers, scale, here, live, mine, other, turned, *refs):
    me = here[0]
    both = swap_halves(rounded(mine, other, live, scale))
    low = low_lanes(*both.shape)
    top = jnp.where(low, both, 0.0).astype(jnp.bfloat16)
    bottom = jnp.where(low, 0.0, both).astype(jnp.bfloat16)
    ranks = jnp.concatenate([top, bottom], axis=0)
    for n, k in enumerate(peers):
        piece = jnp.dot(turned[me ^ k], ranks, preferred_element_type=jnp.float32)
        refs[n][...] = jnp.where(low_lanes(*piece.shape), piece, scale * piece).astype(jnp.bfloat16)


def input_kernel(peers, scale, here, live, mine, other, *refs):
    pairs, out = refs[: len(peers)], refs[len(peers)]
    me = here[0]
    both = swap_halves(rounded(mine, other, live, scale))
    ranks = jnp.where(low_lanes(*both.shape), both, 0.0).astype(jnp.bfloat16)
    rows = pairs[0].shape[0]
    for n, k in enumerate(peers):
        columns = pl.ds(pl.multiple_of((me ^ k) * rows, rows), rows)
        out[:, columns] = lax.dot_general(
            ranks, pairs[n][...], (((1,), (1,)), ((), ())), preferred_element_type=jnp.float32
        ).astype(jnp.bfloat16)


def merge_kernel(peers, handled, others, blocks, here, parts, *refs):
    pieces = dict(zip(peers, refs[:-7]))
    out, total, held, sems, ids, ids_sem = refs[-6:]
    me = here[0]
    others_here = all(k in pieces for k in others)
    ids_copy = pltpu.make_async_copy(blocks, ids, ids_sem)
    ids_copy.start()

    def value(k):
        return pieces[k][...].astype(jnp.float32)

    def store(n, sum_of):
        held[n] = (sum_of * parts[pl.ds(me ^ handled[n], 1), :]).astype(jnp.bfloat16)

    def either(conditions):
        return functools.reduce(jnp.logical_or, conditions, jnp.bool_(False))

    for n, k in enumerate(handled):
        store(n, value(k))
    ids_copy.wait()
    copies, chosen = [], []
    for n, k in enumerate(handled):
        adapter = ids[me ^ k]
        copies.append(pltpu.make_async_copy(held.at[n], out.at[adapter], sems.at[n]))
        same = {other: ids[me ^ other] == adapter for other in (*handled, *others) if other != k}
        skip = either([same[other] for other in handled[:n]])
        adding = list(handled[n + 1 :])
        if others_here:
            adding += others
        else:
            skip |= either([same[other] for other in others])
        more = either([same[other] for other in adding])
        chosen.append(jnp.logical_not(skip))

        @pl.when(chosen[n] & more)
        def _():
            total[...] = value(k)
            for other in adding:

                @pl.when(same[other])
                def _():
                    total[...] += value(other)

            store(n, total[...])

        pl.when(chosen[n])(copies[n].start)

    for n in range(len(handled)):
        pl.when(chosen[n])(copies[n].wait)


def exchange(pieces, ties):
    owners = lax.axis_size("dp")
    out = {}
    for k in sorted(pieces, key=lambda k: k in ties):
        piece = lax.optimization_barrier((pieces[k], out[ties[k]]))[0] if k in ties else pieces[k]
        out[k] = lax.ppermute(piece, "dp", [(i, i ^ k) for i in range(owners)])
    return {k: out[k] for k in pieces}


def across_cores(value):
    cores = lax.axis_size("tensor")
    return lax.ppermute(value, "tensor", [(i, i ^ 1) for i in range(cores)])


def with_kernels(activations, cotangent, adapter_weight_pair, adapter_of_block, block_live_length):
    owners = lax.axis_size("dp")
    here = lax.axis_index("dp").astype(jnp.int32).reshape(1)
    ids, lengths = adapter_of_block[:, 0], block_live_length[:, 0]
    count, _, rows, width = adapter_weight_pair.shape
    table = adapter_weight_pair.reshape(count, rows, width)
    tokens, features = activations.shape
    scale = adapter_alpha / (width // 2)
    bf16, f32 = jnp.bfloat16, jnp.float32
    straight = jax.ShapeDtypeStruct((rows, width), bf16)
    pair_bytes = owners * rows * width * 2
    token_bytes = tokens * features * 2

    sent, me = [], here
    for part in (FETCH[:FETCH_FIRST], FETCH[FETCH_FIRST:]):
        sent += call(
            functools.partial(gather_kernel, part),
            [straight] * len(part),
            [in_smem, in_smem, in_hbm],
            [in_vmem] * len(part),
            [pltpu.SemaphoreType.DMA((len(part),))],
            moved=1024,
            vmem=53,
        )(ids, me, table)
        me = lax.optimization_barrier((here, *sent))[0]
    pairs = exchange(dict(zip(FETCH, sent)), FETCH_TIES)

    step = 8
    turned, own, live, parts, blocks, blank = call(
        prep_kernel,
        [
            jax.ShapeDtypeStruct((owners, rows, 2 * tokens), bf16),
            straight,
            jax.ShapeDtypeStruct((tokens, width), f32),
            jax.ShapeDtypeStruct((owners, width), f32),
            jax.ShapeDtypeStruct((owners,), jnp.int32),
            jax.ShapeDtypeStruct(table.shape, bf16),
        ],
        [in_smem, in_smem, in_smem, in_hbm, in_hbm, in_vmem, in_vmem],
        [in_vmem, in_vmem, in_vmem, in_vmem, in_smem, in_hbm],
        [
            pltpu.VMEM((step, rows, width), bf16),
            pltpu.SemaphoreType.DMA((count // step,)),
            pltpu.SemaphoreType.DMA,
        ],
        moved=4 * token_bytes + 2 * count * rows * width,
    )(ids, here, lengths, table, pairs[PREP_AFTER], activations, cotangent)
    pairs[0] = own

    mine = jnp.zeros((tokens, width), f32)
    for part in ([k for k in pairs if k not in RANK_LAST], RANK_LAST):
        mine = call(
            functools.partial(rank_kernel, tuple(part)),
            jax.ShapeDtypeStruct((tokens, width), f32),
            [in_smem] + [in_vmem] * (3 + len(part)),
            in_vmem,
            moved=1024,
        )(here, lax.optimization_barrier((activations, turned))[0], cotangent, mine, *[pairs[k] for k in part])
    other = across_cores(mine)

    peers = (*SEND, 0)
    pieces = []
    for part in (peers[:SEND_FIRST], peers[SEND_FIRST:]):
        pieces += call(
            functools.partial(piece_kernel, part, scale),
            [straight] * len(part),
            [in_smem] + [in_vmem] * 4,
            [in_vmem] * len(part),
            moved=1024,
        )(here, live, mine, other, turned)
    arrived = exchange(dict(zip(SEND, pieces)), SEND_TIES)
    arrived[0] = pieces[-1]

    grad_input = call(
        functools.partial(input_kernel, tuple(pairs), scale),
        jax.ShapeDtypeStruct((tokens, features), bf16),
        [in_smem] + [in_vmem] * (3 + owners),
        in_vmem,
        flops=2 * tokens * features * width,
        moved=token_bytes + pair_bytes,
    )(here, live, lax.optimization_barrier((mine, *pieces))[0], other, *pairs.values())

    late = tuple(k for k in peers if k in LATE)
    early = tuple(k for k in peers if k not in LATE)

    def merge(handled, others, merged, so_far):
        return call(
            functools.partial(merge_kernel, tuple(merged), handled, others),
            jax.ShapeDtypeStruct(table.shape, bf16),
            [in_hbm, in_smem, in_vmem] + [in_vmem] * len(merged) + [in_hbm],
            in_hbm,
            [
                pltpu.VMEM((rows, width), f32),
                pltpu.VMEM((len(handled), rows, width), bf16),
                pltpu.SemaphoreType.DMA((len(handled),)),
                pltpu.SMEM((owners,), jnp.int32),
                pltpu.SemaphoreType.DMA,
            ],
            moved=2 * pair_bytes,
            aliases={3 + len(merged): 0},
        )(blocks, here, parts, *merged.values(), so_far)

    early_pieces = {k: arrived[k] for k in early}
    gradient = merge(late, early, arrived, merge(early, late, early_pieces, blank))
    return grad_input, gradient[:, None]


def without_kernels(activations, cotangent, adapter_weight_pair, adapter_of_block, block_live_length):
    owners = lax.axis_size("dp")
    here = lax.axis_index("dp")
    count, _, rows, width = adapter_weight_pair.shape
    rank = width // 2
    scale = adapter_alpha / rank
    adapters = adapter_of_block[:, 0]
    lengths = block_live_length[:, 0]
    keep = (jnp.arange(activations.shape[0], dtype=jnp.int32) < lengths[here])[:, None]
    inputs = jnp.where(keep, activations, jnp.zeros_like(activations))
    grads_out = jnp.where(keep, cotangent, jnp.zeros_like(cotangent))
    fetched = lax.all_to_all(
        adapter_weight_pair[:, 0][adapters], "dp", split_axis=0, concat_axis=0, tiled=True
    )
    pair = fetched.reshape(-1, width)
    down, upward = pair[:, :rank], pair[:, rank:]
    f32 = jnp.float32
    hidden_part = jnp.dot(inputs, down, preferred_element_type=f32)
    dhidden_part = scale * jnp.dot(grads_out, upward, preferred_element_type=f32)
    hidden, dhidden = lax.psum((hidden_part, dhidden_part), "tensor")
    hidden16, dhidden16 = hidden.astype(jnp.bfloat16), dhidden.astype(jnp.bfloat16)
    d_down = jnp.dot(inputs.T, dhidden16, preferred_element_type=f32)
    d_up = scale * jnp.dot(grads_out.T, hidden16, preferred_element_type=f32)
    sent = jnp.concatenate([d_down, d_up], axis=1).astype(jnp.bfloat16).reshape(owners, rows, width)
    received = lax.all_to_all(sent, "dp", split_axis=0, concat_axis=0, tiled=True).astype(f32)
    same = adapters[:, None] == adapters[None, :]
    total = jnp.sum(jnp.where(same, lengths[None, :], 0), axis=1).astype(f32)
    summed = jax.ops.segment_sum(received, adapters, num_segments=count)
    denom = jnp.ones((count,), f32).at[adapters].set(jnp.maximum(total, 1.0))
    gradient = (summed / denom[:, None, None]).astype(jnp.bfloat16)
    grad_input = jnp.dot(dhidden16, down.T, preferred_element_type=f32).astype(jnp.bfloat16)
    return grad_input, gradient[:, None]


def solution(mesh):
    owners, cores = mesh.shape["dp"], mesh.shape["tensor"]

    def on_device(activations, cotangent, adapter_weight_pair, *rest):
        rows = adapter_weight_pair.shape[2]
        fits = owners == len(FETCH) + 1 and cores == 2 and rows % 256 == 0
        body = with_kernels if fits else without_kernels
        return body(activations, cotangent, adapter_weight_pair, *rest)

    in_specs = (
        P(("group", "dp"), "tensor"),
        P(("group", "dp"), "tensor"),
        P(None, "tensor", "dp", None),
        P("group", None),
        P("group", None),
    )
    out_specs = (P(("group", "dp"), "tensor"), P("group", "tensor", "dp", None))
    return jax.shard_map(
        on_device, mesh=mesh, in_specs=in_specs, out_specs=out_specs, check_vma=False
    )
```
